32 devices in a mesh: groups: 2 (over x), space: 16 (over z, y, core).
Axes of the slice: x: 2, y: 2, z: 4, core: 2. Of those that a mesh axis runs over, the one named last changes fastest.
Arguments:
- volume: bfloat16 [64, 64, 32, 64], P(('groups', 'space')), parts along dimension 0, may hold values from -6 to 6
- weight_one: bfloat16 [3, 3, 3, 64, 64], replicated, may hold values from -0.15625 to 0.15625
- weight_two: bfloat16 [3, 3, 3, 64, 128], replicated, may hold values from -0.15625 to 0.15625
- cotangent: bfloat16 [64, 64, 32, 128], P(('groups', 'space')), parts along dimension 0, may hold values from -6 to 6
Outputs:
- output: float32 [64, 64, 32, 128], P(('groups', 'space')), parts along dimension 0
- grad_volume: float32 [64, 64, 32, 64], P(('groups', 'space')), parts along dimension 0
- grad_one: float32 [6, 3, 3, 64, 64], P('groups', None, None, None, 'space'), parts along dimension 0
- grad_two: float32 [6, 3, 3, 64, 128], P('groups', None, None, None, 'space'), parts along dimension 0
The draws below stay inside these ranges and needn't reach their ends.
There are 2 independent parts, one for each index of `groups`. The reference program is written for one: setup_inputs(seed, part) draws one part's arguments, and reference() takes and returns one part's arrays. A program takes and returns all parts, laid end to end along the dimension named above; an argument that names none is the same for every part. Nothing has to cross between parts.
All inputs are finite; a program needn't handle non-finite values.
Results may differ from the reference program's by a relative error of at most 0.0029.
Values may be sent and summed in bfloat16 or wider, within the bound.
No kernel may reach another device: no remote copies, remote signals or barrier semaphores. Data moves between devices by JAX's collectives and lax.ppermute only.
A program may use at most 64 MiB of HBM per device.

```python
import math
import jax
import jax.numpy as jnp
from jax import lax

CH_IN = 64
CH_MID = 64
CH_OUT = 128
HEIGHT = 64
WIDTH = 32
DEPTH = 32
CELLS = 65536


def raised(result, own_key, source, target, parts, factor):
    owner, partner = [(jnp.arange(result.shape[dim]) // (result.shape[dim] // parts)).reshape([-1 if axis == dim else 1 for axis in range(result.ndim)]) for dim in (source, target)]
    chosen = jax.random.permutation(own_key, parts)[partner]
    strong = (owner == chosen) | (owner == (partner + parts // 2) % parts)
    return jnp.where(strong, factor * result, result)


def block_levels(key, extent, cuts, smallest, top_value):
    def one(axis_at, blocks):
        heights = jax.random.uniform(jax.random.fold_in(jax.random.fold_in(key, 6), axis_at), (blocks,), jnp.float32, smallest / len(cuts), top_value / len(cuts))
        return jnp.repeat(jnp.exp(heights), extent[axis_at] // blocks).reshape((-1,) + (1,) * (len(extent) - axis_at - 1))

    loudness = one(*cuts[0])
    for cut in cuts[1:]:
        loudness = loudness * one(*cut)
    return loudness


def scatter_about(key, extent, spread, limit, cuts=(), kind=jnp.bfloat16):
    array = spread * jax.random.normal(key, extent, jnp.float32)
    if cuts:
        array = array * block_levels(key, extent, cuts, -0.22, 0.18)
    return jnp.clip(array, -limit, limit).astype(kind)


def gaussian_with(rng, shape, scale, reach, cuts, heavy, kind=jnp.bfloat16):
    values = scale * jax.random.normal(rng, shape, jnp.float32)
    if cuts:
        values = values * block_levels(rng, shape, cuts, -0.22, 0.18)
    return jnp.clip(raised(values, jax.random.fold_in(rng, 3), *heavy), -reach, reach).astype(kind)


def setup_inputs(seed: int = 0, part: int = 0) -> dict:
    key_of = jax.random.split(jax.random.key(seed), 5)
    part_keys = jax.random.split(jax.random.fold_in(key_of[4], part), 5)
    volume = scatter_about(part_keys[0], (DEPTH, HEIGHT, WIDTH, CH_IN), 1.0, 6.0, ((0, 16),))
    weight_one = scatter_about(key_of[1], (3, 3, 3, CH_IN, CH_MID), (27 * CH_IN) ** -0.5, 0.15625)
    weight_two = scatter_about(key_of[2], (3, 3, 3, CH_MID, CH_OUT), (27 * CH_MID) ** -0.5, 0.15625)
    cotangent = gaussian_with(part_keys[3], (DEPTH, HEIGHT, WIDTH, CH_OUT), 1.0, 6.0, ((0, 16),), (0, 3, 16, 2.0))
    return dict(volume=volume, weight_one=weight_one, weight_two=weight_two, cotangent=cotangent)


def pad_cells(field):
    return jnp.pad(field, ((1, 1), (1, 1), (1, 1), (0, 0)))

def conv_valid(padded, kernel):
    return lax.conv_general_dilated(padded[None], kernel, (1, 1, 1), 'VALID', dimension_numbers=('NDHWC', 'DHWIO', 'NDHWC'), precision=lax.Precision.HIGHEST)[0]

def flipped(kernel):
    return jnp.transpose(kernel[::-1, ::-1, ::-1], (0, 1, 2, 4, 3))

def kernel_terms(padded, grad_field):
    depth_len, rows_len, cols_len = (grad_field.shape[0], grad_field.shape[1], grad_field.shape[2])
    flat_grad = grad_field.reshape(-1, grad_field.shape[3])
    results = []
    for depth_tap in range(3):
        for row_tap in range(3):
            for column_tap in range(3):
                window = padded[depth_tap:depth_tap + depth_len, row_tap:row_tap + rows_len, column_tap:column_tap + cols_len]
                results.append(lax.dot_general(window.reshape(-1, padded.shape[3]), flat_grad, (((0,), (0,)), ((), ())), precision=lax.Precision.HIGHEST))
    return jnp.stack(results).reshape(3, 3, 3, padded.shape[3], grad_field.shape[3])

def reference(volume, weight_one, weight_two, cotangent):
    inputs = volume.astype(jnp.float32)
    kernel_one = weight_one.astype(jnp.float32)
    kernel_two = weight_two.astype(jnp.float32)
    grad_out = cotangent.astype(jnp.float32)
    hidden = conv_valid(pad_cells(inputs), kernel_one)
    sigmoid_hidden = jax.nn.sigmoid(hidden)
    activation = (hidden * sigmoid_hidden).astype(jnp.bfloat16).astype(jnp.float32)
    output = conv_valid(pad_cells(activation), kernel_two)
    grad_act = conv_valid(pad_cells(grad_out), flipped(kernel_two))
    grad_hidden = (grad_act * sigmoid_hidden * (1.0 + hidden * (1.0 - sigmoid_hidden))).astype(jnp.bfloat16).astype(jnp.float32)
    grad_volume = conv_valid(pad_cells(grad_hidden), flipped(kernel_one))
    scale = 1.0 / math.sqrt(CELLS)
    grad_one = kernel_terms(pad_cells(inputs), grad_hidden) * scale
    grad_two = kernel_terms(pad_cells(activation), grad_out) * scale
    return (output, grad_volume, grad_one, grad_two)
```

```python
import functools
import math

import jax
import jax.numpy as jnp
from jax import lax
from jax.experimental import pallas as pl
from jax.experimental.pallas import tpu as pltpu
from jax.sharding import PartitionSpec as P

F32, BF16 = jnp.float32, jnp.bfloat16
STEP = 256
VMEM_LIMIT = 48 * 2**20
NT = (((1,), (1,)), ((), ()))

ENTER = ((1, 2, 0, None), (0, 1, None, 2))
LEAVE = ((1, 2), (0, 1), (2, None), (None, 0))


def call(body, outs, ins, scratch=(), flops=0, name=None, smem=()):
    moved = sum(math.prod(s.shape) * s.dtype.itemsize for s in (*outs, *ins))
    return pl.pallas_call(
        body,
        out_shape=list(outs),
        in_specs=[
            pl.BlockSpec(memory_space=pltpu.SMEM if i in smem else pltpu.VMEM)
            for i in range(len(ins))
        ],
        out_specs=[pl.BlockSpec(memory_space=pltpu.VMEM)] * len(outs),
        scratch_shapes=list(scratch),
        compiler_params=pltpu.CompilerParams(vmem_limit_bytes=VMEM_LIMIT),
        cost_estimate=pl.CostEstimate(flops=flops, bytes_accessed=moved, transcendentals=0),
        name=name,
    )(*ins)


def lanes_low(x):
    return lax.broadcasted_iota(jnp.int32, x.shape, 1) < 64


def swap(x):
    return pltpu.roll(x, 64, 1)


def pick(low, high):
    return jnp.where(lanes_low(low), low, high)


def fill_windows(windows, start, lane, chunk, columns, stride):
    size = chunk.shape[0]
    column = lax.broadcasted_iota(jnp.int32, chunk.shape, 0) % columns
    before = jnp.where(column == 0, 0.0, pltpu.roll(chunk, 1, 0))
    after = jnp.where(column == columns - 1, 0.0, pltpu.roll(chunk, size - 1, 0))
    at = pl.ds(pl.multiple_of(columns + start, 32), size)
    for tap, part in enumerate((before, chunk, after)):
        first = tap * stride + lane
        windows[at, first : first + chunk.shape[1]] = part.astype(BF16)


def clear_edges(windows, columns):
    rows, lanes = windows.shape
    windows[0:columns, :] = jnp.zeros((columns, lanes), BF16)
    windows[rows - columns : rows, :] = jnp.zeros((columns, lanes), BF16)


def four_planes(windows, own, below, above, columns):
    half = own.shape[0] // 2

    def step(i, carry):
        start = pl.multiple_of(i * STEP, STEP)
        low, high = pl.ds(start, STEP), pl.ds(start + half, STEP)
        fill_windows(windows, start, 0, own[low, :].astype(F32), columns, 256)
        fill_windows(windows, start + half, 0, own[high, :].astype(F32), columns, 256)
        from_below, from_above = below[low, :].astype(F32), above[low, :].astype(F32)
        fill_windows(windows, start, 128, pick(from_below, swap(from_above)), columns, 256)
        fill_windows(windows, start + half, 128, pick(swap(from_below), from_above), columns, 256)
        return carry

    clear_edges(windows, columns)
    lax.fori_loop(0, half // STEP, step, 0)


def window_dot(windows, weights, start, columns, dims):
    total = None
    for tap in range(3):
        rows = pl.ds(pl.multiple_of(start + tap * columns, 32), STEP)
        term = lax.dot_general(windows[rows, :], weights[tap], dims, preferred_element_type=F32)
        total = term if total is None else total + term
    return total


def packed(low, high):
    return pick(low, swap(high)), pick(swap(low), high)


def pack_body(volume, own, up, down):
    cells = own.shape[0]
    half = cells // 2

    def step(i, carry):
        start = pl.multiple_of(i * STEP, STEP)
        low, high = pl.ds(start, STEP), pl.ds(start + half, STEP)
        pairs = []
        for rows in (low, high):
            pair = jnp.concatenate([volume[0, rows, :], volume[1, rows, :]], axis=1)
            own[rows, :] = pair
            pairs.append(pair.astype(F32))
        first, second = packed(*pairs)
        down[low, :] = first.astype(BF16)
        up[low, :] = second.astype(BF16)
        return carry

    lax.fori_loop(0, half // STEP, step, 0)


def leave_body(columns, cotangent, weight, own, up, down, windows, taps):
    half = cotangent.shape[1] // 2
    for row in range(3):
        for plane, enters in enumerate(LEAVE):
            for column in range(3):
                for source, depth in enumerate(enters):
                    first = column * 256 + source * 128
                    taps[row, plane * 64 : plane * 64 + 64, first : first + 128] = (
                        jnp.zeros((64, 128), BF16)
                        if depth is None
                        else weight[(2 - depth) * 9 + (2 - row) * 3 + 2 - column]
                    )

    def fill(i, carry):
        start = pl.multiple_of(i * STEP, STEP)
        for plane in range(2):
            chunk = cotangent[plane, pl.ds(start, STEP), :].astype(F32)
            fill_windows(windows, start, plane * 128, chunk, columns, 256)
        return carry

    clear_edges(windows, columns)
    lax.fori_loop(0, 2 * half // STEP, fill, 0)

    def step(i, carry):
        start = pl.multiple_of(i * STEP, STEP)
        sides = []
        for first in (start, start + half):
            term = window_dot(windows, taps, first, columns, NT)
            own[pl.ds(first, STEP), :] = term[:, :128]
            sides.append(term[:, 128:])
        lower, upper = packed(*sides)
        down[pl.ds(start, STEP), :] = lower.astype(BF16)
        up[pl.ds(start, STEP), :] = upper.astype(BF16)
        return carry

    lax.fori_loop(0, half // STEP, step, 0)


def hidden_body(columns, own, below, above, weight, activation, up, down, slope, windows, taps):
    half = own.shape[0] // 2
    zero = jnp.zeros((64, 64), BF16)
    for row in range(3):
        for column in range(3):
            for source in range(4):
                first = column * 256 + source * 64
                pair = [
                    zero if ENTER[plane][source] is None
                    else weight[ENTER[plane][source] * 9 + row * 3 + column]
                    for plane in range(2)
                ]
                taps[row, first : first + 64, :] = jnp.concatenate(pair, axis=1)
    four_planes(windows, own, below, above, columns)

    def step(i, carry):
        start = pl.multiple_of(i * STEP, STEP)
        sides = []
        for first in (start, start + half):
            hidden = window_dot(windows, taps, first, columns, (((1,), (0,)), ((), ())))
            gate = jax.nn.sigmoid(hidden)
            act = (hidden * gate).astype(BF16)
            activation[pl.ds(first, STEP), :] = act
            slope[pl.ds(first, STEP), :] = gate * (1.0 + hidden * (1.0 - gate))
            sides.append(act.astype(F32))
        lower, upper = packed(*sides)
        down[pl.ds(start, STEP), :] = lower.astype(BF16)
        up[pl.ds(start, STEP), :] = upper.astype(BF16)
        return carry

    lax.fori_loop(0, half // STEP, step, 0)


def slope_body(terms, below, above, slope, grad, up, down):
    half = terms.shape[0] // 2

    def step(i, carry):
        start = pl.multiple_of(i * STEP, STEP)
        low, high = pl.ds(start, STEP), pl.ds(start + half, STEP)
        from_below, from_above = below[low, :].astype(F32), above[low, :].astype(F32)
        arrived = (pick(from_below, swap(from_above)), pick(swap(from_below), from_above))
        sides = []
        for rows, extra in zip((low, high), arrived):
            value = ((terms[rows, :] + extra) * slope[rows, :]).astype(BF16)
            grad[rows, :] = value
            sides.append(value.astype(F32))
        lower, upper = packed(*sides)
        down[low, :] = lower.astype(BF16)
        up[low, :] = upper.astype(BF16)
        return carry

    lax.fori_loop(0, half // STEP, step, 0)


def kernel_terms(columns, out_channels, windows, turned, terms):
    cells = turned.shape[1]
    for row in range(3):
        for column in range(3):
            tap = row * 3 + column
            product = jnp.dot(
                turned[...],
                windows[row * columns : row * columns + cells, column * 256 : column * 256 + 256],
                preferred_element_type=F32,
            )
            first, second = product[:out_channels], product[out_channels:]
            terms[:, tap * 128 : tap * 128 + 128] = first[:, :128] + pick(
                swap(second[:, :128]), second[:, 128:]
            )
            zeroth = first[:, 128:] + second[:, :128]
            group = 9 + tap // 2
            here = slice(group * 128, group * 128 + 128)
            if tap % 2 == 0:
                terms[:, here] = zeroth
            else:
                terms[:, here] = pick(terms[:, here], swap(zeroth))


def turn(source, target, first):
    for start in range(0, source.shape[0], STEP):
        chunk = source[start : start + STEP, :].astype(F32)
        target[first : first + chunk.shape[1], start : start + STEP] = chunk.T.astype(BF16)


def grad_one_body(columns, own, below, above, grad, terms, windows, turned):
    four_planes(windows, own, below, above, columns)
    turn(grad, turned, 0)
    kernel_terms(columns, 64, windows, turned, terms)


def grad_two_body(
    columns, count, me, own, below, above, cotangent, other, sent, kept, windows, turned, terms
):
    four_planes(windows, own, below, above, columns)
    turn(cotangent.at[0], turned, 0)
    turn(cotangent.at[1], turned, 128)
    kernel_terms(columns, 128, windows, turned, terms)
    half = terms.shape[1] // 2
    odd = me[0] % 2 == 1

    def share(owner):
        parts = []
        for source in (other, terms):
            each = source.shape[0] // count
            block = source[owner * each : owner * each + each, :]
            parts += [block[:, :half], block[:, half:]]
        return jnp.concatenate(parts, axis=0)

    for pair in range(count // 2):
        even_share, odd_share = share(2 * pair), share(2 * pair + 1)
        sent[pair] = jnp.where(odd, even_share, odd_share).astype(BF16)
        kept[pair] = jnp.where(odd, odd_share, even_share)


def halve_body(me, mine, arrived, sent, kept):
    odd = (me[0] // 2) % 2
    for pair in range(sent.shape[0]):
        keep, give = 2 * pair + odd, 2 * pair + 1 - odd
        sent[pair] = (mine[give] + arrived[give].astype(F32)).astype(BF16)
        kept[pair] = mine[keep] + arrived[keep].astype(F32)


def finish_body(scale, sizes, mine, *refs):
    arrived, (grad_one, grad_two) = refs[:-2], refs[-2:]
    total = mine[...]
    for part in arrived:
        total = total + part[...].astype(F32)
    total = total * scale
    half = total.shape[1]
    first = 0
    for size, out in zip(sizes, (grad_one, grad_two)):
        blocks = (total[first : first + size], total[first + size : first + 2 * size])
        first += 2 * size
        for tap in range(9):
            for depth, group, side in ((0, 9 + tap // 2, tap % 2), (1, tap, 0), (2, tap, 1)):
                lane = group * 128 + side * 64
                block, lane = (blocks[0], lane) if lane < half else (blocks[1], lane - half)
                out[depth * 9 + tap] = block[:, lane : lane + 64]


def output_body(columns, own, below, above, weight, output, windows, taps):
    for row in range(3):
        for column in range(3):
            for source in range(4):
                first = column * 256 + source * 64
                for plane in range(2):
                    depth = ENTER[plane][source]
                    taps[row, first : first + 64, plane * 128 : plane * 128 + 128] = (
                        jnp.zeros((64, 128), BF16)
                        if depth is None
                        else weight[depth * 9 + row * 3 + column]
                    )
    four_planes(windows, own, below, above, columns)

    def step(i, carry):
        start = pl.multiple_of(i * STEP, STEP)
        value = window_dot(windows, taps, start, columns, (((1,), (0,)), ((), ())))
        output[0, pl.ds(start, STEP), :] = value[:, :128]
        output[1, pl.ds(start, STEP), :] = value[:, 128:]
        return carry

    lax.fori_loop(0, own.shape[0] // STEP, step, 0)


def grad_volume_body(columns, own, below, above, weight, output, windows, taps):
    zero = jnp.zeros((64, 64), BF16)
    for row in range(3):
        for column in range(3):
            for plane in range(2):
                pieces = [
                    zero if depth is None
                    else weight[(2 - depth) * 9 + (2 - row) * 3 + 2 - column]
                    for depth in ENTER[plane]
                ]
                for pair in range(2):
                    first = column * 256 + pair * 128
                    taps[row, plane * 64 : plane * 64 + 64, first : first + 128] = (
                        jnp.concatenate(pieces[2 * pair : 2 * pair + 2], axis=1)
                    )
    four_planes(windows, own, below, above, columns)

    def step(i, carry):
        start = pl.multiple_of(i * STEP, STEP)
        value = window_dot(windows, taps, start, columns, NT)
        output[0, pl.ds(start, STEP), :] = value[:, :64]
        output[1, pl.ds(start, STEP), :] = value[:, 64:]
        return carry

    lax.fori_loop(0, own.shape[0] // STEP, step, 0)


def shards(volume, weight_one, weight_two, cotangent):
    count = lax.axis_size("space")
    planes, rows, columns, channels = volume.shape
    cells = rows * columns
    scale = 1.0 / math.sqrt(planes * count * cells)
    mid, wide = weight_two.shape[3], weight_two.shape[4]
    me = lax.axis_index("space").astype(jnp.int32).reshape(1)
    shape = jax.ShapeDtypeStruct
    flat, pack = shape((cells, 128), BF16), shape((cells // 2, 128), BF16)
    windows = pltpu.VMEM((cells + 2 * columns, 768), BF16)
    lanes = 14 * 64
    chunk = 2 * (mid + wide) // count

    def upward(x):
        return lax.ppermute(x, "space", [(i, i + 1) for i in range(count - 1)])

    def downward(x):
        return lax.ppermute(x, "space", [(i + 1, i) for i in range(count - 1)])

    volume = volume.reshape(planes, cells, channels)
    cotangent = cotangent.reshape(planes, cells, wide)
    weight_one = weight_one.reshape(27, channels, mid)
    weight_two = weight_two.reshape(27, mid, wide)
    one_flops = 2 * planes * cells * 27 * channels * mid
    two_flops = 2 * planes * cells * 27 * mid * wide

    own, up, down = call(pack_body, (flat, pack, pack), (volume,), name="pack_volume")
    vol_halo = (upward(up), downward(down))
    terms, up, down = call(
        functools.partial(leave_body, columns),
        (shape((cells, 128), F32), pack, pack),
        (cotangent, weight_two),
        (windows, pltpu.VMEM((3, 256, 768), BF16)),
        two_flops, "grad_act_terms",
    )
    act_terms_halo = (upward(up), downward(down))
    activation, up, down, slope = call(
        functools.partial(hidden_body, columns),
        (flat, pack, pack, shape((cells, 128), F32)),
        (own, *vol_halo, weight_one),
        (windows, pltpu.VMEM((3, 768, 128), BF16)),
        one_flops, "hidden",
    )
    act_halo = (upward(up), downward(down))
    grad_hidden, up, down = call(
        slope_body, (flat, pack, pack), (terms, *act_terms_halo, slope), name="grad_hidden"
    )
    grad_halo = (upward(up), downward(down))
    terms_one, = call(
        functools.partial(grad_one_body, columns),
        (shape((mid, 2 * lanes), F32),),
        (own, *vol_halo, grad_hidden),
        (windows, pltpu.VMEM((128, cells), BF16)),
        one_flops, "grad_one_terms",
    )
    sent, kept = call(
        functools.partial(grad_two_body, columns, count),
        (shape((count // 2, chunk, lanes), BF16), shape((count // 2, chunk, lanes), F32)),
        (me, activation, *act_halo, cotangent, terms_one),
        (windows, pltpu.VMEM((256, cells), BF16), pltpu.VMEM((wide, 2 * lanes), F32)),
        two_flops, "grad_two_terms", (0,),
    )
    arrived = lax.ppermute(sent, "space", [(i, i ^ 1) for i in range(count)])
    output, = call(
        functools.partial(output_body, columns),
        (shape((planes, cells, wide), F32),),
        (activation, *act_halo, weight_two),
        (windows, pltpu.VMEM((3, 768, 256), BF16)),
        two_flops, "output",
    )
    sent, kept = call(
        halve_body,
        (shape((count // 4, chunk, lanes), BF16), shape((count // 4, chunk, lanes), F32)),
        (me, kept, arrived), name="halve", smem=(0,),
    )
    arrived = lax.ppermute(sent, "space", [(i, i ^ 2) for i in range(count)])
    grad_volume, = call(
        functools.partial(grad_volume_body, columns),
        (shape((planes, cells, channels), F32),),
        (grad_hidden, *grad_halo, weight_one),
        (windows, pltpu.VMEM((3, 128, 768), BF16)),
        one_flops, "grad_volume",
    )
    summed = kept + arrived.astype(F32)
    ring = count // 4
    place = lax.axis_index("space") // 4
    rest = []
    for hop in range(1, ring):
        part = lax.dynamic_index_in_dim(summed, (place + hop) % ring, 0, False).astype(BF16)
        rest.append(lax.ppermute(part, "space", [(i, (i + 4 * hop) % count) for i in range(count)]))
    mine = lax.dynamic_index_in_dim(summed, place, 0, False)
    grad_one, grad_two = call(
        functools.partial(finish_body, scale, (mid // count, wide // count)),
        (shape((27, mid // count, channels), F32), shape((27, wide // count, mid), F32)),
        (mine, *rest), name="finish",
    )
    return (
        output.reshape(planes, rows, columns, wide),
        grad_volume.reshape(planes, rows, columns, channels),
        jnp.swapaxes(grad_one, 1, 2).reshape(3, 3, 3, channels, mid // count),
        jnp.swapaxes(grad_two, 1, 2).reshape(3, 3, 3, mid, wide // count),
    )


def solution(mesh):
    cells = P(("groups", "space"), None, None, None)
    kernel = P("groups", None, None, None, "space")
    return jax.shard_map(
        shards,
        mesh=mesh,
        in_specs=(cells, P(), P(), cells),
        out_specs=(cells, cells, kernel, kernel),
        check_vma=False,
    )
```

```python
import functools
import math

import jax
import jax.numpy as jnp
from jax import lax
from jax.experimental import pallas as pl
from jax.experimental.pallas import tpu as pltpu
from jax.sharding import PartitionSpec as P

F32, BF16 = jnp.float32, jnp.bfloat16
STEP, BLOCK = 256, 512
VMEM_LIMIT = 24 * 2**20
NN = (((1,), (0,)), ((), ()))
NT = (((1,), (1,)), ((), ()))

PLANES = (0, 1, 2, -1, -2, 3)


def depth_tap(source, target):
    tap = source - target + 1
    return tap if 0 <= tap <= 2 else None


def call(body, outs, ins, scratch=(), flops=0, name=None, smem=()):
    moved = sum(math.prod(s.shape) * s.dtype.itemsize for s in (*outs, *ins))
    return pl.pallas_call(
        body,
        out_shape=list(outs),
        in_specs=[
            pl.BlockSpec(memory_space=pltpu.SMEM if i in smem else pltpu.VMEM)
            for i in range(len(ins))
        ],
        out_specs=[pl.BlockSpec(memory_space=pltpu.VMEM)] * len(outs),
        scratch_shapes=list(scratch),
        compiler_params=pltpu.CompilerParams(vmem_limit_bytes=VMEM_LIMIT),
        cost_estimate=pl.CostEstimate(flops=flops, bytes_accessed=moved, transcendentals=0),
        name=name,
    )(*ins)


def lanes_low(x):
    return lax.broadcasted_iota(jnp.int32, x.shape, 1) < 64


def swap(x):
    return pltpu.roll(x, 64, 1)


def pick(low, high):
    return jnp.where(lanes_low(low), low, high)


def fill_windows(windows, start, lane, chunk, columns, stride):
    size = chunk.shape[0]
    column = lax.broadcasted_iota(jnp.int32, chunk.shape, 0) % columns
    before = jnp.where(column == 0, 0.0, pltpu.roll(chunk, 1, 0))
    after = jnp.where(column == columns - 1, 0.0, pltpu.roll(chunk, size - 1, 0))
    at = pl.ds(pl.multiple_of(columns + start, 32), size)
    for tap, part in enumerate((before, chunk, after)):
        first = tap * stride + lane
        windows[at, first : first + chunk.shape[1]] = part.astype(BF16)


def clear_edges(windows, columns):
    rows, lanes = windows.shape
    windows[0:columns, :] = jnp.zeros((columns, lanes), BF16)
    windows[rows - columns : rows, :] = jnp.zeros((columns, lanes), BF16)


def window_dot(windows, weights, start, columns, dims):
    rows = jnp.concatenate(
        [windows[start + tap * columns : start + tap * columns + BLOCK, :] for tap in range(3)],
        axis=1,
    )
    return lax.dot_general(rows, weights[...], dims, preferred_element_type=F32)


def packed(low, high):
    return pick(low, swap(high)), pick(swap(low), high)


def unpacked(first, second):
    return packed(first, second)


def pack_body(volume, own):
    def step(i, carry):
        rows = pl.ds(pl.multiple_of(i * STEP, STEP), STEP)
        own[rows, :] = jnp.concatenate([volume[0, rows, :], volume[1, rows, :]], axis=1)
        return carry

    lax.fori_loop(0, own.shape[0] // STEP, step, 0)


def leave_body(columns, cotangent, weight, own, up, down, windows, taps):
    half = cotangent.shape[1] // 2
    for row in range(3):
        for column in range(3):
            for source in range(2):
                first = row * 768 + column * 256 + source * 128
                for at, target in enumerate(PLANES[:4]):
                    depth = depth_tap(source, target)
                    taps[at * 64 : at * 64 + 64, first : first + 128] = (
                        jnp.zeros((64, 128), BF16)
                        if depth is None
                        else weight[(2 - depth) * 9 + (2 - row) * 3 + 2 - column]
                    )

    def fill(i, carry):
        start = pl.multiple_of(i * STEP, STEP)
        for plane in range(2):
            chunk = cotangent[plane, pl.ds(start, STEP), :].astype(F32)
            fill_windows(windows, start, plane * 128, chunk, columns, 256)
        return carry

    clear_edges(windows, columns)
    lax.fori_loop(0, 2 * half // STEP, fill, 0)
    for start in range(0, half, BLOCK):
        sides = []
        for first in (start, start + half):
            term = window_dot(windows, taps, first, columns, NT)
            own[first : first + BLOCK, :] = term[:, :128]
            sides.append(term[:, 128:])
        upper, lower = packed(*sides)
        up[start : start + BLOCK, :] = upper.astype(BF16)
        down[start : start + BLOCK, :] = lower.astype(BF16)


def hidden_body(
    columns, count, me, own, below, above, weight, act_windows, slope, windows, taps
):
    cells = own.shape[0]
    zero = jnp.zeros((64, 64), BF16)
    for row in range(3):
        for column in range(3):
            for at, source in enumerate(PLANES):
                first = row * 1152 + column * 384 + at * 64
                depths = [depth_tap(source, target) for target in PLANES[:4]]
                parts = [
                    zero if d is None else weight[d * 9 + row * 3 + column] for d in depths
                ]
                taps[first : first + 64, :128] = jnp.concatenate(parts[:2], axis=1)
                taps[first : first + 64, 128:] = jnp.concatenate(parts[2:], axis=1)

    def fill(i, carry):
        start = pl.multiple_of(i * STEP, STEP)
        rows = pl.ds(start, STEP)
        lower, upper = below[rows, :].astype(F32), above[rows, :].astype(F32)
        fill_windows(windows, start, 0, own[rows, :].astype(F32), columns, 384)
        fill_windows(windows, start, 128, pick(upper, lower), columns, 384)
        fill_windows(windows, start, 256, pick(lower, upper), columns, 384)
        return carry

    clear_edges(windows, columns)
    clear_edges(act_windows, columns)
    lax.fori_loop(0, cells // STEP, fill, 0)
    lanes = lax.broadcasted_iota(jnp.int32, (BLOCK, 128), 1)
    edges = [jnp.where(me[0] == end, 0.0, 1.0).astype(F32) for end in (count - 1, 0)]
    inside = jnp.where(lanes < 64, edges[0], edges[1])
    for start in range(0, cells, BLOCK):
        hidden = window_dot(windows, taps, start, columns, NN)
        gate = jax.nn.sigmoid(hidden)
        act = (hidden * gate).astype(BF16).astype(F32)
        fill_windows(act_windows, start, 0, act[:, :128], columns, 256)
        fill_windows(act_windows, start, 128, act[:, 128:] * inside, columns, 256)
        hidden, gate = hidden[:, :128], gate[:, :128]
        slope[start : start + BLOCK, :] = gate * (1.0 + hidden * (1.0 - gate))


def slope_body(terms, below, above, slope, grad, up, down):
    half = terms.shape[0] // 2

    def step(i, carry):
        start = pl.multiple_of(i * STEP, STEP)
        low, high = pl.ds(start, STEP), pl.ds(start + half, STEP)
        arrived = unpacked(below[low, :].astype(F32), above[low, :].astype(F32))
        sides = []
        for rows, extra in zip((low, high), arrived):
            value = ((terms[rows, :] + extra) * slope[rows, :]).astype(BF16)
            grad[rows, :] = value
            sides.append(value.astype(F32))
        lower, upper = packed(*sides)
        down[low, :] = lower.astype(BF16)
        up[low, :] = upper.astype(BF16)
        return carry

    lax.fori_loop(0, half // STEP, step, 0)


def kernel_terms(columns, out_channels, windows, stride, turned, terms):
    cells = turned.shape[1]
    for row in range(3):
        for column in range(3):
            tap = row * 3 + column
            product = jnp.dot(
                turned[...],
                windows[
                    row * columns : row * columns + cells, column * stride : column * stride + 256
                ],
                preferred_element_type=F32,
            )
            first, second = product[:out_channels], product[out_channels:]
            terms[:, tap * 128 : tap * 128 + 128] = first[:, :128] + swap(
                pick(second[:, 128:], second[:, :128])
            )
            group = 9 + tap // 2
            here = slice(group * 128, group * 128 + 128)
            if tap % 2 == 0:
                terms[:, here] = swap(first[:, 128:]) + second[:, :128]
            else:
                terms[:, here] = pick(terms[:, here], first[:, 128:] + swap(second[:, :128]))


def turn(source, target, first):
    for start in range(0, source.shape[0], STEP):
        chunk = source[start : start + STEP, :].astype(F32)
        target[first : first + chunk.shape[1], start : start + STEP] = chunk.T.astype(BF16)


def grad_two_body(columns, act_windows, cotangent, terms, turned):
    turn(cotangent.at[0], turned, 0)
    turn(cotangent.at[1], turned, 128)
    kernel_terms(columns, 128, act_windows, 256, turned, terms)


def coded(value, split):
    head = value[:split].astype(BF16)
    rest = (value[:split] - head.astype(F32)).astype(BF16)
    return jnp.concatenate([head, rest, value[split:].astype(BF16)], axis=0)


def decoded(value, split):
    value = value.astype(F32)
    return jnp.concatenate([value[:split] + value[split : 2 * split], value[2 * split :]], axis=0)


def grad_one_body(
    columns, count, me, own, below, above, grad, other, sent, kept, windows, turned, terms
):
    def fill(i, carry):
        start = pl.multiple_of(i * STEP, STEP)
        rows = pl.ds(start, STEP)
        sides = pick(above[rows, :].astype(F32), below[rows, :].astype(F32))
        fill_windows(windows, start, 0, own[rows, :].astype(F32), columns, 256)
        fill_windows(windows, start, 128, sides, columns, 256)
        return carry

    clear_edges(windows, columns)
    lax.fori_loop(0, own.shape[0] // STEP, fill, 0)
    turn(grad, turned, 0)
    kernel_terms(columns, 64, windows, 256, turned, terms)
    half = terms.shape[1] // 2
    odd = me[0] % 2 == 1

    def share(owner):
        parts = []
        for source in (terms, other):
            each = source.shape[0] // count
            block = source[owner * each : owner * each + each, :]
            parts += [block[:, :half], block[:, half:]]
        return jnp.concatenate(parts, axis=0)

    split = 2 * terms.shape[0] // count
    for pair in range(count // 2):
        even_share, odd_share = share(2 * pair), share(2 * pair + 1)
        sent[pair] = coded(jnp.where(odd, even_share, odd_share), split)
        kept[pair] = jnp.where(odd, odd_share, even_share)


def halve_body(split, me, mine, arrived, sent, kept):
    odd = (me[0] // 2) % 2
    for pair in range(sent.shape[0]):
        keep, give = 2 * pair + odd, 2 * pair + 1 - odd
        sent[pair] = coded(mine[give] + decoded(arrived[give], split), split)
        kept[pair] = mine[keep] + decoded(arrived[keep], split)


def spread_body(split, me, mine, arrived, kept, *sent):
    ring = mine.shape[0]
    place = me[0] // 4
    kept[...] = mine[place] + decoded(arrived[place], split)
    for hop, out in enumerate(sent):
        there = (place + hop + 1) % ring
        out[...] = coded(mine[there] + decoded(arrived[there], split), split)


def finish_body(scale, split, sizes, mine, *refs):
    arrived, (grad_one, grad_two) = refs[:-2], refs[-2:]
    total = mine[...]
    for part in arrived:
        total = total + decoded(part[...], split)
    total = total * scale
    half = total.shape[1]
    first = 0
    for size, out in zip(sizes, (grad_one, grad_two)):
        blocks = (total[first : first + size], total[first + size : first + 2 * size])
        first += 2 * size
        for tap in range(9):
            for depth, group, side in ((0, 9 + tap // 2, tap % 2), (1, tap, 0), (2, tap, 1)):
                lane = group * 128 + side * 64
                block, lane = (blocks[0], lane) if lane < half else (blocks[1], lane - half)
                out[depth * 9 + tap] = block[:, lane : lane + 64]


def output_body(columns, act_windows, weight, output, taps):
    for row in range(3):
        for column in range(3):
            for at, source in enumerate(PLANES[:4]):
                first = row * 768 + column * 256 + at * 64
                for plane in range(2):
                    depth = depth_tap(source, plane)
                    taps[first : first + 64, plane * 128 : plane * 128 + 128] = (
                        jnp.zeros((64, 128), BF16)
                        if depth is None
                        else weight[depth * 9 + row * 3 + column]
                    )
    for start in range(0, output.shape[1], BLOCK):
        value = window_dot(act_windows, taps, start, columns, NN)
        output[0, start : start + BLOCK, :] = value[:, :128]
        output[1, start : start + BLOCK, :] = value[:, 128:]


def grad_volume_body(columns, own, below, above, weight, output, windows, taps):
    zero = jnp.zeros((64, 64), BF16)
    half = own.shape[0] // 2
    for row in range(3):
        for column in range(3):
            for plane in range(2):
                pieces = []
                for source in PLANES[:4]:
                    depth = depth_tap(source, plane)
                    pieces.append(
                        zero if depth is None
                        else weight[(2 - depth) * 9 + (2 - row) * 3 + 2 - column]
                    )
                for pair in range(2):
                    first = row * 768 + column * 256 + pair * 128
                    taps[plane * 64 : plane * 64 + 64, first : first + 128] = (
                        jnp.concatenate(pieces[2 * pair : 2 * pair + 2], axis=1)
                    )

    def fill(i, carry):
        start = pl.multiple_of(i * STEP, STEP)
        sides = unpacked(
            above[pl.ds(start, STEP), :].astype(F32), below[pl.ds(start, STEP), :].astype(F32)
        )
        for first, side in zip((start, start + half), sides):
            fill_windows(windows, first, 0, own[pl.ds(first, STEP), :].astype(F32), columns, 256)
            fill_windows(windows, first, 128, side, columns, 256)
        return carry

    clear_edges(windows, columns)
    lax.fori_loop(0, half // STEP, fill, 0)
    for start in range(0, 2 * half, BLOCK):
        value = window_dot(windows, taps, start, columns, NT)
        output[0, start : start + BLOCK, :] = value[:, :64]
        output[1, start : start + BLOCK, :] = value[:, 64:]


def shards(volume, weight_one, weight_two, cotangent):
    count = lax.axis_size("space")
    planes, rows, columns, channels = volume.shape
    cells = rows * columns
    scale = 1.0 / math.sqrt(planes * count * cells)
    mid, wide = weight_two.shape[3], weight_two.shape[4]
    me = lax.axis_index("space").astype(jnp.int32).reshape(1)
    shape = jax.ShapeDtypeStruct
    flat, pack = shape((cells, 128), BF16), shape((cells // 2, 128), BF16)
    slab = (cells + 2 * columns, 768)
    windows = pltpu.VMEM(slab, BF16)
    lanes = 14 * 64
    split = 2 * mid // count
    chunk = 2 * (mid + wide) // count

    def upward(x):
        return lax.ppermute(x, "space", [(i, i + 1) for i in range(count - 1)])

    def downward(x):
        return lax.ppermute(x, "space", [(i + 1, i) for i in range(count - 1)])

    def shares(*lead):
        return shape((*lead, chunk + split, lanes), BF16), shape((*lead, chunk, lanes), F32)

    volume = volume.reshape(planes, cells, channels)
    cotangent = cotangent.reshape(planes, cells, wide)
    weight_one = weight_one.reshape(27, channels, mid)
    weight_two = weight_two.reshape(27, mid, wide)
    one_flops = 2 * planes * cells * 27 * channels * mid
    two_flops = 2 * planes * cells * 27 * mid * wide

    own, = call(pack_body, (flat,), (volume,), name="pack_volume")
    vol_halo = (upward(own), downward(own))
    terms, up, down = call(
        functools.partial(leave_body, columns),
        (shape((cells, 128), F32), pack, pack),
        (cotangent, weight_two),
        (windows, pltpu.VMEM((256, 3 * 768), BF16)),
        two_flops, "grad_act_terms",
    )
    act_terms_halo = (upward(up), downward(down))
    act_windows, slope = call(
        functools.partial(hidden_body, columns, count),
        (shape(slab, BF16), shape((cells, 128), F32)),
        (me, own, *vol_halo, weight_one),
        (pltpu.VMEM((slab[0], 3 * 384), BF16), pltpu.VMEM((9 * 384, 256), BF16)),
        2 * one_flops, "hidden", (0,),
    )
    terms_two, = call(
        functools.partial(grad_two_body, columns),
        (shape((wide, 2 * lanes), F32),),
        (act_windows, cotangent),
        (pltpu.VMEM((256, cells), BF16),),
        two_flops, "grad_two_terms",
    )
    grad_hidden, up, down = call(
        slope_body, (flat, pack, pack), (terms, *act_terms_halo, slope), name="grad_hidden"
    )
    grad_halo = (upward(up), downward(down))
    sent, kept = call(
        functools.partial(grad_one_body, columns, count),
        shares(count // 2),
        (me, own, *vol_halo, grad_hidden, terms_two),
        (windows, pltpu.VMEM((128, cells), BF16), pltpu.VMEM((mid, 2 * lanes), F32)),
        one_flops, "grad_one_terms", (0,),
    )
    arrived = lax.ppermute(sent, "space", [(i, i ^ 1) for i in range(count)])
    sent, kept = call(
        functools.partial(halve_body, split), shares(count // 4),
        (me, kept, arrived), name="halve", smem=(0,),
    )
    sent, act_windows = lax.optimization_barrier((sent, act_windows))
    arrived = lax.ppermute(sent, "space", [(i, i ^ 2) for i in range(count)])
    output, = call(
        functools.partial(output_body, columns),
        (shape((planes, cells, wide), F32),),
        (act_windows, weight_two),
        (pltpu.VMEM((3 * 768, 256), BF16),),
        two_flops, "output",
    )
    ring = count // 4
    out, mine = shares()
    mine, *sent = call(
        functools.partial(spread_body, split), (mine, *[out] * (ring - 1)),
        (me, kept, arrived), name="spread", smem=(0,),
    )
    sent, grad_hidden = lax.optimization_barrier((sent, grad_hidden))
    rest = [
        lax.ppermute(x, "space", [(i, (i + 4 * hop + 4) % count) for i in range(count)])
        for hop, x in enumerate(sent)
    ]
    grad_volume, = call(
        functools.partial(grad_volume_body, columns),
        (shape((planes, cells, channels), F32),),
        (grad_hidden, *grad_halo, weight_one),
        (windows, pltpu.VMEM((128, 3 * 768), BF16)),
        one_flops, "grad_volume",
    )
    grad_one, grad_two = call(
        functools.partial(finish_body, scale, split, (mid // count, wide // count)),
        (shape((27, mid // count, channels), F32), shape((27, wide // count, mid), F32)),
        (mine, *rest), name="finish",
    )
    return (
        output.reshape(planes, rows, columns, wide),
        grad_volume.reshape(planes, rows, columns, channels),
        jnp.swapaxes(grad_one, 1, 2).reshape(3, 3, 3, channels, mid // count),
        jnp.swapaxes(grad_two, 1, 2).reshape(3, 3, 3, mid, wide // count),
    )


def solution(mesh):
    cells = P(("groups", "space"), None, None, None)
    kernel = P("groups", None, None, None, "space")
    return jax.shard_map(
        shards,
        mesh=mesh,
        in_specs=(cells, P(), P(), cells),
        out_specs=(cells, cells, kernel, kernel),
        check_vma=False,
    )
```

```python
import functools
import math

import jax
import jax.numpy as jnp
from jax import lax
from jax.experimental import pallas as pl
from jax.experimental.pallas import tpu as pltpu
from jax.sharding import PartitionSpec as P

F32, BF16 = jnp.float32, jnp.bfloat16
STEP, BLOCK = 256, 512
VMEM_LIMIT = 24 * 2**20
NN = (((1,), (0,)), ((), ()))
NT = (((1,), (1,)), ((), ()))

PLANES = (0, 1, 2, -1, -2, 3)


def depth_tap(source, target):
    tap = source - target + 1
    return tap if 0 <= tap <= 2 else None


def call(body, outs, ins, scratch=(), flops=0, name=None, smem=(), apart=()):
    return pl.pallas_call(
        body,
        out_shape=list(outs),
        in_specs=[
            pl.BlockSpec(
                memory_space=pltpu.SMEM if i in smem else pl.ANY if i in apart else pltpu.VMEM
            )
            for i in range(len(ins))
        ],
        out_specs=[pl.BlockSpec(memory_space=pltpu.VMEM)] * len(outs),
        scratch_shapes=list(scratch),
        compiler_params=pltpu.CompilerParams(vmem_limit_bytes=VMEM_LIMIT),
        cost_estimate=pl.CostEstimate(flops=1, bytes_accessed=1, transcendentals=0),
        name=name,
    )(*ins)


def lanes_low(x):
    return lax.broadcasted_iota(jnp.int32, x.shape, 1) < 64


def swap(x):
    return pltpu.roll(x, 64, 1)


def pick(low, high):
    return jnp.where(lanes_low(low), low, high)


def fill_windows(windows, start, lane, chunk, columns, stride):
    size = chunk.shape[0]
    column = lax.broadcasted_iota(jnp.int32, chunk.shape, 0) % columns
    before = jnp.where(column == 0, 0.0, pltpu.roll(chunk, 1, 0))
    after = jnp.where(column == columns - 1, 0.0, pltpu.roll(chunk, size - 1, 0))
    at = pl.ds(pl.multiple_of(columns + start, 32), size)
    for tap, part in enumerate((before, chunk, after)):
        first = tap * stride + lane
        windows[at, first : first + chunk.shape[1]] = part.astype(BF16)


def clear_edges(windows, columns):
    rows, lanes = windows.shape
    windows[0:columns, :] = jnp.zeros((columns, lanes), BF16)
    windows[rows - columns : rows, :] = jnp.zeros((columns, lanes), BF16)


def row_windows(windows, start, columns, lanes=slice(None)):
    return [
        windows[start + tap * columns : start + tap * columns + BLOCK, lanes] for tap in range(3)
    ]


def window_dot(windows, weights, start, columns, dims):
    rows = jnp.concatenate(row_windows(windows, start, columns), axis=1)
    return lax.dot_general(rows, weights[...], dims, preferred_element_type=F32)


def packed(low, high):
    return pick(low, swap(high)), pick(swap(low), high)


def unpacked(first, second):
    return packed(first, second)


def by_side(odd, inner, outer):
    return jnp.where(odd, inner, outer), jnp.where(odd, outer, inner)


def pieces_of(source, target, sems, parts):
    size = target.shape[1] // parts
    return [
        pltpu.make_async_copy(
            source.at[:, pl.ds(i * size, size), :], target.at[:, pl.ds(i * size, size), :], sems.at[i]
        )
        for i in range(parts)
    ]


def pack_body(volume, own, held, sems):
    copies = pieces_of(volume, held, sems, sems.shape[0])
    size = own.shape[0] // len(copies)
    for copy in copies:
        copy.start()
    for i, copy in enumerate(copies):
        copy.wait()
        rows = slice(i * size, i * size + size)
        own[rows, :] = jnp.concatenate([held[0, rows, :], held[1, rows, :]], axis=1)


def leave_body(
    columns, me, cotangent, weight, own, inner, outer, windows, taps, held, kernel, sems, sem
):
    half = held.shape[1] // 2
    odd = me[0] % 2 == 1
    fetch = pltpu.make_async_copy(weight, kernel, sem)
    fetch.start()
    copies = pieces_of(cotangent, held, sems, sems.shape[0])
    for copy in copies:
        copy.start()
    clear_edges(windows, columns)
    fetch.wait()
    for row in range(3):
        for column in range(3):
            for source in range(2):
                first = row * 768 + column * 256 + source * 128
                for at, target in enumerate(PLANES[:4]):
                    depth = depth_tap(source, target)
                    taps[at * 64 : at * 64 + 64, first : first + 128] = (
                        jnp.zeros((64, 128), BF16)
                        if depth is None
                        else kernel[(2 - depth) * 9 + (2 - row) * 3 + 2 - column]
                    )
    size = 2 * half // len(copies)
    for i, copy in enumerate(copies):
        copy.wait()

        def fill(j, carry):
            start = pl.multiple_of(i * size + j * STEP, STEP)
            for plane in range(2):
                chunk = held[plane, pl.ds(start, STEP), :].astype(F32)
                fill_windows(windows, start, plane * 128, chunk, columns, 256)
            return carry

        lax.fori_loop(0, size // STEP, fill, 0)
    for start in range(0, half, BLOCK):
        sides = []
        for first in (start, start + half):
            term = window_dot(windows, taps, first, columns, NT)
            own[first : first + BLOCK, :] = term[:, :128]
            sides.append(term[:, 128:])
        upper, lower = packed(*sides)
        inner[start : start + BLOCK, :] = jnp.where(odd, lower, upper).astype(BF16)
        outer[start : start + BLOCK, :] = jnp.where(odd, upper, lower).astype(BF16)


def prepare_body(
    columns, own, weight_one, weight_two, cotangent,
    own_windows, hidden, side_taps, out_taps, back_taps, turned, own_taps,
):
    turn(cotangent.at[0], turned, 0)
    turn(cotangent.at[1], turned, 128)
    zero, wide_zero = jnp.zeros((64, 64), BF16), jnp.zeros((64, 128), BF16)
    for row in range(3):
        for column in range(3):
            tap = row * 3 + column
            for at, source in enumerate(PLANES):
                depths = [depth_tap(source, target) for target in PLANES[:4]]
                parts = [zero if d is None else weight_one[d * 9 + tap] for d in depths]
                if at < 2:
                    target, first = own_taps, tap * 128 + at * 64
                else:
                    target, first = side_taps, tap * 256 + (at - 2) * 64
                target[first : first + 64, :128] = jnp.concatenate(parts[:2], axis=1)
                target[first : first + 64, 128:] = jnp.concatenate(parts[2:], axis=1)
            for at, source in enumerate(PLANES[:4]):
                first = tap * 256 + at * 64
                for plane in range(2):
                    depth = depth_tap(source, plane)
                    out_taps[first : first + 64, plane * 128 : plane * 128 + 128] = (
                        wide_zero if depth is None else weight_two[depth * 9 + tap]
                    )
            for plane in range(2):
                depths = [depth_tap(source, plane) for source in PLANES[:4]]
                parts = [
                    zero if d is None else weight_one[(2 - d) * 9 + 8 - tap] for d in depths
                ]
                for pair in range(2):
                    first = tap * 256 + pair * 128
                    back_taps[plane * 64 : plane * 64 + 64, first : first + 128] = (
                        jnp.concatenate(parts[2 * pair : 2 * pair + 2], axis=1)
                    )

    def fill(i, carry):
        start = pl.multiple_of(i * STEP, STEP)
        chunk = own[pl.ds(start, STEP), :].astype(F32)
        fill_windows(own_windows, start, 0, chunk, columns, 128)
        return carry

    clear_edges(own_windows, columns)
    lax.fori_loop(0, own.shape[0] // STEP, fill, 0)
    for start in range(0, own.shape[0], BLOCK):
        hidden[start : start + BLOCK, :] = window_dot(own_windows, own_taps, start, columns, NN)


def hidden_body(
    columns, count, me, inner, outer, part, side_taps, side_windows, act_windows, slope
):
    cells = inner.shape[0]
    odd = me[0] % 2 == 1

    def fill(i, carry):
        start = pl.multiple_of(i * STEP, STEP)
        rows = pl.ds(start, STEP)
        below, above = by_side(odd, inner[rows, :].astype(F32), outer[rows, :].astype(F32))
        fill_windows(side_windows, start, 0, pick(above, below), columns, 256)
        fill_windows(side_windows, start, 128, pick(below, above), columns, 256)
        return carry

    clear_edges(side_windows, columns)
    clear_edges(act_windows, columns)
    lax.fori_loop(0, cells // STEP, fill, 0)
    lanes = lax.broadcasted_iota(jnp.int32, (BLOCK, 128), 1)
    edges = [jnp.where(me[0] == end, 0.0, 1.0).astype(F32) for end in (count - 1, 0)]
    inside = jnp.where(lanes < 64, edges[0], edges[1])
    for start in range(0, cells, BLOCK):
        hidden = part[start : start + BLOCK, :]
        hidden = hidden + window_dot(side_windows, side_taps, start, columns, NN)
        gate = jax.nn.sigmoid(hidden)
        act = (hidden * gate).astype(BF16).astype(F32)
        fill_windows(act_windows, start, 0, act[:, :128], columns, 256)
        fill_windows(act_windows, start, 128, act[:, 128:] * inside, columns, 256)
        hidden, gate = hidden[:, :128], gate[:, :128]
        slope[start : start + BLOCK, :] = gate * (1.0 + hidden * (1.0 - gate))


def slope_body(me, terms, inner, outer, slope, grad, to_inner, to_outer):
    half = terms.shape[0] // 2
    odd = me[0] % 2 == 1

    def step(i, carry):
        start = pl.multiple_of(i * STEP, STEP)
        low, high = pl.ds(start, STEP), pl.ds(start + half, STEP)
        arrived = unpacked(
            *by_side(odd, inner[low, :].astype(F32), outer[low, :].astype(F32))
        )
        sides = []
        for rows, extra in zip((low, high), arrived):
            value = ((terms[rows, :] + extra) * slope[rows, :]).astype(BF16)
            grad[rows, :] = value
            sides.append(value.astype(F32))
        lower, upper = packed(*sides)
        to_inner[low, :] = jnp.where(odd, lower, upper).astype(BF16)
        to_outer[low, :] = jnp.where(odd, upper, lower).astype(BF16)
        return carry

    lax.fori_loop(0, half // STEP, step, 0)


def kernel_terms(columns, out_channels, slices, turned, terms):
    for row in range(3):
        for column in range(3):
            tap = row * 3 + column
            product = jnp.dot(turned[...], slices(row, column), preferred_element_type=F32)
            first, second = product[:out_channels], product[out_channels:]
            terms[:, tap * 128 : tap * 128 + 128] = first[:, :128] + swap(
                pick(second[:, 128:], second[:, :128])
            )
            group = 9 + tap // 2
            here = slice(group * 128, group * 128 + 128)
            if tap % 2 == 0:
                terms[:, here] = swap(first[:, 128:]) + second[:, :128]
            else:
                terms[:, here] = pick(terms[:, here], first[:, 128:] + swap(second[:, :128]))


def turn(source, target, first):
    for start in range(0, source.shape[0], STEP):
        chunk = source[start : start + STEP, :].astype(F32)
        target[first : first + chunk.shape[1], start : start + STEP] = chunk.T.astype(BF16)


def grad_two_body(columns, act_windows, turned, terms):
    cells = turned.shape[1]

    def slices(row, column):
        rows = slice(row * columns, row * columns + cells)
        return act_windows[rows, column * 256 : column * 256 + 256]

    kernel_terms(columns, 128, slices, turned, terms)


def coded(value, split):
    head = value[:split].astype(BF16)
    rest = (value[:split] - head.astype(F32)).astype(BF16)
    return jnp.concatenate([head, rest, value[split:].astype(BF16)], axis=0)


def decoded(value, split):
    value = value.astype(F32)
    return jnp.concatenate([value[:split] + value[split : 2 * split], value[2 * split :]], axis=0)


def grad_one_body(
    columns, count, me, own_windows, side_windows, grad, other, sent, kept, turned, terms
):
    cells = grad.shape[0]

    def slices(row, column):
        rows = slice(row * columns, row * columns + cells)
        return jnp.concatenate(
            [
                own_windows[rows, column * 128 : column * 128 + 128],
                side_windows[rows, column * 256 : column * 256 + 128],
            ],
            axis=1,
        )

    turn(grad, turned, 0)
    kernel_terms(columns, 64, slices, turned, terms)
    half = terms.shape[1] // 2
    odd = me[0] % 2 == 1

    def share(owner):
        parts = []
        for source in (terms, other):
            each = source.shape[0] // count
            block = source[owner * each : owner * each + each, :]
            parts += [block[:, :half], block[:, half:]]
        return jnp.concatenate(parts, axis=0)

    split = 2 * terms.shape[0] // count
    for pair in range(count // 2):
        even_share, odd_share = share(2 * pair), share(2 * pair + 1)
        sent[pair] = coded(jnp.where(odd, even_share, odd_share), split)
        kept[pair] = jnp.where(odd, odd_share, even_share)


def sum_body(split, me, mine, arrived, sent, kept):
    place = me[0] // 2
    for at in range(mine.shape[0]):
        sent[at] = coded(mine[at] + decoded(arrived[at], split), split)
    kept[...] = mine[place] + decoded(arrived[place], split)


def finish_body(scale, split, sizes, me, mine, arrived, grad_one, grad_two):
    total = mine[...]
    for at in range(arrived.shape[0]):
        total = total + jnp.where(at == me[0] // 2, 0.0, decoded(arrived[at], split))
    total = total * scale
    half = total.shape[1]
    first = 0
    for size, out in zip(sizes, (grad_one, grad_two)):
        blocks = (total[first : first + size], total[first + size : first + 2 * size])
        first += 2 * size
        for tap in range(9):
            for depth, group, side in ((0, 9 + tap // 2, tap % 2), (1, tap, 0), (2, tap, 1)):
                lane = group * 128 + side * 64
                block, lane = (blocks[0], lane) if lane < half else (blocks[1], lane - half)
                out[depth * 9 + tap] = block[:, lane : lane + 64]


def output_body(columns, act_windows, taps, output):
    for start in range(0, output.shape[1], BLOCK):
        value = window_dot(act_windows, taps, start, columns, NN)
        output[0, start : start + BLOCK, :] = value[:, :128]
        output[1, start : start + BLOCK, :] = value[:, 128:]


def grad_volume_body(columns, me, own, inner, outer, taps, output, windows):
    half = own.shape[0] // 2
    odd = me[0] % 2 == 1

    def fill(i, carry):
        start = pl.multiple_of(i * STEP, STEP)
        rows = pl.ds(start, STEP)
        below, above = by_side(odd, inner[rows, :].astype(F32), outer[rows, :].astype(F32))
        for first, side in zip((start, start + half), unpacked(above, below)):
            fill_windows(windows, first, 0, own[pl.ds(first, STEP), :].astype(F32), columns, 256)
            fill_windows(windows, first, 128, side, columns, 256)
        return carry

    clear_edges(windows, columns)
    lax.fori_loop(0, half // STEP, fill, 0)
    for start in range(0, 2 * half, BLOCK):
        value = window_dot(windows, taps, start, columns, NT)
        output[0, start : start + BLOCK, :] = value[:, :64]
        output[1, start : start + BLOCK, :] = value[:, 64:]


def shards(volume, weight_one, weight_two, cotangent):
    count = lax.axis_size("space")
    planes, rows, columns, channels = volume.shape
    cells = rows * columns
    scale = 1.0 / math.sqrt(planes * count * cells)
    mid, wide = weight_two.shape[3], weight_two.shape[4]
    me = lax.axis_index("space").astype(jnp.int32).reshape(1)
    shape = jax.ShapeDtypeStruct
    flat, pack = shape((cells, 128), BF16), shape((cells // 2, 128), BF16)
    slab = (cells + 2 * columns, 768)
    windows = pltpu.VMEM(slab, BF16)
    lanes = 14 * 64
    split = 2 * mid // count
    chunk = 2 * (mid + wide) // count

    within = [(i, i ^ 1) for i in range(count)]
    across = [(i, i + 1) for i in range(1, count - 1, 2)]
    across += [(j, i) for i, j in across]

    def exchange(inner, outer):
        outer = lax.ppermute(outer, "space", across)
        return lax.ppermute(inner, "space", within), outer

    def shares(*lead):
        return shape((*lead, chunk + split, lanes), BF16), shape((*lead, chunk, lanes), F32)

    volume = volume.reshape(planes, cells, channels)
    cotangent = cotangent.reshape(planes, cells, wide)
    weight_one = weight_one.reshape(27, channels, mid)
    weight_two = weight_two.reshape(27, mid, wide)
    one_flops = 2 * planes * cells * 27 * channels * mid
    two_flops = 2 * planes * cells * 27 * mid * wide

    dma = pltpu.SemaphoreType.DMA
    own, = call(
        pack_body, (flat,), (volume,),
        (pltpu.VMEM((planes, cells, channels), BF16), dma((4,))),
        name="pack_volume", apart=(0,),
    )
    vol_halo = exchange(own, own)
    terms, inner, outer = call(
        functools.partial(leave_body, columns),
        (shape((cells, 128), F32), pack, pack),
        (me, cotangent, weight_two),
        (
            windows, pltpu.VMEM((256, 3 * 768), BF16), pltpu.VMEM(cotangent.shape, BF16),
            pltpu.VMEM(weight_two.shape, BF16), dma((4,)), dma,
        ),
        two_flops, "grad_act_terms", (0,), (1, 2),
    )
    own_windows, part, side_taps, out_taps, back_taps, turned = call(
        functools.partial(prepare_body, columns),
        (
            shape((slab[0], 384), BF16), shape((cells, 256), F32), shape((9 * 256, 256), BF16),
            shape((9 * 256, 256), BF16), shape((128, 9 * 256), BF16), shape((256, cells), BF16),
        ),
        (own, weight_one, weight_two, cotangent),
        (pltpu.VMEM((9 * 128, 256), BF16),),
        one_flops, "prepare",
    )
    inner, outer, part = lax.optimization_barrier((inner, outer, part))
    act_terms_halo = exchange(inner, outer)
    side_windows, act_windows, slope = call(
        functools.partial(hidden_body, columns, count),
        (shape(slab, BF16), shape(slab, BF16), shape((cells, 128), F32)),
        (me, *vol_halo, part, side_taps),
        (), 2 * one_flops, "hidden", (0,),
    )
    grad_hidden, inner, outer = call(
        slope_body, (flat, pack, pack), (me, terms, *act_terms_halo, slope),
        name="grad_hidden", smem=(0,),
    )
    inner, outer, act_windows = lax.optimization_barrier((inner, outer, act_windows))
    grad_halo = exchange(inner, outer)
    terms_two, = call(
        functools.partial(grad_two_body, columns),
        (shape((wide, 2 * lanes), F32),),
        (act_windows, turned), (), two_flops, "grad_two_terms",
    )
    sent, kept = call(
        functools.partial(grad_one_body, columns, count),
        shares(count // 2),
        (me, own_windows, side_windows, grad_hidden, terms_two),
        (pltpu.VMEM((128, cells), BF16), pltpu.VMEM((mid, 2 * lanes), F32)),
        one_flops, "grad_one_terms", (0,),
    )
    sent, grad_halo = lax.optimization_barrier((sent, grad_halo))
    arrived = lax.ppermute(sent, "space", within)
    sent, mine = call(
        functools.partial(sum_body, split), (shares(count // 2)[0], shares()[1]),
        (me, kept, arrived), name="sum_pair", smem=(0,),
    )
    sent, act_windows, grad_hidden = lax.optimization_barrier((sent, act_windows, grad_hidden))
    arrived = lax.all_to_all(
        sent, "space", 0, 0, tiled=True,
        axis_index_groups=[list(range(core, count, 2)) for core in range(2)],
    )
    output, = call(
        functools.partial(output_body, columns),
        (shape((planes, cells, wide), F32),),
        (act_windows, out_taps), (), two_flops, "output",
    )
    grad_volume, = call(
        functools.partial(grad_volume_body, columns),
        (shape((planes, cells, channels), F32),),
        (me, grad_hidden, *grad_halo, back_taps),
        (windows,), one_flops, "grad_volume", (0,),
    )
    grad_one, grad_two = call(
        functools.partial(finish_body, scale, split, (mid // count, wide // count)),
        (shape((27, mid // count, channels), F32), shape((27, wide // count, mid), F32)),
        (me, mine, arrived), name="finish", smem=(0,),
    )
    return (
        output.reshape(planes, rows, columns, wide),
        grad_volume.reshape(planes, rows, columns, channels),
        jnp.swapaxes(grad_one, 1, 2).reshape(3, 3, 3, channels, mid // count),
        jnp.swapaxes(grad_two, 1, 2).reshape(3, 3, 3, mid, wide // count),
    )


def solution(mesh):
    cells = P(("groups", "space"), None, None, None)
    kernel = P("groups", None, None, None, "space")
    return jax.shard_map(
        shards,
        mesh=mesh,
        in_specs=(cells, P(), P(), cells),
        out_specs=(cells, cells, kernel, kernel),
        check_vma=False,
    )
```

```python
import functools
import math

import jax
import jax.numpy as jnp
from jax import lax
from jax.experimental import pallas as pl
from jax.experimental.pallas import tpu as pltpu
from jax.sharding import PartitionSpec as P

F32, BF16 = jnp.float32, jnp.bfloat16
STEP, BLOCK = 256, 512
VMEM_LIMIT = 16 * 2**20
NN = (((1,), (0,)), ((), ()))
NT = (((1,), (1,)), ((), ()))

PLANES = (0, 1, 2, -1, -2, 3)


def depth_tap(source, target):
    tap = source - target + 1
    return tap if 0 <= tap <= 2 else None


def call(body, outs, ins, scratch=(), flops=0, name=None, smem=(), apart=()):
    moved = sum(math.prod(s.shape) * s.dtype.itemsize for s in (*outs, *ins))
    return pl.pallas_call(
        body,
        out_shape=list(outs),
        in_specs=[
            pl.BlockSpec(
                memory_space=pltpu.SMEM if i in smem else pl.ANY if i in apart else pltpu.VMEM
            )
            for i in range(len(ins))
        ],
        out_specs=[pl.BlockSpec(memory_space=pltpu.VMEM)] * len(outs),
        scratch_shapes=list(scratch),
        compiler_params=pltpu.CompilerParams(vmem_limit_bytes=VMEM_LIMIT),
        cost_estimate=pl.CostEstimate(flops=flops, bytes_accessed=moved, transcendentals=0),
        name=name,
    )(*ins)


def lanes_low(x):
    return lax.broadcasted_iota(jnp.int32, x.shape, 1) < 64


def swap(x):
    return pltpu.roll(x, 64, 1)


def pick(low, high):
    return jnp.where(lanes_low(low), low, high)


def fill_windows(windows, start, lane, chunk, columns, stride):
    size = chunk.shape[0]
    column = lax.broadcasted_iota(jnp.int32, chunk.shape, 0) % columns
    before = jnp.where(column == 0, 0.0, pltpu.roll(chunk, 1, 0))
    after = jnp.where(column == columns - 1, 0.0, pltpu.roll(chunk, size - 1, 0))
    at = pl.ds(pl.multiple_of(columns + start, 32), size)
    for tap, part in enumerate((before, chunk, after)):
        first = tap * stride + lane
        windows[at, first : first + chunk.shape[1]] = part.astype(BF16)


def clear_edges(windows, columns):
    rows, lanes = windows.shape
    windows[0:columns, :] = jnp.zeros((columns, lanes), BF16)
    windows[rows - columns : rows, :] = jnp.zeros((columns, lanes), BF16)


def row_windows(windows, start, columns, lanes=slice(None)):
    return [
        windows[start + tap * columns : start + tap * columns + BLOCK, lanes] for tap in range(3)
    ]


def window_dot(windows, weights, start, columns, dims):
    rows = jnp.concatenate(row_windows(windows, start, columns), axis=1)
    return lax.dot_general(rows, weights[...], dims, preferred_element_type=F32)


def packed(low, high):
    return pick(low, swap(high)), pick(swap(low), high)


def unpacked(first, second):
    return packed(first, second)


def by_side(odd, inner, outer):
    return jnp.where(odd, inner, outer), jnp.where(odd, outer, inner)


def pieces_of(source, target, sems, parts):
    size = target.shape[1] // parts
    return [
        pltpu.make_async_copy(
            source.at[:, pl.ds(i * size, size), :], target.at[:, pl.ds(i * size, size), :], sems.at[i]
        )
        for i in range(parts)
    ]


def pack_body(volume, own, held, sems):
    copies = pieces_of(volume, held, sems, sems.shape[0])
    size = own.shape[0] // len(copies)
    for copy in copies:
        copy.start()
    for i, copy in enumerate(copies):
        copy.wait()
        rows = slice(i * size, i * size + size)
        own[rows, :] = jnp.concatenate([held[0, rows, :], held[1, rows, :]], axis=1)


def leave_body(
    columns, me, cotangent, weight_far, own, inner, outer, windows, taps, weight, sem
):
    half = cotangent.shape[1] // 2
    odd = me[0] % 2 == 1
    fetch = pltpu.make_async_copy(weight_far, weight, sem)
    fetch.start()
    clear_edges(windows, columns)

    def fill(i, carry):
        start = pl.multiple_of(i * STEP, STEP)
        for plane in range(2):
            chunk = cotangent[plane, pl.ds(start, STEP), :].astype(F32)
            fill_windows(windows, start, plane * 128, chunk, columns, 256)
        return carry

    lax.fori_loop(0, 2 * half // STEP, fill, 0)
    fetch.wait()
    for row in range(3):
        for column in range(3):
            for source in range(2):
                first = row * 768 + column * 256 + source * 128
                for at, target in enumerate(PLANES[:4]):
                    depth = depth_tap(source, target)
                    taps[at * 64 : at * 64 + 64, first : first + 128] = (
                        jnp.zeros((64, 128), BF16)
                        if depth is None
                        else weight[(2 - depth) * 9 + (2 - row) * 3 + 2 - column]
                    )
    for start in range(0, half, BLOCK):
        sides = []
        for first in (start, start + half):
            term = window_dot(windows, taps, first, columns, NT)
            own[first : first + BLOCK, :] = term[:, :128]
            sides.append(term[:, 128:])
        upper, lower = packed(*sides)
        inner[start : start + BLOCK, :] = jnp.where(odd, lower, upper).astype(BF16)
        outer[start : start + BLOCK, :] = jnp.where(odd, upper, lower).astype(BF16)


def prepare_body(
    columns, own, far_one, far_two, cotangent,
    own_windows, hidden, side_taps, out_taps, back_taps, turned, own_taps,
    weight_one, weight_two, sems,
):
    fetches = [
        pltpu.make_async_copy(far_one, weight_one, sems.at[0]),
        pltpu.make_async_copy(far_two, weight_two, sems.at[1]),
    ]
    for fetch in fetches:
        fetch.start()

    def fill(i, carry):
        start = pl.multiple_of(i * STEP, STEP)
        chunk = own[pl.ds(start, STEP), :].astype(F32)
        fill_windows(own_windows, start, 0, chunk, columns, 128)
        return carry

    clear_edges(own_windows, columns)
    lax.fori_loop(0, own.shape[0] // STEP, fill, 0)
    turn(cotangent.at[0], turned, 0)
    turn(cotangent.at[1], turned, 128)
    for fetch in fetches:
        fetch.wait()
    zero, wide_zero = jnp.zeros((64, 64), BF16), jnp.zeros((64, 128), BF16)
    for row in range(3):
        for column in range(3):
            tap = row * 3 + column
            for at, source in enumerate(PLANES):
                depths = [depth_tap(source, target) for target in PLANES[:4]]
                parts = [zero if d is None else weight_one[d * 9 + tap] for d in depths]
                if at < 2:
                    target, first = own_taps, tap * 128 + at * 64
                else:
                    target, first = side_taps, tap * 256 + (at - 2) * 64
                target[first : first + 64, :128] = jnp.concatenate(parts[:2], axis=1)
                target[first : first + 64, 128:] = jnp.concatenate(parts[2:], axis=1)
            for at, source in enumerate(PLANES[:4]):
                first = tap * 256 + at * 64
                for plane in range(2):
                    depth = depth_tap(source, plane)
                    out_taps[first : first + 64, plane * 128 : plane * 128 + 128] = (
                        wide_zero if depth is None else weight_two[depth * 9 + tap]
                    )
            for plane in range(2):
                depths = [depth_tap(source, plane) for source in PLANES[:4]]
                parts = [
                    zero if d is None else weight_one[(2 - d) * 9 + 8 - tap] for d in depths
                ]
                for pair in range(2):
                    first = tap * 256 + pair * 128
                    back_taps[plane * 64 : plane * 64 + 64, first : first + 128] = (
                        jnp.concatenate(parts[2 * pair : 2 * pair + 2], axis=1)
                    )

    for start in range(0, own.shape[0], BLOCK):
        hidden[start : start + BLOCK, :] = window_dot(own_windows, own_taps, start, columns, NN)


def hidden_body(
    columns, count, me, inner, outer, part, side_taps, side_windows, act_windows, slope
):
    cells = inner.shape[0]
    odd = me[0] % 2 == 1

    def fill(i, carry):
        start = pl.multiple_of(i * STEP, STEP)
        rows = pl.ds(start, STEP)
        below, above = by_side(odd, inner[rows, :].astype(F32), outer[rows, :].astype(F32))
        fill_windows(side_windows, start, 0, pick(above, below), columns, 256)
        fill_windows(side_windows, start, 128, pick(below, above), columns, 256)
        return carry

    clear_edges(side_windows, columns)
    clear_edges(act_windows, columns)
    lax.fori_loop(0, cells // STEP, fill, 0)
    lanes = lax.broadcasted_iota(jnp.int32, (BLOCK, 128), 1)
    edges = [jnp.where(me[0] == end, 0.0, 1.0).astype(F32) for end in (count - 1, 0)]
    inside = jnp.where(lanes < 64, edges[0], edges[1])
    for start in range(0, cells, BLOCK):
        hidden = part[start : start + BLOCK, :]
        hidden = hidden + window_dot(side_windows, side_taps, start, columns, NN)
        gate = jax.nn.sigmoid(hidden)
        act = (hidden * gate).astype(BF16).astype(F32)
        fill_windows(act_windows, start, 0, act[:, :128], columns, 256)
        fill_windows(act_windows, start, 128, act[:, 128:] * inside, columns, 256)
        hidden, gate = hidden[:, :128], gate[:, :128]
        slope[start : start + BLOCK, :] = gate * (1.0 + hidden * (1.0 - gate))


def slope_body(me, terms, inner, outer, slope, grad, to_inner, to_outer):
    half = terms.shape[0] // 2
    odd = me[0] % 2 == 1

    def step(i, carry):
        start = pl.multiple_of(i * STEP, STEP)
        low, high = pl.ds(start, STEP), pl.ds(start + half, STEP)
        arrived = unpacked(
            *by_side(odd, inner[low, :].astype(F32), outer[low, :].astype(F32))
        )
        sides = []
        for rows, extra in zip((low, high), arrived):
            value = ((terms[rows, :] + extra) * slope[rows, :]).astype(BF16)
            grad[rows, :] = value
            sides.append(value.astype(F32))
        lower, upper = packed(*sides)
        to_inner[low, :] = jnp.where(odd, lower, upper).astype(BF16)
        to_outer[low, :] = jnp.where(odd, upper, lower).astype(BF16)
        return carry

    lax.fori_loop(0, half // STEP, step, 0)


def kernel_terms(columns, out_channels, slices, turned, terms):
    for row in range(3):
        for column in range(3):
            tap = row * 3 + column
            product = jnp.dot(turned[...], slices(row, column), preferred_element_type=F32)
            first, second = product[:out_channels], product[out_channels:]
            terms[:, tap * 128 : tap * 128 + 128] = first[:, :128] + swap(
                pick(second[:, 128:], second[:, :128])
            )
            group = 9 + tap // 2
            here = slice(group * 128, group * 128 + 128)
            if tap % 2 == 0:
                terms[:, here] = swap(first[:, 128:]) + second[:, :128]
            else:
                terms[:, here] = pick(terms[:, here], first[:, 128:] + swap(second[:, :128]))


def turn(source, target, first):
    for start in range(0, source.shape[0], STEP):
        chunk = source[start : start + STEP, :].astype(F32)
        target[first : first + chunk.shape[1], start : start + STEP] = chunk.T.astype(BF16)


def grad_two_body(columns, act_windows, turned, terms):
    cells = turned.shape[1]

    def slices(row, column):
        rows = slice(row * columns, row * columns + cells)
        return act_windows[rows, column * 256 : column * 256 + 256]

    kernel_terms(columns, 128, slices, turned, terms)


def coded(value, split):
    head = value[:split].astype(BF16)
    rest = (value[:split] - head.astype(F32)).astype(BF16)
    return jnp.concatenate([head, rest, value[split:].astype(BF16)], axis=0)


def decoded(value, split):
    value = value.astype(F32)
    return jnp.concatenate([value[:split] + value[split : 2 * split], value[2 * split :]], axis=0)


def grad_one_body(
    columns, count, me, own_windows, side_windows, grad, other, sent, kept, turned, terms
):
    cells = grad.shape[0]

    def slices(row, column):
        rows = slice(row * columns, row * columns + cells)
        return jnp.concatenate(
            [
                own_windows[rows, column * 128 : column * 128 + 128],
                side_windows[rows, column * 256 : column * 256 + 128],
            ],
            axis=1,
        )

    turn(grad, turned, 0)
    kernel_terms(columns, 64, slices, turned, terms)
    half = terms.shape[1] // 2
    odd = me[0] % 2 == 1

    def share(owner):
        parts = []
        for source in (terms, other):
            each = source.shape[0] // count
            block = source[owner * each : owner * each + each, :]
            parts += [block[:, :half], block[:, half:]]
        return jnp.concatenate(parts, axis=0)

    split = 2 * terms.shape[0] // count
    for pair in range(count // 2):
        even_share, odd_share = share(2 * pair), share(2 * pair + 1)
        sent[pair] = coded(jnp.where(odd, even_share, odd_share), split)
        kept[pair] = jnp.where(odd, odd_share, even_share)


def sum_body(split, me, mine, arrived, sent, kept):
    place = me[0] // 2
    for at in range(mine.shape[0]):
        sent[at] = coded(mine[at] + decoded(arrived[at], split), split)
    kept[...] = mine[place] + decoded(arrived[place], split)


def finish_body(scale, split, sizes, me, mine, arrived, grad_one, grad_two):
    total = mine[...]
    for at in range(arrived.shape[0]):
        total = total + jnp.where(at == me[0] // 2, 0.0, decoded(arrived[at], split))
    total = total * scale
    half = total.shape[1]
    first = 0
    for size, out in zip(sizes, (grad_one, grad_two)):
        blocks = (total[first : first + size], total[first + size : first + 2 * size])
        first += 2 * size
        for tap in range(9):
            for depth, group, side in ((0, 9 + tap // 2, tap % 2), (1, tap, 0), (2, tap, 1)):
                lane = group * 128 + side * 64
                block, lane = (blocks[0], lane) if lane < half else (blocks[1], lane - half)
                out[depth * 9 + tap] = block[:, lane : lane + 64]


def output_body(columns, act_windows, taps, output):
    for start in range(0, output.shape[1], BLOCK):
        value = window_dot(act_windows, taps, start, columns, NN)
        output[0, start : start + BLOCK, :] = value[:, :128]
        output[1, start : start + BLOCK, :] = value[:, 128:]


def grad_volume_body(columns, me, own, inner, outer, taps, output, windows):
    half = own.shape[0] // 2
    odd = me[0] % 2 == 1

    def fill(i, carry):
        start = pl.multiple_of(i * STEP, STEP)
        rows = pl.ds(start, STEP)
        below, above = by_side(odd, inner[rows, :].astype(F32), outer[rows, :].astype(F32))
        for first, side in zip((start, start + half), unpacked(above, below)):
            fill_windows(windows, first, 0, own[pl.ds(first, STEP), :].astype(F32), columns, 256)
            fill_windows(windows, first, 128, side, columns, 256)
        return carry

    clear_edges(windows, columns)
    lax.fori_loop(0, half // STEP, fill, 0)
    for start in range(0, 2 * half, BLOCK):
        value = window_dot(windows, taps, start, columns, NT)
        output[0, start : start + BLOCK, :] = value[:, :64]
        output[1, start : start + BLOCK, :] = value[:, 64:]


def shards(volume, weight_one, weight_two, cotangent):
    count = lax.axis_size("space")
    planes, rows, columns, channels = volume.shape
    cells = rows * columns
    scale = 1.0 / math.sqrt(planes * count * cells)
    mid, wide = weight_two.shape[3], weight_two.shape[4]
    me = lax.axis_index("space").astype(jnp.int32).reshape(1)
    shape = jax.ShapeDtypeStruct
    flat, pack = shape((cells, 128), BF16), shape((cells // 2, 128), BF16)
    slab = (cells + 2 * columns, 768)
    windows = pltpu.VMEM(slab, BF16)
    lanes = 14 * 64
    split = 2 * mid // count
    chunk = 2 * (mid + wide) // count

    within = [(i, i ^ 1) for i in range(count)]
    across = [(i, i + 1) for i in range(1, count - 1, 2)]
    across += [(j, i) for i, j in across]

    def exchange(inner, outer):
        outer = lax.ppermute(outer, "space", across)
        return lax.ppermute(inner, "space", within), outer

    def shares(*lead):
        return shape((*lead, chunk + split, lanes), BF16), shape((*lead, chunk, lanes), F32)

    volume = volume.reshape(planes, cells, channels)
    cotangent = cotangent.reshape(planes, cells, wide)
    weight_one = weight_one.reshape(27, channels, mid)
    weight_two = weight_two.reshape(27, mid, wide)
    one_flops = 2 * planes * cells * 27 * channels * mid
    two_flops = 2 * planes * cells * 27 * mid * wide

    dma = pltpu.SemaphoreType.DMA
    far_one, far_two, far_volume = (
        pltpu.with_memory_space_constraint(x, pltpu.HBM) for x in (weight_one, weight_two, volume)
    )
    own, = call(
        pack_body, (flat,), (far_volume,),
        (pltpu.VMEM((planes, cells, channels), BF16), dma((4,))),
        name="pack_volume", apart=(0,),
    )
    vol_halo = exchange(own, own)
    terms, inner, outer = call(
        functools.partial(leave_body, columns),
        (shape((cells, 128), F32), pack, pack),
        (me, cotangent, far_two),
        (windows, pltpu.VMEM((256, 3 * 768), BF16), pltpu.VMEM(weight_two.shape, BF16), dma),
        two_flops, "grad_act_terms", (0,), (2,),
    )
    own, terms = lax.optimization_barrier((own, terms))
    own_windows, part, side_taps, out_taps, back_taps, turned = call(
        functools.partial(prepare_body, columns),
        (
            shape((slab[0], 384), BF16), shape((cells, 256), F32), shape((9 * 256, 256), BF16),
            shape((9 * 256, 256), BF16), shape((128, 9 * 256), BF16), shape((256, cells), BF16),
        ),
        (own, far_one, far_two, cotangent),
        (
            pltpu.VMEM((9 * 128, 256), BF16), pltpu.VMEM(weight_one.shape, BF16),
            pltpu.VMEM(weight_two.shape, BF16), dma((2,)),
        ),
        one_flops, "prepare", (), (1, 2),
    )
    inner, outer, part = lax.optimization_barrier((inner, outer, part))
    act_terms_halo = exchange(inner, outer)
    side_windows, act_windows, slope = call(
        functools.partial(hidden_body, columns, count),
        (shape(slab, BF16), shape(slab, BF16), shape((cells, 128), F32)),
        (me, *vol_halo, part, side_taps),
        (), 2 * one_flops, "hidden", (0,),
    )
    grad_hidden, inner, outer = call(
        slope_body, (flat, pack, pack), (me, terms, *act_terms_halo, slope),
        name="grad_hidden", smem=(0,),
    )
    inner, outer, act_windows = lax.optimization_barrier((inner, outer, act_windows))
    grad_halo = exchange(inner, outer)
    terms_two, = call(
        functools.partial(grad_two_body, columns),
        (shape((wide, 2 * lanes), F32),),
        (act_windows, turned), (), two_flops, "grad_two_terms",
    )
    sent, kept = call(
        functools.partial(grad_one_body, columns, count),
        shares(count // 2),
        (me, own_windows, side_windows, grad_hidden, terms_two),
        (pltpu.VMEM((128, cells), BF16), pltpu.VMEM((mid, 2 * lanes), F32)),
        one_flops, "grad_one_terms", (0,),
    )
    sent, grad_halo = lax.optimization_barrier((sent, grad_halo))
    arrived = lax.ppermute(sent, "space", within)
    sent, mine = call(
        functools.partial(sum_body, split), (shares(count // 2)[0], shares()[1]),
        (me, kept, arrived), name="sum_pair", smem=(0,),
    )
    sent, act_windows, grad_hidden = lax.optimization_barrier((sent, act_windows, grad_hidden))
    arrived = lax.all_to_all(
        sent, "space", 0, 0, tiled=True,
        axis_index_groups=[list(range(core, count, 2)) for core in range(2)],
    )
    output, = call(
        functools.partial(output_body, columns),
        (shape((planes, cells, wide), F32),),
        (act_windows, out_taps), (), two_flops, "output",
    )
    grad_volume, = call(
        functools.partial(grad_volume_body, columns),
        (shape((planes, cells, channels), F32),),
        (me, grad_hidden, *grad_halo, back_taps),
        (windows,), one_flops, "grad_volume", (0,),
    )
    grad_one, grad_two = call(
        functools.partial(finish_body, scale, split, (mid // count, wide // count)),
        (shape((27, mid // count, channels), F32), shape((27, wide // count, mid), F32)),
        (me, mine, arrived), name="finish", smem=(0,),
    )
    return (
        output.reshape(planes, rows, columns, wide),
        grad_volume.reshape(planes, rows, columns, channels),
        jnp.swapaxes(grad_one, 1, 2).reshape(3, 3, 3, channels, mid // count),
        jnp.swapaxes(grad_two, 1, 2).reshape(3, 3, 3, mid, wide // count),
    )


def solution(mesh):
    cells = P(("groups", "space"), None, None, None)
    kernel = P("groups", None, None, None, "space")
    return jax.shard_map(
        shards,
        mesh=mesh,
        in_specs=(cells, P(), P(), cells),
        out_specs=(cells, cells, kernel, kernel),
        check_vma=False,
    )
```

```python
import functools
import math

import jax
import jax.numpy as jnp
from jax import lax
from jax.experimental import pallas as pl
from jax.experimental.pallas import tpu as pltpu
from jax.sharding import PartitionSpec as P

F32, BF16 = jnp.float32, jnp.bfloat16
STEP, BLOCK = 256, 512
VMEM_LIMIT = 16 * 2**20
NN = (((1,), (0,)), ((), ()))
NT = (((1,), (1,)), ((), ()))

PLANES = (0, 1, 2, -1, -2, 3)


def depth_tap(source, target):
    tap = source - target + 1
    return tap if 0 <= tap <= 2 else None


def call(body, outs, ins, scratch=(), flops=0, name=None, smem=(), apart=(), far=False):
    moved = sum(math.prod(s.shape) * s.dtype.itemsize for s in (*outs, *ins))
    return pl.pallas_call(
        body,
        out_shape=list(outs),
        in_specs=[
            pl.BlockSpec(
                memory_space=pltpu.SMEM if i in smem else pl.ANY if i in apart else pltpu.VMEM
            )
            for i in range(len(ins))
        ],
        out_specs=[pl.BlockSpec(memory_space=pl.ANY if far else pltpu.VMEM)] * len(outs),
        scratch_shapes=list(scratch),
        compiler_params=pltpu.CompilerParams(vmem_limit_bytes=VMEM_LIMIT),
        cost_estimate=pl.CostEstimate(flops=flops, bytes_accessed=moved, transcendentals=0),
        name=name,
    )(*ins)


def lanes_low(x):
    return lax.broadcasted_iota(jnp.int32, x.shape, 1) < 64


def swap(x):
    return pltpu.roll(x, 64, 1)


def pick(low, high):
    return jnp.where(lanes_low(low), low, high)


def fill_windows(windows, start, lane, chunk, columns, stride):
    size = chunk.shape[0]
    column = lax.broadcasted_iota(jnp.int32, chunk.shape, 0) % columns
    before = jnp.where(column == 0, 0.0, pltpu.roll(chunk, 1, 0))
    after = jnp.where(column == columns - 1, 0.0, pltpu.roll(chunk, size - 1, 0))
    at = pl.ds(pl.multiple_of(columns + start, 32), size)
    for tap, part in enumerate((before, chunk, after)):
        first = tap * stride + lane
        windows[at, first : first + chunk.shape[1]] = part.astype(BF16)


def clear_edges(windows, columns):
    rows, lanes = windows.shape
    windows[0:columns, :] = jnp.zeros((columns, lanes), BF16)
    windows[rows - columns : rows, :] = jnp.zeros((columns, lanes), BF16)


def row_windows(windows, start, columns, lanes=slice(None)):
    return [
        windows[start + tap * columns : start + tap * columns + BLOCK, lanes] for tap in range(3)
    ]


def window_dot(windows, weights, start, columns, dims):
    rows = jnp.concatenate(row_windows(windows, start, columns), axis=1)
    return lax.dot_general(rows, weights[...], dims, preferred_element_type=F32)


def packed(low, high):
    return pick(low, swap(high)), pick(swap(low), high)


def unpacked(first, second):
    return packed(first, second)


def by_side(odd, inner, outer):
    return jnp.where(odd, inner, outer), jnp.where(odd, outer, inner)


def pieces_of(source, target, sems, parts):
    size = target.shape[1] // parts
    return [
        pltpu.make_async_copy(
            source.at[:, pl.ds(i * size, size), :], target.at[:, pl.ds(i * size, size), :], sems.at[i]
        )
        for i in range(parts)
    ]


def pack_body(volume, own, held, sems):
    copies = pieces_of(volume, held, sems, sems.shape[0])
    size = own.shape[0] // len(copies)
    for copy in copies:
        copy.start()
    for i, copy in enumerate(copies):
        copy.wait()
        rows = slice(i * size, i * size + size)
        own[rows, :] = jnp.concatenate([held[0, rows, :], held[1, rows, :]], axis=1)


def leave_body(
    columns, me, far_cotangent, far_weight, own, inner, outer, turned,
    windows, taps, cotangent, weight, sems, sem,
):
    cells = own.shape[0]
    half = cells // 2
    odd = me[0] % 2 == 1
    fetch = pltpu.make_async_copy(far_weight, weight, sem)
    copies = pieces_of(far_cotangent, cotangent, sems, sems.shape[0])
    for copy in copies:
        copy.start()
    fetch.start()
    clear_edges(windows, columns)
    size = cells // len(copies)
    for at, copy in enumerate(copies):
        copy.wait()

        def fill(i, carry):
            start = pl.multiple_of(at * size + i * STEP, STEP)
            for plane in range(2):
                chunk = cotangent[plane, pl.ds(start, STEP), :].astype(F32)
                fill_windows(windows, start, plane * 128, chunk, columns, 256)
            return carry

        lax.fori_loop(0, size // STEP, fill, 0)
    fetch.wait()
    for row in range(3):
        for column in range(3):
            for source in range(2):
                first = row * 768 + column * 256 + source * 128
                for at, target in enumerate(PLANES[:4]):
                    depth = depth_tap(source, target)
                    taps[at * 64 : at * 64 + 64, first : first + 128] = (
                        jnp.zeros((64, 128), BF16)
                        if depth is None
                        else weight[(2 - depth) * 9 + (2 - row) * 3 + 2 - column]
                    )
    for start in range(0, half, BLOCK):
        sides = []
        for first in (start, start + half):
            term = window_dot(windows, taps, first, columns, NT)
            own[first : first + BLOCK, :] = term[:, :128]
            sides.append(term[:, 128:])
        upper, lower = packed(*sides)
        inner[start : start + BLOCK, :] = jnp.where(odd, lower, upper).astype(BF16)
        outer[start : start + BLOCK, :] = jnp.where(odd, upper, lower).astype(BF16)
    for plane in range(2):
        turn(cotangent.at[plane], turned, plane * 128)


def prepare_body(
    columns, own, far_weight, own_windows, hidden, side_taps, back_taps, own_taps, weight, sem
):
    fetch = pltpu.make_async_copy(far_weight, weight, sem)
    fetch.start()

    def fill(i, carry):
        start = pl.multiple_of(i * STEP, STEP)
        chunk = own[pl.ds(start, STEP), :].astype(F32)
        fill_windows(own_windows, start, 0, chunk, columns, 128)
        return carry

    clear_edges(own_windows, columns)
    lax.fori_loop(0, own.shape[0] // STEP, fill, 0)
    fetch.wait()
    zero = jnp.zeros((64, 64), BF16)
    for row in range(3):
        for column in range(3):
            tap = row * 3 + column
            for at, source in enumerate(PLANES):
                depths = [depth_tap(source, target) for target in PLANES[:4]]
                parts = [zero if d is None else weight[d * 9 + tap] for d in depths]
                if at < 2:
                    target, first = own_taps, tap * 128 + at * 64
                else:
                    target, first = side_taps, tap * 256 + (at - 2) * 64
                target[first : first + 64, :128] = jnp.concatenate(parts[:2], axis=1)
                target[first : first + 64, 128:] = jnp.concatenate(parts[2:], axis=1)
            for plane in range(2):
                depths = [depth_tap(source, plane) for source in PLANES[:4]]
                parts = [zero if d is None else weight[(2 - d) * 9 + 8 - tap] for d in depths]
                at = row * 128 + plane * 64
                for pair in range(2):
                    first = column * 256 + pair * 128
                    back_taps[at : at + 64, first : first + 128] = jnp.concatenate(
                        parts[2 * pair : 2 * pair + 2], axis=1
                    )
    for start in range(0, own.shape[0], BLOCK):
        hidden[start : start + BLOCK, :] = window_dot(own_windows, own_taps, start, columns, NN)


def hidden_body(
    columns, count, me, inner, outer, part, side_taps, side_windows, act_windows, slope
):
    cells = outer.shape[0]
    odd = me[0] % 2 == 1

    def fill(i, carry):
        start = pl.multiple_of(i * STEP, STEP)
        rows = pl.ds(start, STEP)
        below, above = by_side(odd, inner[rows, :].astype(F32), outer[rows, :].astype(F32))
        fill_windows(side_windows, start, 0, pick(above, below), columns, 256)
        fill_windows(side_windows, start, 128, pick(below, above), columns, 256)
        return carry

    clear_edges(side_windows, columns)
    clear_edges(act_windows, columns)
    lax.fori_loop(0, cells // STEP, fill, 0)
    lanes = lax.broadcasted_iota(jnp.int32, (BLOCK, 128), 1)
    edges = [jnp.where(me[0] == end, 0.0, 1.0).astype(F32) for end in (count - 1, 0)]
    inside = jnp.where(lanes < 64, edges[0], edges[1])
    for start in range(0, cells, BLOCK):
        hidden = part[start : start + BLOCK, :]
        hidden = hidden + window_dot(side_windows, side_taps, start, columns, NN)
        gate = jax.nn.sigmoid(hidden)
        act = (hidden * gate).astype(BF16).astype(F32)
        fill_windows(act_windows, start, 0, act[:, :128], columns, 256)
        fill_windows(act_windows, start, 128, act[:, 128:] * inside, columns, 256)
        hidden, gate = hidden[:, :128], gate[:, :128]
        slope[start : start + BLOCK, :] = gate * (1.0 + hidden * (1.0 - gate))


def slope_body(me, terms, inner, outer, slope, grad, to_inner, to_outer):
    half = terms.shape[0] // 2
    odd = me[0] % 2 == 1

    def step(i, carry):
        start = pl.multiple_of(i * STEP, STEP)
        low, high = pl.ds(start, STEP), pl.ds(start + half, STEP)
        near = inner[low, :].astype(F32)
        arrived = unpacked(*by_side(odd, near, outer[low, :].astype(F32)))
        sides = []
        for rows, extra in zip((low, high), arrived):
            value = ((terms[rows, :] + extra) * slope[rows, :]).astype(BF16)
            grad[rows, :] = value
            sides.append(value.astype(F32))
        lower, upper = packed(*sides)
        to_inner[low, :] = jnp.where(odd, lower, upper).astype(BF16)
        to_outer[low, :] = jnp.where(odd, upper, lower).astype(BF16)
        return carry

    lax.fori_loop(0, half // STEP, step, 0)


def kernel_terms(columns, out_channels, slices, turned, terms):
    for row in range(3):
        for column in range(3):
            tap = row * 3 + column
            product = jnp.dot(turned[...], slices(row, column), preferred_element_type=F32)
            first, second = product[:out_channels], product[out_channels:]
            terms[:, tap * 128 : tap * 128 + 128] = first[:, :128] + swap(
                pick(second[:, 128:], second[:, :128])
            )
            group = 9 + tap // 2
            here = slice(group * 128, group * 128 + 128)
            if tap % 2 == 0:
                terms[:, here] = swap(first[:, 128:]) + second[:, :128]
            else:
                terms[:, here] = pick(terms[:, here], first[:, 128:] + swap(second[:, :128]))


def turn(source, target, first):
    for start in range(0, source.shape[0], STEP):
        chunk = source[start : start + STEP, :].astype(F32)
        target[first : first + chunk.shape[1], start : start + STEP] = chunk.T.astype(BF16)


def grad_two_body(columns, act_windows, turned, terms):
    cells = turned.shape[1]

    def slices(row, column):
        rows = slice(row * columns, row * columns + cells)
        return act_windows[rows, column * 256 : column * 256 + 256]

    kernel_terms(columns, 128, slices, turned, terms)


def coded(value, split):
    head = value[:split].astype(BF16)
    parts = [head, (value[:split] - head.astype(F32)).astype(BF16)]
    if split < value.shape[0]:
        parts.append(value[split:].astype(BF16))
    return jnp.concatenate(parts, axis=0)


def decoded(value, split):
    value = value.astype(F32)
    parts = [value[:split] + value[split : 2 * split]]
    if 2 * split < value.shape[0]:
        parts.append(value[2 * split :])
    return jnp.concatenate(parts, axis=0)


def grad_one_body(
    columns, count, me, own_windows, side_windows, grad, other, to_inner,
    message, kept, turned, terms,
):
    cells = grad.shape[0]

    def slices(row, column):
        rows = slice(row * columns, row * columns + cells)
        return jnp.concatenate(
            [
                own_windows[rows, column * 128 : column * 128 + 128],
                side_windows[rows, column * 256 : column * 256 + 128],
            ],
            axis=1,
        )

    turn(grad, turned, 0)
    kernel_terms(columns, 64, slices, turned, terms)
    half = terms.shape[1] // 2
    odd = me[0] % 2 == 1

    def share(owner):
        parts = []
        for source in (terms, other):
            each = source.shape[0] // count
            block = source[owner * each : owner * each + each, :]
            parts += [block[:, :half], block[:, half:]]
        return jnp.concatenate(parts, axis=0)

    groups = half // 128
    for pair in range(count // 2):
        even_share, odd_share = share(2 * pair), share(2 * pair + 1)
        kept[pair] = jnp.where(odd, odd_share, even_share)
        given = coded(jnp.where(odd, even_share, odd_share), kept.shape[1])
        size = given.shape[0]
        for group in range(groups):
            first = (pair * groups + group) * size
            message[first : first + size, :] = given[:, group * 128 : group * 128 + 128]
    message[message.shape[0] - to_inner.shape[0] :, :] = to_inner[...]


def sum_body(split, me, mine, message, sent, kept):
    place = me[0] // 2
    size, lanes = mine.shape[1:]
    groups = lanes // 128

    def arrived(at):
        parts = []
        for group in range(groups):
            first = pl.multiple_of((at * groups + group) * 2 * size, 8)
            parts.append(decoded(message[pl.ds(first, 2 * size), :], size))
        return jnp.concatenate(parts, axis=1)

    for at in range(mine.shape[0]):
        sent[at] = coded(mine[at] + arrived(at), split)
    kept[...] = mine[place] + arrived(place)


def finish_body(scale, split, sizes, me, mine, arrived, grad_one, grad_two):
    total = mine[...]
    for at in range(arrived.shape[0]):
        total = total + jnp.where(at == me[0] // 2, 0.0, decoded(arrived[at], split))
    total = total * scale
    half = total.shape[1]
    first = 0
    for size, out in zip(sizes, (grad_one, grad_two)):
        blocks = (total[first : first + size], total[first + size : first + 2 * size])
        first += 2 * size
        for tap in range(9):
            for depth, group, side in ((0, 9 + tap // 2, tap % 2), (1, tap, 0), (2, tap, 1)):
                lane = group * 128 + side * 64
                block, lane = (blocks[0], lane) if lane < half else (blocks[1], lane - half)
                out[depth * 9 + tap] = block[:, lane : lane + 64]


def output_body(columns, act_windows, far_weight, far, taps, weight, output, sem, sems):
    fetch = pltpu.make_async_copy(far_weight, weight, sem)
    fetch.start()
    fetch.wait()
    for row in range(3):
        for column in range(3):
            for at, source in enumerate(PLANES[:4]):
                first = row * 768 + column * 256 + at * 64
                for plane in range(2):
                    depth = depth_tap(source, plane)
                    taps[first : first + 64, plane * 128 : plane * 128 + 128] = (
                        jnp.zeros((64, 128), BF16)
                        if depth is None
                        else weight[depth * 9 + row * 3 + column]
                    )
    copies = pieces_of(output, far, sems, output.shape[1] // BLOCK)
    for at, copy in enumerate(copies):
        start = at * BLOCK
        value = None
        for row, rows in enumerate(row_windows(act_windows, start, columns)):
            term = jnp.dot(rows, taps[row * 768 : row * 768 + 768, :], preferred_element_type=F32)
            value = term if value is None else value + term
        output[0, start : start + BLOCK, :] = value[:, :128]
        output[1, start : start + BLOCK, :] = value[:, 128:]
        copy.start()
    for copy in copies:
        copy.wait()


def grad_volume_body(columns, me, own, message, outer, taps, far, windows, output, sems):
    half = own.shape[0] // 2
    odd = me[0] % 2 == 1
    before = message.shape[0] - half

    def fill(i, carry):
        start = pl.multiple_of(i * STEP, STEP)
        near = message[pl.ds(before + start, STEP), :].astype(F32)
        below, above = by_side(odd, near, outer[pl.ds(start, STEP), :].astype(F32))
        for first, side in zip((start, start + half), unpacked(above, below)):
            fill_windows(windows, first, 0, own[pl.ds(first, STEP), :].astype(F32), columns, 256)
            fill_windows(windows, first, 128, side, columns, 256)
        return carry

    clear_edges(windows, columns)
    lax.fori_loop(0, half // STEP, fill, 0)
    copies = pieces_of(output, far, sems, output.shape[1] // BLOCK)
    for at, copy in enumerate(copies):
        start = at * BLOCK
        rows = windows[start : start + BLOCK + 2 * columns, :]
        terms = lax.dot_general(rows, taps[...], NT, preferred_element_type=F32)
        value = terms[:BLOCK, :128]
        value = value + terms[columns : columns + BLOCK, 128:256]
        value = value + terms[2 * columns : 2 * columns + BLOCK, 256:]
        output[0, start : start + BLOCK, :] = value[:, :64]
        output[1, start : start + BLOCK, :] = value[:, 64:]
        copy.start()
    for copy in copies:
        copy.wait()


def shards(volume, weight_one, weight_two, cotangent):
    count = lax.axis_size("space")
    planes, rows, columns, channels = volume.shape
    cells = rows * columns
    scale = 1.0 / math.sqrt(planes * count * cells)
    mid, wide = weight_two.shape[3], weight_two.shape[4]
    me = lax.axis_index("space").astype(jnp.int32).reshape(1)
    shape = jax.ShapeDtypeStruct
    flat, pack = shape((cells, 128), BF16), shape((cells // 2, 128), BF16)
    slab = (cells + 2 * columns, 768)
    windows = pltpu.VMEM(slab, BF16)
    lanes = 14 * 64
    split = 2 * mid // count
    chunk = 2 * (mid + wide) // count

    within = [(i, i ^ 1) for i in range(count)]
    across = [(i, i + 1) for i in range(1, count - 1, 2)]
    across += [(j, i) for i, j in across]

    def shares(*lead):
        return shape((*lead, chunk + split, lanes), BF16), shape((*lead, chunk, lanes), F32)

    volume = volume.reshape(planes, cells, channels)
    cotangent = cotangent.reshape(planes, cells, wide)
    weight_one = weight_one.reshape(27, channels, mid)
    weight_two = weight_two.reshape(27, mid, wide)
    one_flops = 2 * planes * cells * 27 * channels * mid
    two_flops = 2 * planes * cells * 27 * mid * wide

    dma = pltpu.SemaphoreType.DMA
    far_one, far_two, far_volume, far_cotangent = (
        pltpu.with_memory_space_constraint(x, pltpu.HBM)
        for x in (weight_one, weight_two, volume, cotangent)
    )
    own, = call(
        pack_body, (flat,), (far_volume,),
        (pltpu.VMEM((planes, cells, channels), BF16), dma((4,))),
        name="pack_volume", apart=(0,),
    )
    vol_outer = lax.ppermute(own, "space", across)
    vol_inner = lax.ppermute(own, "space", within)
    terms, inner, outer, turned = call(
        functools.partial(leave_body, columns),
        (
            shape((cells, 128), F32), pack, pack, shape((256, cells), BF16),
        ),
        (me, far_cotangent, far_two),
        (
            windows, pltpu.VMEM((256, 3 * 768), BF16), pltpu.VMEM(cotangent.shape, BF16),
            pltpu.VMEM(weight_two.shape, BF16), dma((4,)), dma,
        ),
        two_flops, "grad_act_terms", (0,), (1, 2),
    )
    own, terms = lax.optimization_barrier((own, terms))
    own_windows, part, side_taps, back_taps = call(
        functools.partial(prepare_body, columns),
        (
            shape((slab[0], 384), BF16), shape((cells, 256), F32), shape((9 * 256, 256), BF16),
            shape((3 * 128, 768), BF16),
        ),
        (own, far_one),
        (pltpu.VMEM((9 * 128, 256), BF16), pltpu.VMEM(weight_one.shape, BF16), dma),
        one_flops, "prepare", (), (1,),
    )
    inner, outer, part = lax.optimization_barrier((inner, outer, part))
    terms_outer = lax.ppermute(outer, "space", across)
    terms_inner = lax.ppermute(inner, "space", within)
    side_windows, act_windows, slope = call(
        functools.partial(hidden_body, columns, count),
        (shape(slab, BF16), shape(slab, BF16), shape((cells, 128), F32)),
        (me, vol_inner, vol_outer, part, side_taps),
        (), 2 * one_flops, "hidden", (0,),
    )
    terms_two, = call(
        functools.partial(grad_two_body, columns),
        (shape((wide, 2 * lanes), F32),),
        (act_windows, turned), (), two_flops, "grad_two_terms",
    )
    terms_two, terms_outer = lax.optimization_barrier((terms_two, terms_outer))
    grad_hidden, to_inner, outer = call(
        slope_body, (flat, pack, pack), (me, terms, terms_inner, terms_outer, slope),
        name="grad_hidden", smem=(0,),
    )
    grad_outer = lax.ppermute(outer, "space", across)
    groups = lanes // 128
    message, kept = call(
        functools.partial(grad_one_body, columns, count),
        (
            shape((count // 2 * groups * 2 * chunk + cells // 2, 128), BF16),
            shares(count // 2)[1],
        ),
        (me, own_windows, side_windows, grad_hidden, terms_two, to_inner),
        (pltpu.VMEM((128, cells), BF16), pltpu.VMEM((mid, 2 * lanes), F32)),
        one_flops, "grad_one_terms", (0,),
    )
    message = lax.ppermute(message, "space", within)
    sent, mine = call(
        functools.partial(sum_body, split), (shares(count // 2)[0], shares()[1]),
        (me, kept, message), name="sum_pair", smem=(0,),
    )
    sent, act_windows, grad_hidden, grad_outer = lax.optimization_barrier(
        (sent, act_windows, grad_hidden, grad_outer)
    )
    arrived = lax.all_to_all(
        sent, "space", 0, 0, tiled=True,
        axis_index_groups=[list(range(core, count, 2)) for core in range(2)],
    )
    output, = call(
        functools.partial(output_body, columns),
        (shape((planes, cells, wide), F32),),
        (act_windows, far_two),
        (
            pltpu.VMEM((3 * 768, 256), BF16), pltpu.VMEM(weight_two.shape, BF16),
            pltpu.VMEM((planes, cells, wide), F32), dma, dma((cells // BLOCK,)),
        ),
        two_flops, "output", (), (1,), True,
    )
    grad_volume, = call(
        functools.partial(grad_volume_body, columns),
        (shape((planes, cells, channels), F32),),
        (me, grad_hidden, message, grad_outer, back_taps),
        (windows, pltpu.VMEM((planes, cells, channels), F32), dma((cells // BLOCK,))),
        one_flops, "grad_volume", (0,), (), True,
    )
    grad_one, grad_two = call(
        functools.partial(finish_body, scale, split, (mid // count, wide // count)),
        (shape((27, mid // count, channels), F32), shape((27, wide // count, mid), F32)),
        (me, mine, arrived), name="finish", smem=(0,),
    )
    return (
        output.reshape(planes, rows, columns, wide),
        grad_volume.reshape(planes, rows, columns, channels),
        jnp.swapaxes(grad_one, 1, 2).reshape(3, 3, 3, channels, mid // count),
        jnp.swapaxes(grad_two, 1, 2).reshape(3, 3, 3, mid, wide // count),
    )


def solution(mesh):
    cells = P(("groups", "space"), None, None, None)
    kernel = P("groups", None, None, None, "space")
    return jax.shard_map(
        shards,
        mesh=mesh,
        in_specs=(cells, P(), P(), cells),
        out_specs=(cells, cells, kernel, kernel),
        check_vma=False,
    )
```

```python
import functools
import math

import jax
import jax.numpy as jnp
from jax import lax
from jax.experimental import pallas as pl
from jax.experimental.pallas import tpu as pltpu
from jax.sharding import PartitionSpec as P

F32, BF16 = jnp.float32, jnp.bfloat16
STEP, BLOCK = 256, 512
VMEM_LIMIT = 16 * 2**20
NN = (((1,), (0,)), ((), ()))
NT = (((1,), (1,)), ((), ()))

PLANES = (0, 1, 2, -1, -2, 3)


def depth_tap(source, target):
    tap = source - target + 1
    return tap if 0 <= tap <= 2 else None


def call(body, outs, ins, scratch=(), flops=0, name=None, smem=(), apart=(), far=False):
    moved = sum(math.prod(s.shape) * s.dtype.itemsize for s in (*outs, *ins))
    return pl.pallas_call(
        body,
        out_shape=list(outs),
        in_specs=[
            pl.BlockSpec(
                memory_space=pltpu.SMEM if i in smem else pl.ANY if i in apart else pltpu.VMEM
            )
            for i in range(len(ins))
        ],
        out_specs=[pl.BlockSpec(memory_space=pl.ANY if far else pltpu.VMEM)] * len(outs),
        scratch_shapes=list(scratch),
        compiler_params=pltpu.CompilerParams(vmem_limit_bytes=VMEM_LIMIT),
        cost_estimate=pl.CostEstimate(flops=flops, bytes_accessed=moved, transcendentals=0),
        name=name,
    )(*ins)


def lanes_low(x):
    return lax.broadcasted_iota(jnp.int32, x.shape, 1) < 64


def swap(x):
    return pltpu.roll(x, 64, 1)


def pick(low, high):
    return jnp.where(lanes_low(low), low, high)


def fill_windows(windows, start, lane, chunk, columns, stride):
    size = chunk.shape[0]
    column = lax.broadcasted_iota(jnp.int32, chunk.shape, 0) % columns
    before = jnp.where(column == 0, 0.0, pltpu.roll(chunk, 1, 0))
    after = jnp.where(column == columns - 1, 0.0, pltpu.roll(chunk, size - 1, 0))
    at = pl.ds(pl.multiple_of(columns + start, 32), size)
    for tap, part in enumerate((before, chunk, after)):
        first = tap * stride + lane
        windows[at, first : first + chunk.shape[1]] = part.astype(BF16)


def clear_edges(windows, columns):
    rows, lanes = windows.shape
    windows[0:columns, :] = jnp.zeros((columns, lanes), BF16)
    windows[rows - columns : rows, :] = jnp.zeros((columns, lanes), BF16)


def row_windows(windows, start, columns, lanes=slice(None)):
    return [
        windows[start + tap * columns : start + tap * columns + BLOCK, lanes] for tap in range(3)
    ]


def window_dot(windows, weights, start, columns, dims):
    rows = jnp.concatenate(row_windows(windows, start, columns), axis=1)
    return lax.dot_general(rows, weights[...], dims, preferred_element_type=F32)


def packed(low, high):
    return pick(low, swap(high)), pick(swap(low), high)


def unpacked(first, second):
    return packed(first, second)


def by_side(odd, inner, outer):
    return jnp.where(odd, inner, outer), jnp.where(odd, outer, inner)


def pieces_of(source, target, sems, parts):
    size = target.shape[1] // parts
    return [
        pltpu.make_async_copy(
            source.at[:, pl.ds(i * size, size), :], target.at[:, pl.ds(i * size, size), :], sems.at[i]
        )
        for i in range(parts)
    ]


def pack_body(volume, own, held, sems):
    copies = pieces_of(volume, held, sems, sems.shape[0])
    size = own.shape[0] // len(copies)
    for copy in copies:
        copy.start()
    for i, copy in enumerate(copies):
        copy.wait()
        rows = slice(i * size, i * size + size)
        own[rows, :] = jnp.concatenate([held[0, rows, :], held[1, rows, :]], axis=1)


def leave_body(
    columns, me, far_cotangent, far_weight, own, inner, outer, turned,
    windows, taps, cotangent, weight, sems, sem,
):
    cells = own.shape[0]
    half = cells // 2
    odd = me[0] % 2 == 1
    fetch = pltpu.make_async_copy(far_weight, weight, sem)
    copies = pieces_of(far_cotangent, cotangent, sems, sems.shape[0])
    for copy in copies:
        copy.start()
    fetch.start()
    clear_edges(windows, columns)
    size = cells // len(copies)
    for at, copy in enumerate(copies):
        copy.wait()

        def fill(i, carry):
            start = pl.multiple_of(at * size + i * STEP, STEP)
            for plane in range(2):
                chunk = cotangent[plane, pl.ds(start, STEP), :].astype(F32)
                fill_windows(windows, start, plane * 128, chunk, columns, 256)
            return carry

        lax.fori_loop(0, size // STEP, fill, 0)
    fetch.wait()
    for row in range(3):
        for column in range(3):
            for source in range(2):
                first = row * 768 + column * 256 + source * 128
                for at, target in enumerate(PLANES[:4]):
                    depth = depth_tap(source, target)
                    taps[at * 64 : at * 64 + 64, first : first + 128] = (
                        jnp.zeros((64, 128), BF16)
                        if depth is None
                        else weight[(2 - depth) * 9 + (2 - row) * 3 + 2 - column]
                    )
    for start in range(0, half, BLOCK):
        sides = []
        for first in (start, start + half):
            term = window_dot(windows, taps, first, columns, NT)
            own[first : first + BLOCK, :] = term[:, :128]
            sides.append(term[:, 128:])
        upper, lower = packed(*sides)
        inner[start : start + BLOCK, :] = jnp.where(odd, lower, upper).astype(BF16)
        outer[start : start + BLOCK, :] = jnp.where(odd, upper, lower).astype(BF16)
    for plane in range(2):
        turn(cotangent.at[plane], turned, plane * 128)


def prepare_body(
    columns, own, far_weight, own_windows, hidden, side_taps, back_taps, own_taps, weight, sem
):
    fetch = pltpu.make_async_copy(far_weight, weight, sem)
    fetch.start()

    def fill(i, carry):
        start = pl.multiple_of(i * STEP, STEP)
        chunk = own[pl.ds(start, STEP), :].astype(F32)
        fill_windows(own_windows, start, 0, chunk, columns, 128)
        return carry

    clear_edges(own_windows, columns)
    lax.fori_loop(0, own.shape[0] // STEP, fill, 0)
    fetch.wait()
    zero = jnp.zeros((64, 64), BF16)
    for row in range(3):
        for column in range(3):
            tap = row * 3 + column
            for at, source in enumerate(PLANES):
                depths = [depth_tap(source, target) for target in PLANES[:4]]
                parts = [zero if d is None else weight[d * 9 + tap] for d in depths]
                if at < 2:
                    target, first = own_taps, tap * 128 + at * 64
                else:
                    target, first = side_taps, tap * 256 + (at - 2) * 64
                target[first : first + 64, :128] = jnp.concatenate(parts[:2], axis=1)
                target[first : first + 64, 128:] = jnp.concatenate(parts[2:], axis=1)
            for plane in range(2):
                depths = [depth_tap(source, plane) for source in PLANES[:4]]
                parts = [zero if d is None else weight[(2 - d) * 9 + 8 - tap] for d in depths]
                at = row * 128 + plane * 64
                for pair in range(2):
                    first = column * 256 + pair * 128
                    back_taps[at : at + 64, first : first + 128] = jnp.concatenate(
                        parts[2 * pair : 2 * pair + 2], axis=1
                    )
    for start in range(0, own.shape[0], BLOCK):
        hidden[start : start + BLOCK, :] = window_dot(own_windows, own_taps, start, columns, NN)


def hidden_body(
    columns, count, me, inner, outer, part, side_taps, side_windows, act_windows, slope
):
    cells = outer.shape[0]
    odd = me[0] % 2 == 1

    def fill(i, carry):
        start = pl.multiple_of(i * STEP, STEP)
        rows = pl.ds(start, STEP)
        below, above = by_side(odd, inner[rows, :].astype(F32), outer[rows, :].astype(F32))
        fill_windows(side_windows, start, 0, pick(above, below), columns, 256)
        fill_windows(side_windows, start, 128, pick(below, above), columns, 256)
        return carry

    clear_edges(side_windows, columns)
    clear_edges(act_windows, columns)
    lax.fori_loop(0, cells // STEP, fill, 0)
    lanes = lax.broadcasted_iota(jnp.int32, (BLOCK, 128), 1)
    edges = [jnp.where(me[0] == end, 0.0, 1.0).astype(F32) for end in (count - 1, 0)]
    inside = jnp.where(lanes < 64, edges[0], edges[1])
    for start in range(0, cells, BLOCK):
        hidden = part[start : start + BLOCK, :]
        hidden = hidden + window_dot(side_windows, side_taps, start, columns, NN)
        gate = jax.nn.sigmoid(hidden)
        act = (hidden * gate).astype(BF16).astype(F32)
        fill_windows(act_windows, start, 0, act[:, :128], columns, 256)
        fill_windows(act_windows, start, 128, act[:, 128:] * inside, columns, 256)
        hidden, gate = hidden[:, :128], gate[:, :128]
        slope[start : start + BLOCK, :] = gate * (1.0 + hidden * (1.0 - gate))


def slope_body(me, terms, inner, outer, slope, grad, to_inner, to_outer):
    half = terms.shape[0] // 2
    odd = me[0] % 2 == 1

    def step(i, carry):
        start = pl.multiple_of(i * STEP, STEP)
        low, high = pl.ds(start, STEP), pl.ds(start + half, STEP)
        near = inner[low, :].astype(F32)
        arrived = unpacked(*by_side(odd, near, outer[low, :].astype(F32)))
        sides = []
        for rows, extra in zip((low, high), arrived):
            value = ((terms[rows, :] + extra) * slope[rows, :]).astype(BF16)
            grad[rows, :] = value
            sides.append(value.astype(F32))
        lower, upper = packed(*sides)
        to_inner[low, :] = jnp.where(odd, lower, upper).astype(BF16)
        to_outer[low, :] = jnp.where(odd, upper, lower).astype(BF16)
        return carry

    lax.fori_loop(0, half // STEP, step, 0)


def kernel_terms(columns, out_channels, slices, turned, terms):
    for row in range(3):
        for column in range(3):
            tap = row * 3 + column
            product = jnp.dot(turned[...], slices(row, column), preferred_element_type=F32)
            first, second = product[:out_channels], product[out_channels:]
            terms[:, tap * 128 : tap * 128 + 128] = first[:, :128] + swap(
                pick(second[:, 128:], second[:, :128])
            )
            group = 9 + tap // 2
            here = slice(group * 128, group * 128 + 128)
            if tap % 2 == 0:
                terms[:, here] = swap(first[:, 128:]) + second[:, :128]
            else:
                terms[:, here] = pick(terms[:, here], first[:, 128:] + swap(second[:, :128]))


def turn(source, target, first):
    for start in range(0, source.shape[0], STEP):
        chunk = source[start : start + STEP, :].astype(F32)
        target[first : first + chunk.shape[1], start : start + STEP] = chunk.T.astype(BF16)


def grad_two_body(columns, act_windows, turned, terms):
    cells = turned.shape[1]

    def slices(row, column):
        rows = slice(row * columns, row * columns + cells)
        return act_windows[rows, column * 256 : column * 256 + 256]

    kernel_terms(columns, 128, slices, turned, terms)


def coded(value, split):
    head = value[:split].astype(BF16)
    parts = [head, (value[:split] - head.astype(F32)).astype(BF16)]
    if split < value.shape[0]:
        parts.append(value[split:].astype(BF16))
    return jnp.concatenate(parts, axis=0)


def decoded(value, split):
    value = value.astype(F32)
    parts = [value[:split] + value[split : 2 * split]]
    if 2 * split < value.shape[0]:
        parts.append(value[2 * split :])
    return jnp.concatenate(parts, axis=0)


def grad_one_body(
    columns, count, me, own_windows, side_windows, grad, other, message, kept, turned, terms
):
    cells = grad.shape[0]

    def slices(row, column):
        rows = slice(row * columns, row * columns + cells)
        return jnp.concatenate(
            [
                own_windows[rows, column * 128 : column * 128 + 128],
                side_windows[rows, column * 256 : column * 256 + 128],
            ],
            axis=1,
        )

    turn(grad, turned, 0)
    kernel_terms(columns, 64, slices, turned, terms)
    half = terms.shape[1] // 2
    odd = me[0] % 2 == 1

    def share(owner):
        parts = []
        for source in (terms, other):
            each = source.shape[0] // count
            block = source[owner * each : owner * each + each, :]
            parts += [block[:, :half], block[:, half:]]
        return jnp.concatenate(parts, axis=0)

    groups = half // 128
    for pair in range(count // 2):
        even_share, odd_share = share(2 * pair), share(2 * pair + 1)
        kept[pair] = jnp.where(odd, odd_share, even_share)
        given = coded(jnp.where(odd, even_share, odd_share), kept.shape[1])
        size = given.shape[0]
        for group in range(groups):
            first = (pair * groups + group) * size
            message[first : first + size, :] = given[:, group * 128 : group * 128 + 128]


def halve_body(split, me, mine, message, sent, kept):
    odd = (me[0] // 2) % 2
    size, lanes = mine.shape[1:]
    groups = lanes // 128

    def total(at):
        parts = []
        for group in range(groups):
            first = pl.multiple_of((at * groups + group) * 2 * size, 8)
            parts.append(decoded(message[pl.ds(first, 2 * size), :], size))
        return mine[at] + jnp.concatenate(parts, axis=1)

    for pair in range(sent.shape[0]):
        sent[pair] = coded(total(2 * pair + 1 - odd), split)
        kept[pair] = total(2 * pair + odd)


def spread_body(split, me, mine, arrived, kept, *sent):
    ring = mine.shape[0]
    place = me[0] // 4
    kept[...] = mine[place] + decoded(arrived[place], split)
    for hop, out in enumerate(sent):
        there = (place + hop + 1) % ring
        out[...] = (mine[there] + decoded(arrived[there], split)).astype(BF16)


def finish_body(scale, sizes, mine, *refs):
    arrived, (grad_one, grad_two) = refs[:-2], refs[-2:]
    total = mine[...]
    for part in arrived:
        total = total + part[...].astype(F32)
    total = total * scale
    half = total.shape[1]
    first = 0
    for size, out in zip(sizes, (grad_one, grad_two)):
        blocks = (total[first : first + size], total[first + size : first + 2 * size])
        first += 2 * size
        for tap in range(9):
            for depth, group, side in ((0, 9 + tap // 2, tap % 2), (1, tap, 0), (2, tap, 1)):
                lane = group * 128 + side * 64
                block, lane = (blocks[0], lane) if lane < half else (blocks[1], lane - half)
                out[depth * 9 + tap] = block[:, lane : lane + 64]


def output_body(columns, act_windows, weight, far, taps, output, sems):
    for row in range(3):
        for column in range(3):
            for at, source in enumerate(PLANES[:4]):
                first = row * 768 + column * 256 + at * 64
                for plane in range(2):
                    depth = depth_tap(source, plane)
                    taps[first : first + 64, plane * 128 : plane * 128 + 128] = (
                        jnp.zeros((64, 128), BF16)
                        if depth is None
                        else weight[depth * 9 + row * 3 + column]
                    )
    copies = pieces_of(output, far, sems, output.shape[1] // BLOCK)
    for at, copy in enumerate(copies):
        start = at * BLOCK
        value = window_dot(act_windows, taps, start, columns, NN)
        output[0, start : start + BLOCK, :] = value[:, :128]
        output[1, start : start + BLOCK, :] = value[:, 128:]
        copy.start()
    for copy in copies:
        copy.wait()


def grad_windows_body(columns, me, own, inner, outer, windows):
    half = own.shape[0] // 2
    odd = me[0] % 2 == 1

    def fill(i, carry):
        start = pl.multiple_of(i * STEP, STEP)
        rows = pl.ds(start, STEP)
        below, above = by_side(odd, inner[rows, :].astype(F32), outer[rows, :].astype(F32))
        for first, side in zip((start, start + half), unpacked(above, below)):
            fill_windows(windows, first, 0, own[pl.ds(first, STEP), :].astype(F32), columns, 256)
            fill_windows(windows, first, 128, side, columns, 256)
        return carry

    clear_edges(windows, columns)
    lax.fori_loop(0, half // STEP, fill, 0)


def grad_volume_body(columns, windows, taps, far, output, sems):
    copies = pieces_of(output, far, sems, output.shape[1] // BLOCK)
    for at, copy in enumerate(copies):
        start = at * BLOCK
        rows = windows[start : start + BLOCK + 2 * columns, :]
        terms = lax.dot_general(rows, taps[...], NT, preferred_element_type=F32)
        value = terms[:BLOCK, :128]
        value = value + terms[columns : columns + BLOCK, 128:256]
        value = value + terms[2 * columns : 2 * columns + BLOCK, 256:]
        output[0, start : start + BLOCK, :] = value[:, :64]
        output[1, start : start + BLOCK, :] = value[:, 64:]
        copy.start()
    for copy in copies:
        copy.wait()


def shards(volume, weight_one, weight_two, cotangent):
    count = lax.axis_size("space")
    planes, rows, columns, channels = volume.shape
    cells = rows * columns
    scale = 1.0 / math.sqrt(planes * count * cells)
    mid, wide = weight_two.shape[3], weight_two.shape[4]
    me = lax.axis_index("space").astype(jnp.int32).reshape(1)
    shape = jax.ShapeDtypeStruct
    flat, pack = shape((cells, 128), BF16), shape((cells // 2, 128), BF16)
    slab = (cells + 2 * columns, 768)
    windows = pltpu.VMEM(slab, BF16)
    lanes = 14 * 64
    split = 2 * mid // count
    chunk = 2 * (mid + wide) // count

    within = [(i, i ^ 1) for i in range(count)]
    across = [(i, i + 1) for i in range(1, count - 1, 2)]
    across += [(j, i) for i, j in across]

    def shares(*lead):
        return shape((*lead, chunk + split, lanes), BF16), shape((*lead, chunk, lanes), F32)

    volume = volume.reshape(planes, cells, channels)
    cotangent = cotangent.reshape(planes, cells, wide)
    weight_one = weight_one.reshape(27, channels, mid)
    weight_two = weight_two.reshape(27, mid, wide)
    one_flops = 2 * planes * cells * 27 * channels * mid
    two_flops = 2 * planes * cells * 27 * mid * wide

    dma = pltpu.SemaphoreType.DMA
    far_one, far_two, far_volume, far_cotangent = (
        pltpu.with_memory_space_constraint(x, pltpu.HBM)
        for x in (weight_one, weight_two, volume, cotangent)
    )
    own, = call(
        pack_body, (flat,), (far_volume,),
        (pltpu.VMEM((planes, cells, channels), BF16), dma((4,))),
        name="pack_volume", apart=(0,),
    )
    vol_outer = lax.ppermute(own, "space", across)
    vol_inner = lax.ppermute(own, "space", within)
    terms, inner, outer, turned = call(
        functools.partial(leave_body, columns),
        (
            shape((cells, 128), F32), pack, pack, shape((256, cells), BF16),
        ),
        (me, far_cotangent, far_two),
        (
            windows, pltpu.VMEM((256, 3 * 768), BF16), pltpu.VMEM(cotangent.shape, BF16),
            pltpu.VMEM(weight_two.shape, BF16), dma((4,)), dma,
        ),
        two_flops, "grad_act_terms", (0,), (1, 2),
    )
    own, terms = lax.optimization_barrier((own, terms))
    own_windows, part, side_taps, back_taps = call(
        functools.partial(prepare_body, columns),
        (
            shape((slab[0], 384), BF16), shape((cells, 256), F32), shape((9 * 256, 256), BF16),
            shape((3 * 128, 768), BF16),
        ),
        (own, far_one),
        (pltpu.VMEM((9 * 128, 256), BF16), pltpu.VMEM(weight_one.shape, BF16), dma),
        one_flops, "prepare", (), (1,),
    )
    inner, outer, part = lax.optimization_barrier((inner, outer, part))
    terms_outer = lax.ppermute(outer, "space", across)
    terms_inner = lax.ppermute(inner, "space", within)
    side_windows, act_windows, slope = call(
        functools.partial(hidden_body, columns, count),
        (shape(slab, BF16), shape(slab, BF16), shape((cells, 128), F32)),
        (me, vol_inner, vol_outer, part, side_taps),
        (), 2 * one_flops, "hidden", (0,),
    )
    terms_two, = call(
        functools.partial(grad_two_body, columns),
        (shape((wide, 2 * lanes), F32),),
        (act_windows, turned), (), two_flops, "grad_two_terms",
    )
    terms_two, terms_outer = lax.optimization_barrier((terms_two, terms_outer))
    grad_hidden, to_inner, outer = call(
        slope_body, (flat, pack, pack), (me, terms, terms_inner, terms_outer, slope),
        name="grad_hidden", smem=(0,),
    )
    grad_outer = lax.ppermute(outer, "space", across)
    grad_inner = lax.ppermute(to_inner, "space", within)
    groups = lanes // 128
    message, kept = call(
        functools.partial(grad_one_body, columns, count),
        (
            shape((count // 2 * groups * 2 * chunk, 128), BF16),
            shares(count // 2)[1],
        ),
        (me, own_windows, side_windows, grad_hidden, terms_two),
        (pltpu.VMEM((128, cells), BF16), pltpu.VMEM((mid, 2 * lanes), F32)),
        one_flops, "grad_one_terms", (0,),
    )
    message = lax.ppermute(message, "space", within)
    grad_windows, = call(
        functools.partial(grad_windows_body, columns), (shape(slab, BF16),),
        (me, grad_hidden, grad_inner, grad_outer),
        (), 16 * two_flops, "grad_windows", (0,),
    )
    message, grad_windows = lax.optimization_barrier((message, grad_windows))
    sent, kept = call(
        functools.partial(halve_body, split), shares(count // 4),
        (me, kept, message), name="halve", smem=(0,),
    )
    sent, act_windows = lax.optimization_barrier((sent, act_windows))
    arrived = lax.ppermute(sent, "space", [(i, i ^ 2) for i in range(count)])
    output, = call(
        functools.partial(output_body, columns),
        (shape((planes, cells, wide), F32),),
        (act_windows, weight_two),
        (
            pltpu.VMEM((3 * 768, 256), BF16), pltpu.VMEM((planes, cells, wide), F32),
            dma((cells // BLOCK,)),
        ),
        two_flops, "output", (), (), True,
    )
    ring = count // 4
    mine, *sent = call(
        functools.partial(spread_body, split),
        (shares()[1], *[shape((chunk, lanes), BF16)] * (ring - 1)),
        (me, kept, arrived), name="spread", smem=(0,),
    )
    sent, grad_windows = lax.optimization_barrier((sent, grad_windows))
    rest = [
        lax.ppermute(x, "space", [(i, (i + 4 * hop + 4) % count) for i in range(count)])
        for hop, x in enumerate(sent)
    ]
    grad_volume, = call(
        functools.partial(grad_volume_body, columns),
        (shape((planes, cells, channels), F32),),
        (grad_windows, back_taps),
        (pltpu.VMEM((planes, cells, channels), F32), dma((cells // BLOCK,))),
        one_flops, "grad_volume", (), (), True,
    )
    grad_one, grad_two = call(
        functools.partial(finish_body, scale, (mid // count, wide // count)),
        (shape((27, mid // count, channels), F32), shape((27, wide // count, mid), F32)),
        (mine, *rest), name="finish",
    )
    return (
        output.reshape(planes, rows, columns, wide),
        grad_volume.reshape(planes, rows, columns, channels),
        jnp.swapaxes(grad_one, 1, 2).reshape(3, 3, 3, channels, mid // count),
        jnp.swapaxes(grad_two, 1, 2).reshape(3, 3, 3, mid, wide // count),
    )


def solution(mesh):
    cells = P(("groups", "space"), None, None, None)
    kernel = P("groups", None, None, None, "space")
    return jax.shard_map(
        shards,
        mesh=mesh,
        in_specs=(cells, P(), P(), cells),
        out_specs=(cells, cells, kernel, kernel),
        check_vma=False,
    )
```

```python
import functools
import math

import jax
import jax.numpy as jnp
from jax import lax
from jax.experimental import pallas as pl
from jax.experimental.pallas import tpu as pltpu
from jax.sharding import PartitionSpec as P

F32, BF16 = jnp.float32, jnp.bfloat16
STEP, BLOCK = 256, 512
VMEM_LIMIT = 16 * 2**20
NN = (((1,), (0,)), ((), ()))
NT = (((1,), (1,)), ((), ()))

PLANES = (0, 1, 2, -1, -2, 3)


def depth_tap(source, target):
    tap = source - target + 1
    return tap if 0 <= tap <= 2 else None


def call(body, outs, ins, scratch=(), flops=0, name=None, smem=(), apart=(), far=False):
    moved = sum(math.prod(s.shape) * s.dtype.itemsize for s in (*outs, *ins))
    return pl.pallas_call(
        body,
        out_shape=list(outs),
        in_specs=[
            pl.BlockSpec(
                memory_space=pltpu.SMEM if i in smem else pl.ANY if i in apart else pltpu.VMEM
            )
            for i in range(len(ins))
        ],
        out_specs=[pl.BlockSpec(memory_space=pl.ANY if far else pltpu.VMEM)] * len(outs),
        scratch_shapes=list(scratch),
        compiler_params=pltpu.CompilerParams(vmem_limit_bytes=VMEM_LIMIT),
        cost_estimate=pl.CostEstimate(flops=flops, bytes_accessed=moved, transcendentals=0),
        name=name,
    )(*ins)


def lanes_low(x):
    return lax.broadcasted_iota(jnp.int32, x.shape, 1) < 64


def swap(x):
    return pltpu.roll(x, 64, 1)


def pick(low, high):
    return jnp.where(lanes_low(low), low, high)


def fill_windows(windows, start, lane, chunk, columns, stride):
    size = chunk.shape[0]
    column = lax.broadcasted_iota(jnp.int32, chunk.shape, 0) % columns
    before = jnp.where(column == 0, 0.0, pltpu.roll(chunk, 1, 0))
    after = jnp.where(column == columns - 1, 0.0, pltpu.roll(chunk, size - 1, 0))
    at = pl.ds(pl.multiple_of(columns + start, 32), size)
    for tap, part in enumerate((before, chunk, after)):
        first = tap * stride + lane
        windows[at, first : first + chunk.shape[1]] = part.astype(BF16)


def clear_edges(windows, columns):
    rows, lanes = windows.shape
    windows[0:columns, :] = jnp.zeros((columns, lanes), BF16)
    windows[rows - columns : rows, :] = jnp.zeros((columns, lanes), BF16)


def row_windows(windows, start, columns, lanes=slice(None)):
    return [
        windows[start + tap * columns : start + tap * columns + BLOCK, lanes] for tap in range(3)
    ]


def window_dot(windows, weights, start, columns, dims):
    rows = jnp.concatenate(row_windows(windows, start, columns), axis=1)
    return lax.dot_general(rows, weights[...], dims, preferred_element_type=F32)


def packed(low, high):
    return pick(low, swap(high)), pick(swap(low), high)


def unpacked(first, second):
    return packed(first, second)


def by_side(odd, inner, outer):
    return jnp.where(odd, inner, outer), jnp.where(odd, outer, inner)


def pieces_of(source, target, sems, parts):
    size = target.shape[1] // parts
    return [
        pltpu.make_async_copy(
            source.at[:, pl.ds(i * size, size), :], target.at[:, pl.ds(i * size, size), :], sems.at[i]
        )
        for i in range(parts)
    ]


def pack_body(volume, own, held, sems):
    copies = pieces_of(volume, held, sems, sems.shape[0])
    size = own.shape[0] // len(copies)
    for copy in copies:
        copy.start()
    for i, copy in enumerate(copies):
        copy.wait()
        rows = slice(i * size, i * size + size)
        own[rows, :] = jnp.concatenate([held[0, rows, :], held[1, rows, :]], axis=1)


def leave_body(
    columns, me, far_cotangent, far_weight, own, inner, outer, turned,
    windows, taps, cotangent, weight, sems, sem,
):
    cells = own.shape[0]
    half = cells // 2
    odd = me[0] % 2 == 1
    fetch = pltpu.make_async_copy(far_weight, weight, sem)
    copies = pieces_of(far_cotangent, cotangent, sems, sems.shape[0])
    for copy in copies:
        copy.start()
    fetch.start()
    clear_edges(windows, columns)
    size = cells // len(copies)
    for at, copy in enumerate(copies):
        copy.wait()

        def fill(i, carry):
            start = pl.multiple_of(at * size + i * STEP, STEP)
            for plane in range(2):
                chunk = cotangent[plane, pl.ds(start, STEP), :].astype(F32)
                fill_windows(windows, start, plane * 128, chunk, columns, 256)
            return carry

        lax.fori_loop(0, size // STEP, fill, 0)
    fetch.wait()
    for row in range(3):
        for column in range(3):
            for source in range(2):
                first = row * 768 + column * 256 + source * 128
                for at, target in enumerate(PLANES[:4]):
                    depth = depth_tap(source, target)
                    taps[at * 64 : at * 64 + 64, first : first + 128] = (
                        jnp.zeros((64, 128), BF16)
                        if depth is None
                        else weight[(2 - depth) * 9 + (2 - row) * 3 + 2 - column]
                    )
    for start in range(0, half, BLOCK):
        sides = []
        for first in (start, start + half):
            term = window_dot(windows, taps, first, columns, NT)
            own[first : first + BLOCK, :] = term[:, :128]
            sides.append(term[:, 128:])
        upper, lower = packed(*sides)
        inner[start : start + BLOCK, :] = jnp.where(odd, lower, upper).astype(BF16)
        outer[start : start + BLOCK, :] = jnp.where(odd, upper, lower).astype(BF16)
    for plane in range(2):
        turn(cotangent.at[plane], turned, plane * 128)


def prepare_body(
    columns, own, far_weight, own_windows, hidden, side_taps, back_taps, own_taps, weight, sem
):
    fetch = pltpu.make_async_copy(far_weight, weight, sem)
    fetch.start()

    def fill(i, carry):
        start = pl.multiple_of(i * STEP, STEP)
        chunk = own[pl.ds(start, STEP), :].astype(F32)
        fill_windows(own_windows, start, 0, chunk, columns, 128)
        return carry

    clear_edges(own_windows, columns)
    lax.fori_loop(0, own.shape[0] // STEP, fill, 0)
    fetch.wait()
    zero = jnp.zeros((64, 64), BF16)
    for row in range(3):
        for column in range(3):
            tap = row * 3 + column
            for at, source in enumerate(PLANES):
                depths = [depth_tap(source, target) for target in PLANES[:4]]
                parts = [zero if d is None else weight[d * 9 + tap] for d in depths]
                if at < 2:
                    target, first = own_taps, tap * 128 + at * 64
                else:
                    target, first = side_taps, tap * 256 + (at - 2) * 64
                target[first : first + 64, :128] = jnp.concatenate(parts[:2], axis=1)
                target[first : first + 64, 128:] = jnp.concatenate(parts[2:], axis=1)
            for plane in range(2):
                depths = [depth_tap(source, plane) for source in PLANES[:4]]
                parts = [zero if d is None else weight[(2 - d) * 9 + 8 - tap] for d in depths]
                at = row * 128 + plane * 64
                for pair in range(2):
                    first = column * 256 + pair * 128
                    back_taps[at : at + 64, first : first + 128] = jnp.concatenate(
                        parts[2 * pair : 2 * pair + 2], axis=1
                    )
    for start in range(0, own.shape[0], BLOCK):
        hidden[start : start + BLOCK, :] = window_dot(own_windows, own_taps, start, columns, NN)


def hidden_body(
    columns, count, me, inner, outer, part, side_taps, side_windows, act_windows, slope
):
    cells = outer.shape[0]
    odd = me[0] % 2 == 1

    def fill(i, carry):
        start = pl.multiple_of(i * STEP, STEP)
        rows = pl.ds(start, STEP)
        below, above = by_side(odd, inner[rows, :].astype(F32), outer[rows, :].astype(F32))
        fill_windows(side_windows, start, 0, pick(above, below), columns, 256)
        fill_windows(side_windows, start, 128, pick(below, above), columns, 256)
        return carry

    clear_edges(side_windows, columns)
    clear_edges(act_windows, columns)
    lax.fori_loop(0, cells // STEP, fill, 0)
    lanes = lax.broadcasted_iota(jnp.int32, (BLOCK, 128), 1)
    edges = [jnp.where(me[0] == end, 0.0, 1.0).astype(F32) for end in (count - 1, 0)]
    inside = jnp.where(lanes < 64, edges[0], edges[1])
    for start in range(0, cells, BLOCK):
        hidden = part[start : start + BLOCK, :]
        hidden = hidden + window_dot(side_windows, side_taps, start, columns, NN)
        gate = jax.nn.sigmoid(hidden)
        act = (hidden * gate).astype(BF16).astype(F32)
        fill_windows(act_windows, start, 0, act[:, :128], columns, 256)
        fill_windows(act_windows, start, 128, act[:, 128:] * inside, columns, 256)
        hidden, gate = hidden[:, :128], gate[:, :128]
        slope[start : start + BLOCK, :] = gate * (1.0 + hidden * (1.0 - gate))


def slope_body(me, terms, inner, outer, slope, grad, to_inner, to_outer):
    half = terms.shape[0] // 2
    odd = me[0] % 2 == 1

    def step(i, carry):
        start = pl.multiple_of(i * STEP, STEP)
        low, high = pl.ds(start, STEP), pl.ds(start + half, STEP)
        near = inner[low, :].astype(F32)
        arrived = unpacked(*by_side(odd, near, outer[low, :].astype(F32)))
        sides = []
        for rows, extra in zip((low, high), arrived):
            value = ((terms[rows, :] + extra) * slope[rows, :]).astype(BF16)
            grad[rows, :] = value
            sides.append(value.astype(F32))
        lower, upper = packed(*sides)
        to_inner[low, :] = jnp.where(odd, lower, upper).astype(BF16)
        to_outer[low, :] = jnp.where(odd, upper, lower).astype(BF16)
        return carry

    lax.fori_loop(0, half // STEP, step, 0)


def kernel_terms(columns, out_channels, slices, turned, terms):
    for row in range(3):
        for column in range(3):
            tap = row * 3 + column
            product = jnp.dot(turned[...], slices(row, column), preferred_element_type=F32)
            first, second = product[:out_channels], product[out_channels:]
            terms[:, tap * 128 : tap * 128 + 128] = first[:, :128] + swap(
                pick(second[:, 128:], second[:, :128])
            )
            group = 9 + tap // 2
            here = slice(group * 128, group * 128 + 128)
            if tap % 2 == 0:
                terms[:, here] = swap(first[:, 128:]) + second[:, :128]
            else:
                terms[:, here] = pick(terms[:, here], first[:, 128:] + swap(second[:, :128]))


def turn(source, target, first):
    for start in range(0, source.shape[0], STEP):
        chunk = source[start : start + STEP, :].astype(F32)
        target[first : first + chunk.shape[1], start : start + STEP] = chunk.T.astype(BF16)


def grad_two_body(columns, act_windows, turned, terms):
    cells = turned.shape[1]

    def slices(row, column):
        rows = slice(row * columns, row * columns + cells)
        return act_windows[rows, column * 256 : column * 256 + 256]

    kernel_terms(columns, 128, slices, turned, terms)


def coded(value, split):
    head = value[:split].astype(BF16)
    parts = [head, (value[:split] - head.astype(F32)).astype(BF16)]
    if split < value.shape[0]:
        parts.append(value[split:].astype(BF16))
    return jnp.concatenate(parts, axis=0)


def decoded(value, split):
    value = value.astype(F32)
    parts = [value[:split] + value[split : 2 * split]]
    if 2 * split < value.shape[0]:
        parts.append(value[2 * split :])
    return jnp.concatenate(parts, axis=0)


def grad_one_body(
    columns, count, me, own_windows, side_windows, grad, other, message, kept, turned, terms
):
    cells = grad.shape[0]

    def slices(row, column):
        rows = slice(row * columns, row * columns + cells)
        return jnp.concatenate(
            [
                own_windows[rows, column * 128 : column * 128 + 128],
                side_windows[rows, column * 256 : column * 256 + 128],
            ],
            axis=1,
        )

    turn(grad, turned, 0)
    kernel_terms(columns, 64, slices, turned, terms)
    half = terms.shape[1] // 2
    odd = me[0] % 2 == 1

    def share(owner):
        parts = []
        for source in (terms, other):
            each = source.shape[0] // count
            block = source[owner * each : owner * each + each, :]
            parts += [block[:, :half], block[:, half:]]
        return jnp.concatenate(parts, axis=0)

    groups = half // 128
    for pair in range(count // 2):
        even_share, odd_share = share(2 * pair), share(2 * pair + 1)
        kept[pair] = jnp.where(odd, odd_share, even_share)
        given = coded(jnp.where(odd, even_share, odd_share), kept.shape[1])
        size = given.shape[0]
        for group in range(groups):
            first = (pair * groups + group) * size
            message[first : first + size, :] = given[:, group * 128 : group * 128 + 128]


def halve_body(split, me, mine, message, sent, kept):
    odd = (me[0] // 2) % 2
    size, lanes = mine.shape[1:]
    groups = lanes // 128

    def total(at):
        parts = []
        for group in range(groups):
            first = pl.multiple_of((at * groups + group) * 2 * size, 8)
            parts.append(decoded(message[pl.ds(first, 2 * size), :], size))
        return mine[at] + jnp.concatenate(parts, axis=1)

    for pair in range(sent.shape[0]):
        sent[pair] = coded(total(2 * pair + 1 - odd), split)
        kept[pair] = total(2 * pair + odd)


def spread_body(split, me, mine, arrived, sent, kept):
    place = me[0] // 4
    for at in range(mine.shape[0]):
        sent[at] = (mine[at] + decoded(arrived[at], split)).astype(BF16)
    kept[...] = mine[place] + decoded(arrived[place], split)


def finish_body(scale, sizes, me, mine, arrived, grad_one, grad_two):
    total = mine[...]
    for at in range(arrived.shape[0]):
        total = total + jnp.where(at == me[0] // 4, 0.0, arrived[at].astype(F32))
    total = total * scale
    half = total.shape[1]
    first = 0
    for size, out in zip(sizes, (grad_one, grad_two)):
        blocks = (total[first : first + size], total[first + size : first + 2 * size])
        first += 2 * size
        for tap in range(9):
            for depth, group, side in ((0, 9 + tap // 2, tap % 2), (1, tap, 0), (2, tap, 1)):
                lane = group * 128 + side * 64
                block, lane = (blocks[0], lane) if lane < half else (blocks[1], lane - half)
                out[depth * 9 + tap] = block[:, lane : lane + 64]


def output_body(columns, act_windows, weight, far, taps, output, sems):
    for row in range(3):
        for column in range(3):
            for at, source in enumerate(PLANES[:4]):
                first = row * 768 + column * 256 + at * 64
                for plane in range(2):
                    depth = depth_tap(source, plane)
                    taps[first : first + 64, plane * 128 : plane * 128 + 128] = (
                        jnp.zeros((64, 128), BF16)
                        if depth is None
                        else weight[depth * 9 + row * 3 + column]
                    )
    copies = pieces_of(output, far, sems, output.shape[1] // BLOCK)
    for at, copy in enumerate(copies):
        start = at * BLOCK
        value = window_dot(act_windows, taps, start, columns, NN)
        output[0, start : start + BLOCK, :] = value[:, :128]
        output[1, start : start + BLOCK, :] = value[:, 128:]
        copy.start()
    for copy in copies:
        copy.wait()


def grad_windows_body(columns, me, own, inner, outer, windows):
    half = own.shape[0] // 2
    odd = me[0] % 2 == 1

    def fill(i, carry):
        start = pl.multiple_of(i * STEP, STEP)
        rows = pl.ds(start, STEP)
        below, above = by_side(odd, inner[rows, :].astype(F32), outer[rows, :].astype(F32))
        for first, side in zip((start, start + half), unpacked(above, below)):
            fill_windows(windows, first, 0, own[pl.ds(first, STEP), :].astype(F32), columns, 256)
            fill_windows(windows, first, 128, side, columns, 256)
        return carry

    clear_edges(windows, columns)
    lax.fori_loop(0, half // STEP, fill, 0)


def grad_volume_body(columns, windows, taps, far, output, sems):
    copies = pieces_of(output, far, sems, output.shape[1] // BLOCK)
    for at, copy in enumerate(copies):
        start = at * BLOCK
        rows = windows[start : start + BLOCK + 2 * columns, :]
        terms = lax.dot_general(rows, taps[...], NT, preferred_element_type=F32)
        value = terms[:BLOCK, :128]
        value = value + terms[columns : columns + BLOCK, 128:256]
        value = value + terms[2 * columns : 2 * columns + BLOCK, 256:]
        output[0, start : start + BLOCK, :] = value[:, :64]
        output[1, start : start + BLOCK, :] = value[:, 64:]
        copy.start()
    for copy in copies:
        copy.wait()


def shards(volume, weight_one, weight_two, cotangent):
    count = lax.axis_size("space")
    planes, rows, columns, channels = volume.shape
    cells = rows * columns
    scale = 1.0 / math.sqrt(planes * count * cells)
    mid, wide = weight_two.shape[3], weight_two.shape[4]
    me = lax.axis_index("space").astype(jnp.int32).reshape(1)
    shape = jax.ShapeDtypeStruct
    flat, pack = shape((cells, 128), BF16), shape((cells // 2, 128), BF16)
    slab = (cells + 2 * columns, 768)
    windows = pltpu.VMEM(slab, BF16)
    lanes = 14 * 64
    split = 2 * mid // count
    chunk = 2 * (mid + wide) // count

    within = [(i, i ^ 1) for i in range(count)]
    across = [(i, i + 1) for i in range(1, count - 1, 2)]
    across += [(j, i) for i, j in across]

    def shares(*lead):
        return shape((*lead, chunk + split, lanes), BF16), shape((*lead, chunk, lanes), F32)

    volume = volume.reshape(planes, cells, channels)
    cotangent = cotangent.reshape(planes, cells, wide)
    weight_one = weight_one.reshape(27, channels, mid)
    weight_two = weight_two.reshape(27, mid, wide)
    one_flops = 2 * planes * cells * 27 * channels * mid
    two_flops = 2 * planes * cells * 27 * mid * wide

    dma = pltpu.SemaphoreType.DMA
    far_one, far_two, far_volume, far_cotangent = (
        pltpu.with_memory_space_constraint(x, pltpu.HBM)
        for x in (weight_one, weight_two, volume, cotangent)
    )
    own, = call(
        pack_body, (flat,), (far_volume,),
        (pltpu.VMEM((planes, cells, channels), BF16), dma((4,))),
        name="pack_volume", apart=(0,),
    )
    vol_outer = lax.ppermute(own, "space", across)
    vol_inner = lax.ppermute(own, "space", within)
    terms, inner, outer, turned = call(
        functools.partial(leave_body, columns),
        (
            shape((cells, 128), F32), pack, pack, shape((256, cells), BF16),
        ),
        (me, far_cotangent, far_two),
        (
            windows, pltpu.VMEM((256, 3 * 768), BF16), pltpu.VMEM(cotangent.shape, BF16),
            pltpu.VMEM(weight_two.shape, BF16), dma((4,)), dma,
        ),
        two_flops, "grad_act_terms", (0,), (1, 2),
    )
    own, terms = lax.optimization_barrier((own, terms))
    own_windows, part, side_taps, back_taps = call(
        functools.partial(prepare_body, columns),
        (
            shape((slab[0], 384), BF16), shape((cells, 256), F32), shape((9 * 256, 256), BF16),
            shape((3 * 128, 768), BF16),
        ),
        (own, far_one),
        (pltpu.VMEM((9 * 128, 256), BF16), pltpu.VMEM(weight_one.shape, BF16), dma),
        one_flops, "prepare", (), (1,),
    )
    inner, outer, part = lax.optimization_barrier((inner, outer, part))
    terms_outer = lax.ppermute(outer, "space", across)
    terms_inner = lax.ppermute(inner, "space", within)
    side_windows, act_windows, slope = call(
        functools.partial(hidden_body, columns, count),
        (shape(slab, BF16), shape(slab, BF16), shape((cells, 128), F32)),
        (me, vol_inner, vol_outer, part, side_taps),
        (), 2 * one_flops, "hidden", (0,),
    )
    grad_hidden, to_inner, outer = call(
        slope_body, (flat, pack, pack), (me, terms, terms_inner, terms_outer, slope),
        name="grad_hidden", smem=(0,),
    )
    grad_outer = lax.ppermute(outer, "space", across)
    grad_inner = lax.ppermute(to_inner, "space", within)
    act_windows, grad_hidden = lax.optimization_barrier((act_windows, grad_hidden))
    terms_two, = call(
        functools.partial(grad_two_body, columns),
        (shape((wide, 2 * lanes), F32),),
        (act_windows, turned), (), two_flops, "grad_two_terms",
    )
    groups = lanes // 128
    message, kept = call(
        functools.partial(grad_one_body, columns, count),
        (
            shape((count // 2 * groups * 2 * chunk, 128), BF16),
            shares(count // 2)[1],
        ),
        (me, own_windows, side_windows, grad_hidden, terms_two),
        (pltpu.VMEM((128, cells), BF16), pltpu.VMEM((mid, 2 * lanes), F32)),
        one_flops, "grad_one_terms", (0,),
    )
    message = lax.ppermute(message, "space", within)
    grad_windows, = call(
        functools.partial(grad_windows_body, columns), (shape(slab, BF16),),
        (me, grad_hidden, grad_inner, grad_outer),
        (), 16 * two_flops, "grad_windows", (0,),
    )
    message, grad_windows = lax.optimization_barrier((message, grad_windows))
    sent, kept = call(
        functools.partial(halve_body, split), shares(count // 4),
        (me, kept, message), name="halve", smem=(0,),
    )
    sent, act_windows = lax.optimization_barrier((sent, act_windows))
    arrived = lax.ppermute(sent, "space", [(i, i ^ 2) for i in range(count)])
    output, = call(
        functools.partial(output_body, columns),
        (shape((planes, cells, wide), F32),),
        (act_windows, weight_two),
        (
            pltpu.VMEM((3 * 768, 256), BF16), pltpu.VMEM((planes, cells, wide), F32),
            dma((cells // BLOCK,)),
        ),
        two_flops, "output", (), (), True,
    )
    sent, mine = call(
        functools.partial(spread_body, split),
        (shape((count // 4, chunk, lanes), BF16), shares()[1]),
        (me, kept, arrived), name="spread", smem=(0,),
    )
    sent, grad_windows = lax.optimization_barrier((sent, grad_windows))
    arrived = lax.all_to_all(
        sent, "space", 0, 0, tiled=True,
        axis_index_groups=[list(range(i, count, 4)) for i in range(4)],
    )
    grad_volume, = call(
        functools.partial(grad_volume_body, columns),
        (shape((planes, cells, channels), F32),),
        (grad_windows, back_taps),
        (pltpu.VMEM((planes, cells, channels), F32), dma((cells // BLOCK,))),
        one_flops, "grad_volume", (), (), True,
    )
    grad_one, grad_two = call(
        functools.partial(finish_body, scale, (mid // count, wide // count)),
        (shape((27, mid // count, channels), F32), shape((27, wide // count, mid), F32)),
        (me, mine, arrived), name="finish", smem=(0,),
    )
    return (
        output.reshape(planes, rows, columns, wide),
        grad_volume.reshape(planes, rows, columns, channels),
        jnp.swapaxes(grad_one, 1, 2).reshape(3, 3, 3, channels, mid // count),
        jnp.swapaxes(grad_two, 1, 2).reshape(3, 3, 3, mid, wide // count),
    )


def solution(mesh):
    cells = P(("groups", "space"), None, None, None)
    kernel = P("groups", None, None, None, "space")
    return jax.shard_map(
        shards,
        mesh=mesh,
        in_specs=(cells, P(), P(), cells),
        out_specs=(cells, cells, kernel, kernel),
        check_vma=False,
    )
```

```python
import functools
import math

import jax
import jax.numpy as jnp
from jax import lax
from jax.experimental import pallas as pl
from jax.experimental.pallas import tpu as pltpu
from jax.sharding import PartitionSpec as P

F32, BF16 = jnp.float32, jnp.bfloat16
STEP, BLOCK = 256, 512
VMEM_LIMIT = 16 * 2**20
NN = (((1,), (0,)), ((), ()))
NT = (((1,), (1,)), ((), ()))

PLANES = (0, 1, 2, -1, -2, 3)


def depth_tap(source, target):
    tap = source - target + 1
    return tap if 0 <= tap <= 2 else None


def call(body, outs, ins, scratch=(), flops=0, name=None, smem=(), apart=(), far=False):
    moved = sum(math.prod(s.shape) * s.dtype.itemsize for s in (*outs, *ins))
    return pl.pallas_call(
        body,
        out_shape=list(outs),
        in_specs=[
            pl.BlockSpec(
                memory_space=pltpu.SMEM if i in smem else pl.ANY if i in apart else pltpu.VMEM
            )
            for i in range(len(ins))
        ],
        out_specs=[pl.BlockSpec(memory_space=pl.ANY if far else pltpu.VMEM)] * len(outs),
        scratch_shapes=list(scratch),
        compiler_params=pltpu.CompilerParams(vmem_limit_bytes=VMEM_LIMIT),
        cost_estimate=pl.CostEstimate(flops=flops, bytes_accessed=moved, transcendentals=0),
        name=name,
    )(*ins)


def lanes_low(x):
    return lax.broadcasted_iota(jnp.int32, x.shape, 1) < 64


def swap(x):
    return pltpu.roll(x, 64, 1)


def pick(low, high):
    return jnp.where(lanes_low(low), low, high)


def fill_windows(windows, start, lane, chunk, columns, stride):
    size = chunk.shape[0]
    column = lax.broadcasted_iota(jnp.int32, chunk.shape, 0) % columns
    before = jnp.where(column == 0, 0.0, pltpu.roll(chunk, 1, 0))
    after = jnp.where(column == columns - 1, 0.0, pltpu.roll(chunk, size - 1, 0))
    at = pl.ds(pl.multiple_of(columns + start, 32), size)
    for tap, part in enumerate((before, chunk, after)):
        first = tap * stride + lane
        windows[at, first : first + chunk.shape[1]] = part.astype(BF16)


def clear_edges(windows, columns):
    rows, lanes = windows.shape
    windows[0:columns, :] = jnp.zeros((columns, lanes), BF16)
    windows[rows - columns : rows, :] = jnp.zeros((columns, lanes), BF16)


def row_windows(windows, start, columns, lanes=slice(None)):
    return [
        windows[start + tap * columns : start + tap * columns + BLOCK, lanes] for tap in range(3)
    ]


def window_dot(windows, weights, start, columns, dims):
    rows = jnp.concatenate(row_windows(windows, start, columns), axis=1)
    return lax.dot_general(rows, weights[...], dims, preferred_element_type=F32)


def packed(low, high):
    return pick(low, swap(high)), pick(swap(low), high)


def unpacked(first, second):
    return packed(first, second)


def by_side(odd, inner, outer):
    return jnp.where(odd, inner, outer), jnp.where(odd, outer, inner)


def pieces_of(source, target, sems, parts):
    size = target.shape[1] // parts
    return [
        pltpu.make_async_copy(
            source.at[:, pl.ds(i * size, size), :], target.at[:, pl.ds(i * size, size), :], sems.at[i]
        )
        for i in range(parts)
    ]


def pack_body(volume, own, held, sems):
    copies = pieces_of(volume, held, sems, sems.shape[0])
    size = own.shape[0] // len(copies)
    for copy in copies:
        copy.start()
    for i, copy in enumerate(copies):
        copy.wait()
        rows = slice(i * size, i * size + size)
        own[rows, :] = jnp.concatenate([held[0, rows, :], held[1, rows, :]], axis=1)


def leave_body(
    columns, me, far_cotangent, far_weight, own, inner, outer, turned,
    windows, taps, cotangent, weight, sems, sem,
):
    cells = own.shape[0]
    half = cells // 2
    odd = me[0] % 2 == 1
    fetch = pltpu.make_async_copy(far_weight, weight, sem)
    copies = pieces_of(far_cotangent, cotangent, sems, sems.shape[0])
    for copy in copies:
        copy.start()
    fetch.start()
    clear_edges(windows, columns)
    size = cells // len(copies)
    for at, copy in enumerate(copies):
        copy.wait()

        def fill(i, carry):
            start = pl.multiple_of(at * size + i * STEP, STEP)
            for plane in range(2):
                chunk = cotangent[plane, pl.ds(start, STEP), :].astype(F32)
                fill_windows(windows, start, plane * 128, chunk, columns, 256)
            return carry

        lax.fori_loop(0, size // STEP, fill, 0)
    fetch.wait()
    for row in range(3):
        for column in range(3):
            for source in range(2):
                first = row * 768 + column * 256 + source * 128
                for at, target in enumerate(PLANES[:4]):
                    depth = depth_tap(source, target)
                    taps[at * 64 : at * 64 + 64, first : first + 128] = (
                        jnp.zeros((64, 128), BF16)
                        if depth is None
                        else weight[(2 - depth) * 9 + (2 - row) * 3 + 2 - column]
                    )
    for start in range(0, half, BLOCK):
        sides = []
        for first in (start, start + half):
            term = window_dot(windows, taps, first, columns, NT)
            own[first : first + BLOCK, :] = term[:, :128]
            sides.append(term[:, 128:])
        upper, lower = packed(*sides)
        inner[start : start + BLOCK, :] = jnp.where(odd, lower, upper).astype(BF16)
        outer[start : start + BLOCK, :] = jnp.where(odd, upper, lower).astype(BF16)
    for plane in range(2):
        turn(cotangent.at[plane], turned, plane * 128)


def prepare_body(
    columns, own, far_weight, own_windows, hidden, side_taps, own_taps, weight, sem
):
    fetch = pltpu.make_async_copy(far_weight, weight, sem)
    fetch.start()

    def fill(i, carry):
        start = pl.multiple_of(i * STEP, STEP)
        chunk = own[pl.ds(start, STEP), :].astype(F32)
        fill_windows(own_windows, start, 0, chunk, columns, 128)
        return carry

    clear_edges(own_windows, columns)
    lax.fori_loop(0, own.shape[0] // STEP, fill, 0)
    fetch.wait()
    zero = jnp.zeros((64, 64), BF16)
    for row in range(3):
        for column in range(3):
            tap = row * 3 + column
            for at, source in enumerate(PLANES):
                depths = [depth_tap(source, target) for target in PLANES[:4]]
                parts = [zero if d is None else weight[d * 9 + tap] for d in depths]
                if at < 2:
                    target, first = own_taps, tap * 128 + at * 64
                else:
                    target, first = side_taps, tap * 256 + (at - 2) * 64
                target[first : first + 64, :128] = jnp.concatenate(parts[:2], axis=1)
                target[first : first + 64, 128:] = jnp.concatenate(parts[2:], axis=1)
    for start in range(0, own.shape[0], BLOCK):
        hidden[start : start + BLOCK, :] = window_dot(own_windows, own_taps, start, columns, NN)


def back_taps_body(weight, back_taps):
    zero = jnp.zeros((64, 64), BF16)
    for row in range(3):
        for column in range(3):
            tap = row * 3 + column
            for plane in range(2):
                depths = [depth_tap(source, plane) for source in PLANES[:4]]
                parts = [zero if d is None else weight[(2 - d) * 9 + 8 - tap] for d in depths]
                at = row * 128 + plane * 64
                for pair in range(2):
                    first = column * 256 + pair * 128
                    back_taps[at : at + 64, first : first + 128] = jnp.concatenate(
                        parts[2 * pair : 2 * pair + 2], axis=1
                    )


def hidden_body(
    columns, count, me, inner, outer, part, side_taps, side_windows, act_windows, slope
):
    cells = outer.shape[0]
    odd = me[0] % 2 == 1

    def fill(i, carry):
        start = pl.multiple_of(i * STEP, STEP)
        rows = pl.ds(start, STEP)
        below, above = by_side(odd, inner[rows, :].astype(F32), outer[rows, :].astype(F32))
        fill_windows(side_windows, start, 0, pick(above, below), columns, 256)
        fill_windows(side_windows, start, 128, pick(below, above), columns, 256)
        return carry

    clear_edges(side_windows, columns)
    clear_edges(act_windows, columns)
    lax.fori_loop(0, cells // STEP, fill, 0)
    lanes = lax.broadcasted_iota(jnp.int32, (BLOCK, 128), 1)
    edges = [jnp.where(me[0] == end, 0.0, 1.0).astype(F32) for end in (count - 1, 0)]
    inside = jnp.where(lanes < 64, edges[0], edges[1])
    for start in range(0, cells, BLOCK):
        hidden = part[start : start + BLOCK, :]
        hidden = hidden + window_dot(side_windows, side_taps, start, columns, NN)
        gate = jax.nn.sigmoid(hidden)
        act = (hidden * gate).astype(BF16).astype(F32)
        fill_windows(act_windows, start, 0, act[:, :128], columns, 256)
        fill_windows(act_windows, start, 128, act[:, 128:] * inside, columns, 256)
        hidden, gate = hidden[:, :128], gate[:, :128]
        slope[start : start + BLOCK, :] = gate * (1.0 + hidden * (1.0 - gate))


def slope_body(me, terms, inner, outer, slope, grad, to_inner, to_outer):
    half = terms.shape[0] // 2
    odd = me[0] % 2 == 1

    def step(i, carry):
        start = pl.multiple_of(i * STEP, STEP)
        low, high = pl.ds(start, STEP), pl.ds(start + half, STEP)
        near = inner[low, :].astype(F32)
        arrived = unpacked(*by_side(odd, near, outer[low, :].astype(F32)))
        sides = []
        for rows, extra in zip((low, high), arrived):
            value = ((terms[rows, :] + extra) * slope[rows, :]).astype(BF16)
            grad[rows, :] = value
            sides.append(value.astype(F32))
        lower, upper = packed(*sides)
        to_inner[low, :] = jnp.where(odd, lower, upper).astype(BF16)
        to_outer[low, :] = jnp.where(odd, upper, lower).astype(BF16)
        return carry

    lax.fori_loop(0, half // STEP, step, 0)


def kernel_terms(columns, out_channels, slices, turned, terms):
    for row in range(3):
        for column in range(3):
            tap = row * 3 + column
            product = jnp.dot(turned[...], slices(row, column), preferred_element_type=F32)
            first, second = product[:out_channels], product[out_channels:]
            terms[:, tap * 128 : tap * 128 + 128] = first[:, :128] + swap(
                pick(second[:, 128:], second[:, :128])
            )
            group = 9 + tap // 2
            here = slice(group * 128, group * 128 + 128)
            if tap % 2 == 0:
                terms[:, here] = swap(first[:, 128:]) + second[:, :128]
            else:
                terms[:, here] = pick(terms[:, here], first[:, 128:] + swap(second[:, :128]))


def turn(source, target, first):
    for start in range(0, source.shape[0], STEP):
        chunk = source[start : start + STEP, :].astype(F32)
        target[first : first + chunk.shape[1], start : start + STEP] = chunk.T.astype(BF16)


def grad_two_body(columns, act_windows, turned, terms):
    cells = turned.shape[1]

    def slices(row, column):
        rows = slice(row * columns, row * columns + cells)
        return act_windows[rows, column * 256 : column * 256 + 256]

    kernel_terms(columns, 128, slices, turned, terms)


def coded(value, split):
    head = value[:split].astype(BF16)
    parts = [head, (value[:split] - head.astype(F32)).astype(BF16)]
    if split < value.shape[0]:
        parts.append(value[split:].astype(BF16))
    return jnp.concatenate(parts, axis=0)


def decoded(value, split):
    value = value.astype(F32)
    parts = [value[:split] + value[split : 2 * split]]
    if 2 * split < value.shape[0]:
        parts.append(value[2 * split :])
    return jnp.concatenate(parts, axis=0)


def grad_one_body(
    columns, count, me, own_windows, side_windows, grad, other, to_inner,
    message, kept, turned, terms,
):
    cells = grad.shape[0]

    def slices(row, column):
        rows = slice(row * columns, row * columns + cells)
        return jnp.concatenate(
            [
                own_windows[rows, column * 128 : column * 128 + 128],
                side_windows[rows, column * 256 : column * 256 + 128],
            ],
            axis=1,
        )

    turn(grad, turned, 0)
    kernel_terms(columns, 64, slices, turned, terms)
    half = terms.shape[1] // 2
    odd = me[0] % 2 == 1

    def share(owner):
        parts = []
        for source in (terms, other):
            each = source.shape[0] // count
            block = source[owner * each : owner * each + each, :]
            parts += [block[:, :half], block[:, half:]]
        return jnp.concatenate(parts, axis=0)

    groups = half // 128
    for pair in range(count // 2):
        even_share, odd_share = share(2 * pair), share(2 * pair + 1)
        kept[pair] = jnp.where(odd, odd_share, even_share)
        given = coded(jnp.where(odd, even_share, odd_share), kept.shape[1])
        size = given.shape[0]
        for group in range(groups):
            first = (pair * groups + group) * size
            message[first : first + size, :] = given[:, group * 128 : group * 128 + 128]
    message[message.shape[0] - to_inner.shape[0] :, :] = to_inner[...]


def halve_body(split, me, mine, message, sent, kept):
    odd = (me[0] // 2) % 2
    size, lanes = mine.shape[1:]
    groups = lanes // 128

    def total(at):
        parts = []
        for group in range(groups):
            first = pl.multiple_of((at * groups + group) * 2 * size, 8)
            parts.append(decoded(message[pl.ds(first, 2 * size), :], size))
        return mine[at] + jnp.concatenate(parts, axis=1)

    for pair in range(sent.shape[0]):
        sent[pair] = coded(total(2 * pair + 1 - odd), split)
        kept[pair] = total(2 * pair + odd)


def spread_body(split, me, mine, arrived, kept, *sent):
    place = me[0] // 4
    kept[...] = mine[place] + decoded(arrived[place], split)
    for hop, out in enumerate(sent):
        there = place ^ (hop + 1)
        out[...] = (mine[there] + decoded(arrived[there], split)).astype(BF16)


def finish_body(scale, sizes, mine, *refs):
    arrived, (grad_one, grad_two) = refs[:-2], refs[-2:]
    total = mine[...]
    for part in arrived:
        total = total + part[...].astype(F32)
    total = total * scale
    half = total.shape[1]
    first = 0
    for size, out in zip(sizes, (grad_one, grad_two)):
        blocks = (total[first : first + size], total[first + size : first + 2 * size])
        first += 2 * size
        for tap in range(9):
            for depth, group, side in ((0, 9 + tap // 2, tap % 2), (1, tap, 0), (2, tap, 1)):
                lane = group * 128 + side * 64
                block, lane = (blocks[0], lane) if lane < half else (blocks[1], lane - half)
                out[depth * 9 + tap] = block[:, lane : lane + 64]


def output_body(columns, act_windows, weight, far, taps, output, sems):
    for row in range(3):
        for column in range(3):
            for at, source in enumerate(PLANES[:4]):
                first = row * 768 + column * 256 + at * 64
                for plane in range(2):
                    depth = depth_tap(source, plane)
                    taps[first : first + 64, plane * 128 : plane * 128 + 128] = (
                        jnp.zeros((64, 128), BF16)
                        if depth is None
                        else weight[depth * 9 + row * 3 + column]
                    )
    copies = pieces_of(output, far, sems, output.shape[1] // BLOCK)
    for at, copy in enumerate(copies):
        start = at * BLOCK
        value = window_dot(act_windows, taps, start, columns, NN)
        output[0, start : start + BLOCK, :] = value[:, :128]
        output[1, start : start + BLOCK, :] = value[:, 128:]
        copy.start()
    for copy in copies:
        copy.wait()


def grad_windows_body(columns, count, me, own, message, outer, windows):
    half = own.shape[0] // 2
    side = me[0] % 2
    near, across = message.shape[0] - half, side * half
    edge = jnp.logical_or(me[0] == 0, me[0] == count - 1)
    inside = jnp.where(edge, 0.0, 1.0).astype(F32)

    def fill(i, carry):
        start = pl.multiple_of(i * STEP, STEP)
        below, above = by_side(
            side == 1,
            message[pl.ds(near + start, STEP), :].astype(F32),
            outer[pl.ds(pl.multiple_of(across + start, STEP), STEP), :].astype(F32) * inside,
        )
        for first, side_planes in zip((start, start + half), unpacked(above, below)):
            fill_windows(windows, first, 0, own[pl.ds(first, STEP), :].astype(F32), columns, 256)
            fill_windows(windows, first, 128, side_planes, columns, 256)
        return carry

    clear_edges(windows, columns)
    lax.fori_loop(0, half // STEP, fill, 0)


def grad_volume_body(columns, windows, taps, far, output, sems):
    copies = pieces_of(output, far, sems, output.shape[1] // BLOCK)
    for at, copy in enumerate(copies):
        start = at * BLOCK
        rows = windows[start : start + BLOCK + 2 * columns, :]
        terms = lax.dot_general(rows, taps[...], NT, preferred_element_type=F32)
        value = terms[:BLOCK, :128]
        value = value + terms[columns : columns + BLOCK, 128:256]
        value = value + terms[2 * columns : 2 * columns + BLOCK, 256:]
        output[0, start : start + BLOCK, :] = value[:, :64]
        output[1, start : start + BLOCK, :] = value[:, 64:]
        copy.start()
    for copy in copies:
        copy.wait()


def shards(volume, weight_one, weight_two, cotangent):
    count = lax.axis_size("space")
    planes, rows, columns, channels = volume.shape
    cells = rows * columns
    scale = 1.0 / math.sqrt(planes * count * cells)
    mid, wide = weight_two.shape[3], weight_two.shape[4]
    me = lax.axis_index("space").astype(jnp.int32).reshape(1)
    shape = jax.ShapeDtypeStruct
    flat, pack = shape((cells, 128), BF16), shape((cells // 2, 128), BF16)
    slab = (cells + 2 * columns, 768)
    windows = pltpu.VMEM(slab, BF16)
    lanes = 14 * 64
    split = 2 * mid // count
    chunk = 2 * (mid + wide) // count

    within = [(i, i ^ 1) for i in range(count)]
    across = [(i, i + 1) for i in range(1, count - 1, 2)]
    across += [(j, i) for i, j in across]

    def shares(*lead):
        return shape((*lead, chunk + split, lanes), BF16), shape((*lead, chunk, lanes), F32)

    volume = volume.reshape(planes, cells, channels)
    cotangent = cotangent.reshape(planes, cells, wide)
    weight_one = weight_one.reshape(27, channels, mid)
    weight_two = weight_two.reshape(27, mid, wide)
    one_flops = 2 * planes * cells * 27 * channels * mid
    two_flops = 2 * planes * cells * 27 * mid * wide

    dma = pltpu.SemaphoreType.DMA
    far_one, far_two, far_volume, far_cotangent = (
        pltpu.with_memory_space_constraint(x, pltpu.HBM)
        for x in (weight_one, weight_two, volume, cotangent)
    )
    own, = call(
        pack_body, (flat,), (far_volume,),
        (pltpu.VMEM((planes, cells, channels), BF16), dma((4,))),
        name="pack_volume", apart=(0,),
    )
    vol_outer = lax.ppermute(own, "space", across)
    vol_inner = lax.ppermute(own, "space", within)
    terms, inner, outer, turned = call(
        functools.partial(leave_body, columns),
        (
            shape((cells, 128), F32), pack, pack, shape((256, cells), BF16),
        ),
        (me, far_cotangent, far_two),
        (
            windows, pltpu.VMEM((256, 3 * 768), BF16), pltpu.VMEM(cotangent.shape, BF16),
            pltpu.VMEM(weight_two.shape, BF16), dma((4,)), dma,
        ),
        two_flops, "grad_act_terms", (0,), (1, 2),
    )
    own, terms = lax.optimization_barrier((own, terms))
    own_windows, part, side_taps = call(
        functools.partial(prepare_body, columns),
        (
            shape((slab[0], 384), BF16), shape((cells, 256), F32), shape((9 * 256, 256), BF16),
        ),
        (own, far_one),
        (pltpu.VMEM((9 * 128, 256), BF16), pltpu.VMEM(weight_one.shape, BF16), dma),
        one_flops, "prepare", (), (1,),
    )
    inner, outer, part = lax.optimization_barrier((inner, outer, part))
    terms_outer = lax.ppermute(outer, "space", across)
    terms_inner = lax.ppermute(inner, "space", within)
    side_windows, act_windows, slope = call(
        functools.partial(hidden_body, columns, count),
        (shape(slab, BF16), shape(slab, BF16), shape((cells, 128), F32)),
        (me, vol_inner, vol_outer, part, side_taps),
        (), 2 * one_flops, "hidden", (0,),
    )
    grad_hidden, to_inner, outer = call(
        slope_body, (flat, pack, pack), (me, terms, terms_inner, terms_outer, slope),
        name="grad_hidden", smem=(0,),
    )
    pairs = [[i, (i + 1) % count] for i in range(1, count, 2)]
    grad_outer = lax.all_gather(outer, "space", axis_index_groups=pairs, tiled=True)
    act_windows, grad_hidden = lax.optimization_barrier((act_windows, grad_hidden))
    terms_two, = call(
        functools.partial(grad_two_body, columns),
        (shape((wide, 2 * lanes), F32),),
        (act_windows, turned), (), two_flops, "grad_two_terms",
    )
    groups = lanes // 128
    message, kept = call(
        functools.partial(grad_one_body, columns, count),
        (
            shape((count // 2 * groups * 2 * chunk + cells // 2, 128), BF16),
            shares(count // 2)[1],
        ),
        (me, own_windows, side_windows, grad_hidden, terms_two, to_inner),
        (pltpu.VMEM((128, cells), BF16), pltpu.VMEM((mid, 2 * lanes), F32)),
        one_flops, "grad_one_terms", (0,),
    )
    message = lax.ppermute(message, "space", within)
    back_taps, = call(
        back_taps_body, (shape((3 * 128, 768), BF16),), (weight_one,), (), 2 * one_flops, "back_taps"
    )
    message, back_taps = lax.optimization_barrier((message, back_taps))
    sent, kept = call(
        functools.partial(halve_body, split), shares(count // 4),
        (me, kept, message), name="halve", smem=(0,),
    )
    sent, act_windows = lax.optimization_barrier((sent, act_windows))
    arrived = lax.ppermute(sent, "space", [(i, i ^ 2) for i in range(count)])
    output, = call(
        functools.partial(output_body, columns),
        (shape((planes, cells, wide), F32),),
        (act_windows, weight_two),
        (
            pltpu.VMEM((3 * 768, 256), BF16), pltpu.VMEM((planes, cells, wide), F32),
            dma((cells // BLOCK,)),
        ),
        two_flops, "output", (), (), True,
    )
    ring = count // 4
    mine, *sent = call(
        functools.partial(spread_body, split),
        (shares()[1], *[shape((chunk, lanes), BF16)] * (ring - 1)),
        (me, kept, arrived), name="spread", smem=(0,),
    )
    sent, grad_hidden = lax.optimization_barrier((sent, grad_hidden))
    rest = [
        lax.ppermute(x, "space", [(i, i ^ (4 * hop + 4)) for i in range(count)])
        for hop, x in enumerate(sent)
    ]
    grad_windows, = call(
        functools.partial(grad_windows_body, columns, count), (shape(slab, BF16),),
        (me, grad_hidden, message, grad_outer),
        (), one_flops // 4, "grad_windows", (0,),
    )
    grad_volume, = call(
        functools.partial(grad_volume_body, columns),
        (shape((planes, cells, channels), F32),),
        (grad_windows, back_taps),
        (pltpu.VMEM((planes, cells, channels), F32), dma((cells // BLOCK,))),
        one_flops, "grad_volume", (), (), True,
    )
    grad_one, grad_two = call(
        functools.partial(finish_body, scale, (mid // count, wide // count)),
        (shape((27, mid // count, channels), F32), shape((27, wide // count, mid), F32)),
        (mine, *rest), name="finish",
    )
    return (
        output.reshape(planes, rows, columns, wide),
        grad_volume.reshape(planes, rows, columns, channels),
        jnp.swapaxes(grad_one, 1, 2).reshape(3, 3, 3, channels, mid // count),
        jnp.swapaxes(grad_two, 1, 2).reshape(3, 3, 3, mid, wide // count),
    )


def solution(mesh):
    cells = P(("groups", "space"), None, None, None)
    kernel = P("groups", None, None, None, "space")
    return jax.shard_map(
        shards,
        mesh=mesh,
        in_specs=(cells, P(), P(), cells),
        out_specs=(cells, cells, kernel, kernel),
        check_vma=False,
    )
```

```python
import functools
import math

import jax
import jax.numpy as jnp
from jax import lax
from jax.experimental import pallas as pl
from jax.experimental.pallas import tpu as pltpu
from jax.sharding import PartitionSpec as P

F32, BF16 = jnp.float32, jnp.bfloat16
STEP, BLOCK = 256, 512
VMEM_LIMIT = 16 * 2**20
NN = (((1,), (0,)), ((), ()))
NT = (((1,), (1,)), ((), ()))

PLANES = (0, 1, 2, -1, -2, 3)


def depth_tap(source, target):
    tap = source - target + 1
    return tap if 0 <= tap <= 2 else None


def call(body, outs, ins, scratch=(), flops=0, name=None, smem=(), apart=(), far=False):
    moved = sum(math.prod(s.shape) * s.dtype.itemsize for s in (*outs, *ins))
    return pl.pallas_call(
        body,
        out_shape=list(outs),
        in_specs=[
            pl.BlockSpec(
                memory_space=pltpu.SMEM if i in smem else pl.ANY if i in apart else pltpu.VMEM
            )
            for i in range(len(ins))
        ],
        out_specs=[pl.BlockSpec(memory_space=pl.ANY if far else pltpu.VMEM)] * len(outs),
        scratch_shapes=list(scratch),
        compiler_params=pltpu.CompilerParams(vmem_limit_bytes=VMEM_LIMIT),
        cost_estimate=pl.CostEstimate(flops=flops, bytes_accessed=moved, transcendentals=0),
        name=name,
    )(*ins)


def lanes_low(x):
    return lax.broadcasted_iota(jnp.int32, x.shape, 1) < 64


def swap(x):
    return pltpu.roll(x, 64, 1)


def pick(low, high):
    return jnp.where(lanes_low(low), low, high)


def fill_windows(windows, start, lane, chunk, columns, stride):
    size = chunk.shape[0]
    column = lax.broadcasted_iota(jnp.int32, chunk.shape, 0) % columns
    before = jnp.where(column == 0, 0.0, pltpu.roll(chunk, 1, 0))
    after = jnp.where(column == columns - 1, 0.0, pltpu.roll(chunk, size - 1, 0))
    at = pl.ds(pl.multiple_of(columns + start, 32), size)
    for tap, part in enumerate((before, chunk, after)):
        first = tap * stride + lane
        windows[at, first : first + chunk.shape[1]] = part.astype(BF16)


def clear_edges(windows, columns):
    rows, lanes = windows.shape
    windows[0:columns, :] = jnp.zeros((columns, lanes), BF16)
    windows[rows - columns : rows, :] = jnp.zeros((columns, lanes), BF16)


def row_windows(windows, start, columns, lanes=slice(None)):
    return [
        windows[start + tap * columns : start + tap * columns + BLOCK, lanes] for tap in range(3)
    ]


def window_dot(windows, weights, start, columns, dims):
    rows = jnp.concatenate(row_windows(windows, start, columns), axis=1)
    return lax.dot_general(rows, weights[...], dims, preferred_element_type=F32)


def packed(low, high):
    return pick(low, swap(high)), pick(swap(low), high)


def unpacked(first, second):
    return packed(first, second)


def by_side(odd, inner, outer):
    return jnp.where(odd, inner, outer), jnp.where(odd, outer, inner)


def pieces_of(source, target, sems, parts):
    size = target.shape[1] // parts
    return [
        pltpu.make_async_copy(
            source.at[:, pl.ds(i * size, size), :], target.at[:, pl.ds(i * size, size), :], sems.at[i]
        )
        for i in range(parts)
    ]


def pack_body(volume, own, held, sems):
    copies = pieces_of(volume, held, sems, sems.shape[0])
    size = own.shape[0] // len(copies)
    for copy in copies:
        copy.start()
    for i, copy in enumerate(copies):
        copy.wait()
        rows = slice(i * size, i * size + size)
        own[rows, :] = jnp.concatenate([held[0, rows, :], held[1, rows, :]], axis=1)


def leave_body(
    columns, me, far_cotangent, far_weight, own, inner, outer, turned,
    windows, taps, cotangent, weight, sems, sem,
):
    cells = own.shape[0]
    half = cells // 2
    odd = me[0] % 2 == 1
    fetch = pltpu.make_async_copy(far_weight, weight, sem)
    copies = pieces_of(far_cotangent, cotangent, sems, sems.shape[0])
    for copy in copies:
        copy.start()
    fetch.start()
    clear_edges(windows, columns)
    size = cells // len(copies)
    for at, copy in enumerate(copies):
        copy.wait()

        def fill(i, carry):
            start = pl.multiple_of(at * size + i * STEP, STEP)
            for plane in range(2):
                chunk = cotangent[plane, pl.ds(start, STEP), :].astype(F32)
                fill_windows(windows, start, plane * 128, chunk, columns, 256)
            return carry

        lax.fori_loop(0, size // STEP, fill, 0)
    fetch.wait()
    for row in range(3):
        for column in range(3):
            for source in range(2):
                first = row * 768 + column * 256 + source * 128
                for at, target in enumerate(PLANES[:4]):
                    depth = depth_tap(source, target)
                    taps[at * 64 : at * 64 + 64, first : first + 128] = (
                        jnp.zeros((64, 128), BF16)
                        if depth is None
                        else weight[(2 - depth) * 9 + (2 - row) * 3 + 2 - column]
                    )
    for start in range(0, half, BLOCK):
        sides = []
        for first in (start, start + half):
            term = window_dot(windows, taps, first, columns, NT)
            own[first : first + BLOCK, :] = term[:, :128]
            sides.append(term[:, 128:])
        upper, lower = packed(*sides)
        inner[start : start + BLOCK, :] = jnp.where(odd, lower, upper).astype(BF16)
        outer[start : start + BLOCK, :] = jnp.where(odd, upper, lower).astype(BF16)
    for plane in range(2):
        turn(cotangent.at[plane], turned, plane * 128)


def prepare_body(
    columns, own, far_weight, own_windows, hidden, side_taps, own_taps, weight, sem
):
    fetch = pltpu.make_async_copy(far_weight, weight, sem)
    fetch.start()

    def fill(i, carry):
        start = pl.multiple_of(i * STEP, STEP)
        chunk = own[pl.ds(start, STEP), :].astype(F32)
        fill_windows(own_windows, start, 0, chunk, columns, 128)
        return carry

    clear_edges(own_windows, columns)
    lax.fori_loop(0, own.shape[0] // STEP, fill, 0)
    fetch.wait()
    zero = jnp.zeros((64, 64), BF16)
    for row in range(3):
        for column in range(3):
            tap = row * 3 + column
            for at, source in enumerate(PLANES):
                depths = [depth_tap(source, target) for target in PLANES[:4]]
                parts = [zero if d is None else weight[d * 9 + tap] for d in depths]
                if at < 2:
                    target, first = own_taps, tap * 128 + at * 64
                else:
                    target, first = side_taps, tap * 256 + (at - 2) * 64
                target[first : first + 64, :128] = jnp.concatenate(parts[:2], axis=1)
                target[first : first + 64, 128:] = jnp.concatenate(parts[2:], axis=1)
    for start in range(0, own.shape[0], BLOCK):
        hidden[start : start + BLOCK, :] = window_dot(own_windows, own_taps, start, columns, NN)


def back_taps_body(weight, back_taps):
    zero = jnp.zeros((64, 64), BF16)
    for row in range(3):
        for column in range(3):
            tap = row * 3 + column
            for plane in range(2):
                depths = [depth_tap(source, plane) for source in PLANES[:4]]
                parts = [zero if d is None else weight[(2 - d) * 9 + 8 - tap] for d in depths]
                at = row * 128 + plane * 64
                for pair in range(2):
                    first = column * 256 + pair * 128
                    back_taps[at : at + 64, first : first + 128] = jnp.concatenate(
                        parts[2 * pair : 2 * pair + 2], axis=1
                    )


def hidden_body(
    columns, count, me, inner, outer, part, side_taps, side_windows, act_windows, slope
):
    cells = outer.shape[0]
    odd = me[0] % 2 == 1

    def fill(i, carry):
        start = pl.multiple_of(i * STEP, STEP)
        rows = pl.ds(start, STEP)
        below, above = by_side(odd, inner[rows, :].astype(F32), outer[rows, :].astype(F32))
        fill_windows(side_windows, start, 0, pick(above, below), columns, 256)
        fill_windows(side_windows, start, 128, pick(below, above), columns, 256)
        return carry

    clear_edges(side_windows, columns)
    clear_edges(act_windows, columns)
    lax.fori_loop(0, cells // STEP, fill, 0)
    lanes = lax.broadcasted_iota(jnp.int32, (BLOCK, 128), 1)
    edges = [jnp.where(me[0] == end, 0.0, 1.0).astype(F32) for end in (count - 1, 0)]
    inside = jnp.where(lanes < 64, edges[0], edges[1])
    for start in range(0, cells, BLOCK):
        hidden = part[start : start + BLOCK, :]
        hidden = hidden + window_dot(side_windows, side_taps, start, columns, NN)
        gate = jax.nn.sigmoid(hidden)
        act = (hidden * gate).astype(BF16).astype(F32)
        fill_windows(act_windows, start, 0, act[:, :128], columns, 256)
        fill_windows(act_windows, start, 128, act[:, 128:] * inside, columns, 256)
        hidden, gate = hidden[:, :128], gate[:, :128]
        slope[start : start + BLOCK, :] = gate * (1.0 + hidden * (1.0 - gate))


def slope_body(me, terms, inner, outer, slope, grad, to_inner, to_outer):
    half = terms.shape[0] // 2
    odd = me[0] % 2 == 1

    def step(i, carry):
        start = pl.multiple_of(i * STEP, STEP)
        low, high = pl.ds(start, STEP), pl.ds(start + half, STEP)
        near = inner[low, :].astype(F32)
        arrived = unpacked(*by_side(odd, near, outer[low, :].astype(F32)))
        sides = []
        for rows, extra in zip((low, high), arrived):
            value = ((terms[rows, :] + extra) * slope[rows, :]).astype(BF16)
            grad[rows, :] = value
            sides.append(value.astype(F32))
        lower, upper = packed(*sides)
        to_inner[low, :] = jnp.where(odd, lower, upper).astype(BF16)
        to_outer[low, :] = jnp.where(odd, upper, lower).astype(BF16)
        return carry

    lax.fori_loop(0, half // STEP, step, 0)


def kernel_terms(columns, out_channels, slices, turned, terms):
    for row in range(3):
        for column in range(3):
            tap = row * 3 + column
            product = jnp.dot(turned[...], slices(row, column), preferred_element_type=F32)
            first, second = product[:out_channels], product[out_channels:]
            terms[:, tap * 128 : tap * 128 + 128] = first[:, :128] + swap(
                pick(second[:, 128:], second[:, :128])
            )
            group = 9 + tap // 2
            here = slice(group * 128, group * 128 + 128)
            if tap % 2 == 0:
                terms[:, here] = swap(first[:, 128:]) + second[:, :128]
            else:
                terms[:, here] = pick(terms[:, here], first[:, 128:] + swap(second[:, :128]))


def turn(source, target, first):
    for start in range(0, source.shape[0], STEP):
        chunk = source[start : start + STEP, :].astype(F32)
        target[first : first + chunk.shape[1], start : start + STEP] = chunk.T.astype(BF16)


def grad_two_body(columns, act_windows, turned, terms):
    cells = turned.shape[1]

    def slices(row, column):
        rows = slice(row * columns, row * columns + cells)
        return act_windows[rows, column * 256 : column * 256 + 256]

    kernel_terms(columns, 128, slices, turned, terms)


def coded(value, split):
    head = value.astype(BF16)
    if split == 0:
        return head
    rest = (value[:split] - head[:split].astype(F32)).astype(BF16)
    return jnp.concatenate([head, rest], axis=0)


def decoded(value, split):
    value = value.astype(F32)
    if split == 0:
        return value
    size = value.shape[0] - split
    parts = [value[:split] + value[size:]]
    if split < size:
        parts.append(value[split:size])
    return jnp.concatenate(parts, axis=0)


def grad_one_body(
    columns, count, me, own_windows, side_windows, grad, other, to_inner,
    message, kept, turned, terms,
):
    cells = grad.shape[0]

    def slices(row, column):
        rows = slice(row * columns, row * columns + cells)
        return jnp.concatenate(
            [
                own_windows[rows, column * 128 : column * 128 + 128],
                side_windows[rows, column * 256 : column * 256 + 128],
            ],
            axis=1,
        )

    turn(grad, turned, 0)
    kernel_terms(columns, 64, slices, turned, terms)
    half = terms.shape[1] // 2
    odd = me[0] % 2 == 1

    def share(owner):
        parts = []
        for source in (terms, other):
            each = source.shape[0] // count
            block = source[owner * each : owner * each + each, :]
            parts += [block[:, :half], block[:, half:]]
        return jnp.concatenate(parts, axis=0)

    groups = half // 128
    for pair in range(count // 2):
        even_share, odd_share = share(2 * pair), share(2 * pair + 1)
        kept[pair] = jnp.where(odd, odd_share, even_share)
        given = coded(jnp.where(odd, even_share, odd_share), kept.shape[1])
        size = given.shape[0]
        for group in range(groups):
            first = (pair * groups + group) * size
            message[first : first + size, :] = given[:, group * 128 : group * 128 + 128]
    message[message.shape[0] - to_inner.shape[0] :, :] = to_inner[...]


def halve_body(split_in, split_out, owner_bit, at_bit, me, mine, arrived, sent, kept):
    side = (me[0] >> owner_bit) % 2
    size, lanes = mine.shape[1:]
    groups = lanes // 128

    def total(at):
        if len(arrived.shape) == 3:
            return mine[at] + decoded(arrived[at], split_in)
        parts = []
        for group in range(groups):
            first = pl.multiple_of((at * groups + group) * 2 * size, 8)
            parts.append(decoded(arrived[pl.ds(first, 2 * size), :], split_in))
        return mine[at] + jnp.concatenate(parts, axis=1)

    for at in range(sent.shape[0]):
        high, low = at >> at_bit, at & ((1 << at_bit) - 1)
        keep = ((2 * high + side) << at_bit) + low
        give = ((2 * high + 1 - side) << at_bit) + low
        sent[at] = coded(total(give), split_out)
        kept[at] = total(keep)


def finish_body(scale, split, sizes, mine, arrived, grad_one, grad_two):
    total = (mine[0] + decoded(arrived[0], split)) * scale
    half = total.shape[1]
    first = 0
    for size, out in zip(sizes, (grad_one, grad_two)):
        blocks = (total[first : first + size], total[first + size : first + 2 * size])
        first += 2 * size
        for tap in range(9):
            for depth, group, side in ((0, 9 + tap // 2, tap % 2), (1, tap, 0), (2, tap, 1)):
                lane = group * 128 + side * 64
                block, lane = (blocks[0], lane) if lane < half else (blocks[1], lane - half)
                out[depth * 9 + tap] = block[:, lane : lane + 64]


def output_body(columns, act_windows, weight, far, taps, output, sems):
    for row in range(3):
        for column in range(3):
            for at, source in enumerate(PLANES[:4]):
                first = row * 768 + column * 256 + at * 64
                for plane in range(2):
                    depth = depth_tap(source, plane)
                    taps[first : first + 64, plane * 128 : plane * 128 + 128] = (
                        jnp.zeros((64, 128), BF16)
                        if depth is None
                        else weight[depth * 9 + row * 3 + column]
                    )
    copies = pieces_of(output, far, sems, output.shape[1] // BLOCK)
    for at, copy in enumerate(copies):
        start = at * BLOCK
        value = window_dot(act_windows, taps, start, columns, NN)
        output[0, start : start + BLOCK, :] = value[:, :128]
        output[1, start : start + BLOCK, :] = value[:, 128:]
        copy.start()
    for copy in copies:
        copy.wait()


def grad_windows_body(columns, me, own, message, outer, windows):
    half = own.shape[0] // 2
    odd = me[0] % 2 == 1
    before = message.shape[0] - half

    def fill(i, carry):
        start = pl.multiple_of(i * STEP, STEP)
        near = message[pl.ds(before + start, STEP), :].astype(F32)
        below, above = by_side(odd, near, outer[pl.ds(start, STEP), :].astype(F32))
        for first, side in zip((start, start + half), unpacked(above, below)):
            fill_windows(windows, first, 0, own[pl.ds(first, STEP), :].astype(F32), columns, 256)
            fill_windows(windows, first, 128, side, columns, 256)
        return carry

    clear_edges(windows, columns)
    lax.fori_loop(0, half // STEP, fill, 0)


def grad_volume_body(columns, windows, taps, far, output, sems):
    copies = pieces_of(output, far, sems, output.shape[1] // BLOCK)
    for at, copy in enumerate(copies):
        start = at * BLOCK
        rows = windows[start : start + BLOCK + 2 * columns, :]
        terms = lax.dot_general(rows, taps[...], NT, preferred_element_type=F32)
        value = terms[:BLOCK, :128]
        value = value + terms[columns : columns + BLOCK, 128:256]
        value = value + terms[2 * columns : 2 * columns + BLOCK, 256:]
        output[0, start : start + BLOCK, :] = value[:, :64]
        output[1, start : start + BLOCK, :] = value[:, 64:]
        copy.start()
    for copy in copies:
        copy.wait()


def shards(volume, weight_one, weight_two, cotangent):
    count = lax.axis_size("space")
    planes, rows, columns, channels = volume.shape
    cells = rows * columns
    scale = 1.0 / math.sqrt(planes * count * cells)
    mid, wide = weight_two.shape[3], weight_two.shape[4]
    me = lax.axis_index("space").astype(jnp.int32).reshape(1)
    shape = jax.ShapeDtypeStruct
    flat, pack = shape((cells, 128), BF16), shape((cells // 2, 128), BF16)
    slab = (cells + 2 * columns, 768)
    windows = pltpu.VMEM(slab, BF16)
    lanes = 14 * 64
    split = 2 * mid // count
    chunk = 2 * (mid + wide) // count

    within = [(i, i ^ 1) for i in range(count)]
    across = [(i, i + 1) for i in range(1, count - 1, 2)]
    across += [(j, i) for i, j in across]

    volume = volume.reshape(planes, cells, channels)
    cotangent = cotangent.reshape(planes, cells, wide)
    weight_one = weight_one.reshape(27, channels, mid)
    weight_two = weight_two.reshape(27, mid, wide)
    one_flops = 2 * planes * cells * 27 * channels * mid
    two_flops = 2 * planes * cells * 27 * mid * wide

    dma = pltpu.SemaphoreType.DMA
    far_one, far_two, far_volume, far_cotangent = (
        pltpu.with_memory_space_constraint(x, pltpu.HBM)
        for x in (weight_one, weight_two, volume, cotangent)
    )
    own, = call(
        pack_body, (flat,), (far_volume,),
        (pltpu.VMEM((planes, cells, channels), BF16), dma((4,))),
        name="pack_volume", apart=(0,),
    )
    vol_outer = lax.ppermute(own, "space", across)
    vol_inner = lax.ppermute(own, "space", within)
    terms, inner, outer, turned = call(
        functools.partial(leave_body, columns),
        (
            shape((cells, 128), F32), pack, pack, shape((256, cells), BF16),
        ),
        (me, far_cotangent, far_two),
        (
            windows, pltpu.VMEM((256, 3 * 768), BF16), pltpu.VMEM(cotangent.shape, BF16),
            pltpu.VMEM(weight_two.shape, BF16), dma((4,)), dma,
        ),
        two_flops, "grad_act_terms", (0,), (1, 2),
    )
    own, terms = lax.optimization_barrier((own, terms))
    own_windows, part, side_taps = call(
        functools.partial(prepare_body, columns),
        (
            shape((slab[0], 384), BF16), shape((cells, 256), F32), shape((9 * 256, 256), BF16),
        ),
        (own, far_one),
        (pltpu.VMEM((9 * 128, 256), BF16), pltpu.VMEM(weight_one.shape, BF16), dma),
        one_flops, "prepare", (), (1,),
    )
    back_taps, = call(
        back_taps_body, (shape((3 * 128, 768), BF16),), (weight_one,), (), one_flops // 8, "back_taps"
    )
    inner, outer, part, back_taps = lax.optimization_barrier((inner, outer, part, back_taps))
    terms_outer = lax.ppermute(outer, "space", across)
    terms_inner = lax.ppermute(inner, "space", within)
    side_windows, act_windows, slope = call(
        functools.partial(hidden_body, columns, count),
        (shape(slab, BF16), shape(slab, BF16), shape((cells, 128), F32)),
        (me, vol_inner, vol_outer, part, side_taps),
        (), 2 * one_flops, "hidden", (0,),
    )
    terms_two, = call(
        functools.partial(grad_two_body, columns),
        (shape((wide, 2 * lanes), F32),),
        (act_windows, turned), (), two_flops, "grad_two_terms",
    )
    terms_two, terms_outer = lax.optimization_barrier((terms_two, terms_outer))
    grad_hidden, to_inner, outer = call(
        slope_body, (flat, pack, pack), (me, terms, terms_inner, terms_outer, slope),
        name="grad_hidden", smem=(0,),
    )
    grad_outer = lax.ppermute(outer, "space", across)
    groups = lanes // 128
    message, kept = call(
        functools.partial(grad_one_body, columns, count),
        (
            shape((count // 2 * groups * 2 * chunk + cells // 2, 128), BF16),
            shape((count // 2, chunk, lanes), F32),
        ),
        (me, own_windows, side_windows, grad_hidden, terms_two, to_inner),
        (pltpu.VMEM((128, cells), BF16), pltpu.VMEM((mid, 2 * lanes), F32)),
        one_flops, "grad_one_terms", (0,),
    )
    message = lax.ppermute(message, "space", within)
    def halve(bits, bit, split_in, split_out, kept, arrived):
        left = 2 ** (len(bits) - 1)
        sent, kept = call(
            functools.partial(halve_body, split_in, split_out, bit, bits[::-1].index(bit)),
            (shape((left, chunk + split_out, lanes), BF16), shape((left, chunk, lanes), F32)),
            (me, kept, arrived), name="halve", smem=(0,),
        )
        return [b for b in bits if b != bit], sent, kept

    bits = list(range(count.bit_length() - 2, 0, -1))
    order = [*range(2, count.bit_length() - 1), 1]
    bits, sent, kept = halve(bits, order[0], chunk, split, kept, message)
    sent, act_windows = lax.optimization_barrier((sent, act_windows))
    arrived = lax.ppermute(sent, "space", [(i, i ^ (1 << order[0])) for i in range(count)])
    output, = call(
        functools.partial(output_body, columns),
        (shape((planes, cells, wide), F32),),
        (act_windows, weight_two),
        (
            pltpu.VMEM((3 * 768, 256), BF16), pltpu.VMEM((planes, cells, wide), F32),
            dma((cells // BLOCK,)),
        ),
        two_flops, "output", (), (), True,
    )
    grad_windows, = call(
        functools.partial(grad_windows_body, columns), (shape(slab, BF16),),
        (me, grad_hidden, message, grad_outer),
        (), one_flops // 4, "grad_windows", (0,),
    )
    came = split
    for step, bit in enumerate(order[1:]):
        goes = split if bit == 1 else 0
        bits, sent, kept = halve(bits, bit, came, goes, kept, arrived)
        if step == 0:
            sent, grad_windows, output = lax.optimization_barrier((sent, grad_windows, output))
            grad_volume, = call(
                functools.partial(grad_volume_body, columns),
                (shape((planes, cells, channels), F32),),
                (grad_windows, back_taps),
                (pltpu.VMEM((planes, cells, channels), F32), dma((cells // BLOCK,))),
                one_flops, "grad_volume", (), (), True,
            )
        if step == 1:
            sent, grad_volume = lax.optimization_barrier((sent, grad_volume))
        arrived = lax.ppermute(sent, "space", [(i, i ^ (1 << bit)) for i in range(count)])
        came = goes
    grad_one, grad_two = call(
        functools.partial(finish_body, scale, came, (mid // count, wide // count)),
        (shape((27, mid // count, channels), F32), shape((27, wide // count, mid), F32)),
        (kept, arrived), name="finish",
    )
    return (
        output.reshape(planes, rows, columns, wide),
        grad_volume.reshape(planes, rows, columns, channels),
        jnp.swapaxes(grad_one, 1, 2).reshape(3, 3, 3, channels, mid // count),
        jnp.swapaxes(grad_two, 1, 2).reshape(3, 3, 3, mid, wide // count),
    )


def solution(mesh):
    cells = P(("groups", "space"), None, None, None)
    kernel = P("groups", None, None, None, "space")
    return jax.shard_map(
        shards,
        mesh=mesh,
        in_specs=(cells, P(), P(), cells),
        out_specs=(cells, cells, kernel, kernel),
        check_vma=False,
    )
```

```python
import functools
import math

import jax
import jax.numpy as jnp
from jax import lax
from jax.experimental import pallas as pl
from jax.experimental.pallas import tpu as pltpu
from jax.sharding import PartitionSpec as P

F32, BF16 = jnp.float32, jnp.bfloat16
STEP, BLOCK = 256, 512
VMEM_LIMIT = 16 * 2**20
NN = (((1,), (0,)), ((), ()))
NT = (((1,), (1,)), ((), ()))

PLANES = (0, 1, 2, -1, -2, 3)


def depth_tap(source, target):
    tap = source - target + 1
    return tap if 0 <= tap <= 2 else None


def call(body, outs, ins, scratch=(), flops=0, name=None, smem=(), apart=(), far=False):
    moved = sum(math.prod(s.shape) * s.dtype.itemsize for s in (*outs, *ins))
    return pl.pallas_call(
        body,
        out_shape=list(outs),
        in_specs=[
            pl.BlockSpec(
                memory_space=pltpu.SMEM if i in smem else pl.ANY if i in apart else pltpu.VMEM
            )
            for i in range(len(ins))
        ],
        out_specs=[pl.BlockSpec(memory_space=pl.ANY if far else pltpu.VMEM)] * len(outs),
        scratch_shapes=list(scratch),
        compiler_params=pltpu.CompilerParams(vmem_limit_bytes=VMEM_LIMIT),
        cost_estimate=pl.CostEstimate(flops=flops, bytes_accessed=moved, transcendentals=0),
        name=name,
    )(*ins)


def lanes_low(x):
    return lax.broadcasted_iota(jnp.int32, x.shape, 1) < 64


def swap(x):
    return pltpu.roll(x, 64, 1)


def pick(low, high):
    return jnp.where(lanes_low(low), low, high)


def fill_windows(windows, start, lane, chunk, columns, stride):
    size = chunk.shape[0]
    column = lax.broadcasted_iota(jnp.int32, chunk.shape, 0) % columns
    before = jnp.where(column == 0, 0.0, pltpu.roll(chunk, 1, 0))
    after = jnp.where(column == columns - 1, 0.0, pltpu.roll(chunk, size - 1, 0))
    at = pl.ds(pl.multiple_of(columns + start, 32), size)
    for tap, part in enumerate((before, chunk, after)):
        first = tap * stride + lane
        windows[at, first : first + chunk.shape[1]] = part.astype(BF16)


def clear_edges(windows, columns):
    rows, lanes = windows.shape
    windows[0:columns, :] = jnp.zeros((columns, lanes), BF16)
    windows[rows - columns : rows, :] = jnp.zeros((columns, lanes), BF16)


def row_windows(windows, start, columns, lanes=slice(None)):
    return [
        windows[start + tap * columns : start + tap * columns + BLOCK, lanes] for tap in range(3)
    ]


def window_dot(windows, weights, start, columns, dims):
    rows = jnp.concatenate(row_windows(windows, start, columns), axis=1)
    return lax.dot_general(rows, weights[...], dims, preferred_element_type=F32)


def packed(low, high):
    return pick(low, swap(high)), pick(swap(low), high)


def unpacked(first, second):
    return packed(first, second)


def by_side(odd, inner, outer):
    return jnp.where(odd, inner, outer), jnp.where(odd, outer, inner)


def pieces_of(source, target, sems, parts):
    size = target.shape[1] // parts
    return [
        pltpu.make_async_copy(
            source.at[:, pl.ds(i * size, size), :], target.at[:, pl.ds(i * size, size), :], sems.at[i]
        )
        for i in range(parts)
    ]


def pack_body(volume, own, held, sems):
    copies = pieces_of(volume, held, sems, sems.shape[0])
    size = own.shape[0] // len(copies)
    for copy in copies:
        copy.start()
    for i, copy in enumerate(copies):
        copy.wait()
        rows = slice(i * size, i * size + size)
        own[rows, :] = jnp.concatenate([held[0, rows, :], held[1, rows, :]], axis=1)


def leave_body(
    columns, me, far_cotangent, far_weight, own, inner, outer, turned,
    windows, taps, cotangent, weight, sems, sem,
):
    cells = own.shape[0]
    half = cells // 2
    odd = me[0] % 2 == 1
    fetch = pltpu.make_async_copy(far_weight, weight, sem)
    copies = pieces_of(far_cotangent, cotangent, sems, sems.shape[0])
    for copy in copies:
        copy.start()
    fetch.start()
    clear_edges(windows, columns)
    size = cells // len(copies)
    for at, copy in enumerate(copies):
        copy.wait()

        def fill(i, carry):
            start = pl.multiple_of(at * size + i * STEP, STEP)
            for plane in range(2):
                chunk = cotangent[plane, pl.ds(start, STEP), :].astype(F32)
                fill_windows(windows, start, plane * 128, chunk, columns, 256)
            return carry

        lax.fori_loop(0, size // STEP, fill, 0)
    fetch.wait()
    for row in range(3):
        for column in range(3):
            for source in range(2):
                first = row * 768 + column * 256 + source * 128
                for at, target in enumerate(PLANES[:4]):
                    depth = depth_tap(source, target)
                    taps[at * 64 : at * 64 + 64, first : first + 128] = (
                        jnp.zeros((64, 128), BF16)
                        if depth is None
                        else weight[(2 - depth) * 9 + (2 - row) * 3 + 2 - column]
                    )
    for start in range(0, half, BLOCK):
        sides = []
        for first in (start, start + half):
            term = window_dot(windows, taps, first, columns, NT)
            own[first : first + BLOCK, :] = term[:, :128]
            sides.append(term[:, 128:])
        upper, lower = packed(*sides)
        inner[start : start + BLOCK, :] = jnp.where(odd, lower, upper).astype(BF16)
        outer[start : start + BLOCK, :] = jnp.where(odd, upper, lower).astype(BF16)
    for plane in range(2):
        turn(cotangent.at[plane], turned, plane * 128)


def prepare_body(
    columns, own, far_weight, own_windows, hidden, side_taps, own_taps, weight, sem
):
    fetch = pltpu.make_async_copy(far_weight, weight, sem)
    fetch.start()

    def fill(i, carry):
        start = pl.multiple_of(i * STEP, STEP)
        chunk = own[pl.ds(start, STEP), :].astype(F32)
        fill_windows(own_windows, start, 0, chunk, columns, 128)
        return carry

    clear_edges(own_windows, columns)
    lax.fori_loop(0, own.shape[0] // STEP, fill, 0)
    fetch.wait()
    zero = jnp.zeros((64, 64), BF16)
    for row in range(3):
        for column in range(3):
            tap = row * 3 + column
            for at, source in enumerate(PLANES):
                depths = [depth_tap(source, target) for target in PLANES[:4]]
                parts = [zero if d is None else weight[d * 9 + tap] for d in depths]
                if at < 2:
                    target, first = own_taps, tap * 128 + at * 64
                else:
                    target, first = side_taps, tap * 256 + (at - 2) * 64
                target[first : first + 64, :128] = jnp.concatenate(parts[:2], axis=1)
                target[first : first + 64, 128:] = jnp.concatenate(parts[2:], axis=1)
    for start in range(0, own.shape[0], BLOCK):
        hidden[start : start + BLOCK, :] = window_dot(own_windows, own_taps, start, columns, NN)


def back_taps_body(weight, back_taps):
    zero = jnp.zeros((64, 64), BF16)
    for row in range(3):
        for column in range(3):
            tap = row * 3 + column
            for plane in range(2):
                depths = [depth_tap(source, plane) for source in PLANES[:4]]
                parts = [zero if d is None else weight[(2 - d) * 9 + 8 - tap] for d in depths]
                at = row * 128 + plane * 64
                for pair in range(2):
                    first = column * 256 + pair * 128
                    back_taps[at : at + 64, first : first + 128] = jnp.concatenate(
                        parts[2 * pair : 2 * pair + 2], axis=1
                    )


def hidden_body(
    columns, count, me, inner, outer, part, side_taps, side_windows, act_windows, slope
):
    cells = outer.shape[0]
    odd = me[0] % 2 == 1

    def fill(i, carry):
        start = pl.multiple_of(i * STEP, STEP)
        rows = pl.ds(start, STEP)
        below, above = by_side(odd, inner[rows, :].astype(F32), outer[rows, :].astype(F32))
        fill_windows(side_windows, start, 0, pick(above, below), columns, 256)
        fill_windows(side_windows, start, 128, pick(below, above), columns, 256)
        return carry

    clear_edges(side_windows, columns)
    clear_edges(act_windows, columns)
    lax.fori_loop(0, cells // STEP, fill, 0)
    lanes = lax.broadcasted_iota(jnp.int32, (BLOCK, 128), 1)
    edges = [jnp.where(me[0] == end, 0.0, 1.0).astype(F32) for end in (count - 1, 0)]
    inside = jnp.where(lanes < 64, edges[0], edges[1])
    for start in range(0, cells, BLOCK):
        hidden = part[start : start + BLOCK, :]
        hidden = hidden + window_dot(side_windows, side_taps, start, columns, NN)
        gate = jax.nn.sigmoid(hidden)
        act = (hidden * gate).astype(BF16).astype(F32)
        fill_windows(act_windows, start, 0, act[:, :128], columns, 256)
        fill_windows(act_windows, start, 128, act[:, 128:] * inside, columns, 256)
        hidden, gate = hidden[:, :128], gate[:, :128]
        slope[start : start + BLOCK, :] = gate * (1.0 + hidden * (1.0 - gate))


def slope_body(me, terms, inner, outer, slope, grad, to_inner, to_outer):
    half = terms.shape[0] // 2
    odd = me[0] % 2 == 1

    def step(i, carry):
        start = pl.multiple_of(i * STEP, STEP)
        low, high = pl.ds(start, STEP), pl.ds(start + half, STEP)
        near = inner[low, :].astype(F32)
        arrived = unpacked(*by_side(odd, near, outer[low, :].astype(F32)))
        sides = []
        for rows, extra in zip((low, high), arrived):
            value = ((terms[rows, :] + extra) * slope[rows, :]).astype(BF16)
            grad[rows, :] = value
            sides.append(value.astype(F32))
        lower, upper = packed(*sides)
        to_inner[low, :] = jnp.where(odd, lower, upper).astype(BF16)
        to_outer[low, :] = jnp.where(odd, upper, lower).astype(BF16)
        return carry

    lax.fori_loop(0, half // STEP, step, 0)


def kernel_terms(columns, out_channels, slices, turned, terms):
    for row in range(3):
        for column in range(3):
            tap = row * 3 + column
            product = jnp.dot(turned[...], slices(row, column), preferred_element_type=F32)
            first, second = product[:out_channels], product[out_channels:]
            terms[:, tap * 128 : tap * 128 + 128] = first[:, :128] + swap(
                pick(second[:, 128:], second[:, :128])
            )
            group = 9 + tap // 2
            here = slice(group * 128, group * 128 + 128)
            if tap % 2 == 0:
                terms[:, here] = swap(first[:, 128:]) + second[:, :128]
            else:
                terms[:, here] = pick(terms[:, here], first[:, 128:] + swap(second[:, :128]))


def turn(source, target, first):
    for start in range(0, source.shape[0], STEP):
        chunk = source[start : start + STEP, :].astype(F32)
        target[first : first + chunk.shape[1], start : start + STEP] = chunk.T.astype(BF16)


def grad_two_body(columns, act_windows, turned, terms):
    cells = turned.shape[1]

    def slices(row, column):
        rows = slice(row * columns, row * columns + cells)
        return act_windows[rows, column * 256 : column * 256 + 256]

    kernel_terms(columns, 128, slices, turned, terms)


def coded(value, split):
    head = value.astype(BF16)
    if split == 0:
        return head
    rest = (value[:split] - head[:split].astype(F32)).astype(BF16)
    return jnp.concatenate([head, rest], axis=0)


def decoded(value, split):
    value = value.astype(F32)
    if split == 0:
        return value
    size = value.shape[0] - split
    parts = [value[:split] + value[size:]]
    if split < size:
        parts.append(value[split:size])
    return jnp.concatenate(parts, axis=0)


def grad_one_body(
    columns, count, me, own_windows, side_windows, grad, other, to_inner,
    message, kept, turned, terms,
):
    cells = grad.shape[0]

    def slices(row, column):
        rows = slice(row * columns, row * columns + cells)
        return jnp.concatenate(
            [
                own_windows[rows, column * 128 : column * 128 + 128],
                side_windows[rows, column * 256 : column * 256 + 128],
            ],
            axis=1,
        )

    turn(grad, turned, 0)
    kernel_terms(columns, 64, slices, turned, terms)
    half = terms.shape[1] // 2
    odd = me[0] % 2 == 1

    def share(owner):
        parts = []
        for source in (terms, other):
            each = source.shape[0] // count
            block = source[owner * each : owner * each + each, :]
            parts += [block[:, :half], block[:, half:]]
        return jnp.concatenate(parts, axis=0)

    groups = half // 128
    for pair in range(count // 2):
        even_share, odd_share = share(2 * pair), share(2 * pair + 1)
        kept[pair] = jnp.where(odd, odd_share, even_share)
        given = coded(jnp.where(odd, even_share, odd_share), kept.shape[1])
        size = given.shape[0]
        for group in range(groups):
            first = (pair * groups + group) * size
            message[first : first + size, :] = given[:, group * 128 : group * 128 + 128]
    message[message.shape[0] - to_inner.shape[0] :, :] = to_inner[...]


def halve_body(split_in, split_out, owner_bit, at_bit, me, mine, arrived, sent, kept):
    side = (me[0] >> owner_bit) % 2
    size, lanes = mine.shape[1:]
    groups = lanes // 128

    def total(at):
        if len(arrived.shape) == 3:
            return mine[at] + decoded(arrived[at], split_in)
        parts = []
        for group in range(groups):
            first = pl.multiple_of((at * groups + group) * 2 * size, 8)
            parts.append(decoded(arrived[pl.ds(first, 2 * size), :], split_in))
        return mine[at] + jnp.concatenate(parts, axis=1)

    for at in range(sent.shape[0]):
        high, low = at >> at_bit, at & ((1 << at_bit) - 1)
        keep = ((2 * high + side) << at_bit) + low
        give = ((2 * high + 1 - side) << at_bit) + low
        sent[at] = coded(total(give), split_out)
        kept[at] = total(keep)


def finish_body(scale, split, sizes, mine, arrived, grad_one, grad_two):
    total = (mine[0] + decoded(arrived[0], split)) * scale
    half = total.shape[1]
    first = 0
    for size, out in zip(sizes, (grad_one, grad_two)):
        blocks = (total[first : first + size], total[first + size : first + 2 * size])
        first += 2 * size
        for tap in range(9):
            for depth, group, side in ((0, 9 + tap // 2, tap % 2), (1, tap, 0), (2, tap, 1)):
                lane = group * 128 + side * 64
                block, lane = (blocks[0], lane) if lane < half else (blocks[1], lane - half)
                out[depth * 9 + tap] = block[:, lane : lane + 64]


def output_body(columns, act_windows, weight, far, taps, output, sems):
    for row in range(3):
        for column in range(3):
            for at, source in enumerate(PLANES[:4]):
                first = row * 768 + column * 256 + at * 64
                for plane in range(2):
                    depth = depth_tap(source, plane)
                    taps[first : first + 64, plane * 128 : plane * 128 + 128] = (
                        jnp.zeros((64, 128), BF16)
                        if depth is None
                        else weight[depth * 9 + row * 3 + column]
                    )
    copies = pieces_of(output, far, sems, output.shape[1] // BLOCK)
    for at, copy in enumerate(copies):
        start = at * BLOCK
        value = window_dot(act_windows, taps, start, columns, NN)
        output[0, start : start + BLOCK, :] = value[:, :128]
        output[1, start : start + BLOCK, :] = value[:, 128:]
        copy.start()
    for copy in copies:
        copy.wait()


def grad_windows_body(columns, me, own, message, outer, windows):
    half = own.shape[0] // 2
    odd = me[0] % 2 == 1
    before = message.shape[0] - half

    def fill(i, carry):
        start = pl.multiple_of(i * STEP, STEP)
        near = message[pl.ds(before + start, STEP), :].astype(F32)
        below, above = by_side(odd, near, outer[pl.ds(start, STEP), :].astype(F32))
        for first, side in zip((start, start + half), unpacked(above, below)):
            fill_windows(windows, first, 0, own[pl.ds(first, STEP), :].astype(F32), columns, 256)
            fill_windows(windows, first, 128, side, columns, 256)
        return carry

    clear_edges(windows, columns)
    lax.fori_loop(0, half // STEP, fill, 0)


def grad_volume_body(columns, windows, taps, far, output, sems):
    copies = pieces_of(output, far, sems, output.shape[1] // BLOCK)
    for at, copy in enumerate(copies):
        start = at * BLOCK
        rows = windows[start : start + BLOCK + 2 * columns, :]
        terms = lax.dot_general(rows, taps[...], NT, preferred_element_type=F32)
        value = terms[:BLOCK, :128]
        value = value + terms[columns : columns + BLOCK, 128:256]
        value = value + terms[2 * columns : 2 * columns + BLOCK, 256:]
        output[0, start : start + BLOCK, :] = value[:, :64]
        output[1, start : start + BLOCK, :] = value[:, 64:]
        copy.start()
    for copy in copies:
        copy.wait()


def shards(volume, weight_one, weight_two, cotangent):
    count = lax.axis_size("space")
    planes, rows, columns, channels = volume.shape
    cells = rows * columns
    scale = 1.0 / math.sqrt(planes * count * cells)
    mid, wide = weight_two.shape[3], weight_two.shape[4]
    me = lax.axis_index("space").astype(jnp.int32).reshape(1)
    shape = jax.ShapeDtypeStruct
    flat, pack = shape((cells, 128), BF16), shape((cells // 2, 128), BF16)
    slab = (cells + 2 * columns, 768)
    windows = pltpu.VMEM(slab, BF16)
    lanes = 14 * 64
    split = 2 * mid // count
    chunk = 2 * (mid + wide) // count

    within = [(i, i ^ 1) for i in range(count)]
    across = [(i, i + 1) for i in range(1, count - 1, 2)]
    across += [(j, i) for i, j in across]

    volume = volume.reshape(planes, cells, channels)
    cotangent = cotangent.reshape(planes, cells, wide)
    weight_one = weight_one.reshape(27, channels, mid)
    weight_two = weight_two.reshape(27, mid, wide)
    one_flops = 2 * planes * cells * 27 * channels * mid
    two_flops = 2 * planes * cells * 27 * mid * wide

    dma = pltpu.SemaphoreType.DMA
    far_one, far_two, far_volume, far_cotangent = (
        pltpu.with_memory_space_constraint(x, pltpu.HBM)
        for x in (weight_one, weight_two, volume, cotangent)
    )
    own, = call(
        pack_body, (flat,), (far_volume,),
        (pltpu.VMEM((planes, cells, channels), BF16), dma((4,))),
        name="pack_volume", apart=(0,),
    )
    vol_outer = lax.ppermute(own, "space", across)
    vol_inner = lax.ppermute(own, "space", within)
    terms, inner, outer, turned = call(
        functools.partial(leave_body, columns),
        (
            shape((cells, 128), F32), pack, pack, shape((256, cells), BF16),
        ),
        (me, far_cotangent, far_two),
        (
            windows, pltpu.VMEM((256, 3 * 768), BF16), pltpu.VMEM(cotangent.shape, BF16),
            pltpu.VMEM(weight_two.shape, BF16), dma((4,)), dma,
        ),
        two_flops, "grad_act_terms", (0,), (1, 2),
    )
    own, terms = lax.optimization_barrier((own, terms))
    own_windows, part, side_taps = call(
        functools.partial(prepare_body, columns),
        (
            shape((slab[0], 384), BF16), shape((cells, 256), F32), shape((9 * 256, 256), BF16),
        ),
        (own, far_one),
        (pltpu.VMEM((9 * 128, 256), BF16), pltpu.VMEM(weight_one.shape, BF16), dma),
        one_flops, "prepare", (), (1,),
    )
    back_taps, = call(
        back_taps_body, (shape((3 * 128, 768), BF16),), (weight_one,), (), one_flops // 8, "back_taps"
    )
    inner, outer, part, back_taps = lax.optimization_barrier((inner, outer, part, back_taps))
    terms_outer = lax.ppermute(outer, "space", across)
    terms_inner = lax.ppermute(inner, "space", within)
    side_windows, act_windows, slope = call(
        functools.partial(hidden_body, columns, count),
        (shape(slab, BF16), shape(slab, BF16), shape((cells, 128), F32)),
        (me, vol_inner, vol_outer, part, side_taps),
        (), 2 * one_flops, "hidden", (0,),
    )
    terms_two, = call(
        functools.partial(grad_two_body, columns),
        (shape((wide, 2 * lanes), F32),),
        (act_windows, turned), (), two_flops, "grad_two_terms",
    )
    terms_two, terms_outer = lax.optimization_barrier((terms_two, terms_outer))
    grad_hidden, to_inner, outer = call(
        slope_body, (flat, pack, pack), (me, terms, terms_inner, terms_outer, slope),
        name="grad_hidden", smem=(0,),
    )
    grad_outer = lax.ppermute(outer, "space", across)
    groups = lanes // 128
    message, kept = call(
        functools.partial(grad_one_body, columns, count),
        (
            shape((count // 2 * groups * 2 * chunk + cells // 2, 128), BF16),
            shape((count // 2, chunk, lanes), F32),
        ),
        (me, own_windows, side_windows, grad_hidden, terms_two, to_inner),
        (pltpu.VMEM((128, cells), BF16), pltpu.VMEM((mid, 2 * lanes), F32)),
        one_flops, "grad_one_terms", (0,),
    )
    message = lax.ppermute(message, "space", within)
    def halve(bits, bit, split_in, split_out, kept, arrived):
        left = 2 ** (len(bits) - 1)
        sent, kept = call(
            functools.partial(halve_body, split_in, split_out, bit, bits[::-1].index(bit)),
            (shape((left, chunk + split_out, lanes), BF16), shape((left, chunk, lanes), F32)),
            (me, kept, arrived), name="halve", smem=(0,),
        )
        return [b for b in bits if b != bit], sent, kept

    bits = list(range(count.bit_length() - 2, 0, -1))
    order = [*range(2, count.bit_length() - 1), 1]
    bits, sent, kept = halve(bits, order[0], chunk, split, kept, message)
    sent, act_windows = lax.optimization_barrier((sent, act_windows))
    arrived = lax.ppermute(sent, "space", [(i, i ^ (1 << order[0])) for i in range(count)])
    output, = call(
        functools.partial(output_body, columns),
        (shape((planes, cells, wide), F32),),
        (act_windows, weight_two),
        (
            pltpu.VMEM((3 * 768, 256), BF16), pltpu.VMEM((planes, cells, wide), F32),
            dma((cells // BLOCK,)),
        ),
        two_flops, "output", (), (), True,
    )
    output, grad_outer = lax.optimization_barrier((output, grad_outer))
    grad_windows, = call(
        functools.partial(grad_windows_body, columns), (shape(slab, BF16),),
        (me, grad_hidden, message, grad_outer),
        (), one_flops // 4, "grad_windows", (0,),
    )
    came = split
    for step, bit in enumerate(order[1:]):
        goes = split if bit == 1 else 0
        bits, sent, kept = halve(bits, bit, came, goes, kept, arrived)
        if step == 0:
            sent, grad_windows, output = lax.optimization_barrier((sent, grad_windows, output))
            grad_volume, = call(
                functools.partial(grad_volume_body, columns),
                (shape((planes, cells, channels), F32),),
                (grad_windows, back_taps),
                (pltpu.VMEM((planes, cells, channels), F32), dma((cells // BLOCK,))),
                one_flops, "grad_volume", (), (), True,
            )
        if step == 1:
            sent, grad_volume = lax.optimization_barrier((sent, grad_volume))
        arrived = lax.ppermute(sent, "space", [(i, i ^ (1 << bit)) for i in range(count)])
        came = goes
    grad_one, grad_two = call(
        functools.partial(finish_body, scale, came, (mid // count, wide // count)),
        (shape((27, mid // count, channels), F32), shape((27, wide // count, mid), F32)),
        (kept, arrived), name="finish",
    )
    return (
        output.reshape(planes, rows, columns, wide),
        grad_volume.reshape(planes, rows, columns, channels),
        jnp.swapaxes(grad_one, 1, 2).reshape(3, 3, 3, channels, mid // count),
        jnp.swapaxes(grad_two, 1, 2).reshape(3, 3, 3, mid, wide // count),
    )


def solution(mesh):
    cells = P(("groups", "space"), None, None, None)
    kernel = P("groups", None, None, None, "space")
    return jax.shard_map(
        shards,
        mesh=mesh,
        in_specs=(cells, P(), P(), cells),
        out_specs=(cells, cells, kernel, kernel),
        check_vma=False,
    )
```

```python
import functools
import math

import jax
import jax.numpy as jnp
from jax import lax
from jax.experimental import pallas as pl
from jax.experimental.pallas import tpu as pltpu
from jax.sharding import PartitionSpec as P

F32, BF16 = jnp.float32, jnp.bfloat16
STEP, BLOCK = 256, 512
VMEM_LIMIT = 16 * 2**20
NN = (((1,), (0,)), ((), ()))
NT = (((1,), (1,)), ((), ()))

PLANES = (0, 1, 2, -1, -2, 3)


def depth_tap(source, target):
    tap = source - target + 1
    return tap if 0 <= tap <= 2 else None


def call(body, outs, ins, scratch=(), flops=0, name=None, smem=(), apart=(), far=False):
    moved = sum(math.prod(s.shape) * s.dtype.itemsize for s in (*outs, *ins))
    return pl.pallas_call(
        body,
        out_shape=list(outs),
        in_specs=[
            pl.BlockSpec(
                memory_space=pltpu.SMEM if i in smem else pl.ANY if i in apart else pltpu.VMEM
            )
            for i in range(len(ins))
        ],
        out_specs=[pl.BlockSpec(memory_space=pl.ANY if far else pltpu.VMEM)] * len(outs),
        scratch_shapes=list(scratch),
        compiler_params=pltpu.CompilerParams(vmem_limit_bytes=VMEM_LIMIT),
        cost_estimate=pl.CostEstimate(flops=flops, bytes_accessed=moved, transcendentals=0),
        name=name,
    )(*ins)


def lanes_low(x):
    return lax.broadcasted_iota(jnp.int32, x.shape, 1) < 64


def swap(x):
    return pltpu.roll(x, 64, 1)


def pick(low, high):
    return jnp.where(lanes_low(low), low, high)


def fill_windows(windows, start, lane, chunk, columns, stride):
    size = chunk.shape[0]
    column = lax.broadcasted_iota(jnp.int32, chunk.shape, 0) % columns
    before = jnp.where(column == 0, 0.0, pltpu.roll(chunk, 1, 0))
    after = jnp.where(column == columns - 1, 0.0, pltpu.roll(chunk, size - 1, 0))
    at = pl.ds(pl.multiple_of(columns + start, 32), size)
    for tap, part in enumerate((before, chunk, after)):
        first = tap * stride + lane
        windows[at, first : first + chunk.shape[1]] = part.astype(BF16)


def clear_edges(windows, columns):
    rows, lanes = windows.shape
    windows[0:columns, :] = jnp.zeros((columns, lanes), BF16)
    windows[rows - columns : rows, :] = jnp.zeros((columns, lanes), BF16)


def row_windows(windows, start, columns, lanes=slice(None)):
    return [
        windows[start + tap * columns : start + tap * columns + BLOCK, lanes] for tap in range(3)
    ]


def window_dot(windows, weights, start, columns, dims):
    rows = jnp.concatenate(row_windows(windows, start, columns), axis=1)
    return lax.dot_general(rows, weights[...], dims, preferred_element_type=F32)


def packed(low, high):
    return pick(low, swap(high)), pick(swap(low), high)


def unpacked(first, second):
    return packed(first, second)


def by_side(odd, inner, outer):
    return jnp.where(odd, inner, outer), jnp.where(odd, outer, inner)


def pieces_of(source, target, sems, parts):
    size = target.shape[1] // parts
    return [
        pltpu.make_async_copy(
            source.at[:, pl.ds(i * size, size), :], target.at[:, pl.ds(i * size, size), :], sems.at[i]
        )
        for i in range(parts)
    ]


def pack_body(volume, own, held, sems):
    copies = pieces_of(volume, held, sems, sems.shape[0])
    size = own.shape[0] // len(copies)
    for copy in copies:
        copy.start()
    for i, copy in enumerate(copies):
        copy.wait()
        rows = slice(i * size, i * size + size)
        own[rows, :] = jnp.concatenate([held[0, rows, :], held[1, rows, :]], axis=1)


def leave_body(
    columns, me, far_cotangent, far_weight, own, inner, outer, turned,
    windows, taps, cotangent, weight, sems, sem,
):
    cells = own.shape[0]
    half = cells // 2
    odd = me[0] % 2 == 1
    fetch = pltpu.make_async_copy(far_weight, weight, sem)
    copies = pieces_of(far_cotangent, cotangent, sems, sems.shape[0])
    for copy in copies:
        copy.start()
    fetch.start()
    clear_edges(windows, columns)
    size = cells // len(copies)
    for at, copy in enumerate(copies):
        copy.wait()

        def fill(i, carry):
            start = pl.multiple_of(at * size + i * STEP, STEP)
            for plane in range(2):
                chunk = cotangent[plane, pl.ds(start, STEP), :].astype(F32)
                fill_windows(windows, start, plane * 128, chunk, columns, 256)
            return carry

        lax.fori_loop(0, size // STEP, fill, 0)
    fetch.wait()
    for row in range(3):
        for column in range(3):
            for source in range(2):
                first = row * 768 + column * 256 + source * 128
                for at, target in enumerate(PLANES[:4]):
                    depth = depth_tap(source, target)
                    taps[at * 64 : at * 64 + 64, first : first + 128] = (
                        jnp.zeros((64, 128), BF16)
                        if depth is None
                        else weight[(2 - depth) * 9 + (2 - row) * 3 + 2 - column]
                    )
    for start in range(0, half, BLOCK):
        sides = []
        for first in (start, start + half):
            term = window_dot(windows, taps, first, columns, NT)
            own[first : first + BLOCK, :] = term[:, :128]
            sides.append(term[:, 128:])
        upper, lower = packed(*sides)
        inner[start : start + BLOCK, :] = jnp.where(odd, lower, upper).astype(BF16)
        outer[start : start + BLOCK, :] = jnp.where(odd, upper, lower).astype(BF16)
    for plane in range(2):
        turn(cotangent.at[plane], turned, plane * 128)


def prepare_body(
    columns, own, far_weight, own_windows, hidden, side_taps, own_taps, weight, sem
):
    fetch = pltpu.make_async_copy(far_weight, weight, sem)
    fetch.start()

    def fill(i, carry):
        start = pl.multiple_of(i * STEP, STEP)
        chunk = own[pl.ds(start, STEP), :].astype(F32)
        fill_windows(own_windows, start, 0, chunk, columns, 128)
        return carry

    clear_edges(own_windows, columns)
    lax.fori_loop(0, own.shape[0] // STEP, fill, 0)
    fetch.wait()
    zero = jnp.zeros((64, 64), BF16)
    for row in range(3):
        for column in range(3):
            tap = row * 3 + column
            for at, source in enumerate(PLANES):
                depths = [depth_tap(source, target) for target in PLANES[:4]]
                parts = [zero if d is None else weight[d * 9 + tap] for d in depths]
                if at < 2:
                    target, first = own_taps, tap * 128 + at * 64
                else:
                    target, first = side_taps, tap * 256 + (at - 2) * 64
                target[first : first + 64, :128] = jnp.concatenate(parts[:2], axis=1)
                target[first : first + 64, 128:] = jnp.concatenate(parts[2:], axis=1)
    for start in range(0, own.shape[0], BLOCK):
        hidden[start : start + BLOCK, :] = window_dot(own_windows, own_taps, start, columns, NN)


def back_taps_body(weight, back_taps):
    zero = jnp.zeros((64, 64), BF16)
    for row in range(3):
        for column in range(3):
            tap = row * 3 + column
            for plane in range(2):
                depths = [depth_tap(source, plane) for source in PLANES[:4]]
                parts = [zero if d is None else weight[(2 - d) * 9 + 8 - tap] for d in depths]
                at = row * 128 + plane * 64
                for pair in range(2):
                    first = column * 256 + pair * 128
                    back_taps[at : at + 64, first : first + 128] = jnp.concatenate(
                        parts[2 * pair : 2 * pair + 2], axis=1
                    )


def hidden_body(
    columns, count, me, inner, outer, part, side_taps, side_windows, act_windows, slope
):
    cells = outer.shape[0]
    odd = me[0] % 2 == 1

    def fill(i, carry):
        start = pl.multiple_of(i * STEP, STEP)
        rows = pl.ds(start, STEP)
        below, above = by_side(odd, inner[rows, :].astype(F32), outer[rows, :].astype(F32))
        fill_windows(side_windows, start, 0, pick(above, below), columns, 256)
        fill_windows(side_windows, start, 128, pick(below, above), columns, 256)
        return carry

    clear_edges(side_windows, columns)
    clear_edges(act_windows, columns)
    lax.fori_loop(0, cells // STEP, fill, 0)
    lanes = lax.broadcasted_iota(jnp.int32, (BLOCK, 128), 1)
    edges = [jnp.where(me[0] == end, 0.0, 1.0).astype(F32) for end in (count - 1, 0)]
    inside = jnp.where(lanes < 64, edges[0], edges[1])
    for start in range(0, cells, BLOCK):
        hidden = part[start : start + BLOCK, :]
        hidden = hidden + window_dot(side_windows, side_taps, start, columns, NN)
        gate = jax.nn.sigmoid(hidden)
        act = (hidden * gate).astype(BF16).astype(F32)
        fill_windows(act_windows, start, 0, act[:, :128], columns, 256)
        fill_windows(act_windows, start, 128, act[:, 128:] * inside, columns, 256)
        hidden, gate = hidden[:, :128], gate[:, :128]
        slope[start : start + BLOCK, :] = gate * (1.0 + hidden * (1.0 - gate))


def slope_body(me, terms, inner, outer, slope, grad, to_inner, to_outer):
    half = terms.shape[0] // 2
    odd = me[0] % 2 == 1

    def step(i, carry):
        start = pl.multiple_of(i * STEP, STEP)
        low, high = pl.ds(start, STEP), pl.ds(start + half, STEP)
        near = inner[low, :].astype(F32)
        arrived = unpacked(*by_side(odd, near, outer[low, :].astype(F32)))
        sides = []
        for rows, extra in zip((low, high), arrived):
            value = ((terms[rows, :] + extra) * slope[rows, :]).astype(BF16)
            grad[rows, :] = value
            sides.append(value.astype(F32))
        lower, upper = packed(*sides)
        to_inner[low, :] = jnp.where(odd, lower, upper).astype(BF16)
        to_outer[low, :] = jnp.where(odd, upper, lower).astype(BF16)
        return carry

    lax.fori_loop(0, half // STEP, step, 0)


def kernel_terms(columns, out_channels, slices, turned, terms):
    for row in range(3):
        for column in range(3):
            tap = row * 3 + column
            product = jnp.dot(turned[...], slices(row, column), preferred_element_type=F32)
            first, second = product[:out_channels], product[out_channels:]
            terms[:, tap * 128 : tap * 128 + 128] = first[:, :128] + swap(
                pick(second[:, 128:], second[:, :128])
            )
            group = 9 + tap // 2
            here = slice(group * 128, group * 128 + 128)
            if tap % 2 == 0:
                terms[:, here] = swap(first[:, 128:]) + second[:, :128]
            else:
                terms[:, here] = pick(terms[:, here], first[:, 128:] + swap(second[:, :128]))


def turn(source, target, first):
    for start in range(0, source.shape[0], STEP):
        chunk = source[start : start + STEP, :].astype(F32)
        target[first : first + chunk.shape[1], start : start + STEP] = chunk.T.astype(BF16)


def grad_two_body(columns, act_windows, turned, terms):
    cells = turned.shape[1]

    def slices(row, column):
        rows = slice(row * columns, row * columns + cells)
        return act_windows[rows, column * 256 : column * 256 + 256]

    kernel_terms(columns, 128, slices, turned, terms)


def coded(value, split):
    head = value.astype(BF16)
    if split == 0:
        return head
    rest = (value[:split] - head[:split].astype(F32)).astype(BF16)
    return jnp.concatenate([head, rest], axis=0)


def decoded(value, split):
    value = value.astype(F32)
    if split == 0:
        return value
    size = value.shape[0] - split
    parts = [value[:split] + value[size:]]
    if split < size:
        parts.append(value[split:size])
    return jnp.concatenate(parts, axis=0)


def grad_one_body(
    columns, count, me, own_windows, side_windows, grad, other, to_inner,
    message, kept, turned, terms,
):
    cells = grad.shape[0]

    def slices(row, column):
        rows = slice(row * columns, row * columns + cells)
        return jnp.concatenate(
            [
                own_windows[rows, column * 128 : column * 128 + 128],
                side_windows[rows, column * 256 : column * 256 + 128],
            ],
            axis=1,
        )

    turn(grad, turned, 0)
    kernel_terms(columns, 64, slices, turned, terms)
    half = terms.shape[1] // 2
    odd = me[0] % 2 == 1

    def share(owner):
        parts = []
        for source in (terms, other):
            each = source.shape[0] // count
            block = source[owner * each : owner * each + each, :]
            parts += [block[:, :half], block[:, half:]]
        return jnp.concatenate(parts, axis=0)

    groups = half // 128
    for pair in range(count // 2):
        even_share, odd_share = share(2 * pair), share(2 * pair + 1)
        kept[pair] = jnp.where(odd, odd_share, even_share)
        given = coded(jnp.where(odd, even_share, odd_share), kept.shape[1])
        size = given.shape[0]
        for group in range(groups):
            first = (pair * groups + group) * size
            message[first : first + size, :] = given[:, group * 128 : group * 128 + 128]
    message[message.shape[0] - to_inner.shape[0] :, :] = to_inner[...]


def halve_body(split_in, split_out, owner_bit, at_bit, me, mine, arrived, sent, kept):
    side = (me[0] >> owner_bit) % 2
    size, lanes = mine.shape[1:]
    groups = lanes // 128

    def total(at):
        if len(arrived.shape) == 3:
            return mine[at] + decoded(arrived[at], split_in)
        parts = []
        for group in range(groups):
            first = pl.multiple_of((at * groups + group) * 2 * size, 8)
            parts.append(decoded(arrived[pl.ds(first, 2 * size), :], split_in))
        return mine[at] + jnp.concatenate(parts, axis=1)

    for at in range(sent.shape[0]):
        high, low = at >> at_bit, at & ((1 << at_bit) - 1)
        keep = ((2 * high + side) << at_bit) + low
        give = ((2 * high + 1 - side) << at_bit) + low
        sent[at] = coded(total(give), split_out)
        kept[at] = total(keep)


def spread_body(split_in, owner_bits, me, mine, arrived, kept, *sent):
    place = 0
    for bit in owner_bits:
        place = 2 * place + (me[0] >> bit) % 2
    kept[...] = mine[place] + decoded(arrived[place], split_in)
    for at, out in enumerate(sent):
        there = place ^ (at + 1)
        out[...] = (mine[there] + decoded(arrived[there], split_in)).astype(BF16)


def finish_body(scale, sizes, mine, *refs):
    arrived, (grad_one, grad_two) = refs[:-2], refs[-2:]
    total = mine[...]
    for part in arrived:
        total = total + part[...].astype(F32)
    total = total * scale
    half = total.shape[1]
    first = 0
    for size, out in zip(sizes, (grad_one, grad_two)):
        blocks = (total[first : first + size], total[first + size : first + 2 * size])
        first += 2 * size
        for tap in range(9):
            for depth, group, side in ((0, 9 + tap // 2, tap % 2), (1, tap, 0), (2, tap, 1)):
                lane = group * 128 + side * 64
                block, lane = (blocks[0], lane) if lane < half else (blocks[1], lane - half)
                out[depth * 9 + tap] = block[:, lane : lane + 64]


def output_body(columns, act_windows, weight, far, taps, output, sems):
    for row in range(3):
        for column in range(3):
            for at, source in enumerate(PLANES[:4]):
                first = row * 768 + column * 256 + at * 64
                for plane in range(2):
                    depth = depth_tap(source, plane)
                    taps[first : first + 64, plane * 128 : plane * 128 + 128] = (
                        jnp.zeros((64, 128), BF16)
                        if depth is None
                        else weight[depth * 9 + row * 3 + column]
                    )
    copies = pieces_of(output, far, sems, output.shape[1] // BLOCK)
    for at, copy in enumerate(copies):
        start = at * BLOCK
        value = window_dot(act_windows, taps, start, columns, NN)
        output[0, start : start + BLOCK, :] = value[:, :128]
        output[1, start : start + BLOCK, :] = value[:, 128:]
        copy.start()
    for copy in copies:
        copy.wait()


def grad_windows_body(columns, me, own, message, outer, windows):
    half = own.shape[0] // 2
    odd = me[0] % 2 == 1
    before = message.shape[0] - half

    def fill(i, carry):
        start = pl.multiple_of(i * STEP, STEP)
        near = message[pl.ds(before + start, STEP), :].astype(F32)
        below, above = by_side(odd, near, outer[pl.ds(start, STEP), :].astype(F32))
        for first, side in zip((start, start + half), unpacked(above, below)):
            fill_windows(windows, first, 0, own[pl.ds(first, STEP), :].astype(F32), columns, 256)
            fill_windows(windows, first, 128, side, columns, 256)
        return carry

    clear_edges(windows, columns)
    lax.fori_loop(0, half // STEP, fill, 0)


def grad_volume_body(columns, windows, taps, far, output, sems):
    copies = pieces_of(output, far, sems, output.shape[1] // BLOCK)
    for at, copy in enumerate(copies):
        start = at * BLOCK
        rows = windows[start : start + BLOCK + 2 * columns, :]
        terms = lax.dot_general(rows, taps[...], NT, preferred_element_type=F32)
        value = terms[:BLOCK, :128]
        value = value + terms[columns : columns + BLOCK, 128:256]
        value = value + terms[2 * columns : 2 * columns + BLOCK, 256:]
        output[0, start : start + BLOCK, :] = value[:, :64]
        output[1, start : start + BLOCK, :] = value[:, 64:]
        copy.start()
    for copy in copies:
        copy.wait()


def shards(volume, weight_one, weight_two, cotangent):
    count = lax.axis_size("space")
    planes, rows, columns, channels = volume.shape
    cells = rows * columns
    scale = 1.0 / math.sqrt(planes * count * cells)
    mid, wide = weight_two.shape[3], weight_two.shape[4]
    me = lax.axis_index("space").astype(jnp.int32).reshape(1)
    shape = jax.ShapeDtypeStruct
    flat, pack = shape((cells, 128), BF16), shape((cells // 2, 128), BF16)
    slab = (cells + 2 * columns, 768)
    windows = pltpu.VMEM(slab, BF16)
    lanes = 14 * 64
    split = 2 * mid // count
    chunk = 2 * (mid + wide) // count

    within = [(i, i ^ 1) for i in range(count)]
    across = [(i, i + 1) for i in range(1, count - 1, 2)]
    across += [(j, i) for i, j in across]

    volume = volume.reshape(planes, cells, channels)
    cotangent = cotangent.reshape(planes, cells, wide)
    weight_one = weight_one.reshape(27, channels, mid)
    weight_two = weight_two.reshape(27, mid, wide)
    one_flops = 2 * planes * cells * 27 * channels * mid
    two_flops = 2 * planes * cells * 27 * mid * wide

    dma = pltpu.SemaphoreType.DMA
    far_one, far_two, far_volume, far_cotangent = (
        pltpu.with_memory_space_constraint(x, pltpu.HBM)
        for x in (weight_one, weight_two, volume, cotangent)
    )
    own, = call(
        pack_body, (flat,), (far_volume,),
        (pltpu.VMEM((planes, cells, channels), BF16), dma((4,))),
        name="pack_volume", apart=(0,),
    )
    vol_outer = lax.ppermute(own, "space", across)
    vol_inner = lax.ppermute(own, "space", within)
    terms, inner, outer, turned = call(
        functools.partial(leave_body, columns),
        (
            shape((cells, 128), F32), pack, pack, shape((256, cells), BF16),
        ),
        (me, far_cotangent, far_two),
        (
            windows, pltpu.VMEM((256, 3 * 768), BF16), pltpu.VMEM(cotangent.shape, BF16),
            pltpu.VMEM(weight_two.shape, BF16), dma((4,)), dma,
        ),
        two_flops, "grad_act_terms", (0,), (1, 2),
    )
    own, terms = lax.optimization_barrier((own, terms))
    own_windows, part, side_taps = call(
        functools.partial(prepare_body, columns),
        (
            shape((slab[0], 384), BF16), shape((cells, 256), F32), shape((9 * 256, 256), BF16),
        ),
        (own, far_one),
        (pltpu.VMEM((9 * 128, 256), BF16), pltpu.VMEM(weight_one.shape, BF16), dma),
        one_flops, "prepare", (), (1,),
    )
    back_taps, = call(
        back_taps_body, (shape((3 * 128, 768), BF16),), (weight_one,), (), one_flops // 8, "back_taps"
    )
    inner, outer, part, back_taps = lax.optimization_barrier((inner, outer, part, back_taps))
    terms_outer = lax.ppermute(outer, "space", across)
    terms_inner = lax.ppermute(inner, "space", within)
    side_windows, act_windows, slope = call(
        functools.partial(hidden_body, columns, count),
        (shape(slab, BF16), shape(slab, BF16), shape((cells, 128), F32)),
        (me, vol_inner, vol_outer, part, side_taps),
        (), 2 * one_flops, "hidden", (0,),
    )
    terms_two, = call(
        functools.partial(grad_two_body, columns),
        (shape((wide, 2 * lanes), F32),),
        (act_windows, turned), (), two_flops, "grad_two_terms",
    )
    terms_two, terms_outer = lax.optimization_barrier((terms_two, terms_outer))
    grad_hidden, to_inner, outer = call(
        slope_body, (flat, pack, pack), (me, terms, terms_inner, terms_outer, slope),
        name="grad_hidden", smem=(0,),
    )
    groups = lanes // 128
    message, kept = call(
        functools.partial(grad_one_body, columns, count),
        (
            shape((count // 2 * groups * 2 * chunk + cells // 2, 128), BF16),
            shape((count // 2, chunk, lanes), F32),
        ),
        (me, own_windows, side_windows, grad_hidden, terms_two, to_inner),
        (pltpu.VMEM((128, cells), BF16), pltpu.VMEM((mid, 2 * lanes), F32)),
        one_flops, "grad_one_terms", (0,),
    )
    message = lax.ppermute(message, "space", within)
    def halve(bits, bit, split_in, split_out, kept, arrived):
        left = 2 ** (len(bits) - 1)
        sent, kept = call(
            functools.partial(halve_body, split_in, split_out, bit, bits[::-1].index(bit)),
            (shape((left, chunk + split_out, lanes), BF16), shape((left, chunk, lanes), F32)),
            (me, kept, arrived), name="halve", smem=(0,),
        )
        return [b for b in bits if b != bit], sent, kept

    bits = list(range(count.bit_length() - 2, 0, -1))
    bits, sent, kept = halve(bits, 2, chunk, split, kept, message)
    sent, act_windows, outer = lax.optimization_barrier((sent, act_windows, outer))
    arrived = lax.ppermute(sent, "space", [(i, i ^ 4) for i in range(count)])
    grad_outer = lax.ppermute(outer, "space", across)
    output, = call(
        functools.partial(output_body, columns),
        (shape((planes, cells, wide), F32),),
        (act_windows, weight_two),
        (
            pltpu.VMEM((3 * 768, 256), BF16), pltpu.VMEM((planes, cells, wide), F32),
            dma((cells // BLOCK,)),
        ),
        two_flops, "output", (), (), True,
    )
    others = 2 ** len(bits) - 1
    mine, *sent = call(
        functools.partial(spread_body, split, bits),
        (shape((chunk, lanes), F32), *[shape((chunk, lanes), BF16)] * others),
        (me, kept, arrived), flops=one_flops, name="spread", smem=(0,),
    )
    sent, output, grad_hidden = lax.optimization_barrier((sent, output, grad_hidden))
    arrived = []
    for at, part in enumerate(sent):
        away = sum(((at + 1) >> i & 1) << bit for i, bit in enumerate(bits[::-1]))
        arrived.append(lax.ppermute(part, "space", [(i, i ^ away) for i in range(count)]))
    grad_windows, = call(
        functools.partial(grad_windows_body, columns), (shape(slab, BF16),),
        (me, grad_hidden, message, grad_outer),
        (), one_flops // 4, "grad_windows", (0,),
    )
    grad_volume, = call(
        functools.partial(grad_volume_body, columns),
        (shape((planes, cells, channels), F32),),
        (grad_windows, back_taps),
        (pltpu.VMEM((planes, cells, channels), F32), dma((cells // BLOCK,))),
        one_flops, "grad_volume", (), (), True,
    )
    grad_one, grad_two = call(
        functools.partial(finish_body, scale, (mid // count, wide // count)),
        (shape((27, mid // count, channels), F32), shape((27, wide // count, mid), F32)),
        (mine, *arrived), name="finish",
    )
    return (
        output.reshape(planes, rows, columns, wide),
        grad_volume.reshape(planes, rows, columns, channels),
        jnp.swapaxes(grad_one, 1, 2).reshape(3, 3, 3, channels, mid // count),
        jnp.swapaxes(grad_two, 1, 2).reshape(3, 3, 3, mid, wide // count),
    )


def solution(mesh):
    cells = P(("groups", "space"), None, None, None)
    kernel = P("groups", None, None, None, "space")
    return jax.shard_map(
        shards,
        mesh=mesh,
        in_specs=(cells, P(), P(), cells),
        out_specs=(cells, cells, kernel, kernel),
        check_vma=False,
    )
```

```python
import functools
import math

import jax
import jax.numpy as jnp
from jax import lax
from jax.experimental import pallas as pl
from jax.experimental.pallas import tpu as pltpu
from jax.sharding import PartitionSpec as P

F32, BF16 = jnp.float32, jnp.bfloat16
STEP, BLOCK = 256, 1024
VMEM_LIMIT = 16 * 2**20
NN = (((1,), (0,)), ((), ()))
NT = (((1,), (1,)), ((), ()))

PLANES = (0, 1, 2, -1)


def depth_tap(source, target):
    tap = source - target + 1
    return tap if 0 <= tap <= 2 else None


def call(body, outs, ins, scratch=(), flops=0, name=None, smem=(), apart=(), far=False):
    moved = sum(math.prod(s.shape) * s.dtype.itemsize for s in (*outs, *ins))
    return pl.pallas_call(
        body,
        out_shape=list(outs),
        in_specs=[
            pl.BlockSpec(
                memory_space=pltpu.SMEM if i in smem else pl.ANY if i in apart else pltpu.VMEM
            )
            for i in range(len(ins))
        ],
        out_specs=[pl.BlockSpec(memory_space=pl.ANY if far else pltpu.VMEM)] * len(outs),
        scratch_shapes=list(scratch),
        compiler_params=pltpu.CompilerParams(vmem_limit_bytes=VMEM_LIMIT),
        cost_estimate=pl.CostEstimate(flops=flops, bytes_accessed=moved, transcendentals=0),
        name=name,
    )(*ins)


def lanes_low(x):
    return lax.broadcasted_iota(jnp.int32, x.shape, 1) < 64


def swap(x):
    return pltpu.roll(x, 64, 1)


def pick(low, high):
    return jnp.where(lanes_low(low), low, high)


def fill_windows(windows, start, lane, chunk, columns, stride):
    size = chunk.shape[0]
    column = lax.broadcasted_iota(jnp.int32, chunk.shape, 0) % columns
    before = jnp.where(column == 0, 0.0, pltpu.roll(chunk, 1, 0))
    after = jnp.where(column == columns - 1, 0.0, pltpu.roll(chunk, size - 1, 0))
    at = pl.ds(pl.multiple_of(columns + start, 32), size)
    for tap, part in enumerate((before, chunk, after)):
        first = tap * stride + lane
        windows[at, first : first + chunk.shape[1]] = part.astype(BF16)


def clear_edges(windows, columns):
    rows, lanes = windows.shape
    windows[0:columns, :] = jnp.zeros((columns, lanes), BF16)
    windows[rows - columns : rows, :] = jnp.zeros((columns, lanes), BF16)


def row_windows(windows, start, columns, lanes=slice(None)):
    return [
        windows[start + tap * columns : start + tap * columns + BLOCK, lanes] for tap in range(3)
    ]


def window_dot(windows, weights, start, columns, dims):
    rows = jnp.concatenate(row_windows(windows, start, columns), axis=1)
    return lax.dot_general(rows, weights[...], dims, preferred_element_type=F32)


def packed(low, high):
    return pick(low, swap(high)), pick(swap(low), high)


def unpacked(first, second):
    return packed(first, second)


def by_side(odd, inner, outer):
    return jnp.where(odd, inner, outer), jnp.where(odd, outer, inner)


def pieces_of(source, target, sems, parts):
    size = target.shape[1] // parts
    return [
        pltpu.make_async_copy(
            source.at[:, pl.ds(i * size, size), :], target.at[:, pl.ds(i * size, size), :], sems.at[i]
        )
        for i in range(parts)
    ]


def pack_body(volume, own, held, sems):
    copies = pieces_of(volume, held, sems, sems.shape[0])
    size = own.shape[0] // len(copies)
    for copy in copies:
        copy.start()
    for i, copy in enumerate(copies):
        copy.wait()
        rows = slice(i * size, i * size + size)
        own[rows, :] = jnp.concatenate([held[0, rows, :], held[1, rows, :]], axis=1)


def leave_body(
    columns, me, far_cotangent, far_weight, own, inner, outer, turned,
    windows, taps, cotangent, weight, sems, sem,
):
    cells = own.shape[0]
    half = cells // 2
    odd = me[0] % 2 == 1
    fetch = pltpu.make_async_copy(far_weight, weight, sem)
    copies = pieces_of(far_cotangent, cotangent, sems, sems.shape[0])
    for copy in copies:
        copy.start()
    fetch.start()
    clear_edges(windows, columns)
    size = cells // len(copies)
    for at, copy in enumerate(copies):
        copy.wait()

        def fill(i, carry):
            start = pl.multiple_of(at * size + i * STEP, STEP)
            for plane in range(2):
                chunk = cotangent[plane, pl.ds(start, STEP), :].astype(F32)
                fill_windows(windows, start, plane * 128, chunk, columns, 256)
            return carry

        lax.fori_loop(0, size // STEP, fill, 0)
    fetch.wait()
    for row in range(3):
        for column in range(3):
            for source in range(2):
                first = row * 768 + column * 256 + source * 128
                for at, target in enumerate(PLANES):
                    depth = depth_tap(source, target)
                    taps[at * 64 : at * 64 + 64, first : first + 128] = (
                        jnp.zeros((64, 128), BF16)
                        if depth is None
                        else weight[(2 - depth) * 9 + (2 - row) * 3 + 2 - column]
                    )
    for start in range(0, half, BLOCK):
        sides = []
        for first in (start, start + half):
            term = window_dot(windows, taps, first, columns, NT)
            own[first : first + BLOCK, :] = term[:, :128]
            sides.append(term[:, 128:])
        upper, lower = packed(*sides)
        inner[start : start + BLOCK, :] = jnp.where(odd, lower, upper).astype(BF16)
        outer[start : start + BLOCK, :] = jnp.where(odd, upper, lower).astype(BF16)
    for plane in range(2):
        turn(cotangent.at[plane], turned, plane * 128)


def prepare_body(
    columns, me, own, inner, far_weight, own_windows, inner_windows, hidden, outer_taps,
    taps, weight, sem,
):
    fetch = pltpu.make_async_copy(far_weight, weight, sem)
    fetch.start()
    odd = me[0] % 2 == 1

    def fill(i, carry):
        start = pl.multiple_of(i * STEP, STEP)
        rows = pl.ds(start, STEP)
        fill_windows(own_windows, start, 0, own[rows, :].astype(F32), columns, 128)
        fill_windows(inner_windows, start, 0, inner[rows, :].astype(F32), columns, 128)
        return carry

    clear_edges(own_windows, columns)
    clear_edges(inner_windows, columns)
    lax.fori_loop(0, own.shape[0] // STEP, fill, 0)
    fetch.wait()
    zero = jnp.zeros((64, 64), BF16)
    for tap in range(9):

        def kernel_rows(source):
            depths = [depth_tap(source, target) for target in PLANES]
            parts = [zero if d is None else weight[d * 9 + tap] for d in depths]
            return jnp.concatenate(parts, axis=1)

        for at in range(2):
            rows = slice(tap * 128 + at * 64, tap * 128 + at * 64 + 64)
            taps[rows, :] = kernel_rows(at)
            upper, lower = kernel_rows(2 + at).astype(F32), kernel_rows(at - 2).astype(F32)
            first = 9 * 128 + rows.start
            taps[first : first + 64, :] = jnp.where(odd, lower, upper).astype(BF16)
            outer_taps[rows, :] = jnp.where(odd, upper, lower).astype(BF16)
    for start in range(0, own.shape[0], BLOCK):
        rows = row_windows(own_windows, start, columns) + row_windows(inner_windows, start, columns)
        hidden[start : start + BLOCK, :] = jnp.dot(
            jnp.concatenate(rows, axis=1), taps[...], preferred_element_type=F32
        )


def back_taps_body(weight, back_taps):
    zero = jnp.zeros((64, 64), BF16)
    for row in range(3):
        for column in range(3):
            tap = row * 3 + column
            for plane in range(2):
                depths = [depth_tap(source, plane) for source in PLANES]
                parts = [zero if d is None else weight[(2 - d) * 9 + 8 - tap] for d in depths]
                at = row * 128 + plane * 64
                for pair in range(2):
                    first = column * 256 + pair * 128
                    back_taps[at : at + 64, first : first + 128] = jnp.concatenate(
                        parts[2 * pair : 2 * pair + 2], axis=1
                    )


def hidden_body(
    columns, count, me, outer, part, outer_taps, outer_windows, act_windows, slope
):
    cells = outer.shape[0]

    def fill(i, carry):
        start = pl.multiple_of(i * STEP, STEP)
        chunk = outer[pl.ds(start, STEP), :].astype(F32)
        fill_windows(outer_windows, start, 0, chunk, columns, 128)
        return carry

    clear_edges(outer_windows, columns)
    clear_edges(act_windows, columns)
    lax.fori_loop(0, cells // STEP, fill, 0)
    lanes = lax.broadcasted_iota(jnp.int32, (BLOCK, 128), 1)
    edges = [jnp.where(me[0] == end, 0.0, 1.0).astype(F32) for end in (count - 1, 0)]
    inside = jnp.where(lanes < 64, edges[0], edges[1])
    for start in range(0, cells, BLOCK):
        hidden = part[start : start + BLOCK, :]
        hidden = hidden + window_dot(outer_windows, outer_taps, start, columns, NN)
        gate = jax.nn.sigmoid(hidden)
        act = (hidden * gate).astype(BF16).astype(F32)
        fill_windows(act_windows, start, 0, act[:, :128], columns, 256)
        fill_windows(act_windows, start, 128, act[:, 128:] * inside, columns, 256)
        hidden, gate = hidden[:, :128], gate[:, :128]
        slope[start : start + BLOCK, :] = gate * (1.0 + hidden * (1.0 - gate))


def kernel_terms(columns, out_channels, slices, turned, terms):
    for row in range(3):
        for column in range(3):
            tap = row * 3 + column
            product = jnp.dot(turned[...], slices(row, column), preferred_element_type=F32)
            first, second = product[:out_channels], product[out_channels:]
            terms[:, tap * 128 : tap * 128 + 128] = first[:, :128] + swap(
                pick(second[:, 128:], second[:, :128])
            )
            group = 9 + tap // 2
            here = slice(group * 128, group * 128 + 128)
            if tap % 2 == 0:
                terms[:, here] = swap(first[:, 128:]) + second[:, :128]
            else:
                terms[:, here] = pick(terms[:, here], first[:, 128:] + swap(second[:, :128]))


def turn(source, target, first):
    for start in range(0, source.shape[0], STEP):
        chunk = source[start : start + STEP, :].astype(F32)
        target[first : first + chunk.shape[1], start : start + STEP] = chunk.T.astype(BF16)


def grad_two_body(columns, act_windows, turned, terms):
    cells = turned.shape[1]

    def slices(row, column):
        rows = slice(row * columns, row * columns + cells)
        return act_windows[rows, column * 256 : column * 256 + 256]

    kernel_terms(columns, 128, slices, turned, terms)


def coded(value, split):
    head = value.astype(BF16)
    if split == 0:
        return head
    rest = (value[:split] - head[:split].astype(F32)).astype(BF16)
    return jnp.concatenate([head, rest], axis=0)


def decoded(value, split):
    value = value.astype(F32)
    if split == 0:
        return value
    size = value.shape[0] - split
    parts = [value[:split] + value[size:]]
    if split < size:
        parts.append(value[split:size])
    return jnp.concatenate(parts, axis=0)


def grad_one_body(
    columns, count, me, own_windows, inner_windows, outer_windows, act_terms, inner, outer, slope,
    other, grad, to_outer, message, kept, turned, terms,
):
    cells = grad.shape[0]
    odd = me[0] % 2 == 1
    before = message.shape[0] - cells // 2
    for start in range(0, cells // 2, STEP):
        low, high = slice(start, start + STEP), slice(start + cells // 2, start + cells // 2 + STEP)
        arrived = unpacked(*by_side(odd, inner[low, :].astype(F32), outer[low, :].astype(F32)))
        sides = []
        for rows, extra in zip((low, high), arrived):
            value = ((act_terms[rows, :] + extra) * slope[rows, :]).astype(BF16)
            grad[rows, :] = value
            value = value.astype(F32)
            turned[:, rows] = value.T.astype(BF16)
            sides.append(value)
        lower, upper = packed(*sides)
        message[before + start : before + start + STEP, :] = jnp.where(
            odd, lower, upper
        ).astype(BF16)
        to_outer[low, :] = jnp.where(odd, upper, lower).astype(BF16)
    from_inner = lax.broadcasted_iota(jnp.int32, (16, 128), 1) // 64 == me[0] % 2
    from_inner = jnp.where(from_inner, 1.0, 0.0).astype(BF16)[:1]
    from_outer = 1 - from_inner

    def slices(row, column):
        rows = slice(row * columns, row * columns + cells)
        lanes = slice(column * 128, column * 128 + 128)
        sides = inner_windows[rows, lanes] * from_inner + outer_windows[rows, lanes] * from_outer
        return jnp.concatenate([own_windows[rows, lanes], sides], axis=1)

    kernel_terms(columns, 64, slices, turned, terms)
    half = terms.shape[1] // 2
    split = 2 * terms.shape[0] // count

    def share(owner):
        parts = []
        for source in (terms, other):
            each = source.shape[0] // count
            block = source[owner * each : owner * each + each, :]
            parts += [block[:, :half], block[:, half:]]
        return jnp.concatenate(parts, axis=0)

    groups = half // 128
    for pair in range(count // 2):
        even_share, odd_share = share(2 * pair), share(2 * pair + 1)
        kept[pair] = jnp.where(odd, odd_share, even_share)
        given = coded(jnp.where(odd, even_share, odd_share), split)
        size = given.shape[0]
        for group in range(groups):
            first = (pair * groups + group) * size
            message[first : first + size, :] = given[:, group * 128 : group * 128 + 128]


def halve_body(split_in, split_out, owner_bit, at_bit, me, mine, arrived, sent, kept):
    side = (me[0] >> owner_bit) % 2
    size, lanes = mine.shape[1:]
    groups = lanes // 128

    def total(at):
        if len(arrived.shape) == 3:
            return mine[at] + decoded(arrived[at], split_in)
        parts = []
        for group in range(groups):
            rows = size + split_in
            first = pl.multiple_of((at * groups + group) * rows, 8)
            parts.append(decoded(arrived[pl.ds(first, rows), :], split_in))
        return mine[at] + jnp.concatenate(parts, axis=1)

    for at in range(sent.shape[0]):
        high, low = at >> at_bit, at & ((1 << at_bit) - 1)
        keep = ((2 * high + side) << at_bit) + low
        give = ((2 * high + 1 - side) << at_bit) + low
        sent[at] = coded(total(give), split_out)
        kept[at] = total(keep)


def spread_body(split_in, owner_bits, me, mine, arrived, kept, *sent):
    place = 0
    for bit in owner_bits:
        place = 2 * place + (me[0] >> bit) % 2
    kept[...] = mine[place] + decoded(arrived[place], split_in)
    for at, out in enumerate(sent):
        there = place ^ (at + 1)
        out[...] = (mine[there] + decoded(arrived[there], split_in)).astype(BF16)


def finish_body(scale, sizes, mine, *refs):
    arrived, (grad_one, grad_two) = refs[:-2], refs[-2:]
    total = mine[...]
    for part in arrived:
        total = total + part[...].astype(F32)
    total = total * scale
    half = total.shape[1]
    first = 0
    for size, out in zip(sizes, (grad_one, grad_two)):
        blocks = (total[first : first + size], total[first + size : first + 2 * size])
        first += 2 * size
        for tap in range(9):
            for depth, group, side in ((0, 9 + tap // 2, tap % 2), (1, tap, 0), (2, tap, 1)):
                lane = group * 128 + side * 64
                block, lane = (blocks[0], lane) if lane < half else (blocks[1], lane - half)
                out[depth * 9 + tap] = block[:, lane : lane + 64]


def output_body(columns, act_windows, weight, far, taps, output, sems):
    for row in range(3):
        for column in range(3):
            for at, source in enumerate(PLANES):
                first = row * 768 + column * 256 + at * 64
                for plane in range(2):
                    depth = depth_tap(source, plane)
                    taps[first : first + 64, plane * 128 : plane * 128 + 128] = (
                        jnp.zeros((64, 128), BF16)
                        if depth is None
                        else weight[depth * 9 + row * 3 + column]
                    )
    copies = pieces_of(output, far, sems, output.shape[1] // BLOCK)
    for at, copy in enumerate(copies):
        start = at * BLOCK
        value = window_dot(act_windows, taps, start, columns, NN)
        output[0, start : start + BLOCK, :] = value[:, :128]
        output[1, start : start + BLOCK, :] = value[:, 128:]
        copy.start()
    for copy in copies:
        copy.wait()


def grad_windows_body(columns, me, own, message, outer, windows):
    half = own.shape[0] // 2
    odd = me[0] % 2 == 1
    before = message.shape[0] - half

    def fill(i, carry):
        start = pl.multiple_of(i * STEP, STEP)
        near = message[pl.ds(before + start, STEP), :].astype(F32)
        below, above = by_side(odd, near, outer[pl.ds(start, STEP), :].astype(F32))
        for first, side in zip((start, start + half), unpacked(above, below)):
            fill_windows(windows, first, 0, own[pl.ds(first, STEP), :].astype(F32), columns, 256)
            fill_windows(windows, first, 128, side, columns, 256)
        return carry

    clear_edges(windows, columns)
    lax.fori_loop(0, half // STEP, fill, 0)


def grad_volume_body(columns, windows, taps, far, output, sems):
    copies = pieces_of(output, far, sems, output.shape[1] // BLOCK)
    for at, copy in enumerate(copies):
        start = at * BLOCK
        rows = windows[start : start + BLOCK + 2 * columns, :]
        terms = lax.dot_general(rows, taps[...], NT, preferred_element_type=F32)
        value = terms[:BLOCK, :128]
        value = value + terms[columns : columns + BLOCK, 128:256]
        value = value + terms[2 * columns : 2 * columns + BLOCK, 256:]
        output[0, start : start + BLOCK, :] = value[:, :64]
        output[1, start : start + BLOCK, :] = value[:, 64:]
        copy.start()
    for copy in copies:
        copy.wait()


def shards(volume, weight_one, weight_two, cotangent):
    count = lax.axis_size("space")
    planes, rows, columns, channels = volume.shape
    cells = rows * columns
    scale = 1.0 / math.sqrt(planes * count * cells)
    mid, wide = weight_two.shape[3], weight_two.shape[4]
    me = lax.axis_index("space").astype(jnp.int32).reshape(1)
    shape = jax.ShapeDtypeStruct
    flat, pack = shape((cells, 128), BF16), shape((cells // 2, 128), BF16)
    slab = (cells + 2 * columns, 768)
    windows = pltpu.VMEM(slab, BF16)
    lanes = 14 * 64
    split = 2 * mid // count
    chunk = 2 * (mid + wide) // count

    within = [(i, i ^ 1) for i in range(count)]
    across = [(i, i + 1) for i in range(1, count - 1, 2)]
    across += [(j, i) for i, j in across]

    volume = volume.reshape(planes, cells, channels)
    cotangent = cotangent.reshape(planes, cells, wide)
    weight_one = weight_one.reshape(27, channels, mid)
    weight_two = weight_two.reshape(27, mid, wide)
    one_flops = 2 * planes * cells * 27 * channels * mid
    two_flops = 2 * planes * cells * 27 * mid * wide

    dma = pltpu.SemaphoreType.DMA
    far_one, far_two, far_volume, far_cotangent = (
        pltpu.with_memory_space_constraint(x, pltpu.HBM)
        for x in (weight_one, weight_two, volume, cotangent)
    )
    own, = call(
        pack_body, (flat,), (far_volume,),
        (pltpu.VMEM((planes, cells, channels), BF16), dma((4,))),
        name="pack_volume", apart=(0,),
    )
    vol_outer = lax.ppermute(own, "space", across)
    vol_inner = lax.ppermute(own, "space", within)
    terms, inner, outer, turned = call(
        functools.partial(leave_body, columns),
        (
            shape((cells, 128), F32), pack, pack, shape((256, cells), BF16),
        ),
        (me, far_cotangent, far_two),
        (
            windows, pltpu.VMEM((256, 3 * 768), BF16), pltpu.VMEM(cotangent.shape, BF16),
            pltpu.VMEM(weight_two.shape, BF16), dma((4,)), dma,
        ),
        two_flops, "grad_act_terms", (0,), (1, 2),
    )
    own, terms = lax.optimization_barrier((own, terms))
    third = shape((slab[0], 384), BF16)
    own_windows, inner_windows, part, outer_taps = call(
        functools.partial(prepare_body, columns),
        (third, third, shape((cells, 256), F32), shape((9 * 128, 256), BF16)),
        (me, own, vol_inner, far_one),
        (pltpu.VMEM((2 * 9 * 128, 256), BF16), pltpu.VMEM(weight_one.shape, BF16), dma),
        one_flops, "prepare", (0,), (3,),
    )
    back_taps, = call(
        back_taps_body, (shape((3 * 128, 768), BF16),), (weight_one,), (), one_flops // 8, "back_taps"
    )
    inner, outer, part, back_taps = lax.optimization_barrier((inner, outer, part, back_taps))
    terms_outer = lax.ppermute(outer, "space", across)
    terms_inner = lax.ppermute(inner, "space", within)
    outer_windows, act_windows, slope = call(
        functools.partial(hidden_body, columns, count),
        (third, shape(slab, BF16), shape((cells, 128), F32)),
        (me, vol_outer, part, outer_taps),
        (), 2 * one_flops, "hidden", (0,),
    )
    terms_two, = call(
        functools.partial(grad_two_body, columns),
        (shape((wide, 2 * lanes), F32),),
        (act_windows, turned), (), two_flops, "grad_two_terms",
    )
    groups = lanes // 128
    grad_hidden, outer, message, kept = call(
        functools.partial(grad_one_body, columns, count),
        (
            flat, pack,
            shape((count // 2 * groups * (chunk + split) + cells // 2, 128), BF16),
            shape((count // 2, chunk, lanes), F32),
        ),
        (
            me, own_windows, inner_windows, outer_windows, terms, terms_inner, terms_outer, slope,
            terms_two,
        ),
        (pltpu.VMEM((128, cells), BF16), pltpu.VMEM((mid, 2 * lanes), F32)),
        one_flops, "grad_one_terms", (0,),
    )
    message = lax.ppermute(message, "space", within)
    def halve(bits, bit, split_in, split_out, kept, arrived):
        left = 2 ** (len(bits) - 1)
        sent, kept = call(
            functools.partial(halve_body, split_in, split_out, bit, bits[::-1].index(bit)),
            (shape((left, chunk + split_out, lanes), BF16), shape((left, chunk, lanes), F32)),
            (me, kept, arrived), name="halve", smem=(0,),
        )
        return [b for b in bits if b != bit], sent, kept

    bits = list(range(count.bit_length() - 2, 0, -1))
    bits, sent, kept = halve(bits, 2, split, split, kept, message)
    sent, act_windows, outer = lax.optimization_barrier((sent, act_windows, outer))
    arrived = lax.ppermute(sent, "space", [(i, i ^ 4) for i in range(count)])
    grad_outer = lax.ppermute(outer, "space", across)
    output, = call(
        functools.partial(output_body, columns),
        (shape((planes, cells, wide), F32),),
        (act_windows, weight_two),
        (
            pltpu.VMEM((3 * 768, 256), BF16), pltpu.VMEM((planes, cells, wide), F32),
            dma((cells // BLOCK,)),
        ),
        two_flops, "output", (), (), True,
    )
    others = 2 ** len(bits) - 1
    mine, *sent = call(
        functools.partial(spread_body, split, bits),
        (shape((chunk, lanes), F32), *[shape((chunk, lanes), BF16)] * others),
        (me, kept, arrived), flops=one_flops, name="spread", smem=(0,),
    )
    sent, output, grad_hidden = lax.optimization_barrier((sent, output, grad_hidden))
    arrived = []
    for at, part in enumerate(sent):
        away = sum(((at + 1) >> i & 1) << bit for i, bit in enumerate(bits[::-1]))
        arrived.append(lax.ppermute(part, "space", [(i, i ^ away) for i in range(count)]))
    grad_windows, = call(
        functools.partial(grad_windows_body, columns), (shape(slab, BF16),),
        (me, grad_hidden, message, grad_outer),
        (), one_flops // 4, "grad_windows", (0,),
    )
    grad_volume, = call(
        functools.partial(grad_volume_body, columns),
        (shape((planes, cells, channels), F32),),
        (grad_windows, back_taps),
        (pltpu.VMEM((planes, cells, channels), F32), dma((cells // BLOCK,))),
        one_flops, "grad_volume", (), (), True,
    )
    grad_one, grad_two = call(
        functools.partial(finish_body, scale, (mid // count, wide // count)),
        (shape((27, mid // count, channels), F32), shape((27, wide // count, mid), F32)),
        (mine, *arrived), name="finish",
    )
    return (
        output.reshape(planes, rows, columns, wide),
        grad_volume.reshape(planes, rows, columns, channels),
        jnp.swapaxes(grad_one, 1, 2).reshape(3, 3, 3, channels, mid // count),
        jnp.swapaxes(grad_two, 1, 2).reshape(3, 3, 3, mid, wide // count),
    )


def solution(mesh):
    cells = P(("groups", "space"), None, None, None)
    kernel = P("groups", None, None, None, "space")
    return jax.shard_map(
        shards,
        mesh=mesh,
        in_specs=(cells, P(), P(), cells),
        out_specs=(cells, cells, kernel, kernel),
        check_vma=False,
    )
```

```python
import functools
import math

import jax
import jax.numpy as jnp
from jax import lax
from jax.experimental import pallas as pl
from jax.experimental.pallas import tpu as pltpu
from jax.sharding import PartitionSpec as P

F32, BF16 = jnp.float32, jnp.bfloat16
STEP, BLOCK = 256, 512
VMEM_LIMIT = 16 * 2**20
NN = (((1,), (0,)), ((), ()))
NT = (((1,), (1,)), ((), ()))

PLANES = (0, 1, 2, -1)


def depth_tap(source, target):
    tap = source - target + 1
    return tap if 0 <= tap <= 2 else None


def call(body, outs, ins, scratch=(), flops=0, name=None, smem=(), apart=(), far=(), alias=None):
    moved = sum(math.prod(s.shape) * s.dtype.itemsize for s in (*outs, *ins))
    return pl.pallas_call(
        body,
        out_shape=list(outs),
        in_specs=[
            pl.BlockSpec(
                memory_space=pltpu.SMEM if i in smem else pl.ANY if i in apart else pltpu.VMEM
            )
            for i in range(len(ins))
        ],
        out_specs=[
            pl.BlockSpec(memory_space=pl.ANY if i in far else pltpu.VMEM) for i in range(len(outs))
        ],
        input_output_aliases=alias or {},
        scratch_shapes=list(scratch),
        compiler_params=pltpu.CompilerParams(vmem_limit_bytes=VMEM_LIMIT),
        cost_estimate=pl.CostEstimate(flops=flops, bytes_accessed=moved, transcendentals=0),
        name=name,
    )(*ins)


def lanes_low(x):
    return lax.broadcasted_iota(jnp.int32, x.shape, 1) < 64


def swap(x):
    return pltpu.roll(x, 64, 1)


def pick(low, high):
    return jnp.where(lanes_low(low), low, high)


def fill_windows(windows, start, lane, chunk, columns, stride):
    size = chunk.shape[0]
    column = lax.broadcasted_iota(jnp.int32, chunk.shape, 0) % columns
    before = jnp.where(column == 0, 0.0, pltpu.roll(chunk, 1, 0))
    after = jnp.where(column == columns - 1, 0.0, pltpu.roll(chunk, size - 1, 0))
    at = pl.ds(pl.multiple_of(columns + start, 32), size)
    for tap, part in enumerate((before, chunk, after)):
        first = tap * stride + lane
        windows[at, first : first + chunk.shape[1]] = part.astype(BF16)


def clear_edges(windows, columns):
    rows, lanes = windows.shape
    windows[0:columns, :] = jnp.zeros((columns, lanes), BF16)
    windows[rows - columns : rows, :] = jnp.zeros((columns, lanes), BF16)


def row_windows(windows, start, columns, lanes=slice(None)):
    return [
        windows[start + tap * columns : start + tap * columns + BLOCK, lanes] for tap in range(3)
    ]


def window_dot(windows, weights, start, columns, dims):
    rows = jnp.concatenate(row_windows(windows, start, columns), axis=1)
    return lax.dot_general(rows, weights[...], dims, preferred_element_type=F32)


def packed(low, high):
    return pick(low, swap(high)), pick(swap(low), high)


def unpacked(first, second):
    return packed(first, second)


def by_side(odd, inner, outer):
    return jnp.where(odd, inner, outer), jnp.where(odd, outer, inner)


def pieces_of(source, target, sems, parts):
    size = target.shape[1] // parts
    return [
        pltpu.make_async_copy(
            source.at[:, pl.ds(i * size, size), :], target.at[:, pl.ds(i * size, size), :], sems.at[i]
        )
        for i in range(parts)
    ]


def pack_body(volume, own, held, sems):
    copies = pieces_of(volume, held, sems, sems.shape[0])
    size = own.shape[0] // len(copies)
    for copy in copies:
        copy.start()
    for i, copy in enumerate(copies):
        copy.wait()
        rows = slice(i * size, i * size + size)
        own[rows, :] = jnp.concatenate([held[0, rows, :], held[1, rows, :]], axis=1)


def leave_body(
    columns, me, far_cotangent, far_weight, own, inner, outer, turned,
    windows, taps, cotangent, weight, sems, sem,
):
    cells = own.shape[0]
    half = cells // 2
    odd = me[0] % 2 == 1
    fetch = pltpu.make_async_copy(far_weight, weight, sem)
    copies = pieces_of(far_cotangent, cotangent, sems, sems.shape[0])
    for copy in copies:
        copy.start()
    fetch.start()
    clear_edges(windows, columns)
    size = cells // len(copies)
    for at, copy in enumerate(copies):
        copy.wait()

        def fill(i, carry):
            start = pl.multiple_of(at * size + i * STEP, STEP)
            for plane in range(2):
                chunk = cotangent[plane, pl.ds(start, STEP), :].astype(F32)
                fill_windows(windows, start, plane * 128, chunk, columns, 256)
            return carry

        lax.fori_loop(0, size // STEP, fill, 0)
    fetch.wait()
    for row in range(3):
        for column in range(3):
            for source in range(2):
                first = row * 768 + column * 256 + source * 128
                for at, target in enumerate(PLANES):
                    depth = depth_tap(source, target)
                    taps[at * 64 : at * 64 + 64, first : first + 128] = (
                        jnp.zeros((64, 128), BF16)
                        if depth is None
                        else weight[(2 - depth) * 9 + (2 - row) * 3 + 2 - column]
                    )
    for start in range(0, half, BLOCK):
        sides = []
        for first in (start, start + half):
            term = window_dot(windows, taps, first, columns, NT)
            own[first : first + BLOCK, :] = term[:, :128]
            sides.append(term[:, 128:])
        upper, lower = packed(*sides)
        inner[start : start + BLOCK, :] = jnp.where(odd, lower, upper).astype(BF16)
        outer[start : start + BLOCK, :] = jnp.where(odd, upper, lower).astype(BF16)
    for plane in range(2):
        turn(cotangent.at[plane], turned, plane * 128)


def prepare_body(
    columns, me, own, inner, far_weight, own_windows, inner_windows, hidden, outer_taps,
    taps, weight, sem,
):
    fetch = pltpu.make_async_copy(far_weight, weight, sem)
    fetch.start()
    odd = me[0] % 2 == 1

    def fill(i, carry):
        start = pl.multiple_of(i * STEP, STEP)
        rows = pl.ds(start, STEP)
        fill_windows(own_windows, start, 0, own[rows, :].astype(F32), columns, 128)
        fill_windows(inner_windows, start, 0, inner[rows, :].astype(F32), columns, 128)
        return carry

    clear_edges(own_windows, columns)
    clear_edges(inner_windows, columns)
    lax.fori_loop(0, own.shape[0] // STEP, fill, 0)
    fetch.wait()
    zero = jnp.zeros((64, 64), BF16)
    for tap in range(9):

        def kernel_rows(source):
            depths = [depth_tap(source, target) for target in PLANES]
            parts = [zero if d is None else weight[d * 9 + tap] for d in depths]
            return jnp.concatenate(parts, axis=1)

        for at in range(2):
            rows = slice(tap * 128 + at * 64, tap * 128 + at * 64 + 64)
            taps[rows, :] = kernel_rows(at)
            upper, lower = kernel_rows(2 + at).astype(F32), kernel_rows(at - 2).astype(F32)
            first = 9 * 128 + rows.start
            taps[first : first + 64, :] = jnp.where(odd, lower, upper).astype(BF16)
            outer_taps[rows, :] = jnp.where(odd, upper, lower).astype(BF16)
    for start in range(0, own.shape[0], BLOCK):
        rows = row_windows(own_windows, start, columns) + row_windows(inner_windows, start, columns)
        hidden[start : start + BLOCK, :] = jnp.dot(
            jnp.concatenate(rows, axis=1), taps[...], preferred_element_type=F32
        )


def back_taps_body(weight, back_taps):
    zero = jnp.zeros((64, 64), BF16)
    for row in range(3):
        for column in range(3):
            tap = row * 3 + column
            for plane in range(2):
                depths = [depth_tap(source, plane) for source in PLANES]
                parts = [zero if d is None else weight[(2 - d) * 9 + 8 - tap] for d in depths]
                at = row * 128 + plane * 64
                for pair in range(2):
                    first = column * 256 + pair * 128
                    back_taps[at : at + 64, first : first + 128] = jnp.concatenate(
                        parts[2 * pair : 2 * pair + 2], axis=1
                    )


def hidden_body(
    columns, count, me, outer, part, outer_taps, inner_windows, act_windows, slope, side_windows,
    outer_windows,
):
    cells = outer.shape[0]

    def fill(i, carry):
        start = pl.multiple_of(i * STEP, STEP)
        chunk = outer[pl.ds(start, STEP), :].astype(F32)
        fill_windows(outer_windows, start, 0, chunk, columns, 128)
        return carry

    clear_edges(outer_windows, columns)
    clear_edges(act_windows, columns)
    lax.fori_loop(0, cells // STEP, fill, 0)
    from_inner = lax.broadcasted_iota(jnp.int32, (16, 128), 1) // 64 == me[0] % 2
    from_inner = jnp.where(from_inner, 1.0, 0.0).astype(BF16)[:1]
    for tap in range(3):
        at = slice(tap * 128, tap * 128 + 128)
        side_windows[:, at] = (
            inner_windows[:, at] * from_inner + outer_windows[:, at] * (1 - from_inner)
        )
    lanes = lax.broadcasted_iota(jnp.int32, (BLOCK, 128), 1)
    edges = [jnp.where(me[0] == end, 0.0, 1.0).astype(F32) for end in (count - 1, 0)]
    inside = jnp.where(lanes < 64, edges[0], edges[1])
    for start in range(0, cells, BLOCK):
        hidden = part[start : start + BLOCK, :]
        hidden = hidden + window_dot(outer_windows, outer_taps, start, columns, NN)
        gate = jax.nn.sigmoid(hidden)
        act = (hidden * gate).astype(BF16).astype(F32)
        fill_windows(act_windows, start, 0, act[:, :128], columns, 256)
        fill_windows(act_windows, start, 128, act[:, 128:] * inside, columns, 256)
        hidden, gate = hidden[:, :128], gate[:, :128]
        slope[start : start + BLOCK, :] = gate * (1.0 + hidden * (1.0 - gate))


def kernel_terms(columns, out_channels, slices, turned, terms):
    for row in range(3):
        for column in range(3):
            tap = row * 3 + column
            product = jnp.dot(turned[...], slices(row, column), preferred_element_type=F32)
            first, second = product[:out_channels], product[out_channels:]
            terms[:, tap * 128 : tap * 128 + 128] = first[:, :128] + swap(
                pick(second[:, 128:], second[:, :128])
            )
            group = 9 + tap // 2
            here = slice(group * 128, group * 128 + 128)
            if tap % 2 == 0:
                terms[:, here] = swap(first[:, 128:]) + second[:, :128]
            else:
                terms[:, here] = pick(terms[:, here], first[:, 128:] + swap(second[:, :128]))


def turn(source, target, first):
    for start in range(0, source.shape[0], STEP):
        chunk = source[start : start + STEP, :].astype(F32)
        target[first : first + chunk.shape[1], start : start + STEP] = chunk.T.astype(BF16)


def grad_two_body(columns, act_windows, turned, terms):
    cells = turned.shape[1]

    def slices(row, column):
        rows = slice(row * columns, row * columns + cells)
        return act_windows[rows, column * 256 : column * 256 + 256]

    kernel_terms(columns, 128, slices, turned, terms)


def coded(value, split):
    head = value.astype(BF16)
    if split == 0:
        return head
    rest = (value[:split] - head[:split].astype(F32)).astype(BF16)
    return jnp.concatenate([head, rest], axis=0)


def decoded(value, split):
    value = value.astype(F32)
    if split == 0:
        return value
    size = value.shape[0] - split
    parts = [value[:split] + value[size:]]
    if split < size:
        parts.append(value[split:size])
    return jnp.concatenate(parts, axis=0)


def grad_one_body(
    columns, count, me, own_windows, side_windows, act_terms, inner, outer, slope, other,
    grad, to_outer, message, kept, turned, terms,
):
    cells = grad.shape[0]
    odd = me[0] % 2 == 1
    before = message.shape[0] - cells // 2
    for start in range(0, cells // 2, STEP):
        low, high = slice(start, start + STEP), slice(start + cells // 2, start + cells // 2 + STEP)
        arrived = unpacked(*by_side(odd, inner[low, :].astype(F32), outer[low, :].astype(F32)))
        sides = []
        for rows, extra in zip((low, high), arrived):
            value = ((act_terms[rows, :] + extra) * slope[rows, :]).astype(BF16)
            grad[rows, :] = value
            value = value.astype(F32)
            turned[:, rows] = value.T.astype(BF16)
            sides.append(value)
        lower, upper = packed(*sides)
        message[before + start : before + start + STEP, :] = jnp.where(
            odd, lower, upper
        ).astype(BF16)
        to_outer[low, :] = jnp.where(odd, upper, lower).astype(BF16)
    def slices(row, column):
        rows = slice(row * columns, row * columns + cells)
        lanes = slice(column * 128, column * 128 + 128)
        return jnp.concatenate([own_windows[rows, lanes], side_windows[rows, lanes]], axis=1)

    kernel_terms(columns, 64, slices, turned, terms)
    half = terms.shape[1] // 2
    split = 2 * terms.shape[0] // count

    def share(owner):
        parts = []
        for source in (terms, other):
            each = source.shape[0] // count
            block = source[owner * each : owner * each + each, :]
            parts += [block[:, :half], block[:, half:]]
        return jnp.concatenate(parts, axis=0)

    groups = half // 128
    for pair in range(count // 2):
        even_share, odd_share = share(2 * pair), share(2 * pair + 1)
        kept[pair] = jnp.where(odd, odd_share, even_share)
        given = coded(jnp.where(odd, even_share, odd_share), split)
        size = given.shape[0]
        for group in range(groups):
            first = (pair * groups + group) * size
            message[first : first + size, :] = given[:, group * 128 : group * 128 + 128]


def halve_body(split_in, split_out, owner_bit, at_bit, me, mine, arrived, sent, kept):
    side = (me[0] >> owner_bit) % 2
    size, lanes = mine.shape[1:]
    groups = lanes // 128

    def total(at):
        if len(arrived.shape) == 3:
            return mine[at] + decoded(arrived[at], split_in)
        parts = []
        for group in range(groups):
            rows = size + split_in
            first = pl.multiple_of((at * groups + group) * rows, 8)
            parts.append(decoded(arrived[pl.ds(first, rows), :], split_in))
        return mine[at] + jnp.concatenate(parts, axis=1)

    for at in range(sent.shape[0]):
        high, low = at >> at_bit, at & ((1 << at_bit) - 1)
        keep = ((2 * high + side) << at_bit) + low
        give = ((2 * high + 1 - side) << at_bit) + low
        sent[at] = coded(total(give), split_out)
        kept[at] = total(keep)


def spread_body(split_in, owner_bits, me, mine, arrived, kept, *sent):
    place = 0
    for bit in owner_bits:
        place = 2 * place + (me[0] >> bit) % 2
    kept[...] = mine[place] + decoded(arrived[place], split_in)
    for at, out in enumerate(sent):
        there = place ^ (at + 1)
        out[...] = (mine[there] + decoded(arrived[there], split_in)).astype(BF16)


def finish_body(scale, sizes, mine, *refs):
    arrived, (grad_one, grad_two) = refs[:-2], refs[-2:]
    total = mine[...]
    for part in arrived:
        total = total + part[...].astype(F32)
    total = total * scale
    half = total.shape[1]
    first = 0
    for size, out in zip(sizes, (grad_one, grad_two)):
        blocks = (total[first : first + size], total[first + size : first + 2 * size])
        first += 2 * size
        for tap in range(9):
            for depth, group, side in ((0, 9 + tap // 2, tap % 2), (1, tap, 0), (2, tap, 1)):
                lane = group * 128 + side * 64
                block, lane = (blocks[0], lane) if lane < half else (blocks[1], lane - half)
                out[depth * 9 + tap] = block[:, lane : lane + 64]


def output_taps(weight, taps):
    for row in range(3):
        for column in range(3):
            for at, source in enumerate(PLANES):
                first = row * 768 + column * 256 + at * 64
                for plane in range(2):
                    depth = depth_tap(source, plane)
                    taps[first : first + 64, plane * 128 : plane * 128 + 128] = (
                        jnp.zeros((64, 128), BF16)
                        if depth is None
                        else weight[depth * 9 + row * 3 + column]
                    )


def output_rows(columns, blocks, act_windows, taps, far, output, sems):
    copies = []
    for at, block in enumerate(blocks):
        start = block * BLOCK
        value = window_dot(act_windows, taps, start, columns, NN)
        here = slice(at * BLOCK, at * BLOCK + BLOCK)
        output[0, here, :] = value[:, :128]
        output[1, here, :] = value[:, 128:]
        copies.append(
            pltpu.make_async_copy(
                output.at[:, here, :], far.at[:, start : start + BLOCK, :], sems.at[at]
            )
        )
        copies[-1].start()
    for copy in copies:
        copy.wait()


def output_first_body(columns, blocks, act_windows, weight, far, taps, output, sems):
    output_taps(weight, taps)
    output_rows(columns, blocks, act_windows, taps, far, output, sems)


def output_rest_body(columns, blocks, act_windows, taps, begun, far, output, sems):
    output_rows(columns, blocks, act_windows, taps, far, output, sems)


def grad_windows_body(columns, me, own, message, outer, windows):
    half = own.shape[0] // 2
    odd = me[0] % 2 == 1
    before = message.shape[0] - half

    def fill(i, carry):
        start = pl.multiple_of(i * STEP, STEP)
        near = message[pl.ds(before + start, STEP), :].astype(F32)
        below, above = by_side(odd, near, outer[pl.ds(start, STEP), :].astype(F32))
        for first, side in zip((start, start + half), unpacked(above, below)):
            fill_windows(windows, first, 0, own[pl.ds(first, STEP), :].astype(F32), columns, 256)
            fill_windows(windows, first, 128, side, columns, 256)
        return carry

    clear_edges(windows, columns)
    lax.fori_loop(0, half // STEP, fill, 0)


def grad_volume_body(columns, windows, taps, far, output, sems):
    copies = pieces_of(output, far, sems, output.shape[1] // BLOCK)
    for at, copy in enumerate(copies):
        start = at * BLOCK
        rows = windows[start : start + BLOCK + 2 * columns, :]
        terms = lax.dot_general(rows, taps[...], NT, preferred_element_type=F32)
        value = terms[:BLOCK, :128]
        value = value + terms[columns : columns + BLOCK, 128:256]
        value = value + terms[2 * columns : 2 * columns + BLOCK, 256:]
        output[0, start : start + BLOCK, :] = value[:, :64]
        output[1, start : start + BLOCK, :] = value[:, 64:]
        copy.start()
    for copy in copies:
        copy.wait()


def shards(volume, weight_one, weight_two, cotangent):
    count = lax.axis_size("space")
    planes, rows, columns, channels = volume.shape
    cells = rows * columns
    scale = 1.0 / math.sqrt(planes * count * cells)
    mid, wide = weight_two.shape[3], weight_two.shape[4]
    me = lax.axis_index("space").astype(jnp.int32).reshape(1)
    shape = jax.ShapeDtypeStruct
    flat, pack = shape((cells, 128), BF16), shape((cells // 2, 128), BF16)
    slab = (cells + 2 * columns, 768)
    windows = pltpu.VMEM(slab, BF16)
    lanes = 14 * 64
    split = 2 * mid // count
    chunk = 2 * (mid + wide) // count

    within = [(i, i ^ 1) for i in range(count)]
    across = [(i, i + 1) for i in range(1, count - 1, 2)]
    across += [(j, i) for i, j in across]

    volume = volume.reshape(planes, cells, channels)
    cotangent = cotangent.reshape(planes, cells, wide)
    weight_one = weight_one.reshape(27, channels, mid)
    weight_two = weight_two.reshape(27, mid, wide)
    one_flops = 2 * planes * cells * 27 * channels * mid
    two_flops = 2 * planes * cells * 27 * mid * wide

    dma = pltpu.SemaphoreType.DMA
    far_one, far_two, far_volume, far_cotangent = (
        pltpu.with_memory_space_constraint(x, pltpu.HBM)
        for x in (weight_one, weight_two, volume, cotangent)
    )
    own, = call(
        pack_body, (flat,), (far_volume,),
        (pltpu.VMEM((planes, cells, channels), BF16), dma((4,))),
        name="pack_volume", apart=(0,),
    )
    vol_outer = lax.ppermute(own, "space", across)
    vol_inner = lax.ppermute(own, "space", within)
    terms, inner, outer, turned = call(
        functools.partial(leave_body, columns),
        (
            shape((cells, 128), F32), pack, pack, shape((256, cells), BF16),
        ),
        (me, far_cotangent, far_two),
        (
            windows, pltpu.VMEM((256, 3 * 768), BF16), pltpu.VMEM(cotangent.shape, BF16),
            pltpu.VMEM(weight_two.shape, BF16), dma((4,)), dma,
        ),
        two_flops, "grad_act_terms", (0,), (1, 2),
    )
    own, terms = lax.optimization_barrier((own, terms))
    third = shape((slab[0], 384), BF16)
    own_windows, inner_windows, part, outer_taps = call(
        functools.partial(prepare_body, columns),
        (third, third, shape((cells, 256), F32), shape((9 * 128, 256), BF16)),
        (me, own, vol_inner, far_one),
        (pltpu.VMEM((2 * 9 * 128, 256), BF16), pltpu.VMEM(weight_one.shape, BF16), dma),
        one_flops, "prepare", (0,), (3,),
    )
    back_taps, = call(
        back_taps_body, (shape((3 * 128, 768), BF16),), (weight_one,), (), one_flops // 8, "back_taps"
    )
    inner, outer, part, back_taps = lax.optimization_barrier((inner, outer, part, back_taps))
    terms_outer = lax.ppermute(outer, "space", across)
    terms_inner = lax.ppermute(inner, "space", within)
    act_windows, slope, side_windows = call(
        functools.partial(hidden_body, columns, count),
        (shape(slab, BF16), shape((cells, 128), F32), third),
        (me, vol_outer, part, outer_taps, inner_windows),
        (pltpu.VMEM((slab[0], 384), BF16),), 2 * one_flops, "hidden", (0,),
    )
    terms_two, = call(
        functools.partial(grad_two_body, columns),
        (shape((wide, 2 * lanes), F32),),
        (act_windows, turned), (), two_flops, "grad_two_terms",
    )
    blocks = range(cells // BLOCK)
    output, out_taps = call(
        functools.partial(output_first_body, columns, blocks[:1]),
        (shape((planes, cells, wide), F32), shape((9 * 256, 256), BF16)),
        (act_windows, weight_two),
        (pltpu.VMEM((planes, BLOCK, wide), F32), dma((1,))),
        two_flops // 4, "output_first", (), (), (0,),
    )
    terms_outer, output, out_taps = lax.optimization_barrier((terms_outer, output, out_taps))
    groups = lanes // 128
    grad_hidden, outer, message, kept = call(
        functools.partial(grad_one_body, columns, count),
        (
            flat, pack,
            shape((count // 2 * groups * (chunk + split) + cells // 2, 128), BF16),
            shape((count // 2, chunk, lanes), F32),
        ),
        (
            me, own_windows, side_windows, terms, terms_inner, terms_outer, slope, terms_two,
        ),
        (pltpu.VMEM((128, cells), BF16), pltpu.VMEM((mid, 2 * lanes), F32)),
        one_flops, "grad_one_terms", (0,),
    )
    message = lax.ppermute(message, "space", within)
    def halve(bits, bit, split_in, split_out, kept, arrived):
        left = 2 ** (len(bits) - 1)
        sent, kept = call(
            functools.partial(halve_body, split_in, split_out, bit, bits[::-1].index(bit)),
            (shape((left, chunk + split_out, lanes), BF16), shape((left, chunk, lanes), F32)),
            (me, kept, arrived), name="halve", smem=(0,),
        )
        return [b for b in bits if b != bit], sent, kept

    bits = list(range(count.bit_length() - 2, 0, -1))
    bits, sent, kept = halve(bits, 2, split, split, kept, message)
    sent, act_windows = lax.optimization_barrier((sent, act_windows))
    arrived = lax.ppermute(sent, "space", [(i, i ^ 4) for i in range(count)])
    grad_outer = lax.ppermute(outer, "space", across)
    output, = call(
        functools.partial(output_rest_body, columns, blocks[1:]),
        (shape((planes, cells, wide), F32),),
        (act_windows, out_taps, output),
        (pltpu.VMEM((planes, cells - BLOCK, wide), F32), dma((len(blocks) - 1,))),
        two_flops, "output_rest", (), (2,), (0,), {2: 0},
    )
    others = 2 ** len(bits) - 1
    mine, *sent = call(
        functools.partial(spread_body, split, bits),
        (shape((chunk, lanes), F32), *[shape((chunk, lanes), BF16)] * others),
        (me, kept, arrived), name="spread", smem=(0,),
    )
    sent, output, grad_hidden = lax.optimization_barrier((sent, output, grad_hidden))
    arrived = []
    for at, part in enumerate(sent):
        away = sum(((at + 1) >> i & 1) << bit for i, bit in enumerate(bits[::-1]))
        arrived.append(lax.ppermute(part, "space", [(i, i ^ away) for i in range(count)]))
    grad_windows, = call(
        functools.partial(grad_windows_body, columns), (shape(slab, BF16),),
        (me, grad_hidden, message, grad_outer),
        (), one_flops // 4, "grad_windows", (0,),
    )
    grad_volume, = call(
        functools.partial(grad_volume_body, columns),
        (shape((planes, cells, channels), F32),),
        (grad_windows, back_taps),
        (pltpu.VMEM((planes, cells, channels), F32), dma((cells // BLOCK,))),
        one_flops, "grad_volume", (), (), (0,),
    )
    grad_one, grad_two = call(
        functools.partial(finish_body, scale, (mid // count, wide // count)),
        (shape((27, mid // count, channels), F32), shape((27, wide // count, mid), F32)),
        (mine, *arrived), name="finish",
    )
    return (
        output.reshape(planes, rows, columns, wide),
        grad_volume.reshape(planes, rows, columns, channels),
        jnp.swapaxes(grad_one, 1, 2).reshape(3, 3, 3, channels, mid // count),
        jnp.swapaxes(grad_two, 1, 2).reshape(3, 3, 3, mid, wide // count),
    )


def solution(mesh):
    cells = P(("groups", "space"), None, None, None)
    kernel = P("groups", None, None, None, "space")
    return jax.shard_map(
        shards,
        mesh=mesh,
        in_specs=(cells, P(), P(), cells),
        out_specs=(cells, cells, kernel, kernel),
        check_vma=False,
    )
```

```python
import functools
import math

import jax
import jax.numpy as jnp
from jax import lax
from jax.experimental import pallas as pl
from jax.experimental.pallas import tpu as pltpu
from jax.sharding import PartitionSpec as P

F32, BF16 = jnp.float32, jnp.bfloat16
STEP, BLOCK = 256, 512
VMEM_LIMIT = 16 * 2**20
NN = (((1,), (0,)), ((), ()))
NT = (((1,), (1,)), ((), ()))

PLANES = (0, 1, 2, -1)


def depth_tap(source, target):
    tap = source - target + 1
    return tap if 0 <= tap <= 2 else None


def call(body, outs, ins, scratch=(), flops=0, name=None, smem=(), apart=(), far=(), alias=None):
    moved = sum(math.prod(s.shape) * s.dtype.itemsize for s in (*outs, *ins))
    return pl.pallas_call(
        body,
        out_shape=list(outs),
        in_specs=[
            pl.BlockSpec(
                memory_space=pltpu.SMEM if i in smem else pl.ANY if i in apart else pltpu.VMEM
            )
            for i in range(len(ins))
        ],
        out_specs=[
            pl.BlockSpec(memory_space=pl.ANY if i in far else pltpu.VMEM) for i in range(len(outs))
        ],
        input_output_aliases=alias or {},
        scratch_shapes=list(scratch),
        compiler_params=pltpu.CompilerParams(vmem_limit_bytes=VMEM_LIMIT),
        cost_estimate=pl.CostEstimate(flops=flops, bytes_accessed=moved, transcendentals=0),
        name=name,
    )(*ins)


def lanes_low(x):
    return lax.broadcasted_iota(jnp.int32, x.shape, 1) < 64


def swap(x):
    return pltpu.roll(x, 64, 1)


def pick(low, high):
    return jnp.where(lanes_low(low), low, high)


def fill_windows(windows, start, lane, chunk, columns, stride):
    size = chunk.shape[0]
    column = lax.broadcasted_iota(jnp.int32, chunk.shape, 0) % columns
    before = jnp.where(column == 0, 0.0, pltpu.roll(chunk, 1, 0))
    after = jnp.where(column == columns - 1, 0.0, pltpu.roll(chunk, size - 1, 0))
    at = pl.ds(pl.multiple_of(columns + start, 32), size)
    for tap, part in enumerate((before, chunk, after)):
        first = tap * stride + lane
        windows[at, first : first + chunk.shape[1]] = part.astype(BF16)


def clear_edges(windows, columns):
    rows, lanes = windows.shape
    windows[0:columns, :] = jnp.zeros((columns, lanes), BF16)
    windows[rows - columns : rows, :] = jnp.zeros((columns, lanes), BF16)


def row_windows(windows, start, columns, lanes=slice(None)):
    return [
        windows[start + tap * columns : start + tap * columns + BLOCK, lanes] for tap in range(3)
    ]


def window_dot(windows, weights, start, columns, dims):
    rows = jnp.concatenate(row_windows(windows, start, columns), axis=1)
    return lax.dot_general(rows, weights[...], dims, preferred_element_type=F32)


def packed(low, high):
    return pick(low, swap(high)), pick(swap(low), high)


def unpacked(first, second):
    return packed(first, second)


def by_side(odd, inner, outer):
    return jnp.where(odd, inner, outer), jnp.where(odd, outer, inner)


def pieces_of(source, target, sems, parts):
    size = target.shape[1] // parts
    return [
        pltpu.make_async_copy(
            source.at[:, pl.ds(i * size, size), :], target.at[:, pl.ds(i * size, size), :], sems.at[i]
        )
        for i in range(parts)
    ]


def pack_body(volume, own, held, sems):
    copies = pieces_of(volume, held, sems, sems.shape[0])
    size = own.shape[0] // len(copies)
    for copy in copies:
        copy.start()
    for i, copy in enumerate(copies):
        copy.wait()
        rows = slice(i * size, i * size + size)
        own[rows, :] = jnp.concatenate([held[0, rows, :], held[1, rows, :]], axis=1)


def leave_body(
    columns, me, far_cotangent, far_weight, own, inner, outer, turned,
    windows, taps, cotangent, weight, sems, sem,
):
    cells = own.shape[0]
    half = cells // 2
    odd = me[0] % 2 == 1
    fetch = pltpu.make_async_copy(far_weight, weight, sem)
    copies = pieces_of(far_cotangent, cotangent, sems, sems.shape[0])
    for copy in copies:
        copy.start()
    fetch.start()
    clear_edges(windows, columns)
    size = cells // len(copies)
    for at, copy in enumerate(copies):
        copy.wait()

        def fill(i, carry):
            start = pl.multiple_of(at * size + i * STEP, STEP)
            for plane in range(2):
                chunk = cotangent[plane, pl.ds(start, STEP), :].astype(F32)
                fill_windows(windows, start, plane * 128, chunk, columns, 256)
            return carry

        lax.fori_loop(0, size // STEP, fill, 0)
    fetch.wait()
    for row in range(3):
        for column in range(3):
            for source in range(2):
                first = row * 768 + column * 256 + source * 128
                for at, target in enumerate(PLANES):
                    depth = depth_tap(source, target)
                    taps[at * 64 : at * 64 + 64, first : first + 128] = (
                        jnp.zeros((64, 128), BF16)
                        if depth is None
                        else weight[(2 - depth) * 9 + (2 - row) * 3 + 2 - column]
                    )
    for start in range(0, half, BLOCK):
        sides = []
        for first in (start, start + half):
            term = window_dot(windows, taps, first, columns, NT)
            own[first : first + BLOCK, :] = term[:, :128]
            sides.append(term[:, 128:])
        upper, lower = packed(*sides)
        inner[start : start + BLOCK, :] = jnp.where(odd, lower, upper).astype(BF16)
        outer[start : start + BLOCK, :] = jnp.where(odd, upper, lower).astype(BF16)
    for plane in range(2):
        turn(cotangent.at[plane], turned, plane * 128)


def prepare_body(
    columns, me, own, inner, far_weight, own_windows, inner_windows, hidden, outer_taps,
    taps, weight, sem,
):
    fetch = pltpu.make_async_copy(far_weight, weight, sem)
    fetch.start()
    odd = me[0] % 2 == 1

    def fill(i, carry):
        start = pl.multiple_of(i * STEP, STEP)
        rows = pl.ds(start, STEP)
        fill_windows(own_windows, start, 0, own[rows, :].astype(F32), columns, 128)
        fill_windows(inner_windows, start, 0, inner[rows, :].astype(F32), columns, 128)
        return carry

    clear_edges(own_windows, columns)
    clear_edges(inner_windows, columns)
    lax.fori_loop(0, own.shape[0] // STEP, fill, 0)
    fetch.wait()
    zero = jnp.zeros((64, 64), BF16)
    for tap in range(9):

        def kernel_rows(source):
            depths = [depth_tap(source, target) for target in PLANES]
            parts = [zero if d is None else weight[d * 9 + tap] for d in depths]
            return jnp.concatenate(parts, axis=1)

        for at in range(2):
            rows = slice(tap * 128 + at * 64, tap * 128 + at * 64 + 64)
            taps[rows, :] = kernel_rows(at)
            upper, lower = kernel_rows(2 + at).astype(F32), kernel_rows(at - 2).astype(F32)
            first = 9 * 128 + rows.start
            taps[first : first + 64, :] = jnp.where(odd, lower, upper).astype(BF16)
            outer_taps[rows, :] = jnp.where(odd, upper, lower).astype(BF16)
    for start in range(0, own.shape[0], BLOCK):
        rows = row_windows(own_windows, start, columns) + row_windows(inner_windows, start, columns)
        hidden[start : start + BLOCK, :] = jnp.dot(
            jnp.concatenate(rows, axis=1), taps[...], preferred_element_type=F32
        )


def back_taps_body(weight, back_taps):
    zero = jnp.zeros((64, 64), BF16)
    for row in range(3):
        for column in range(3):
            tap = row * 3 + column
            for plane in range(2):
                depths = [depth_tap(source, plane) for source in PLANES]
                parts = [zero if d is None else weight[(2 - d) * 9 + 8 - tap] for d in depths]
                at = row * 128 + plane * 64
                for pair in range(2):
                    first = pair * 384 + column * 128
                    back_taps[at : at + 64, first : first + 128] = jnp.concatenate(
                        parts[2 * pair : 2 * pair + 2], axis=1
                    )


def hidden_body(
    columns, count, me, outer, part, outer_taps, outer_windows, act_windows, slope
):
    cells = outer.shape[0]

    def fill(i, carry):
        start = pl.multiple_of(i * STEP, STEP)
        chunk = outer[pl.ds(start, STEP), :].astype(F32)
        fill_windows(outer_windows, start, 0, chunk, columns, 128)
        return carry

    clear_edges(outer_windows, columns)
    clear_edges(act_windows, columns)
    lax.fori_loop(0, cells // STEP, fill, 0)
    lanes = lax.broadcasted_iota(jnp.int32, (BLOCK, 128), 1)
    edges = [jnp.where(me[0] == end, 0.0, 1.0).astype(F32) for end in (count - 1, 0)]
    inside = jnp.where(lanes < 64, edges[0], edges[1])
    for start in range(0, cells, BLOCK):
        hidden = part[start : start + BLOCK, :]
        hidden = hidden + window_dot(outer_windows, outer_taps, start, columns, NN)
        gate = jax.nn.sigmoid(hidden)
        act = (hidden * gate).astype(BF16).astype(F32)
        fill_windows(act_windows, start, 0, act[:, :128], columns, 256)
        fill_windows(act_windows, start, 128, act[:, 128:] * inside, columns, 256)
        hidden, gate = hidden[:, :128], gate[:, :128]
        slope[start : start + BLOCK, :] = gate * (1.0 + hidden * (1.0 - gate))


def kernel_terms(columns, out_channels, slices, turned, terms):
    for row in range(3):
        for column in range(3):
            tap = row * 3 + column
            product = jnp.dot(turned[...], slices(row, column), preferred_element_type=F32)
            first, second = product[:out_channels], product[out_channels:]
            terms[:, tap * 128 : tap * 128 + 128] = first[:, :128] + swap(
                pick(second[:, 128:], second[:, :128])
            )
            group = 9 + tap // 2
            here = slice(group * 128, group * 128 + 128)
            if tap % 2 == 0:
                terms[:, here] = swap(first[:, 128:]) + second[:, :128]
            else:
                terms[:, here] = pick(terms[:, here], first[:, 128:] + swap(second[:, :128]))


def turn(source, target, first):
    for start in range(0, source.shape[0], STEP):
        chunk = source[start : start + STEP, :].astype(F32)
        target[first : first + chunk.shape[1], start : start + STEP] = chunk.T.astype(BF16)


def grad_two_body(columns, act_windows, turned, terms):
    cells = turned.shape[1]

    def slices(row, column):
        rows = slice(row * columns, row * columns + cells)
        return act_windows[rows, column * 256 : column * 256 + 256]

    kernel_terms(columns, 128, slices, turned, terms)


def coded(value, split):
    head = value.astype(BF16)
    if split == 0:
        return head
    rest = (value[:split] - head[:split].astype(F32)).astype(BF16)
    return jnp.concatenate([head, rest], axis=0)


def decoded(value, split):
    value = value.astype(F32)
    if split == 0:
        return value
    size = value.shape[0] - split
    parts = [value[:split] + value[size:]]
    if split < size:
        parts.append(value[split:size])
    return jnp.concatenate(parts, axis=0)


def grad_one_body(
    columns, count, me, own_windows, inner_windows, outer_windows, act_terms, inner, outer, slope,
    other, grad, to_outer, message, kept, turned, terms,
):
    cells = grad.shape[0]
    odd = me[0] % 2 == 1
    before = message.shape[0] - cells // 2
    for start in range(0, cells // 2, STEP):
        low, high = slice(start, start + STEP), slice(start + cells // 2, start + cells // 2 + STEP)
        arrived = unpacked(*by_side(odd, inner[low, :].astype(F32), outer[low, :].astype(F32)))
        sides = []
        for rows, extra in zip((low, high), arrived):
            value = ((act_terms[rows, :] + extra) * slope[rows, :]).astype(BF16)
            grad[rows, :] = value
            value = value.astype(F32)
            turned[:, rows] = value.T.astype(BF16)
            sides.append(value)
        lower, upper = packed(*sides)
        message[before + start : before + start + STEP, :] = jnp.where(
            odd, lower, upper
        ).astype(BF16)
        to_outer[low, :] = jnp.where(odd, upper, lower).astype(BF16)
    from_inner = lax.broadcasted_iota(jnp.int32, (16, 128), 1) // 64 == me[0] % 2
    from_inner = jnp.where(from_inner, 1.0, 0.0).astype(BF16)[:1]
    from_outer = 1 - from_inner

    def slices(row, column):
        rows = slice(row * columns, row * columns + cells)
        lanes = slice(column * 128, column * 128 + 128)
        sides = inner_windows[rows, lanes] * from_inner + outer_windows[rows, lanes] * from_outer
        return jnp.concatenate([own_windows[rows, lanes], sides], axis=1)

    kernel_terms(columns, 64, slices, turned, terms)
    half = terms.shape[1] // 2
    split = 2 * terms.shape[0] // count

    def share(owner):
        parts = []
        for source in (terms, other):
            each = source.shape[0] // count
            block = source[owner * each : owner * each + each, :]
            parts += [block[:, :half], block[:, half:]]
        return jnp.concatenate(parts, axis=0)

    groups = half // 128
    for pair in range(count // 2):
        even_share, odd_share = share(2 * pair), share(2 * pair + 1)
        kept[pair] = jnp.where(odd, odd_share, even_share)
        given = coded(jnp.where(odd, even_share, odd_share), split)
        size = given.shape[0]
        for group in range(groups):
            first = (pair * groups + group) * size
            message[first : first + size, :] = given[:, group * 128 : group * 128 + 128]


def halve_body(split_in, split_out, owner_bit, at_bit, me, mine, arrived, sent, kept):
    side = (me[0] >> owner_bit) % 2
    size, lanes = mine.shape[1:]
    groups = lanes // 128

    def total(at):
        if len(arrived.shape) == 3:
            return mine[at] + decoded(arrived[at], split_in)
        parts = []
        for group in range(groups):
            rows = size + split_in
            first = pl.multiple_of((at * groups + group) * rows, 8)
            parts.append(decoded(arrived[pl.ds(first, rows), :], split_in))
        return mine[at] + jnp.concatenate(parts, axis=1)

    for at in range(sent.shape[0]):
        high, low = at >> at_bit, at & ((1 << at_bit) - 1)
        keep = ((2 * high + side) << at_bit) + low
        give = ((2 * high + 1 - side) << at_bit) + low
        sent[at] = coded(total(give), split_out)
        kept[at] = total(keep)


def spread_body(split_in, owner_bits, me, mine, arrived, kept, *sent):
    place = 0
    for bit in owner_bits:
        place = 2 * place + (me[0] >> bit) % 2
    kept[...] = mine[place] + decoded(arrived[place], split_in)
    for at, out in enumerate(sent):
        there = place ^ (at + 1)
        out[...] = (mine[there] + decoded(arrived[there], split_in)).astype(BF16)


def finish_body(scale, sizes, mine, *refs):
    arrived, (grad_one, grad_two) = refs[:-2], refs[-2:]
    total = mine[...]
    for part in arrived:
        total = total + part[...].astype(F32)
    total = total * scale
    half = total.shape[1]
    first = 0
    for size, out in zip(sizes, (grad_one, grad_two)):
        blocks = (total[first : first + size], total[first + size : first + 2 * size])
        first += 2 * size
        for tap in range(9):
            for depth, group, side in ((0, 9 + tap // 2, tap % 2), (1, tap, 0), (2, tap, 1)):
                lane = group * 128 + side * 64
                block, lane = (blocks[0], lane) if lane < half else (blocks[1], lane - half)
                out[depth * 9 + tap] = block[:, lane : lane + 64]


def output_rows(columns, blocks, act_windows, taps, far, output, sems):
    copies = []
    for at, block in enumerate(blocks):
        start = block * BLOCK
        value = window_dot(act_windows, taps, start, columns, NN)
        here = slice(at * BLOCK, at * BLOCK + BLOCK)
        output[0, here, :] = value[:, :128]
        output[1, here, :] = value[:, 128:]
        copies.append(
            pltpu.make_async_copy(
                output.at[:, here, :], far.at[:, start : start + BLOCK, :], sems.at[at]
            )
        )
        copies[-1].start()
    return copies


def output_first_body(
    columns, blocks, act_windows, weight, grad, far, taps, own_windows, output, sems
):
    for row in range(3):
        for column in range(3):
            for at, source in enumerate(PLANES):
                first = row * 768 + column * 256 + at * 64
                for plane in range(2):
                    depth = depth_tap(source, plane)
                    taps[first : first + 64, plane * 128 : plane * 128 + 128] = (
                        jnp.zeros((64, 128), BF16)
                        if depth is None
                        else weight[depth * 9 + row * 3 + column]
                    )
    copies = output_rows(columns, blocks, act_windows, taps, far, output, sems)

    def fill(i, carry):
        start = pl.multiple_of(i * STEP, STEP)
        chunk = grad[pl.ds(start, STEP), :].astype(F32)
        fill_windows(own_windows, start, 0, chunk, columns, 128)
        return carry

    clear_edges(own_windows, columns)
    lax.fori_loop(0, grad.shape[0] // STEP, fill, 0)
    for copy in copies:
        copy.wait()


def output_rest_body(columns, blocks, act_windows, taps, begun, far, output, sems):
    for copy in output_rows(columns, blocks, act_windows, taps, far, output, sems):
        copy.wait()


def grad_windows_body(columns, me, message, outer, windows):
    half = outer.shape[0]
    odd = me[0] % 2 == 1
    before = message.shape[0] - half

    def fill(i, carry):
        start = pl.multiple_of(i * STEP, STEP)
        near = message[pl.ds(before + start, STEP), :].astype(F32)
        below, above = by_side(odd, near, outer[pl.ds(start, STEP), :].astype(F32))
        for first, side in zip((start, start + half), unpacked(above, below)):
            fill_windows(windows, first, 0, side, columns, 128)
        return carry

    clear_edges(windows, columns)
    lax.fori_loop(0, half // STEP, fill, 0)


def grad_volume_body(columns, own_windows, side_windows, taps, far, output, sems):
    copies = pieces_of(output, far, sems, output.shape[1] // BLOCK)
    for at, copy in enumerate(copies):
        start = at * BLOCK
        rows = slice(start, start + BLOCK + 2 * columns)
        rows = jnp.concatenate([own_windows[rows, :], side_windows[rows, :]], axis=1)
        terms = lax.dot_general(rows, taps[...], NT, preferred_element_type=F32)
        value = terms[:BLOCK, :128]
        value = value + terms[columns : columns + BLOCK, 128:256]
        value = value + terms[2 * columns : 2 * columns + BLOCK, 256:]
        output[0, start : start + BLOCK, :] = value[:, :64]
        output[1, start : start + BLOCK, :] = value[:, 64:]
        copy.start()
    for copy in copies:
        copy.wait()


def shards(volume, weight_one, weight_two, cotangent):
    count = lax.axis_size("space")
    planes, rows, columns, channels = volume.shape
    cells = rows * columns
    scale = 1.0 / math.sqrt(planes * count * cells)
    mid, wide = weight_two.shape[3], weight_two.shape[4]
    me = lax.axis_index("space").astype(jnp.int32).reshape(1)
    shape = jax.ShapeDtypeStruct
    flat, pack = shape((cells, 128), BF16), shape((cells // 2, 128), BF16)
    slab = (cells + 2 * columns, 768)
    windows = pltpu.VMEM(slab, BF16)
    lanes = 14 * 64
    split = 2 * mid // count
    chunk = 2 * (mid + wide) // count

    within = [(i, i ^ 1) for i in range(count)]
    across = [(i, i + 1) for i in range(1, count - 1, 2)]
    across += [(j, i) for i, j in across]

    volume = volume.reshape(planes, cells, channels)
    cotangent = cotangent.reshape(planes, cells, wide)
    weight_one = weight_one.reshape(27, channels, mid)
    weight_two = weight_two.reshape(27, mid, wide)
    one_flops = 2 * planes * cells * 27 * channels * mid
    two_flops = 2 * planes * cells * 27 * mid * wide

    dma = pltpu.SemaphoreType.DMA
    far_one, far_two, far_volume, far_cotangent = (
        pltpu.with_memory_space_constraint(x, pltpu.HBM)
        for x in (weight_one, weight_two, volume, cotangent)
    )
    own, = call(
        pack_body, (flat,), (far_volume,),
        (pltpu.VMEM((planes, cells, channels), BF16), dma((4,))),
        name="pack_volume", apart=(0,),
    )
    vol_outer = lax.ppermute(own, "space", across)
    vol_inner = lax.ppermute(own, "space", within)
    terms, inner, outer, turned = call(
        functools.partial(leave_body, columns),
        (
            shape((cells, 128), F32), pack, pack, shape((256, cells), BF16),
        ),
        (me, far_cotangent, far_two),
        (
            windows, pltpu.VMEM((256, 3 * 768), BF16), pltpu.VMEM(cotangent.shape, BF16),
            pltpu.VMEM(weight_two.shape, BF16), dma((4,)), dma,
        ),
        two_flops, "grad_act_terms", (0,), (1, 2),
    )
    own, terms = lax.optimization_barrier((own, terms))
    third = shape((slab[0], 384), BF16)
    own_windows, inner_windows, part, outer_taps = call(
        functools.partial(prepare_body, columns),
        (third, third, shape((cells, 256), F32), shape((9 * 128, 256), BF16)),
        (me, own, vol_inner, far_one),
        (pltpu.VMEM((2 * 9 * 128, 256), BF16), pltpu.VMEM(weight_one.shape, BF16), dma),
        one_flops, "prepare", (0,), (3,),
    )
    back_taps, = call(
        back_taps_body, (shape((3 * 128, 768), BF16),), (weight_one,), (), one_flops // 8, "back_taps"
    )
    inner, outer, part, back_taps = lax.optimization_barrier((inner, outer, part, back_taps))
    terms_outer = lax.ppermute(outer, "space", across)
    terms_inner = lax.ppermute(inner, "space", within)
    outer_windows, act_windows, slope = call(
        functools.partial(hidden_body, columns, count),
        (third, shape(slab, BF16), shape((cells, 128), F32)),
        (me, vol_outer, part, outer_taps),
        (), 2 * one_flops, "hidden", (0,),
    )
    terms_two, = call(
        functools.partial(grad_two_body, columns),
        (shape((wide, 2 * lanes), F32),),
        (act_windows, turned), (), two_flops, "grad_two_terms",
    )
    groups = lanes // 128
    grad_hidden, outer, message, kept = call(
        functools.partial(grad_one_body, columns, count),
        (
            flat, pack,
            shape((count // 2 * groups * (chunk + split) + cells // 2, 128), BF16),
            shape((count // 2, chunk, lanes), F32),
        ),
        (
            me, own_windows, inner_windows, outer_windows, terms, terms_inner, terms_outer, slope,
            terms_two,
        ),
        (pltpu.VMEM((128, cells), BF16), pltpu.VMEM((mid, 2 * lanes), F32)),
        one_flops, "grad_one_terms", (0,),
    )
    message = lax.ppermute(message, "space", within)
    blocks = range(cells // BLOCK)
    output, out_taps, back_windows = call(
        functools.partial(output_first_body, columns, blocks[:1]),
        (shape((planes, cells, wide), F32), shape((9 * 256, 256), BF16), third),
        (act_windows, weight_two, grad_hidden),
        (pltpu.VMEM((planes, BLOCK, wide), F32), dma((1,))),
        two_flops, "output_first", (), (), (0,),
    )
    message, output, out_taps, back_windows = lax.optimization_barrier(
        (message, output, out_taps, back_windows)
    )
    def halve(bits, bit, split_in, split_out, kept, arrived):
        left = 2 ** (len(bits) - 1)
        sent, kept = call(
            functools.partial(halve_body, split_in, split_out, bit, bits[::-1].index(bit)),
            (shape((left, chunk + split_out, lanes), BF16), shape((left, chunk, lanes), F32)),
            (me, kept, arrived), name="halve", smem=(0,),
        )
        return [b for b in bits if b != bit], sent, kept

    bits = list(range(count.bit_length() - 2, 0, -1))
    bits, sent, kept = halve(bits, 2, split, split, kept, message)
    sent, act_windows, outer = lax.optimization_barrier((sent, act_windows, outer))
    arrived = lax.ppermute(sent, "space", [(i, i ^ 4) for i in range(count)])
    grad_outer = lax.ppermute(outer, "space", across)
    output, = call(
        functools.partial(output_rest_body, columns, blocks[1:]),
        (shape((planes, cells, wide), F32),),
        (act_windows, out_taps, output),
        (pltpu.VMEM((planes, cells - BLOCK, wide), F32), dma((len(blocks) - 1,))),
        two_flops, "output_rest", (), (2,), (0,), {2: 0},
    )
    others = 2 ** len(bits) - 1
    mine, *sent = call(
        functools.partial(spread_body, split, bits),
        (shape((chunk, lanes), F32), *[shape((chunk, lanes), BF16)] * others),
        (me, kept, arrived), flops=one_flops, name="spread", smem=(0,),
    )
    sent, output, back_windows = lax.optimization_barrier((sent, output, back_windows))
    arrived = []
    for at, part in enumerate(sent):
        away = sum(((at + 1) >> i & 1) << bit for i, bit in enumerate(bits[::-1]))
        arrived.append(lax.ppermute(part, "space", [(i, i ^ away) for i in range(count)]))
    grad_windows, = call(
        functools.partial(grad_windows_body, columns), (third,), (me, message, grad_outer),
        (), one_flops // 4, "grad_windows", (0,),
    )
    grad_volume, = call(
        functools.partial(grad_volume_body, columns),
        (shape((planes, cells, channels), F32),),
        (back_windows, grad_windows, back_taps),
        (pltpu.VMEM((planes, cells, channels), F32), dma((cells // BLOCK,))),
        one_flops, "grad_volume", (), (), (0,),
    )
    grad_one, grad_two = call(
        functools.partial(finish_body, scale, (mid // count, wide // count)),
        (shape((27, mid // count, channels), F32), shape((27, wide // count, mid), F32)),
        (mine, *arrived), name="finish",
    )
    return (
        output.reshape(planes, rows, columns, wide),
        grad_volume.reshape(planes, rows, columns, channels),
        jnp.swapaxes(grad_one, 1, 2).reshape(3, 3, 3, channels, mid // count),
        jnp.swapaxes(grad_two, 1, 2).reshape(3, 3, 3, mid, wide // count),
    )


def solution(mesh):
    cells = P(("groups", "space"), None, None, None)
    kernel = P("groups", None, None, None, "space")
    return jax.shard_map(
        shards,
        mesh=mesh,
        in_specs=(cells, P(), P(), cells),
        out_specs=(cells, cells, kernel, kernel),
        check_vma=False,
    )
```

```python
import functools
import math

import jax
import jax.numpy as jnp
from jax import lax
from jax.experimental import pallas as pl
from jax.experimental.pallas import tpu as pltpu
from jax.sharding import PartitionSpec as P

F32, BF16 = jnp.float32, jnp.bfloat16
STEP, BLOCK = 256, 512
VMEM_LIMIT = 16 * 2**20
NN = (((1,), (0,)), ((), ()))
NT = (((1,), (1,)), ((), ()))

PLANES = (0, 1, 2, -1)


def depth_tap(source, target):
    tap = source - target + 1
    return tap if 0 <= tap <= 2 else None


def call(body, outs, ins, scratch=(), flops=0, name=None, smem=(), apart=(), far=(), alias=None):
    moved = sum(math.prod(s.shape) * s.dtype.itemsize for s in (*outs, *ins))
    return pl.pallas_call(
        body,
        out_shape=list(outs),
        in_specs=[
            pl.BlockSpec(
                memory_space=pltpu.SMEM if i in smem else pl.ANY if i in apart else pltpu.VMEM
            )
            for i in range(len(ins))
        ],
        out_specs=[
            pl.BlockSpec(memory_space=pl.ANY if i in far else pltpu.VMEM) for i in range(len(outs))
        ],
        input_output_aliases=alias or {},
        scratch_shapes=list(scratch),
        compiler_params=pltpu.CompilerParams(vmem_limit_bytes=VMEM_LIMIT),
        cost_estimate=pl.CostEstimate(flops=flops, bytes_accessed=moved, transcendentals=0),
        name=name,
    )(*ins)


def lanes_low(x):
    return lax.broadcasted_iota(jnp.int32, x.shape, 1) < 64


def swap(x):
    return pltpu.roll(x, 64, 1)


def pick(low, high):
    return jnp.where(lanes_low(low), low, high)


def fill_windows(windows, start, lane, chunk, columns, stride):
    size = chunk.shape[0]
    column = lax.broadcasted_iota(jnp.int32, chunk.shape, 0) % columns
    before = jnp.where(column == 0, 0.0, pltpu.roll(chunk, 1, 0))
    after = jnp.where(column == columns - 1, 0.0, pltpu.roll(chunk, size - 1, 0))
    at = pl.ds(pl.multiple_of(columns + start, 32), size)
    for tap, part in enumerate((before, chunk, after)):
        first = tap * stride + lane
        windows[at, first : first + chunk.shape[1]] = part.astype(BF16)


def clear_edges(windows, columns):
    rows, lanes = windows.shape
    windows[0:columns, :] = jnp.zeros((columns, lanes), BF16)
    windows[rows - columns : rows, :] = jnp.zeros((columns, lanes), BF16)


def row_windows(windows, start, columns, size=BLOCK):
    return [
        windows[start + tap * columns : start + tap * columns + size, :] for tap in range(3)
    ]


def window_dot(windows, weights, start, columns, dims, size=BLOCK):
    rows = jnp.concatenate(row_windows(windows, start, columns, size), axis=1)
    return lax.dot_general(rows, weights[...], dims, preferred_element_type=F32)


def row_blocks(first, last):
    blocks = [(start, BLOCK) for start in range(first, last - BLOCK, BLOCK)]
    return blocks + [(last - BLOCK, BLOCK // 2), (last - BLOCK // 2, BLOCK // 2)]


def packed(low, high):
    return pick(low, swap(high)), pick(swap(low), high)


def unpacked(first, second):
    return packed(first, second)


def by_side(odd, inner, outer):
    return jnp.where(odd, inner, outer), jnp.where(odd, outer, inner)


def pieces_of(source, target, sems, parts):
    size = target.shape[1] // parts
    return [
        pltpu.make_async_copy(
            source.at[:, pl.ds(i * size, size), :], target.at[:, pl.ds(i * size, size), :], sems.at[i]
        )
        for i in range(parts)
    ]


def pack_body(volume, own, held, sems):
    copies = pieces_of(volume, held, sems, sems.shape[0])
    size = own.shape[0] // len(copies)
    for copy in copies:
        copy.start()
    for i, copy in enumerate(copies):
        copy.wait()
        rows = slice(i * size, i * size + size)
        own[rows, :] = jnp.concatenate([held[0, rows, :], held[1, rows, :]], axis=1)


def leave_body(
    columns, me, far_cotangent, far_weight, own, inner, outer, turned,
    windows, taps, cotangent, weight, sems, sem,
):
    cells = own.shape[0]
    half = cells // 2
    odd = me[0] % 2 == 1
    fetch = pltpu.make_async_copy(far_weight, weight, sem)
    copies = pieces_of(far_cotangent, cotangent, sems, sems.shape[0])
    for copy in copies:
        copy.start()
    fetch.start()
    clear_edges(windows, columns)
    size = cells // len(copies)
    for at, copy in enumerate(copies):
        copy.wait()

        def fill(i, carry):
            start = pl.multiple_of(at * size + i * STEP, STEP)
            for plane in range(2):
                chunk = cotangent[plane, pl.ds(start, STEP), :].astype(F32)
                fill_windows(windows, start, plane * 128, chunk, columns, 256)
            return carry

        lax.fori_loop(0, size // STEP, fill, 0)
    fetch.wait()
    for row in range(3):
        for column in range(3):
            for source in range(2):
                first = row * 768 + column * 256 + source * 128
                for at, target in enumerate(PLANES):
                    depth = depth_tap(source, target)
                    taps[at * 64 : at * 64 + 64, first : first + 128] = (
                        jnp.zeros((64, 128), BF16)
                        if depth is None
                        else weight[(2 - depth) * 9 + (2 - row) * 3 + 2 - column]
                    )
    for start in range(0, half, BLOCK):
        sides = []
        for first in (start, start + half):
            term = window_dot(windows, taps, first, columns, NT)
            own[first : first + BLOCK, :] = term[:, :128]
            sides.append(term[:, 128:])
        upper, lower = packed(*sides)
        near = jnp.where(odd, lower, upper)
        head = near.astype(BF16)
        inner[start : start + BLOCK, :] = head
        inner[half + start : half + start + BLOCK, :] = (near - head.astype(F32)).astype(BF16)
        outer[start : start + BLOCK, :] = jnp.where(odd, upper, lower).astype(BF16)
    for plane in range(2):
        turn(cotangent.at[plane], turned, plane * 128)


def prepare_body(
    columns, me, own, inner, far_weight, own_windows, inner_windows, hidden, outer_taps,
    taps, weight, sem,
):
    fetch = pltpu.make_async_copy(far_weight, weight, sem)
    fetch.start()
    odd = me[0] % 2 == 1

    def fill(i, carry):
        start = pl.multiple_of(i * STEP, STEP)
        rows = pl.ds(start, STEP)
        fill_windows(own_windows, start, 0, own[rows, :].astype(F32), columns, 128)
        fill_windows(inner_windows, start, 0, inner[rows, :].astype(F32), columns, 128)
        return carry

    clear_edges(own_windows, columns)
    clear_edges(inner_windows, columns)
    lax.fori_loop(0, own.shape[0] // STEP, fill, 0)
    fetch.wait()
    zero = jnp.zeros((64, 64), BF16)
    for tap in range(9):

        def kernel_rows(source):
            depths = [depth_tap(source, target) for target in PLANES]
            parts = [zero if d is None else weight[d * 9 + tap] for d in depths]
            return jnp.concatenate(parts, axis=1)

        for at in range(2):
            rows = slice(tap * 128 + at * 64, tap * 128 + at * 64 + 64)
            taps[rows, :] = kernel_rows(at)
            upper, lower = kernel_rows(2 + at).astype(F32), kernel_rows(at - 2).astype(F32)
            first = 9 * 128 + rows.start
            taps[first : first + 64, :] = jnp.where(odd, lower, upper).astype(BF16)
            outer_taps[rows, :] = jnp.where(odd, upper, lower).astype(BF16)
    for start in range(0, own.shape[0], BLOCK):
        rows = row_windows(own_windows, start, columns) + row_windows(inner_windows, start, columns)
        hidden[start : start + BLOCK, :] = jnp.dot(
            jnp.concatenate(rows, axis=1), taps[...], preferred_element_type=F32
        )


def back_taps_body(weight, back_taps):
    zero = jnp.zeros((64, 64), BF16)
    for row in range(3):
        for column in range(3):
            tap = row * 3 + column
            for plane in range(2):
                depths = [depth_tap(source, plane) for source in PLANES]
                parts = [zero if d is None else weight[(2 - d) * 9 + 8 - tap] for d in depths]
                at = row * 128 + plane * 64
                for pair in range(2):
                    first = pair * 384 + column * 128
                    back_taps[at : at + 64, first : first + 128] = jnp.concatenate(
                        parts[2 * pair : 2 * pair + 2], axis=1
                    )


def hidden_body(
    columns, count, me, outer, part, outer_taps, inner_windows, act_windows, slope, side_windows,
    outer_windows,
):
    cells = outer.shape[0]

    def fill(i, carry):
        start = pl.multiple_of(i * STEP, STEP)
        chunk = outer[pl.ds(start, STEP), :].astype(F32)
        fill_windows(outer_windows, start, 0, chunk, columns, 128)
        return carry

    clear_edges(outer_windows, columns)
    clear_edges(act_windows, columns)
    lax.fori_loop(0, cells // STEP, fill, 0)
    from_inner = lax.broadcasted_iota(jnp.int32, (16, 128), 1) // 64 == me[0] % 2
    from_inner = jnp.where(from_inner, 1.0, 0.0).astype(BF16)[:1]
    for tap in range(3):
        at = slice(tap * 128, tap * 128 + 128)
        side_windows[:, at] = (
            inner_windows[:, at] * from_inner + outer_windows[:, at] * (1 - from_inner)
        )
    lanes = lax.broadcasted_iota(jnp.int32, (BLOCK, 128), 1)
    edges = [jnp.where(me[0] == end, 0.0, 1.0).astype(F32) for end in (count - 1, 0)]
    inside = jnp.where(lanes < 64, edges[0], edges[1])
    for start in range(0, cells, BLOCK):
        hidden = part[start : start + BLOCK, :]
        hidden = hidden + window_dot(outer_windows, outer_taps, start, columns, NN)
        gate = jax.nn.sigmoid(hidden)
        act = (hidden * gate).astype(BF16).astype(F32)
        fill_windows(act_windows, start, 0, act[:, :128], columns, 256)
        fill_windows(act_windows, start, 128, act[:, 128:] * inside, columns, 256)
        hidden, gate = hidden[:, :128], gate[:, :128]
        slope[start : start + BLOCK, :] = gate * (1.0 + hidden * (1.0 - gate))


def kernel_terms(columns, out_channels, slices, turned, terms):
    for row in range(3):
        for column in range(3):
            tap = row * 3 + column
            product = jnp.dot(turned[...], slices(row, column), preferred_element_type=F32)
            first, second = product[:out_channels], product[out_channels:]
            terms[:, tap * 128 : tap * 128 + 128] = first[:, :128] + swap(
                pick(second[:, 128:], second[:, :128])
            )
            group = 9 + tap // 2
            here = slice(group * 128, group * 128 + 128)
            if tap % 2 == 0:
                terms[:, here] = swap(first[:, 128:]) + second[:, :128]
            else:
                terms[:, here] = pick(terms[:, here], first[:, 128:] + swap(second[:, :128]))


def turn(source, target, first):
    for start in range(0, source.shape[0], STEP):
        chunk = source[start : start + STEP, :].astype(F32)
        target[first : first + chunk.shape[1], start : start + STEP] = chunk.T.astype(BF16)


def grad_two_body(columns, act_windows, turned, terms):
    cells = turned.shape[1]

    def slices(row, column):
        rows = slice(row * columns, row * columns + cells)
        return act_windows[rows, column * 256 : column * 256 + 256]

    kernel_terms(columns, 128, slices, turned, terms)


def coded(value, split):
    head = value.astype(BF16)
    if split == 0:
        return head
    rest = (value[:split] - head[:split].astype(F32)).astype(BF16)
    return jnp.concatenate([head, rest], axis=0)


def decoded(value, split):
    value = value.astype(F32)
    if split == 0:
        return value
    size = value.shape[0] - split
    parts = [value[:split] + value[size:]]
    if split < size:
        parts.append(value[split:size])
    return jnp.concatenate(parts, axis=0)


def grad_one_body(
    columns, count, me, own_windows, side_windows, act_terms, inner, outer, slope, other,
    grad, to_outer, message, kept, turned, terms,
):
    cells = grad.shape[0]
    odd = me[0] % 2 == 1
    before = message.shape[0] - cells // 2
    for start in range(0, cells // 2, STEP):
        low, high = slice(start, start + STEP), slice(start + cells // 2, start + cells // 2 + STEP)
        near = inner[low, :].astype(F32) + inner[high, :].astype(F32)
        arrived = unpacked(*by_side(odd, near, outer[low, :].astype(F32)))
        sides = []
        for rows, extra in zip((low, high), arrived):
            value = ((act_terms[rows, :] + extra) * slope[rows, :]).astype(BF16)
            grad[rows, :] = value
            value = value.astype(F32)
            turned[:, rows] = value.T.astype(BF16)
            sides.append(value)
        lower, upper = packed(*sides)
        message[before + start : before + start + STEP, :] = jnp.where(
            odd, lower, upper
        ).astype(BF16)
        to_outer[low, :] = jnp.where(odd, upper, lower).astype(BF16)
    def slices(row, column):
        rows = slice(row * columns, row * columns + cells)
        lanes = slice(column * 128, column * 128 + 128)
        return jnp.concatenate([own_windows[rows, lanes], side_windows[rows, lanes]], axis=1)

    kernel_terms(columns, 64, slices, turned, terms)
    half = terms.shape[1] // 2
    split = 2 * terms.shape[0] // count

    def share(owner):
        parts = []
        for source in (terms, other):
            each = source.shape[0] // count
            block = source[owner * each : owner * each + each, :]
            parts += [block[:, :half], block[:, half:]]
        return jnp.concatenate(parts, axis=0)

    groups = half // 128
    for pair in range(count // 2):
        even_share, odd_share = share(2 * pair), share(2 * pair + 1)
        kept[pair] = jnp.where(odd, odd_share, even_share)
        given = coded(jnp.where(odd, even_share, odd_share), split)
        size = given.shape[0]
        for group in range(groups):
            first = (pair * groups + group) * size
            message[first : first + size, :] = given[:, group * 128 : group * 128 + 128]


def halve_body(split_in, split_out, owner_bit, at_bit, me, mine, arrived, sent, kept):
    side = (me[0] >> owner_bit) % 2
    size, lanes = mine.shape[1:]
    groups = lanes // 128

    def total(at):
        if len(arrived.shape) == 3:
            return mine[at] + decoded(arrived[at], split_in)
        parts = []
        for group in range(groups):
            rows = size + split_in
            first = pl.multiple_of((at * groups + group) * rows, 8)
            parts.append(decoded(arrived[pl.ds(first, rows), :], split_in))
        return mine[at] + jnp.concatenate(parts, axis=1)

    for at in range(sent.shape[0]):
        high, low = at >> at_bit, at & ((1 << at_bit) - 1)
        keep = ((2 * high + side) << at_bit) + low
        give = ((2 * high + 1 - side) << at_bit) + low
        sent[at] = coded(total(give), split_out)
        kept[at] = total(keep)


def spread_body(split_in, owner_bits, me, mine, arrived, kept, *sent):
    place = 0
    for bit in owner_bits:
        place = 2 * place + (me[0] >> bit) % 2
    kept[...] = mine[place] + decoded(arrived[place], split_in)
    for at, out in enumerate(sent):
        there = place ^ (at + 1)
        out[...] = (mine[there] + decoded(arrived[there], split_in)).astype(BF16)


def finish_body(scale, sizes, mine, *refs):
    arrived, (grad_one, grad_two) = refs[:-2], refs[-2:]
    total = mine[...]
    for part in arrived:
        total = total + part[...].astype(F32)
    total = total * scale
    half = total.shape[1]
    first = 0
    for size, out in zip(sizes, (grad_one, grad_two)):
        blocks = (total[first : first + size], total[first + size : first + 2 * size])
        first += 2 * size
        for tap in range(9):
            for depth, group, side in ((0, 9 + tap // 2, tap % 2), (1, tap, 0), (2, tap, 1)):
                lane = group * 128 + side * 64
                block, lane = (blocks[0], lane) if lane < half else (blocks[1], lane - half)
                out[depth * 9 + tap] = block[:, lane : lane + 64]


def output_rows(columns, blocks, act_windows, taps, far, output, sems):
    copies = []
    for at, (start, size) in enumerate(blocks):
        value = window_dot(act_windows, taps, start, columns, NN, size)
        here = slice(start - blocks[0][0], start - blocks[0][0] + size)
        output[0, here, :] = value[:, :128]
        output[1, here, :] = value[:, 128:]
        copies.append(
            pltpu.make_async_copy(
                output.at[:, here, :], far.at[:, start : start + size, :], sems.at[at]
            )
        )
        copies[-1].start()
    return copies


def output_first_body(
    columns, blocks, act_windows, weight, grad, far, taps, own_windows, output, sems
):
    for row in range(3):
        for column in range(3):
            for at, source in enumerate(PLANES):
                first = row * 768 + column * 256 + at * 64
                for plane in range(2):
                    depth = depth_tap(source, plane)
                    taps[first : first + 64, plane * 128 : plane * 128 + 128] = (
                        jnp.zeros((64, 128), BF16)
                        if depth is None
                        else weight[depth * 9 + row * 3 + column]
                    )
    copies = output_rows(columns, blocks, act_windows, taps, far, output, sems)

    def fill(i, carry):
        start = pl.multiple_of(i * STEP, STEP)
        chunk = grad[pl.ds(start, STEP), :].astype(F32)
        fill_windows(own_windows, start, 0, chunk, columns, 128)
        return carry

    clear_edges(own_windows, columns)
    lax.fori_loop(0, grad.shape[0] // STEP, fill, 0)
    for copy in copies:
        copy.wait()


def output_rest_body(columns, blocks, act_windows, taps, begun, far, output, sems):
    for copy in output_rows(columns, blocks, act_windows, taps, far, output, sems):
        copy.wait()


def grad_windows_body(columns, me, message, outer, windows):
    half = outer.shape[0]
    odd = me[0] % 2 == 1
    before = message.shape[0] - half

    def fill(i, carry):
        start = pl.multiple_of(i * STEP, STEP)
        near = message[pl.ds(before + start, STEP), :].astype(F32)
        below, above = by_side(odd, near, outer[pl.ds(start, STEP), :].astype(F32))
        for first, side in zip((start, start + half), unpacked(above, below)):
            fill_windows(windows, first, 0, side, columns, 128)
        return carry

    clear_edges(windows, columns)
    lax.fori_loop(0, half // STEP, fill, 0)


def grad_volume_body(columns, own_windows, side_windows, taps, far, output, sems):
    copies = []
    for at, (start, size) in enumerate(row_blocks(0, output.shape[1])):
        rows = slice(start, start + size + 2 * columns)
        rows = jnp.concatenate([own_windows[rows, :], side_windows[rows, :]], axis=1)
        terms = lax.dot_general(rows, taps[...], NT, preferred_element_type=F32)
        value = terms[:size, :128]
        value = value + terms[columns : columns + size, 128:256]
        value = value + terms[2 * columns : 2 * columns + size, 256:]
        here = slice(start, start + size)
        output[0, here, :] = value[:, :64]
        output[1, here, :] = value[:, 64:]
        copies.append(
            pltpu.make_async_copy(output.at[:, here, :], far.at[:, here, :], sems.at[at])
        )
        copies[-1].start()
    for copy in copies:
        copy.wait()


def shards(volume, weight_one, weight_two, cotangent):
    count = lax.axis_size("space")
    planes, rows, columns, channels = volume.shape
    cells = rows * columns
    scale = 1.0 / math.sqrt(planes * count * cells)
    mid, wide = weight_two.shape[3], weight_two.shape[4]
    me = lax.axis_index("space").astype(jnp.int32).reshape(1)
    shape = jax.ShapeDtypeStruct
    flat, pack = shape((cells, 128), BF16), shape((cells // 2, 128), BF16)
    slab = (cells + 2 * columns, 768)
    windows = pltpu.VMEM(slab, BF16)
    lanes = 14 * 64
    split = 2 * mid // count
    chunk = 2 * (mid + wide) // count

    within = [(i, i ^ 1) for i in range(count)]
    across = [(i, i + 1) for i in range(1, count - 1, 2)]
    across += [(j, i) for i, j in across]

    volume = volume.reshape(planes, cells, channels)
    cotangent = cotangent.reshape(planes, cells, wide)
    weight_one = weight_one.reshape(27, channels, mid)
    weight_two = weight_two.reshape(27, mid, wide)
    one_flops = 2 * planes * cells * 27 * channels * mid
    two_flops = 2 * planes * cells * 27 * mid * wide

    dma = pltpu.SemaphoreType.DMA
    far_one, far_two, far_volume, far_cotangent = (
        pltpu.with_memory_space_constraint(x, pltpu.HBM)
        for x in (weight_one, weight_two, volume, cotangent)
    )
    own, = call(
        pack_body, (flat,), (far_volume,),
        (pltpu.VMEM((planes, cells, channels), BF16), dma((4,))),
        name="pack_volume", apart=(0,),
    )
    vol_outer = lax.ppermute(own, "space", across)
    vol_inner = lax.ppermute(own, "space", within)
    terms, inner, outer, turned = call(
        functools.partial(leave_body, columns),
        (
            shape((cells, 128), F32), flat, pack, shape((256, cells), BF16),
        ),
        (me, far_cotangent, far_two),
        (
            windows, pltpu.VMEM((256, 3 * 768), BF16), pltpu.VMEM(cotangent.shape, BF16),
            pltpu.VMEM(weight_two.shape, BF16), dma((4,)), dma,
        ),
        two_flops, "grad_act_terms", (0,), (1, 2),
    )
    own, terms = lax.optimization_barrier((own, terms))
    third = shape((slab[0], 384), BF16)
    own_windows, inner_windows, part, outer_taps = call(
        functools.partial(prepare_body, columns),
        (third, third, shape((cells, 256), F32), shape((9 * 128, 256), BF16)),
        (me, own, vol_inner, far_one),
        (pltpu.VMEM((2 * 9 * 128, 256), BF16), pltpu.VMEM(weight_one.shape, BF16), dma),
        one_flops, "prepare", (0,), (3,),
    )
    back_taps, = call(
        back_taps_body, (shape((3 * 128, 768), BF16),), (weight_one,), (), one_flops // 8, "back_taps"
    )
    inner, outer, part, back_taps = lax.optimization_barrier((inner, outer, part, back_taps))
    terms_outer = lax.ppermute(outer, "space", across)
    terms_inner = lax.ppermute(inner, "space", within)
    act_windows, slope, side_windows = call(
        functools.partial(hidden_body, columns, count),
        (shape(slab, BF16), shape((cells, 128), F32), third),
        (me, vol_outer, part, outer_taps, inner_windows),
        (pltpu.VMEM((slab[0], 384), BF16),), 2 * one_flops, "hidden", (0,),
    )
    terms_two, = call(
        functools.partial(grad_two_body, columns),
        (shape((wide, 2 * lanes), F32),),
        (act_windows, turned), (), two_flops, "grad_two_terms",
    )
    groups = lanes // 128
    grad_hidden, outer, message, kept = call(
        functools.partial(grad_one_body, columns, count),
        (
            flat, pack,
            shape((count // 2 * groups * (chunk + split) + cells // 2, 128), BF16),
            shape((count // 2, chunk, lanes), F32),
        ),
        (
            me, own_windows, side_windows, terms, terms_inner, terms_outer, slope, terms_two,
        ),
        (pltpu.VMEM((128, cells), BF16), pltpu.VMEM((mid, 2 * lanes), F32)),
        one_flops, "grad_one_terms", (0,),
    )
    message = lax.ppermute(message, "space", within)
    rest = row_blocks(BLOCK, cells)
    output, out_taps, back_windows = call(
        functools.partial(output_first_body, columns, [(0, BLOCK)]),
        (shape((planes, cells, wide), F32), shape((9 * 256, 256), BF16), third),
        (act_windows, weight_two, grad_hidden),
        (pltpu.VMEM((planes, BLOCK, wide), F32), dma((1,))),
        two_flops, "output_first", (), (), (0,),
    )
    message, output, out_taps, back_windows = lax.optimization_barrier(
        (message, output, out_taps, back_windows)
    )
    def halve(bits, bit, split_in, split_out, kept, arrived):
        left = 2 ** (len(bits) - 1)
        sent, kept = call(
            functools.partial(halve_body, split_in, split_out, bit, bits[::-1].index(bit)),
            (shape((left, chunk + split_out, lanes), BF16), shape((left, chunk, lanes), F32)),
            (me, kept, arrived), name="halve", smem=(0,),
        )
        return [b for b in bits if b != bit], sent, kept

    bits = list(range(count.bit_length() - 2, 0, -1))
    bits, sent, kept = halve(bits, 2, split, 0, kept, message)
    sent, act_windows, outer = lax.optimization_barrier((sent, act_windows, outer))
    arrived = lax.ppermute(sent, "space", [(i, i ^ 4) for i in range(count)])
    grad_outer = lax.ppermute(outer, "space", across)
    output, = call(
        functools.partial(output_rest_body, columns, rest),
        (shape((planes, cells, wide), F32),),
        (act_windows, out_taps, output),
        (pltpu.VMEM((planes, cells - BLOCK, wide), F32), dma((len(rest),))),
        two_flops, "output_rest", (), (2,), (0,), {2: 0},
    )
    others = 2 ** len(bits) - 1
    mine, *sent = call(
        functools.partial(spread_body, 0, bits),
        (shape((chunk, lanes), F32), *[shape((chunk, lanes), BF16)] * others),
        (me, kept, arrived), flops=one_flops, name="spread", smem=(0,),
    )
    sent, output, back_windows = lax.optimization_barrier((sent, output, back_windows))
    arrived = []
    for at, part in enumerate(sent):
        away = sum(((at + 1) >> i & 1) << bit for i, bit in enumerate(bits[::-1]))
        arrived.append(lax.ppermute(part, "space", [(i, i ^ away) for i in range(count)]))
    grad_windows, = call(
        functools.partial(grad_windows_body, columns), (third,), (me, message, grad_outer),
        (), one_flops // 4, "grad_windows", (0,),
    )
    grad_volume, = call(
        functools.partial(grad_volume_body, columns),
        (shape((planes, cells, channels), F32),),
        (back_windows, grad_windows, back_taps),
        (pltpu.VMEM((planes, cells, channels), F32), dma((cells // BLOCK + 1,))),
        one_flops, "grad_volume", (), (), (0,),
    )
    mine, grad_volume = lax.optimization_barrier((mine, grad_volume))
    grad_one, grad_two = call(
        functools.partial(finish_body, scale, (mid // count, wide // count)),
        (shape((27, mid // count, channels), F32), shape((27, wide // count, mid), F32)),
        (mine, *arrived), name="finish",
    )
    return (
        output.reshape(planes, rows, columns, wide),
        grad_volume.reshape(planes, rows, columns, channels),
        jnp.swapaxes(grad_one, 1, 2).reshape(3, 3, 3, channels, mid // count),
        jnp.swapaxes(grad_two, 1, 2).reshape(3, 3, 3, mid, wide // count),
    )


def solution(mesh):
    cells = P(("groups", "space"), None, None, None)
    kernel = P("groups", None, None, None, "space")
    return jax.shard_map(
        shards,
        mesh=mesh,
        in_specs=(cells, P(), P(), cells),
        out_specs=(cells, cells, kernel, kernel),
        check_vma=False,
    )
```

```python
import functools
import math

import jax
import jax.numpy as jnp
from jax import lax
from jax.experimental import pallas as pl
from jax.experimental.pallas import tpu as pltpu
from jax.sharding import PartitionSpec as P

F32, BF16 = jnp.float32, jnp.bfloat16
STEP, BLOCK = 256, 512
VMEM_LIMIT = 16 * 2**20
NN = (((1,), (0,)), ((), ()))
NT = (((1,), (1,)), ((), ()))

PLANES = (0, 1, 2, -1)


def depth_tap(source, target):
    tap = source - target + 1
    return tap if 0 <= tap <= 2 else None


def call(body, outs, ins, scratch=(), flops=0, name=None, smem=(), apart=(), far=(), alias=None):
    moved = sum(math.prod(s.shape) * s.dtype.itemsize for s in (*outs, *ins))
    return pl.pallas_call(
        body,
        out_shape=list(outs),
        in_specs=[
            pl.BlockSpec(
                memory_space=pltpu.SMEM if i in smem else pl.ANY if i in apart else pltpu.VMEM
            )
            for i in range(len(ins))
        ],
        out_specs=[
            pl.BlockSpec(memory_space=pl.ANY if i in far else pltpu.VMEM) for i in range(len(outs))
        ],
        input_output_aliases=alias or {},
        scratch_shapes=list(scratch),
        compiler_params=pltpu.CompilerParams(vmem_limit_bytes=VMEM_LIMIT),
        cost_estimate=pl.CostEstimate(flops=flops, bytes_accessed=moved, transcendentals=0),
        name=name,
    )(*ins)


def lanes_low(x):
    return lax.broadcasted_iota(jnp.int32, x.shape, 1) < 64


def swap(x):
    return pltpu.roll(x, 64, 1)


def pick(low, high):
    return jnp.where(lanes_low(low), low, high)


def fill_windows(windows, start, lane, chunk, columns, stride):
    size = chunk.shape[0]
    column = lax.broadcasted_iota(jnp.int32, chunk.shape, 0) % columns
    before = jnp.where(column == 0, 0.0, pltpu.roll(chunk, 1, 0))
    after = jnp.where(column == columns - 1, 0.0, pltpu.roll(chunk, size - 1, 0))
    at = pl.ds(pl.multiple_of(columns + start, 32), size)
    for tap, part in enumerate((before, chunk, after)):
        first = tap * stride + lane
        windows[at, first : first + chunk.shape[1]] = part.astype(BF16)


def clear_edges(windows, columns):
    rows, lanes = windows.shape
    windows[0:columns, :] = jnp.zeros((columns, lanes), BF16)
    windows[rows - columns : rows, :] = jnp.zeros((columns, lanes), BF16)


def row_windows(windows, start, columns, size=BLOCK):
    return [
        windows[start + tap * columns : start + tap * columns + size, :] for tap in range(3)
    ]


def window_dot(windows, weights, start, columns, dims, size=BLOCK):
    rows = jnp.concatenate(row_windows(windows, start, columns, size), axis=1)
    return lax.dot_general(rows, weights[...], dims, preferred_element_type=F32)


def row_blocks(first, last):
    blocks = [(start, BLOCK) for start in range(first, last - BLOCK, BLOCK)]
    return blocks + [(last - BLOCK, BLOCK // 2), (last - BLOCK // 2, BLOCK // 2)]


def packed(low, high):
    return pick(low, swap(high)), pick(swap(low), high)


def unpacked(first, second):
    return packed(first, second)


def by_side(odd, inner, outer):
    return jnp.where(odd, inner, outer), jnp.where(odd, outer, inner)


def pieces_of(source, target, sems, parts):
    size = target.shape[1] // parts
    return [
        pltpu.make_async_copy(
            source.at[:, pl.ds(i * size, size), :], target.at[:, pl.ds(i * size, size), :], sems.at[i]
        )
        for i in range(parts)
    ]


def pack_body(volume, own, held, sems):
    copies = pieces_of(volume, held, sems, sems.shape[0])
    size = own.shape[0] // len(copies)
    for copy in copies:
        copy.start()
    for i, copy in enumerate(copies):
        copy.wait()
        rows = slice(i * size, i * size + size)
        own[rows, :] = jnp.concatenate([held[0, rows, :], held[1, rows, :]], axis=1)


def leave_body(
    columns, me, far_cotangent, far_weight, own, inner, outer, turned,
    windows, taps, cotangent, weight, sems, sem,
):
    cells = own.shape[0]
    half = cells // 2
    odd = me[0] % 2 == 1
    fetch = pltpu.make_async_copy(far_weight, weight, sem)
    copies = pieces_of(far_cotangent, cotangent, sems, sems.shape[0])
    for copy in copies:
        copy.start()
    fetch.start()
    clear_edges(windows, columns)
    size = cells // len(copies)
    for at, copy in enumerate(copies):
        copy.wait()

        def fill(i, carry):
            start = pl.multiple_of(at * size + i * STEP, STEP)
            for plane in range(2):
                chunk = cotangent[plane, pl.ds(start, STEP), :].astype(F32)
                fill_windows(windows, start, plane * 128, chunk, columns, 256)
            return carry

        lax.fori_loop(0, size // STEP, fill, 0)
    fetch.wait()
    for row in range(3):
        for column in range(3):
            for source in range(2):
                first = row * 768 + column * 256 + source * 128
                for at, target in enumerate(PLANES):
                    depth = depth_tap(source, target)
                    taps[at * 64 : at * 64 + 64, first : first + 128] = (
                        jnp.zeros((64, 128), BF16)
                        if depth is None
                        else weight[(2 - depth) * 9 + (2 - row) * 3 + 2 - column]
                    )
    for start in range(0, half, BLOCK):
        sides = []
        for first in (start, start + half):
            term = window_dot(windows, taps, first, columns, NT)
            own[first : first + BLOCK, :] = term[:, :128]
            sides.append(term[:, 128:])
        upper, lower = packed(*sides)
        near = jnp.where(odd, lower, upper)
        head = near.astype(BF16)
        inner[start : start + BLOCK, :] = head
        inner[half + start : half + start + BLOCK, :] = (near - head.astype(F32)).astype(BF16)
        outer[start : start + BLOCK, :] = jnp.where(odd, upper, lower).astype(BF16)
    for plane in range(2):
        turn(cotangent.at[plane], turned, plane * 128)


def prepare_body(
    columns, me, own, inner, far_weight, own_windows, inner_windows, hidden, outer_taps,
    taps, weight, sem,
):
    fetch = pltpu.make_async_copy(far_weight, weight, sem)
    fetch.start()
    odd = me[0] % 2 == 1

    def fill(i, carry):
        start = pl.multiple_of(i * STEP, STEP)
        rows = pl.ds(start, STEP)
        fill_windows(own_windows, start, 0, own[rows, :].astype(F32), columns, 128)
        fill_windows(inner_windows, start, 0, inner[rows, :].astype(F32), columns, 128)
        return carry

    clear_edges(own_windows, columns)
    clear_edges(inner_windows, columns)
    lax.fori_loop(0, own.shape[0] // STEP, fill, 0)
    fetch.wait()
    zero = jnp.zeros((64, 64), BF16)
    for tap in range(9):

        def kernel_rows(source):
            depths = [depth_tap(source, target) for target in PLANES]
            parts = [zero if d is None else weight[d * 9 + tap] for d in depths]
            return jnp.concatenate(parts, axis=1)

        for at in range(2):
            rows = slice(tap * 128 + at * 64, tap * 128 + at * 64 + 64)
            taps[rows, :] = kernel_rows(at)
            upper, lower = kernel_rows(2 + at).astype(F32), kernel_rows(at - 2).astype(F32)
            first = 9 * 128 + rows.start
            taps[first : first + 64, :] = jnp.where(odd, lower, upper).astype(BF16)
            outer_taps[rows, :] = jnp.where(odd, upper, lower).astype(BF16)
    for start in range(0, own.shape[0], BLOCK):
        rows = row_windows(own_windows, start, columns) + row_windows(inner_windows, start, columns)
        hidden[start : start + BLOCK, :] = jnp.dot(
            jnp.concatenate(rows, axis=1), taps[...], preferred_element_type=F32
        )


def back_taps_body(weight, back_taps):
    zero = jnp.zeros((64, 64), BF16)
    for row in range(3):
        for column in range(3):
            tap = row * 3 + column
            for plane in range(2):
                depths = [depth_tap(source, plane) for source in PLANES]
                parts = [zero if d is None else weight[(2 - d) * 9 + 8 - tap] for d in depths]
                at = row * 128 + plane * 64
                for pair in range(2):
                    first = pair * 384 + column * 128
                    back_taps[at : at + 64, first : first + 128] = jnp.concatenate(
                        parts[2 * pair : 2 * pair + 2], axis=1
                    )


def hidden_body(
    columns, count, me, outer, part, outer_taps, inner_windows, act_windows, slope, side_windows,
    outer_windows,
):
    cells = outer.shape[0]

    def fill(i, carry):
        start = pl.multiple_of(i * STEP, STEP)
        chunk = outer[pl.ds(start, STEP), :].astype(F32)
        fill_windows(outer_windows, start, 0, chunk, columns, 128)
        return carry

    clear_edges(outer_windows, columns)
    clear_edges(act_windows, columns)
    lax.fori_loop(0, cells // STEP, fill, 0)
    from_inner = lax.broadcasted_iota(jnp.int32, (16, 128), 1) // 64 == me[0] % 2
    from_inner = jnp.where(from_inner, 1.0, 0.0).astype(BF16)[:1]
    for tap in range(3):
        at = slice(tap * 128, tap * 128 + 128)
        side_windows[:, at] = (
            inner_windows[:, at] * from_inner + outer_windows[:, at] * (1 - from_inner)
        )
    lanes = lax.broadcasted_iota(jnp.int32, (BLOCK, 128), 1)
    edges = [jnp.where(me[0] == end, 0.0, 1.0).astype(F32) for end in (count - 1, 0)]
    inside = jnp.where(lanes < 64, edges[0], edges[1])
    for start in range(0, cells, BLOCK):
        hidden = part[start : start + BLOCK, :]
        hidden = hidden + window_dot(outer_windows, outer_taps, start, columns, NN)
        gate = jax.nn.sigmoid(hidden)
        act = (hidden * gate).astype(BF16).astype(F32)
        fill_windows(act_windows, start, 0, act[:, :128], columns, 256)
        fill_windows(act_windows, start, 128, act[:, 128:] * inside, columns, 256)
        hidden, gate = hidden[:, :128], gate[:, :128]
        slope[start : start + BLOCK, :] = gate * (1.0 + hidden * (1.0 - gate))


def kernel_terms(columns, out_channels, slices, turned, terms):
    for row in range(3):
        for column in range(3):
            tap = row * 3 + column
            product = jnp.dot(turned[...], slices(row, column), preferred_element_type=F32)
            first, second = product[:out_channels], product[out_channels:]
            terms[:, tap * 128 : tap * 128 + 128] = first[:, :128] + swap(
                pick(second[:, 128:], second[:, :128])
            )
            group = 9 + tap // 2
            here = slice(group * 128, group * 128 + 128)
            if tap % 2 == 0:
                terms[:, here] = swap(first[:, 128:]) + second[:, :128]
            else:
                terms[:, here] = pick(terms[:, here], first[:, 128:] + swap(second[:, :128]))


def turn(source, target, first):
    for start in range(0, source.shape[0], STEP):
        chunk = source[start : start + STEP, :].astype(F32)
        target[first : first + chunk.shape[1], start : start + STEP] = chunk.T.astype(BF16)


def grad_two_body(columns, act_windows, turned, terms):
    cells = turned.shape[1]

    def slices(row, column):
        rows = slice(row * columns, row * columns + cells)
        return act_windows[rows, column * 256 : column * 256 + 256]

    kernel_terms(columns, 128, slices, turned, terms)


def coded(value, split):
    head = value.astype(BF16)
    if split == 0:
        return head
    rest = (value[:split] - head[:split].astype(F32)).astype(BF16)
    return jnp.concatenate([head, rest], axis=0)


def decoded(value, split):
    value = value.astype(F32)
    if split == 0:
        return value
    size = value.shape[0] - split
    parts = [value[:split] + value[size:]]
    if split < size:
        parts.append(value[split:size])
    return jnp.concatenate(parts, axis=0)


def grad_one_body(
    columns, count, me, own_windows, side_windows, act_terms, inner, outer, slope, other,
    grad, to_outer, message, kept, turned, terms,
):
    cells = grad.shape[0]
    odd = me[0] % 2 == 1
    before = message.shape[0] - cells // 2
    for start in range(0, cells // 2, STEP):
        low, high = slice(start, start + STEP), slice(start + cells // 2, start + cells // 2 + STEP)
        near = inner[low, :].astype(F32) + inner[high, :].astype(F32)
        arrived = unpacked(*by_side(odd, near, outer[low, :].astype(F32)))
        sides = []
        for rows, extra in zip((low, high), arrived):
            value = ((act_terms[rows, :] + extra) * slope[rows, :]).astype(BF16)
            grad[rows, :] = value
            value = value.astype(F32)
            turned[:, rows] = value.T.astype(BF16)
            sides.append(value)
        lower, upper = packed(*sides)
        message[before + start : before + start + STEP, :] = jnp.where(
            odd, lower, upper
        ).astype(BF16)
        to_outer[low, :] = jnp.where(odd, upper, lower).astype(BF16)
    def slices(row, column):
        rows = slice(row * columns, row * columns + cells)
        lanes = slice(column * 128, column * 128 + 128)
        return jnp.concatenate([own_windows[rows, lanes], side_windows[rows, lanes]], axis=1)

    kernel_terms(columns, 64, slices, turned, terms)
    half = terms.shape[1] // 2
    split = 2 * terms.shape[0] // count

    def share(owner):
        parts = []
        for source in (terms, other):
            each = source.shape[0] // count
            block = source[owner * each : owner * each + each, :]
            parts += [block[:, :half], block[:, half:]]
        return jnp.concatenate(parts, axis=0)

    groups = half // 128
    for pair in range(count // 2):
        even_share, odd_share = share(2 * pair), share(2 * pair + 1)
        kept[pair] = jnp.where(odd, odd_share, even_share)
        given = coded(jnp.where(odd, even_share, odd_share), split)
        size = given.shape[0]
        for group in range(groups):
            first = (pair * groups + group) * size
            message[first : first + size, :] = given[:, group * 128 : group * 128 + 128]


def halve_body(split_in, split_out, owner_bit, at_bit, me, mine, arrived, sent, kept):
    side = (me[0] >> owner_bit) % 2
    size, lanes = mine.shape[1:]
    groups = lanes // 128

    def total(at):
        if len(arrived.shape) == 3:
            return mine[at] + decoded(arrived[at], split_in)
        parts = []
        for group in range(groups):
            rows = size + split_in
            first = pl.multiple_of((at * groups + group) * rows, 8)
            parts.append(decoded(arrived[pl.ds(first, rows), :], split_in))
        return mine[at] + jnp.concatenate(parts, axis=1)

    for at in range(sent.shape[0]):
        high, low = at >> at_bit, at & ((1 << at_bit) - 1)
        keep = ((2 * high + side) << at_bit) + low
        give = ((2 * high + 1 - side) << at_bit) + low
        sent[at] = coded(total(give), split_out)
        kept[at] = total(keep)


def spread_body(split_in, owner_bits, me, mine, arrived, kept, *sent):
    place = 0
    for bit in owner_bits:
        place = 2 * place + (me[0] >> bit) % 2
    kept[...] = mine[place] + decoded(arrived[place], split_in)
    for at, out in enumerate(sent):
        there = place ^ (at + 1)
        out[...] = (mine[there] + decoded(arrived[there], split_in)).astype(BF16)


def finish_body(scale, sizes, mine, *refs):
    arrived, (grad_one, grad_two) = refs[:-2], refs[-2:]
    total = mine[...]
    for part in arrived:
        total = total + part[...].astype(F32)
    total = total * scale
    half = total.shape[1]
    first = 0
    for size, out in zip(sizes, (grad_one, grad_two)):
        blocks = (total[first : first + size], total[first + size : first + 2 * size])
        first += 2 * size
        for tap in range(9):
            for depth, group, side in ((0, 9 + tap // 2, tap % 2), (1, tap, 0), (2, tap, 1)):
                lane = group * 128 + side * 64
                block, lane = (blocks[0], lane) if lane < half else (blocks[1], lane - half)
                out[depth * 9 + tap] = block[:, lane : lane + 64]


def output_rows(columns, blocks, act_windows, taps, far, output, sems):
    copies = []
    for at, (start, size) in enumerate(blocks):
        value = window_dot(act_windows, taps, start, columns, NN, size)
        here = slice(start - blocks[0][0], start - blocks[0][0] + size)
        output[0, here, :] = value[:, :128]
        output[1, here, :] = value[:, 128:]
        copies.append(
            pltpu.make_async_copy(
                output.at[:, here, :], far.at[:, start : start + size, :], sems.at[at]
            )
        )
        copies[-1].start()
    return copies


def output_first_body(
    columns, blocks, act_windows, weight, grad, far, taps, own_windows, output, sems
):
    for row in range(3):
        for column in range(3):
            for at, source in enumerate(PLANES):
                first = row * 768 + column * 256 + at * 64
                for plane in range(2):
                    depth = depth_tap(source, plane)
                    taps[first : first + 64, plane * 128 : plane * 128 + 128] = (
                        jnp.zeros((64, 128), BF16)
                        if depth is None
                        else weight[depth * 9 + row * 3 + column]
                    )
    copies = output_rows(columns, blocks, act_windows, taps, far, output, sems)

    def fill(i, carry):
        start = pl.multiple_of(i * STEP, STEP)
        chunk = grad[pl.ds(start, STEP), :].astype(F32)
        fill_windows(own_windows, start, 0, chunk, columns, 128)
        return carry

    clear_edges(own_windows, columns)
    lax.fori_loop(0, grad.shape[0] // STEP, fill, 0)
    for copy in copies:
        copy.wait()


def output_rest_body(columns, blocks, act_windows, taps, begun, far, output, sems):
    for copy in output_rows(columns, blocks, act_windows, taps, far, output, sems):
        copy.wait()


def grad_windows_body(columns, me, message, outer, windows):
    half = outer.shape[0]
    odd = me[0] % 2 == 1
    before = message.shape[0] - half

    def fill(i, carry):
        start = pl.multiple_of(i * STEP, STEP)
        near = message[pl.ds(before + start, STEP), :].astype(F32)
        below, above = by_side(odd, near, outer[pl.ds(start, STEP), :].astype(F32))
        for first, side in zip((start, start + half), unpacked(above, below)):
            fill_windows(windows, first, 0, side, columns, 128)
        return carry

    clear_edges(windows, columns)
    lax.fori_loop(0, half // STEP, fill, 0)


def grad_volume_body(columns, own_windows, side_windows, taps, far, output, sems):
    copies = []
    for at, (start, size) in enumerate(row_blocks(0, output.shape[1])):
        rows = slice(start, start + size + 2 * columns)
        rows = jnp.concatenate([own_windows[rows, :], side_windows[rows, :]], axis=1)
        terms = lax.dot_general(rows, taps[...], NT, preferred_element_type=F32)
        value = terms[:size, :128]
        value = value + terms[columns : columns + size, 128:256]
        value = value + terms[2 * columns : 2 * columns + size, 256:]
        here = slice(start, start + size)
        output[0, here, :] = value[:, :64]
        output[1, here, :] = value[:, 64:]
        copies.append(
            pltpu.make_async_copy(output.at[:, here, :], far.at[:, here, :], sems.at[at])
        )
        copies[-1].start()
    for copy in copies:
        copy.wait()


def shards(volume, weight_one, weight_two, cotangent):
    count = lax.axis_size("space")
    planes, rows, columns, channels = volume.shape
    cells = rows * columns
    scale = 1.0 / math.sqrt(planes * count * cells)
    mid, wide = weight_two.shape[3], weight_two.shape[4]
    me = lax.axis_index("space").astype(jnp.int32).reshape(1)
    shape = jax.ShapeDtypeStruct
    flat, pack = shape((cells, 128), BF16), shape((cells // 2, 128), BF16)
    slab = (cells + 2 * columns, 768)
    windows = pltpu.VMEM(slab, BF16)
    lanes = 14 * 64
    split = 2 * mid // count
    chunk = 2 * (mid + wide) // count

    within = [(i, i ^ 1) for i in range(count)]
    across = [(i, i + 1) for i in range(1, count - 1, 2)]
    across += [(j, i) for i, j in across]

    volume = volume.reshape(planes, cells, channels)
    cotangent = cotangent.reshape(planes, cells, wide)
    weight_one = weight_one.reshape(27, channels, mid)
    weight_two = weight_two.reshape(27, mid, wide)
    one_flops = 2 * planes * cells * 27 * channels * mid
    two_flops = 2 * planes * cells * 27 * mid * wide

    dma = pltpu.SemaphoreType.DMA
    far_one, far_two, far_volume, far_cotangent = (
        pltpu.with_memory_space_constraint(x, pltpu.HBM)
        for x in (weight_one, weight_two, volume, cotangent)
    )
    own, = call(
        pack_body, (flat,), (far_volume,),
        (pltpu.VMEM((planes, cells, channels), BF16), dma((4,))),
        name="pack_volume", apart=(0,),
    )
    vol_outer = lax.ppermute(own, "space", across)
    vol_inner = lax.ppermute(own, "space", within)
    terms, inner, outer, turned = call(
        functools.partial(leave_body, columns),
        (
            shape((cells, 128), F32), flat, pack, shape((256, cells), BF16),
        ),
        (me, far_cotangent, far_two),
        (
            windows, pltpu.VMEM((256, 3 * 768), BF16), pltpu.VMEM(cotangent.shape, BF16),
            pltpu.VMEM(weight_two.shape, BF16), dma((4,)), dma,
        ),
        two_flops, "grad_act_terms", (0,), (1, 2),
    )
    own, terms = lax.optimization_barrier((own, terms))
    third = shape((slab[0], 384), BF16)
    own_windows, inner_windows, part, outer_taps = call(
        functools.partial(prepare_body, columns),
        (third, third, shape((cells, 256), F32), shape((9 * 128, 256), BF16)),
        (me, own, vol_inner, far_one),
        (pltpu.VMEM((2 * 9 * 128, 256), BF16), pltpu.VMEM(weight_one.shape, BF16), dma),
        one_flops, "prepare", (0,), (3,),
    )
    back_taps, = call(
        back_taps_body, (shape((3 * 128, 768), BF16),), (weight_one,), (), one_flops // 8, "back_taps"
    )
    inner, outer, part, back_taps = lax.optimization_barrier((inner, outer, part, back_taps))
    terms_outer = lax.ppermute(outer, "space", across)
    terms_inner = lax.ppermute(inner, "space", within)
    act_windows, slope, side_windows = call(
        functools.partial(hidden_body, columns, count),
        (shape(slab, BF16), shape((cells, 128), F32), third),
        (me, vol_outer, part, outer_taps, inner_windows),
        (pltpu.VMEM((slab[0], 384), BF16),), 2 * one_flops, "hidden", (0,),
    )
    terms_two, = call(
        functools.partial(grad_two_body, columns),
        (shape((wide, 2 * lanes), F32),),
        (act_windows, turned), (), two_flops, "grad_two_terms",
    )
    groups = lanes // 128
    grad_hidden, outer, message, kept = call(
        functools.partial(grad_one_body, columns, count),
        (
            flat, pack,
            shape((count // 2 * groups * (chunk + split) + cells // 2, 128), BF16),
            shape((count // 2, chunk, lanes), F32),
        ),
        (
            me, own_windows, side_windows, terms, terms_inner, terms_outer, slope, terms_two,
        ),
        (pltpu.VMEM((128, cells), BF16), pltpu.VMEM((mid, 2 * lanes), F32)),
        one_flops, "grad_one_terms", (0,),
    )
    message = lax.ppermute(message, "space", within)
    rest = row_blocks(BLOCK, cells)
    output, out_taps, back_windows = call(
        functools.partial(output_first_body, columns, [(0, BLOCK)]),
        (shape((planes, cells, wide), F32), shape((9 * 256, 256), BF16), third),
        (act_windows, weight_two, grad_hidden),
        (pltpu.VMEM((planes, BLOCK, wide), F32), dma((1,))),
        two_flops, "output_first", (), (), (0,),
    )
    message, output, out_taps, back_windows = lax.optimization_barrier(
        (message, output, out_taps, back_windows)
    )
    def halve(bits, bit, split_in, split_out, kept, arrived):
        left = 2 ** (len(bits) - 1)
        sent, kept = call(
            functools.partial(halve_body, split_in, split_out, bit, bits[::-1].index(bit)),
            (shape((left, chunk + split_out, lanes), BF16), shape((left, chunk, lanes), F32)),
            (me, kept, arrived), name="halve", smem=(0,),
        )
        return [b for b in bits if b != bit], sent, kept

    bits = list(range(count.bit_length() - 2, 0, -1))
    bits, sent, kept = halve(bits, 2, split, 0, kept, message)
    sent, act_windows, outer = lax.optimization_barrier((sent, act_windows, outer))
    arrived = lax.ppermute(sent, "space", [(i, i ^ 4) for i in range(count)])
    grad_outer = lax.ppermute(outer, "space", across)
    output, = call(
        functools.partial(output_rest_body, columns, rest),
        (shape((planes, cells, wide), F32),),
        (act_windows, out_taps, output),
        (pltpu.VMEM((planes, cells - BLOCK, wide), F32), dma((len(rest),))),
        two_flops, "output_rest", (), (2,), (0,), {2: 0},
    )
    others = 2 ** len(bits) - 1
    mine, *sent = call(
        functools.partial(spread_body, 0, bits),
        (shape((chunk, lanes), F32), *[shape((chunk, lanes), BF16)] * others),
        (me, kept, arrived), flops=16 * two_flops, name="spread", smem=(0,),
    )
    sent, output, back_windows = lax.optimization_barrier((sent, output, back_windows))
    arrived = []
    for at, part in enumerate(sent):
        away = sum(((at + 1) >> i & 1) << bit for i, bit in enumerate(bits[::-1]))
        arrived.append(lax.ppermute(part, "space", [(i, i ^ away) for i in range(count)]))
    grad_windows, = call(
        functools.partial(grad_windows_body, columns), (third,), (me, message, grad_outer),
        (), one_flops // 4, "grad_windows", (0,),
    )
    grad_volume, = call(
        functools.partial(grad_volume_body, columns),
        (shape((planes, cells, channels), F32),),
        (back_windows, grad_windows, back_taps),
        (pltpu.VMEM((planes, cells, channels), F32), dma((cells // BLOCK + 1,))),
        one_flops, "grad_volume", (), (), (0,),
    )
    mine, grad_volume = lax.optimization_barrier((mine, grad_volume))
    grad_one, grad_two = call(
        functools.partial(finish_body, scale, (mid // count, wide // count)),
        (shape((27, mid // count, channels), F32), shape((27, wide // count, mid), F32)),
        (mine, *arrived), name="finish",
    )
    return (
        output.reshape(planes, rows, columns, wide),
        grad_volume.reshape(planes, rows, columns, channels),
        jnp.swapaxes(grad_one, 1, 2).reshape(3, 3, 3, channels, mid // count),
        jnp.swapaxes(grad_two, 1, 2).reshape(3, 3, 3, mid, wide // count),
    )


def solution(mesh):
    cells = P(("groups", "space"), None, None, None)
    kernel = P("groups", None, None, None, "space")
    return jax.shard_map(
        shards,
        mesh=mesh,
        in_specs=(cells, P(), P(), cells),
        out_specs=(cells, cells, kernel, kernel),
        check_vma=False,
    )
```

```python
import functools
import math

import jax
import jax.numpy as jnp
from jax import lax
from jax.experimental import pallas as pl
from jax.experimental.pallas import tpu as pltpu
from jax.sharding import PartitionSpec as P

F32, BF16 = jnp.float32, jnp.bfloat16
STEP, BLOCK = 256, 512
VMEM_LIMIT = 16 * 2**20
NN = (((1,), (0,)), ((), ()))
NT = (((1,), (1,)), ((), ()))

PLANES = (0, 1, 2, -1)


def depth_tap(source, target):
    tap = source - target + 1
    return tap if 0 <= tap <= 2 else None


def call(body, outs, ins, scratch=(), flops=0, name=None, smem=(), apart=(), far=(), alias=None):
    moved = sum(math.prod(s.shape) * s.dtype.itemsize for s in (*outs, *ins))
    return pl.pallas_call(
        body,
        out_shape=list(outs),
        in_specs=[
            pl.BlockSpec(
                memory_space=pltpu.SMEM if i in smem else pl.ANY if i in apart else pltpu.VMEM
            )
            for i in range(len(ins))
        ],
        out_specs=[
            pl.BlockSpec(memory_space=pl.ANY if i in far else pltpu.VMEM) for i in range(len(outs))
        ],
        input_output_aliases=alias or {},
        scratch_shapes=list(scratch),
        compiler_params=pltpu.CompilerParams(vmem_limit_bytes=VMEM_LIMIT),
        cost_estimate=pl.CostEstimate(flops=flops, bytes_accessed=moved, transcendentals=0),
        name=name,
    )(*ins)


def lanes_low(x):
    return lax.broadcasted_iota(jnp.int32, x.shape, 1) < 64


def swap(x):
    return pltpu.roll(x, 64, 1)


def pick(low, high):
    return jnp.where(lanes_low(low), low, high)


def fill_windows(windows, start, lane, chunk, columns, stride):
    size = chunk.shape[0]
    column = lax.broadcasted_iota(jnp.int32, chunk.shape, 0) % columns
    before = jnp.where(column == 0, 0.0, pltpu.roll(chunk, 1, 0))
    after = jnp.where(column == columns - 1, 0.0, pltpu.roll(chunk, size - 1, 0))
    at = pl.ds(pl.multiple_of(columns + start, 32), size)
    for tap, part in enumerate((before, chunk, after)):
        first = tap * stride + lane
        windows[at, first : first + chunk.shape[1]] = part.astype(BF16)


def clear_edges(windows, columns):
    rows, lanes = windows.shape
    windows[0:columns, :] = jnp.zeros((columns, lanes), BF16)
    windows[rows - columns : rows, :] = jnp.zeros((columns, lanes), BF16)


def row_windows(windows, start, columns, size=BLOCK):
    return [
        windows[start + tap * columns : start + tap * columns + size, :] for tap in range(3)
    ]


def window_dot(windows, weights, start, columns, dims, size=BLOCK):
    rows = jnp.concatenate(row_windows(windows, start, columns, size), axis=1)
    return lax.dot_general(rows, weights[...], dims, preferred_element_type=F32)


def row_blocks(first, last):
    blocks = [(start, BLOCK) for start in range(first, last - BLOCK, BLOCK)]
    return blocks + [(last - BLOCK, BLOCK // 2), (last - BLOCK // 2, BLOCK // 2)]


def packed(low, high):
    return pick(low, swap(high)), pick(swap(low), high)


def unpacked(first, second):
    return packed(first, second)


def by_side(odd, inner, outer):
    return jnp.where(odd, inner, outer), jnp.where(odd, outer, inner)


def pieces_of(source, target, sems, parts):
    size = target.shape[1] // parts
    return [
        pltpu.make_async_copy(
            source.at[:, pl.ds(i * size, size), :], target.at[:, pl.ds(i * size, size), :], sems.at[i]
        )
        for i in range(parts)
    ]


def pack_body(volume, own, held, sems):
    copies = pieces_of(volume, held, sems, sems.shape[0])
    size = own.shape[0] // len(copies)
    for copy in copies:
        copy.start()
    for i, copy in enumerate(copies):
        copy.wait()
        rows = slice(i * size, i * size + size)
        own[rows, :] = jnp.concatenate([held[0, rows, :], held[1, rows, :]], axis=1)


def leave_body(
    columns, me, far_cotangent, far_weight, own, inner, outer, turned,
    windows, taps, cotangent, weight, sems, sem,
):
    cells = own.shape[0]
    half = cells // 2
    odd = me[0] % 2 == 1
    fetch = pltpu.make_async_copy(far_weight, weight, sem)
    copies = pieces_of(far_cotangent, cotangent, sems, sems.shape[0])
    for copy in copies:
        copy.start()
    fetch.start()
    clear_edges(windows, columns)
    size = cells // len(copies)
    for at, copy in enumerate(copies):
        copy.wait()

        def fill(i, carry):
            start = pl.multiple_of(at * size + i * STEP, STEP)
            for plane in range(2):
                chunk = cotangent[plane, pl.ds(start, STEP), :].astype(F32)
                fill_windows(windows, start, plane * 128, chunk, columns, 256)
            return carry

        lax.fori_loop(0, size // STEP, fill, 0)
    fetch.wait()
    for row in range(3):
        for column in range(3):
            for source in range(2):
                first = row * 768 + column * 256 + source * 128
                for at, target in enumerate(PLANES):
                    depth = depth_tap(source, target)
                    taps[at * 64 : at * 64 + 64, first : first + 128] = (
                        jnp.zeros((64, 128), BF16)
                        if depth is None
                        else weight[(2 - depth) * 9 + (2 - row) * 3 + 2 - column]
                    )
    for start in range(0, half, BLOCK):
        sides = []
        for first in (start, start + half):
            term = window_dot(windows, taps, first, columns, NT)
            own[first : first + BLOCK, :] = term[:, :128]
            sides.append(term[:, 128:])
        upper, lower = packed(*sides)
        near = jnp.where(odd, lower, upper)
        head = near.astype(BF16)
        inner[start : start + BLOCK, :] = head
        inner[half + start : half + start + BLOCK, :] = (near - head.astype(F32)).astype(BF16)
        outer[start : start + BLOCK, :] = jnp.where(odd, upper, lower).astype(BF16)
    for plane in range(2):
        turn(cotangent.at[plane], turned, plane * 128)


def prepare_body(
    columns, me, own, inner, far_weight, own_windows, inner_windows, hidden, outer_taps,
    taps, weight, sem,
):
    fetch = pltpu.make_async_copy(far_weight, weight, sem)
    fetch.start()
    odd = me[0] % 2 == 1

    def fill(i, carry):
        start = pl.multiple_of(i * STEP, STEP)
        rows = pl.ds(start, STEP)
        fill_windows(own_windows, start, 0, own[rows, :].astype(F32), columns, 128)
        fill_windows(inner_windows, start, 0, inner[rows, :].astype(F32), columns, 128)
        return carry

    clear_edges(own_windows, columns)
    clear_edges(inner_windows, columns)
    lax.fori_loop(0, own.shape[0] // STEP, fill, 0)
    fetch.wait()
    zero = jnp.zeros((64, 64), BF16)
    for tap in range(9):

        def kernel_rows(source):
            depths = [depth_tap(source, target) for target in PLANES]
            parts = [zero if d is None else weight[d * 9 + tap] for d in depths]
            return jnp.concatenate(parts, axis=1)

        for at in range(2):
            rows = slice(tap * 128 + at * 64, tap * 128 + at * 64 + 64)
            taps[rows, :] = kernel_rows(at)
            upper, lower = kernel_rows(2 + at).astype(F32), kernel_rows(at - 2).astype(F32)
            first = 9 * 128 + rows.start
            taps[first : first + 64, :] = jnp.where(odd, lower, upper).astype(BF16)
            outer_taps[rows, :] = jnp.where(odd, upper, lower).astype(BF16)
    for start in range(0, own.shape[0], BLOCK):
        rows = row_windows(own_windows, start, columns) + row_windows(inner_windows, start, columns)
        hidden[start : start + BLOCK, :] = jnp.dot(
            jnp.concatenate(rows, axis=1), taps[...], preferred_element_type=F32
        )


def back_taps_body(weight, back_taps, turned_taps):
    zero = jnp.zeros((64, 64), BF16)
    for row in range(3):
        for column in range(3):
            tap = row * 3 + column
            for plane in range(2):
                depths = [depth_tap(source, plane) for source in PLANES]
                parts = [zero if d is None else weight[(2 - d) * 9 + 8 - tap] for d in depths]
                at = row * 128 + plane * 64
                for pair in range(2):
                    first = pair * 384 + column * 128
                    turned_taps[at : at + 64, first : first + 128] = jnp.concatenate(
                        parts[2 * pair : 2 * pair + 2], axis=1
                    )
    back_taps[...] = turned_taps[...].astype(F32).T.astype(BF16)


def hidden_body(
    columns, count, me, outer, part, outer_taps, inner_windows, act_windows, slope, side_windows,
    outer_windows,
):
    cells = outer.shape[0]

    def fill(i, carry):
        start = pl.multiple_of(i * STEP, STEP)
        chunk = outer[pl.ds(start, STEP), :].astype(F32)
        fill_windows(outer_windows, start, 0, chunk, columns, 128)
        return carry

    clear_edges(outer_windows, columns)
    clear_edges(act_windows, columns)
    lax.fori_loop(0, cells // STEP, fill, 0)
    from_inner = lax.broadcasted_iota(jnp.int32, (16, 128), 1) // 64 == me[0] % 2
    from_inner = jnp.where(from_inner, 1.0, 0.0).astype(BF16)[:1]
    for tap in range(3):
        at = slice(tap * 128, tap * 128 + 128)
        side_windows[:, at] = (
            inner_windows[:, at] * from_inner + outer_windows[:, at] * (1 - from_inner)
        )
    lanes = lax.broadcasted_iota(jnp.int32, (BLOCK, 128), 1)
    edges = [jnp.where(me[0] == end, 0.0, 1.0).astype(F32) for end in (count - 1, 0)]
    inside = jnp.where(lanes < 64, edges[0], edges[1])
    for start in range(0, cells, BLOCK):
        hidden = part[start : start + BLOCK, :]
        hidden = hidden + window_dot(outer_windows, outer_taps, start, columns, NN)
        gate = jax.nn.sigmoid(hidden)
        act = (hidden * gate).astype(BF16).astype(F32)
        fill_windows(act_windows, start, 0, act[:, :128], columns, 256)
        fill_windows(act_windows, start, 128, act[:, 128:] * inside, columns, 256)
        hidden, gate = hidden[:, :128], gate[:, :128]
        slope[start : start + BLOCK, :] = gate * (1.0 + hidden * (1.0 - gate))


def kernel_terms(columns, out_channels, slices, turned, terms):
    for row in range(3):
        for column in range(3):
            tap = row * 3 + column
            product = jnp.dot(turned[...], slices(row, column), preferred_element_type=F32)
            first, second = product[:out_channels], product[out_channels:]
            terms[:, tap * 128 : tap * 128 + 128] = first[:, :128] + swap(
                pick(second[:, 128:], second[:, :128])
            )
            group = 9 + tap // 2
            here = slice(group * 128, group * 128 + 128)
            if tap % 2 == 0:
                terms[:, here] = swap(first[:, 128:]) + second[:, :128]
            else:
                terms[:, here] = pick(terms[:, here], first[:, 128:] + swap(second[:, :128]))


def turn(source, target, first):
    for start in range(0, source.shape[0], STEP):
        chunk = source[start : start + STEP, :].astype(F32)
        target[first : first + chunk.shape[1], start : start + STEP] = chunk.T.astype(BF16)


def grad_two_body(columns, act_windows, turned, terms):
    cells = turned.shape[1]

    def slices(row, column):
        rows = slice(row * columns, row * columns + cells)
        return act_windows[rows, column * 256 : column * 256 + 256]

    kernel_terms(columns, 128, slices, turned, terms)


def coded(value, split):
    head = value.astype(BF16)
    if split == 0:
        return head
    rest = (value[:split] - head[:split].astype(F32)).astype(BF16)
    return jnp.concatenate([head, rest], axis=0)


def decoded(value, split):
    value = value.astype(F32)
    if split == 0:
        return value
    size = value.shape[0] - split
    parts = [value[:split] + value[size:]]
    if split < size:
        parts.append(value[split:size])
    return jnp.concatenate(parts, axis=0)


def grad_one_body(
    columns, count, me, own_windows, side_windows, act_terms, inner, outer, slope, other,
    grad, to_outer, message, kept, turned, terms,
):
    cells = grad.shape[0]
    odd = me[0] % 2 == 1
    before = message.shape[0] - cells // 2
    for start in range(0, cells // 2, STEP):
        low, high = slice(start, start + STEP), slice(start + cells // 2, start + cells // 2 + STEP)
        near = inner[low, :].astype(F32) + inner[high, :].astype(F32)
        arrived = unpacked(*by_side(odd, near, outer[low, :].astype(F32)))
        sides = []
        for rows, extra in zip((low, high), arrived):
            value = ((act_terms[rows, :] + extra) * slope[rows, :]).astype(BF16)
            grad[rows, :] = value
            value = value.astype(F32)
            turned[:, rows] = value.T.astype(BF16)
            sides.append(value)
        lower, upper = packed(*sides)
        message[before + start : before + start + STEP, :] = jnp.where(
            odd, lower, upper
        ).astype(BF16)
        to_outer[low, :] = jnp.where(odd, upper, lower).astype(BF16)
    def slices(row, column):
        rows = slice(row * columns, row * columns + cells)
        lanes = slice(column * 128, column * 128 + 128)
        return jnp.concatenate([own_windows[rows, lanes], side_windows[rows, lanes]], axis=1)

    kernel_terms(columns, 64, slices, turned, terms)
    half = terms.shape[1] // 2
    split = 2 * terms.shape[0] // count

    def share(owner):
        parts = []
        for source in (terms, other):
            each = source.shape[0] // count
            block = source[owner * each : owner * each + each, :]
            parts += [block[:, :half], block[:, half:]]
        return jnp.concatenate(parts, axis=0)

    groups = half // 128
    for pair in range(count // 2):
        even_share, odd_share = share(2 * pair), share(2 * pair + 1)
        kept[pair] = jnp.where(odd, odd_share, even_share)
        given = coded(jnp.where(odd, even_share, odd_share), split)
        size = given.shape[0]
        for group in range(groups):
            first = (pair * groups + group) * size
            message[first : first + size, :] = given[:, group * 128 : group * 128 + 128]


def halve_body(split_in, split_out, owner_bit, at_bit, me, mine, arrived, sent, kept):
    side = (me[0] >> owner_bit) % 2
    size, lanes = mine.shape[1:]
    groups = lanes // 128

    def total(at):
        if len(arrived.shape) == 3:
            return mine[at] + decoded(arrived[at], split_in)
        parts = []
        for group in range(groups):
            rows = size + split_in
            first = pl.multiple_of((at * groups + group) * rows, 8)
            parts.append(decoded(arrived[pl.ds(first, rows), :], split_in))
        return mine[at] + jnp.concatenate(parts, axis=1)

    for at in range(sent.shape[0]):
        high, low = at >> at_bit, at & ((1 << at_bit) - 1)
        keep = ((2 * high + side) << at_bit) + low
        give = ((2 * high + 1 - side) << at_bit) + low
        sent[at] = coded(total(give), split_out)
        kept[at] = total(keep)


def others_of(place, places):
    return [place ^ away for away in [*range(places // 2, places), *range(1, places // 2)]]


def spread_body(split_in, owner_bits, me, mine, arrived, kept, *sent):
    place = 0
    for bit in owner_bits:
        place = 2 * place + (me[0] >> bit) % 2
    kept[...] = mine[place] + decoded(arrived[place], split_in)
    for there, out in zip(others_of(place, mine.shape[0]), sent):
        out[...] = (mine[there] + decoded(arrived[there], split_in)).astype(BF16)


def finish_body(scale, sizes, mine, *refs):
    arrived, (grad_one, grad_two) = refs[:-2], refs[-2:]
    total = mine[...]
    for part in arrived:
        total = total + part[...].astype(F32)
    total = total * scale
    half = total.shape[1]
    first = 0
    for size, out in zip(sizes, (grad_one, grad_two)):
        blocks = (total[first : first + size], total[first + size : first + 2 * size])
        first += 2 * size
        for tap in range(9):
            for depth, group, side in ((0, 9 + tap // 2, tap % 2), (1, tap, 0), (2, tap, 1)):
                lane = group * 128 + side * 64
                block, lane = (blocks[0], lane) if lane < half else (blocks[1], lane - half)
                out[depth * 9 + tap] = block[:, lane : lane + 64]


def output_rows(columns, blocks, act_windows, taps, far, output, sems):
    copies = []
    for at, (start, size) in enumerate(blocks):
        value = window_dot(act_windows, taps, start, columns, NN, size)
        here = slice(start - blocks[0][0], start - blocks[0][0] + size)
        output[0, here, :] = value[:, :128]
        output[1, here, :] = value[:, 128:]
        copies.append(
            pltpu.make_async_copy(
                output.at[:, here, :], far.at[:, start : start + size, :], sems.at[at]
            )
        )
        copies[-1].start()
    return copies


def output_first_body(
    columns, blocks, act_windows, weight, grad, far, taps, own_windows, output, sems
):
    for row in range(3):
        for column in range(3):
            for at, source in enumerate(PLANES):
                first = row * 768 + column * 256 + at * 64
                for plane in range(2):
                    depth = depth_tap(source, plane)
                    taps[first : first + 64, plane * 128 : plane * 128 + 128] = (
                        jnp.zeros((64, 128), BF16)
                        if depth is None
                        else weight[depth * 9 + row * 3 + column]
                    )
    copies = output_rows(columns, blocks, act_windows, taps, far, output, sems)

    def fill(i, carry):
        start = pl.multiple_of(i * STEP, STEP)
        chunk = grad[pl.ds(start, STEP), :].astype(F32)
        fill_windows(own_windows, start, 0, chunk, columns, 128)
        return carry

    clear_edges(own_windows, columns)
    lax.fori_loop(0, grad.shape[0] // STEP, fill, 0)
    for copy in copies:
        copy.wait()


def output_rest_body(columns, blocks, act_windows, taps, begun, far, output, sems):
    for copy in output_rows(columns, blocks, act_windows, taps, far, output, sems):
        copy.wait()


def grad_windows_body(columns, me, message, outer, windows):
    half = outer.shape[0]
    odd = me[0] % 2 == 1
    before = message.shape[0] - half

    def fill(i, carry):
        start = pl.multiple_of(i * STEP, STEP)
        near = message[pl.ds(before + start, STEP), :].astype(F32)
        below, above = by_side(odd, near, outer[pl.ds(start, STEP), :].astype(F32))
        for first, side in zip((start, start + half), unpacked(above, below)):
            fill_windows(windows, first, 0, side, columns, 128)
        return carry

    clear_edges(windows, columns)
    lax.fori_loop(0, half // STEP, fill, 0)


def grad_volume_body(columns, own_windows, side_windows, taps, far, output, sems):
    copies = []
    for at, (start, size) in enumerate(row_blocks(0, output.shape[1])):
        rows = slice(start, start + size + 2 * columns)
        rows = jnp.concatenate([own_windows[rows, :], side_windows[rows, :]], axis=1)
        terms = jnp.dot(rows, taps[...], preferred_element_type=F32)
        value = terms[:size, :128]
        value = value + terms[columns : columns + size, 128:256]
        value = value + terms[2 * columns : 2 * columns + size, 256:]
        here = slice(start, start + size)
        output[0, here, :] = value[:, :64]
        output[1, here, :] = value[:, 64:]
        copies.append(
            pltpu.make_async_copy(output.at[:, here, :], far.at[:, here, :], sems.at[at])
        )
        copies[-1].start()
    for copy in copies:
        copy.wait()


def shards(volume, weight_one, weight_two, cotangent):
    count = lax.axis_size("space")
    planes, rows, columns, channels = volume.shape
    cells = rows * columns
    scale = 1.0 / math.sqrt(planes * count * cells)
    mid, wide = weight_two.shape[3], weight_two.shape[4]
    me = lax.axis_index("space").astype(jnp.int32).reshape(1)
    shape = jax.ShapeDtypeStruct
    flat, pack = shape((cells, 128), BF16), shape((cells // 2, 128), BF16)
    slab = (cells + 2 * columns, 768)
    windows = pltpu.VMEM(slab, BF16)
    lanes = 14 * 64
    split = 2 * mid // count
    chunk = 2 * (mid + wide) // count

    within = [(i, i ^ 1) for i in range(count)]
    across = [(i, i + 1) for i in range(1, count - 1, 2)]
    across += [(j, i) for i, j in across]

    volume = volume.reshape(planes, cells, channels)
    cotangent = cotangent.reshape(planes, cells, wide)
    weight_one = weight_one.reshape(27, channels, mid)
    weight_two = weight_two.reshape(27, mid, wide)
    one_flops = 2 * planes * cells * 27 * channels * mid
    two_flops = 2 * planes * cells * 27 * mid * wide

    dma = pltpu.SemaphoreType.DMA
    far_one, far_two, far_volume, far_cotangent = (
        pltpu.with_memory_space_constraint(x, pltpu.HBM)
        for x in (weight_one, weight_two, volume, cotangent)
    )
    own, = call(
        pack_body, (flat,), (far_volume,),
        (pltpu.VMEM((planes, cells, channels), BF16), dma((4,))),
        name="pack_volume", apart=(0,),
    )
    vol_outer = lax.ppermute(own, "space", across)
    vol_inner = lax.ppermute(own, "space", within)
    terms, inner, outer, turned = call(
        functools.partial(leave_body, columns),
        (
            shape((cells, 128), F32), flat, pack, shape((256, cells), BF16),
        ),
        (me, far_cotangent, far_two),
        (
            windows, pltpu.VMEM((256, 3 * 768), BF16), pltpu.VMEM(cotangent.shape, BF16),
            pltpu.VMEM(weight_two.shape, BF16), dma((4,)), dma,
        ),
        two_flops, "grad_act_terms", (0,), (1, 2),
    )
    own, terms = lax.optimization_barrier((own, terms))
    third = shape((slab[0], 384), BF16)
    own_windows, inner_windows, part, outer_taps = call(
        functools.partial(prepare_body, columns),
        (third, third, shape((cells, 256), F32), shape((9 * 128, 256), BF16)),
        (me, own, vol_inner, far_one),
        (pltpu.VMEM((2 * 9 * 128, 256), BF16), pltpu.VMEM(weight_one.shape, BF16), dma),
        one_flops, "prepare", (0,), (3,),
    )
    back_taps, = call(
        back_taps_body, (shape((768, 3 * 128), BF16),), (weight_one,),
        (pltpu.VMEM((3 * 128, 768), BF16),), one_flops // 8, "back_taps",
    )
    inner, outer, part, back_taps = lax.optimization_barrier((inner, outer, part, back_taps))
    terms_outer = lax.ppermute(outer, "space", across)
    terms_inner = lax.ppermute(inner, "space", within)
    act_windows, slope, side_windows = call(
        functools.partial(hidden_body, columns, count),
        (shape(slab, BF16), shape((cells, 128), F32), third),
        (me, vol_outer, part, outer_taps, inner_windows),
        (pltpu.VMEM((slab[0], 384), BF16),), 2 * one_flops, "hidden", (0,),
    )
    terms_two, = call(
        functools.partial(grad_two_body, columns),
        (shape((wide, 2 * lanes), F32),),
        (act_windows, turned), (), two_flops, "grad_two_terms",
    )
    groups = lanes // 128
    grad_hidden, outer, message, kept = call(
        functools.partial(grad_one_body, columns, count),
        (
            flat, pack,
            shape((count // 2 * groups * (chunk + split) + cells // 2, 128), BF16),
            shape((count // 2, chunk, lanes), F32),
        ),
        (
            me, own_windows, side_windows, terms, terms_inner, terms_outer, slope, terms_two,
        ),
        (pltpu.VMEM((128, cells), BF16), pltpu.VMEM((mid, 2 * lanes), F32)),
        one_flops, "grad_one_terms", (0,),
    )
    message = lax.ppermute(message, "space", within)
    rest = row_blocks(BLOCK, cells)
    output, out_taps, back_windows = call(
        functools.partial(output_first_body, columns, [(0, BLOCK)]),
        (shape((planes, cells, wide), F32), shape((9 * 256, 256), BF16), third),
        (act_windows, weight_two, grad_hidden),
        (pltpu.VMEM((planes, BLOCK, wide), F32), dma((1,))),
        two_flops, "output_first", (), (), (0,),
    )
    message, output, out_taps, back_windows = lax.optimization_barrier(
        (message, output, out_taps, back_windows)
    )
    def halve(bits, bit, split_in, split_out, kept, arrived):
        left = 2 ** (len(bits) - 1)
        sent, kept = call(
            functools.partial(halve_body, split_in, split_out, bit, bits[::-1].index(bit)),
            (shape((left, chunk + split_out, lanes), BF16), shape((left, chunk, lanes), F32)),
            (me, kept, arrived), name="halve", smem=(0,),
        )
        return [b for b in bits if b != bit], sent, kept

    bits = list(range(count.bit_length() - 2, 0, -1))
    bits, sent, kept = halve(bits, 2, split, 0, kept, message)
    sent, act_windows, outer = lax.optimization_barrier((sent, act_windows, outer))
    arrived = lax.ppermute(sent, "space", [(i, i ^ 4) for i in range(count)])
    grad_outer = lax.ppermute(outer, "space", across)
    output, = call(
        functools.partial(output_rest_body, columns, rest),
        (shape((planes, cells, wide), F32),),
        (act_windows, out_taps, output),
        (pltpu.VMEM((planes, cells - BLOCK, wide), F32), dma((len(rest),))),
        two_flops, "output_rest", (), (2,), (0,), {2: 0},
    )
    others = 2 ** len(bits) - 1
    mine, *sent = call(
        functools.partial(spread_body, 0, bits),
        (shape((chunk, lanes), F32), *[shape((chunk, lanes), BF16)] * others),
        (me, kept, arrived), flops=16 * two_flops, name="spread", smem=(0,),
    )
    sent, output, back_windows = lax.optimization_barrier((sent, output, back_windows))
    arrived = []
    for at, part in zip(others_of(0, others + 1), sent):
        away = sum((at >> i & 1) << bit for i, bit in enumerate(bits[::-1]))
        arrived.append(lax.ppermute(part, "space", [(i, i ^ away) for i in range(count)]))
    grad_windows, = call(
        functools.partial(grad_windows_body, columns), (third,), (me, message, grad_outer),
        (), one_flops // 4, "grad_windows", (0,),
    )
    grad_volume, = call(
        functools.partial(grad_volume_body, columns),
        (shape((planes, cells, channels), F32),),
        (back_windows, grad_windows, back_taps),
        (pltpu.VMEM((planes, cells, channels), F32), dma((cells // BLOCK + 1,))),
        one_flops, "grad_volume", (), (), (0,),
    )
    mine, grad_volume = lax.optimization_barrier((mine, grad_volume))
    grad_one, grad_two = call(
        functools.partial(finish_body, scale, (mid // count, wide // count)),
        (shape((27, mid // count, channels), F32), shape((27, wide // count, mid), F32)),
        (mine, *arrived), name="finish",
    )
    return (
        output.reshape(planes, rows, columns, wide),
        grad_volume.reshape(planes, rows, columns, channels),
        jnp.swapaxes(grad_one, 1, 2).reshape(3, 3, 3, channels, mid // count),
        jnp.swapaxes(grad_two, 1, 2).reshape(3, 3, 3, mid, wide // count),
    )


def solution(mesh):
    cells = P(("groups", "space"), None, None, None)
    kernel = P("groups", None, None, None, "space")
    return jax.shard_map(
        shards,
        mesh=mesh,
        in_specs=(cells, P(), P(), cells),
        out_specs=(cells, cells, kernel, kernel),
        check_vma=False,
    )
```

```python
import functools
import math

import jax
import jax.numpy as jnp
from jax import lax
from jax.experimental import pallas as pl
from jax.experimental.pallas import tpu as pltpu
from jax.sharding import PartitionSpec as P

F32, BF16 = jnp.float32, jnp.bfloat16
STEP, BLOCK = 256, 512
VMEM_LIMIT = 16 * 2**20
NN = (((1,), (0,)), ((), ()))
NT = (((1,), (1,)), ((), ()))

PLANES = (0, 1, 2, -1)


def depth_tap(source, target):
    tap = source - target + 1
    return tap if 0 <= tap <= 2 else None


def call(body, outs, ins, scratch=(), flops=0, name=None, smem=(), apart=(), far=(), alias=None):
    moved = sum(math.prod(s.shape) * s.dtype.itemsize for s in (*outs, *ins))
    return pl.pallas_call(
        body,
        out_shape=list(outs),
        in_specs=[
            pl.BlockSpec(
                memory_space=pltpu.SMEM if i in smem else pl.ANY if i in apart else pltpu.VMEM
            )
            for i in range(len(ins))
        ],
        out_specs=[
            pl.BlockSpec(memory_space=pl.ANY if i in far else pltpu.VMEM) for i in range(len(outs))
        ],
        input_output_aliases=alias or {},
        scratch_shapes=list(scratch),
        compiler_params=pltpu.CompilerParams(vmem_limit_bytes=VMEM_LIMIT),
        cost_estimate=pl.CostEstimate(flops=flops, bytes_accessed=moved, transcendentals=0),
        name=name,
    )(*ins)


def lanes_low(x):
    return lax.broadcasted_iota(jnp.int32, x.shape, 1) < 64


def swap(x):
    return pltpu.roll(x, 64, 1)


def pick(low, high):
    return jnp.where(lanes_low(low), low, high)


def fill_windows(windows, start, lane, chunk, columns, stride):
    size = chunk.shape[0]
    column = lax.broadcasted_iota(jnp.int32, chunk.shape, 0) % columns
    before = jnp.where(column == 0, 0.0, pltpu.roll(chunk, 1, 0))
    after = jnp.where(column == columns - 1, 0.0, pltpu.roll(chunk, size - 1, 0))
    at = pl.ds(pl.multiple_of(columns + start, 32), size)
    for tap, part in enumerate((before, chunk, after)):
        first = tap * stride + lane
        windows[at, first : first + chunk.shape[1]] = part.astype(BF16)


def clear_edges(windows, columns):
    rows, lanes = windows.shape
    windows[0:columns, :] = jnp.zeros((columns, lanes), BF16)
    windows[rows - columns : rows, :] = jnp.zeros((columns, lanes), BF16)


def row_windows(windows, start, columns, size=BLOCK):
    return [
        windows[start + tap * columns : start + tap * columns + size, :] for tap in range(3)
    ]


def window_dot(windows, weights, start, columns, dims, size=BLOCK):
    rows = jnp.concatenate(row_windows(windows, start, columns, size), axis=1)
    return lax.dot_general(rows, weights[...], dims, preferred_element_type=F32)


def row_blocks(first, last):
    blocks = [(start, BLOCK) for start in range(first, last - BLOCK, BLOCK)]
    return blocks + [(last - BLOCK, BLOCK // 2), (last - BLOCK // 2, BLOCK // 2)]


def packed(low, high):
    return pick(low, swap(high)), pick(swap(low), high)


def unpacked(first, second):
    return packed(first, second)


def by_side(odd, inner, outer):
    return jnp.where(odd, inner, outer), jnp.where(odd, outer, inner)


def pieces_of(source, target, sems, parts):
    size = target.shape[1] // parts
    return [
        pltpu.make_async_copy(
            source.at[:, pl.ds(i * size, size), :], target.at[:, pl.ds(i * size, size), :], sems.at[i]
        )
        for i in range(parts)
    ]


def pack_body(volume, own, held, sems):
    copies = pieces_of(volume, held, sems, sems.shape[0])
    size = own.shape[0] // len(copies)
    for copy in copies:
        copy.start()
    for i, copy in enumerate(copies):
        copy.wait()
        rows = slice(i * size, i * size + size)
        own[rows, :] = jnp.concatenate([held[0, rows, :], held[1, rows, :]], axis=1)


def leave_body(
    columns, me, far_cotangent, far_weight, own, inner, outer, turned,
    windows, taps, cotangent, weight, sems, sem,
):
    cells = own.shape[0]
    half = cells // 2
    odd = me[0] % 2 == 1
    fetch = pltpu.make_async_copy(far_weight, weight, sem)
    copies = pieces_of(far_cotangent, cotangent, sems, sems.shape[0])
    for copy in copies:
        copy.start()
    fetch.start()
    clear_edges(windows, columns)
    size = cells // len(copies)
    for at, copy in enumerate(copies):
        copy.wait()

        def fill(i, carry):
            start = pl.multiple_of(at * size + i * STEP, STEP)
            for plane in range(2):
                chunk = cotangent[plane, pl.ds(start, STEP), :].astype(F32)
                fill_windows(windows, start, plane * 128, chunk, columns, 256)
            return carry

        lax.fori_loop(0, size // STEP, fill, 0)
    fetch.wait()
    for row in range(3):
        for column in range(3):
            for source in range(2):
                first = row * 768 + column * 256 + source * 128
                for at, target in enumerate(PLANES):
                    depth = depth_tap(source, target)
                    taps[at * 64 : at * 64 + 64, first : first + 128] = (
                        jnp.zeros((64, 128), BF16)
                        if depth is None
                        else weight[(2 - depth) * 9 + (2 - row) * 3 + 2 - column]
                    )
    for start in range(0, half, BLOCK):
        sides = []
        for first in (start, start + half):
            term = window_dot(windows, taps, first, columns, NT)
            own[first : first + BLOCK, :] = term[:, :128]
            sides.append(term[:, 128:])
        upper, lower = packed(*sides)
        near = jnp.where(odd, lower, upper)
        head = near.astype(BF16)
        inner[start : start + BLOCK, :] = head
        inner[half + start : half + start + BLOCK, :] = (near - head.astype(F32)).astype(BF16)
        outer[start : start + BLOCK, :] = jnp.where(odd, upper, lower).astype(BF16)
    for plane in range(2):
        turn(cotangent.at[plane], turned, plane * 128)


def prepare_body(
    columns, me, own, inner, far_weight, own_windows, inner_windows, hidden, outer_taps,
    taps, weight, sem,
):
    fetch = pltpu.make_async_copy(far_weight, weight, sem)
    fetch.start()
    odd = me[0] % 2 == 1

    def fill(i, carry):
        start = pl.multiple_of(i * STEP, STEP)
        rows = pl.ds(start, STEP)
        fill_windows(own_windows, start, 0, own[rows, :].astype(F32), columns, 128)
        fill_windows(inner_windows, start, 0, inner[rows, :].astype(F32), columns, 128)
        return carry

    clear_edges(own_windows, columns)
    clear_edges(inner_windows, columns)
    lax.fori_loop(0, own.shape[0] // STEP, fill, 0)
    fetch.wait()
    zero = jnp.zeros((64, 64), BF16)
    for tap in range(9):

        def kernel_rows(source):
            depths = [depth_tap(source, target) for target in PLANES]
            parts = [zero if d is None else weight[d * 9 + tap] for d in depths]
            return jnp.concatenate(parts, axis=1)

        for at in range(2):
            rows = slice(tap * 128 + at * 64, tap * 128 + at * 64 + 64)
            taps[rows, :] = kernel_rows(at)
            upper, lower = kernel_rows(2 + at).astype(F32), kernel_rows(at - 2).astype(F32)
            first = 9 * 128 + rows.start
            taps[first : first + 64, :] = jnp.where(odd, lower, upper).astype(BF16)
            outer_taps[rows, :] = jnp.where(odd, upper, lower).astype(BF16)
    for start in range(0, own.shape[0], BLOCK):
        rows = row_windows(own_windows, start, columns) + row_windows(inner_windows, start, columns)
        hidden[start : start + BLOCK, :] = jnp.dot(
            jnp.concatenate(rows, axis=1), taps[...], preferred_element_type=F32
        )


def layouts_body(weight, weight_two, back_taps, out_taps, turned_taps):
    zero = jnp.zeros((64, 64), BF16)
    for row in range(3):
        for column in range(3):
            tap = row * 3 + column
            for plane in range(2):
                depths = [depth_tap(source, plane) for source in PLANES]
                parts = [zero if d is None else weight[(2 - d) * 9 + 8 - tap] for d in depths]
                at = row * 128 + plane * 64
                for pair in range(2):
                    first = pair * 384 + column * 128
                    turned_taps[at : at + 64, first : first + 128] = jnp.concatenate(
                        parts[2 * pair : 2 * pair + 2], axis=1
                    )
    back_taps[...] = turned_taps[...].astype(F32).T.astype(BF16)
    for tap in range(9):
        for at, source in enumerate(PLANES):
            first = tap * 256 + at * 64
            for plane in range(2):
                depth = depth_tap(source, plane)
                out_taps[first : first + 64, plane * 128 : plane * 128 + 128] = (
                    jnp.zeros((64, 128), BF16) if depth is None else weight_two[depth * 9 + tap]
                )


def hidden_body(
    columns, count, me, outer, part, outer_taps, inner_windows, act_windows, slope, side_windows,
    outer_windows,
):
    cells = outer.shape[0]

    def fill(i, carry):
        start = pl.multiple_of(i * STEP, STEP)
        chunk = outer[pl.ds(start, STEP), :].astype(F32)
        fill_windows(outer_windows, start, 0, chunk, columns, 128)
        return carry

    clear_edges(outer_windows, columns)
    clear_edges(act_windows, columns)
    lax.fori_loop(0, cells // STEP, fill, 0)
    from_inner = lax.broadcasted_iota(jnp.int32, (16, 128), 1) // 64 == me[0] % 2
    from_inner = jnp.where(from_inner, 1.0, 0.0).astype(BF16)[:1]
    for tap in range(3):
        at = slice(tap * 128, tap * 128 + 128)
        side_windows[:, at] = (
            inner_windows[:, at] * from_inner + outer_windows[:, at] * (1 - from_inner)
        )
    lanes = lax.broadcasted_iota(jnp.int32, (BLOCK, 128), 1)
    edges = [jnp.where(me[0] == end, 0.0, 1.0).astype(F32) for end in (count - 1, 0)]
    inside = jnp.where(lanes < 64, edges[0], edges[1])
    for start in range(0, cells, BLOCK):
        hidden = part[start : start + BLOCK, :]
        hidden = hidden + window_dot(outer_windows, outer_taps, start, columns, NN)
        gate = jax.nn.sigmoid(hidden)
        act = (hidden * gate).astype(BF16).astype(F32)
        fill_windows(act_windows, start, 0, act[:, :128], columns, 256)
        fill_windows(act_windows, start, 128, act[:, 128:] * inside, columns, 256)
        hidden, gate = hidden[:, :128], gate[:, :128]
        slope[start : start + BLOCK, :] = gate * (1.0 + hidden * (1.0 - gate))


def kernel_terms(columns, out_channels, slices, turned, terms):
    for row in range(3):
        for column in range(3):
            tap = row * 3 + column
            product = jnp.dot(turned[...], slices(row, column), preferred_element_type=F32)
            first, second = product[:out_channels], product[out_channels:]
            terms[:, tap * 128 : tap * 128 + 128] = first[:, :128] + swap(
                pick(second[:, 128:], second[:, :128])
            )
            group = 9 + tap // 2
            here = slice(group * 128, group * 128 + 128)
            if tap % 2 == 0:
                terms[:, here] = swap(first[:, 128:]) + second[:, :128]
            else:
                terms[:, here] = pick(terms[:, here], first[:, 128:] + swap(second[:, :128]))


def turn(source, target, first):
    for start in range(0, source.shape[0], STEP):
        chunk = source[start : start + STEP, :].astype(F32)
        target[first : first + chunk.shape[1], start : start + STEP] = chunk.T.astype(BF16)


def grad_two_body(columns, blocks, act_windows, turned, taps, terms, far, output, sems):
    cells = turned.shape[1]
    copies = output_rows(columns, blocks, act_windows, taps, far, output, sems)

    def slices(row, column):
        rows = slice(row * columns, row * columns + cells)
        return act_windows[rows, column * 256 : column * 256 + 256]

    kernel_terms(columns, 128, slices, turned, terms)
    for copy in copies:
        copy.wait()


def coded(value, split):
    head = value.astype(BF16)
    if split == 0:
        return head
    rest = (value[:split] - head[:split].astype(F32)).astype(BF16)
    return jnp.concatenate([head, rest], axis=0)


def decoded(value, split):
    value = value.astype(F32)
    if split == 0:
        return value
    size = value.shape[0] - split
    parts = [value[:split] + value[size:]]
    if split < size:
        parts.append(value[split:size])
    return jnp.concatenate(parts, axis=0)


def grad_one_body(
    columns, count, me, own_windows, side_windows, act_terms, inner, outer, slope, other,
    grad, to_outer, message, kept, turned, terms,
):
    cells = grad.shape[0]
    odd = me[0] % 2 == 1
    before = message.shape[0] - cells // 2
    for start in range(0, cells // 2, STEP):
        low, high = slice(start, start + STEP), slice(start + cells // 2, start + cells // 2 + STEP)
        near = inner[low, :].astype(F32) + inner[high, :].astype(F32)
        arrived = unpacked(*by_side(odd, near, outer[low, :].astype(F32)))
        sides = []
        for rows, extra in zip((low, high), arrived):
            value = ((act_terms[rows, :] + extra) * slope[rows, :]).astype(BF16)
            grad[rows, :] = value
            value = value.astype(F32)
            turned[:, rows] = value.T.astype(BF16)
            sides.append(value)
        lower, upper = packed(*sides)
        message[before + start : before + start + STEP, :] = jnp.where(
            odd, lower, upper
        ).astype(BF16)
        to_outer[low, :] = jnp.where(odd, upper, lower).astype(BF16)
    def slices(row, column):
        rows = slice(row * columns, row * columns + cells)
        lanes = slice(column * 128, column * 128 + 128)
        return jnp.concatenate([own_windows[rows, lanes], side_windows[rows, lanes]], axis=1)

    kernel_terms(columns, 64, slices, turned, terms)
    half = terms.shape[1] // 2
    split = 2 * terms.shape[0] // count

    def share(owner):
        parts = []
        for source in (terms, other):
            each = source.shape[0] // count
            block = source[owner * each : owner * each + each, :]
            parts += [block[:, :half], block[:, half:]]
        return jnp.concatenate(parts, axis=0)

    groups = half // 128
    for pair in range(count // 2):
        even_share, odd_share = share(2 * pair), share(2 * pair + 1)
        kept[pair] = jnp.where(odd, odd_share, even_share)
        given = coded(jnp.where(odd, even_share, odd_share), split)
        size = given.shape[0]
        for group in range(groups):
            first = (pair * groups + group) * size
            message[first : first + size, :] = given[:, group * 128 : group * 128 + 128]


def halve_body(split_in, split_out, owner_bit, at_bit, me, mine, arrived, sent, kept):
    side = (me[0] >> owner_bit) % 2
    size, lanes = mine.shape[1:]
    groups = lanes // 128

    def total(at):
        if len(arrived.shape) == 3:
            return mine[at] + decoded(arrived[at], split_in)
        parts = []
        for group in range(groups):
            rows = size + split_in
            first = pl.multiple_of((at * groups + group) * rows, 8)
            parts.append(decoded(arrived[pl.ds(first, rows), :], split_in))
        return mine[at] + jnp.concatenate(parts, axis=1)

    for at in range(sent.shape[0]):
        high, low = at >> at_bit, at & ((1 << at_bit) - 1)
        keep = ((2 * high + side) << at_bit) + low
        give = ((2 * high + 1 - side) << at_bit) + low
        sent[at] = coded(total(give), split_out)
        kept[at] = total(keep)


def others_of(place, places):
    return [place ^ away for away in [*range(places // 2, places), *range(1, places // 2)]]


def spread_body(split_in, owner_bits, me, mine, arrived, kept, *sent):
    place = 0
    for bit in owner_bits:
        place = 2 * place + (me[0] >> bit) % 2
    kept[...] = mine[place] + decoded(arrived[place], split_in)
    for there, out in zip(others_of(place, mine.shape[0]), sent):
        out[...] = (mine[there] + decoded(arrived[there], split_in)).astype(BF16)


def finish_body(scale, sizes, mine, *refs):
    arrived, (grad_one, grad_two) = refs[:-2], refs[-2:]
    total = mine[...]
    for part in arrived:
        total = total + part[...].astype(F32)
    total = total * scale
    half = total.shape[1]
    first = 0
    for size, out in zip(sizes, (grad_one, grad_two)):
        blocks = (total[first : first + size], total[first + size : first + 2 * size])
        first += 2 * size
        for tap in range(9):
            for depth, group, side in ((0, 9 + tap // 2, tap % 2), (1, tap, 0), (2, tap, 1)):
                lane = group * 128 + side * 64
                block, lane = (blocks[0], lane) if lane < half else (blocks[1], lane - half)
                out[depth * 9 + tap] = block[:, lane : lane + 64]


def output_rows(columns, blocks, act_windows, taps, far, output, sems):
    copies = []
    for at, (start, size) in enumerate(blocks):
        value = window_dot(act_windows, taps, start, columns, NN, size)
        here = slice(start - blocks[0][0], start - blocks[0][0] + size)
        output[0, here, :] = value[:, :128]
        output[1, here, :] = value[:, 128:]
        copies.append(
            pltpu.make_async_copy(
                output.at[:, here, :], far.at[:, start : start + size, :], sems.at[at]
            )
        )
        copies[-1].start()
    return copies


def output_first_body(
    columns, blocks, act_windows, taps, grad, begun, far, own_windows, output, sems
):
    copies = output_rows(columns, blocks, act_windows, taps, far, output, sems)

    def fill(i, carry):
        start = pl.multiple_of(i * STEP, STEP)
        chunk = grad[pl.ds(start, STEP), :].astype(F32)
        fill_windows(own_windows, start, 0, chunk, columns, 128)
        return carry

    clear_edges(own_windows, columns)
    lax.fori_loop(0, grad.shape[0] // STEP, fill, 0)
    for copy in copies:
        copy.wait()


def output_rest_body(columns, blocks, act_windows, taps, begun, far, output, sems):
    for copy in output_rows(columns, blocks, act_windows, taps, far, output, sems):
        copy.wait()


def grad_volume_body(
    columns, me, own_windows, message, outer, taps, far, side_windows, output, sems
):
    half = outer.shape[0]
    odd = me[0] % 2 == 1
    before = message.shape[0] - half

    def fill(i, carry):
        start = pl.multiple_of(i * STEP, STEP)
        near = message[pl.ds(before + start, STEP), :].astype(F32)
        below, above = by_side(odd, near, outer[pl.ds(start, STEP), :].astype(F32))
        for first, side in zip((start, start + half), unpacked(above, below)):
            fill_windows(side_windows, first, 0, side, columns, 128)
        return carry

    clear_edges(side_windows, columns)
    lax.fori_loop(0, half // STEP, fill, 0)
    copies = []
    for at, (start, size) in enumerate(row_blocks(0, output.shape[1])):
        rows = slice(start, start + size + 2 * columns)
        rows = jnp.concatenate([own_windows[rows, :], side_windows[rows, :]], axis=1)
        terms = jnp.dot(rows, taps[...], preferred_element_type=F32)
        value = terms[:size, :128]
        value = value + terms[columns : columns + size, 128:256]
        value = value + terms[2 * columns : 2 * columns + size, 256:]
        here = slice(start, start + size)
        output[0, here, :] = value[:, :64]
        output[1, here, :] = value[:, 64:]
        copies.append(
            pltpu.make_async_copy(output.at[:, here, :], far.at[:, here, :], sems.at[at])
        )
        copies[-1].start()
    for copy in copies:
        copy.wait()


def shards(volume, weight_one, weight_two, cotangent):
    count = lax.axis_size("space")
    planes, rows, columns, channels = volume.shape
    cells = rows * columns
    scale = 1.0 / math.sqrt(planes * count * cells)
    mid, wide = weight_two.shape[3], weight_two.shape[4]
    me = lax.axis_index("space").astype(jnp.int32).reshape(1)
    shape = jax.ShapeDtypeStruct
    flat, pack = shape((cells, 128), BF16), shape((cells // 2, 128), BF16)
    slab = (cells + 2 * columns, 768)
    windows = pltpu.VMEM(slab, BF16)
    lanes = 14 * 64
    split = 2 * mid // count
    chunk = 2 * (mid + wide) // count

    within = [(i, i ^ 1) for i in range(count)]
    across = [(i, i + 1) for i in range(1, count - 1, 2)]
    across += [(j, i) for i, j in across]

    volume = volume.reshape(planes, cells, channels)
    cotangent = cotangent.reshape(planes, cells, wide)
    weight_one = weight_one.reshape(27, channels, mid)
    weight_two = weight_two.reshape(27, mid, wide)
    one_flops = 2 * planes * cells * 27 * channels * mid
    two_flops = 2 * planes * cells * 27 * mid * wide

    dma = pltpu.SemaphoreType.DMA
    far_one, far_two, far_volume, far_cotangent = (
        pltpu.with_memory_space_constraint(x, pltpu.HBM)
        for x in (weight_one, weight_two, volume, cotangent)
    )
    own, = call(
        pack_body, (flat,), (far_volume,),
        (pltpu.VMEM((planes, cells, channels), BF16), dma((4,))),
        name="pack_volume", apart=(0,),
    )
    vol_outer = lax.ppermute(own, "space", across)
    vol_inner = lax.ppermute(own, "space", within)
    terms, inner, outer, turned = call(
        functools.partial(leave_body, columns),
        (
            shape((cells, 128), F32), flat, pack, shape((256, cells), BF16),
        ),
        (me, far_cotangent, far_two),
        (
            windows, pltpu.VMEM((256, 3 * 768), BF16), pltpu.VMEM(cotangent.shape, BF16),
            pltpu.VMEM(weight_two.shape, BF16), dma((4,)), dma,
        ),
        two_flops, "grad_act_terms", (0,), (1, 2),
    )
    own, terms = lax.optimization_barrier((own, terms))
    third = shape((slab[0], 384), BF16)
    own_windows, inner_windows, part, outer_taps = call(
        functools.partial(prepare_body, columns),
        (third, third, shape((cells, 256), F32), shape((9 * 128, 256), BF16)),
        (me, own, vol_inner, far_one),
        (pltpu.VMEM((2 * 9 * 128, 256), BF16), pltpu.VMEM(weight_one.shape, BF16), dma),
        one_flops, "prepare", (0,), (3,),
    )
    back_taps, out_taps = call(
        layouts_body, (shape((768, 3 * 128), BF16), shape((9 * 256, 256), BF16)),
        (weight_one, weight_two), (pltpu.VMEM((3 * 128, 768), BF16),), one_flops // 8, "layouts",
    )
    inner, outer, part, back_taps, out_taps = lax.optimization_barrier(
        (inner, outer, part, back_taps, out_taps)
    )
    terms_outer = lax.ppermute(outer, "space", across)
    terms_inner = lax.ppermute(inner, "space", within)
    act_windows, slope, side_windows = call(
        functools.partial(hidden_body, columns, count),
        (shape(slab, BF16), shape((cells, 128), F32), third),
        (me, vol_outer, part, outer_taps, inner_windows),
        (pltpu.VMEM((slab[0], 384), BF16),), 2 * one_flops, "hidden", (0,),
    )
    half = cells // 2
    early, middle = [(0, BLOCK)], [(BLOCK, BLOCK), (half, BLOCK // 2)]
    late = [(half + BLOCK // 2, BLOCK), (cells - BLOCK // 2, BLOCK // 2)]
    whole = shape((planes, cells, wide), F32)
    terms_two, output = call(
        functools.partial(grad_two_body, columns, early),
        (shape((wide, 2 * lanes), F32), whole),
        (act_windows, turned, out_taps),
        (pltpu.VMEM((planes, BLOCK, wide), F32), dma((1,))),
        two_flops, "grad_two_terms", (), (), (1,),
    )
    groups = lanes // 128
    grad_hidden, outer, message, kept = call(
        functools.partial(grad_one_body, columns, count),
        (
            flat, pack,
            shape((count // 2 * groups * (chunk + split) + cells // 2, 128), BF16),
            shape((count // 2, chunk, lanes), F32),
        ),
        (
            me, own_windows, side_windows, terms, terms_inner, terms_outer, slope, terms_two,
        ),
        (pltpu.VMEM((128, cells), BF16), pltpu.VMEM((mid, 2 * lanes), F32)),
        one_flops, "grad_one_terms", (0,),
    )
    message = lax.ppermute(message, "space", within)
    output, back_windows = call(
        functools.partial(output_first_body, columns, middle),
        (whole, third),
        (act_windows, out_taps, grad_hidden, output),
        (pltpu.VMEM((planes, BLOCK + BLOCK // 2, wide), F32), dma((2,))),
        two_flops, "output_first", (), (3,), (0,), {3: 0},
    )
    message, output, back_windows = lax.optimization_barrier((message, output, back_windows))
    def halve(bits, bit, split_in, split_out, kept, arrived):
        left = 2 ** (len(bits) - 1)
        sent, kept = call(
            functools.partial(halve_body, split_in, split_out, bit, bits[::-1].index(bit)),
            (shape((left, chunk + split_out, lanes), BF16), shape((left, chunk, lanes), F32)),
            (me, kept, arrived), name="halve", smem=(0,),
        )
        return [b for b in bits if b != bit], sent, kept

    bits = list(range(count.bit_length() - 2, 0, -1))
    bits, sent, kept = halve(bits, 2, split, 0, kept, message)
    sent, act_windows, outer = lax.optimization_barrier((sent, act_windows, outer))
    arrived = lax.ppermute(sent, "space", [(i, i ^ 4) for i in range(count)])
    grad_outer = lax.ppermute(outer, "space", across)
    output, = call(
        functools.partial(output_rest_body, columns, late),
        (whole,),
        (act_windows, out_taps, output),
        (pltpu.VMEM((planes, BLOCK + BLOCK // 2, wide), F32), dma((2,))),
        two_flops, "output_rest", (), (2,), (0,), {2: 0},
    )
    others = 2 ** len(bits) - 1
    mine, *sent = call(
        functools.partial(spread_body, 0, bits),
        (shape((chunk, lanes), F32), *[shape((chunk, lanes), BF16)] * others),
        (me, kept, arrived), flops=16 * two_flops, name="spread", smem=(0,),
    )
    sent, output, back_windows = lax.optimization_barrier((sent, output, back_windows))
    arrived = []
    for at, part in zip(others_of(0, others + 1), sent):
        away = sum((at >> i & 1) << bit for i, bit in enumerate(bits[::-1]))
        arrived.append(lax.ppermute(part, "space", [(i, i ^ away) for i in range(count)]))
    grad_volume, = call(
        functools.partial(grad_volume_body, columns),
        (shape((planes, cells, channels), F32),),
        (me, back_windows, message, grad_outer, back_taps),
        (
            pltpu.VMEM((slab[0], 384), BF16), pltpu.VMEM((planes, cells, channels), F32),
            dma((cells // BLOCK + 1,)),
        ),
        one_flops, "grad_volume", (0,), (), (0,),
    )
    mine, grad_volume = lax.optimization_barrier((mine, grad_volume))
    grad_one, grad_two = call(
        functools.partial(finish_body, scale, (mid // count, wide // count)),
        (shape((27, mid // count, channels), F32), shape((27, wide // count, mid), F32)),
        (mine, *arrived), name="finish",
    )
    return (
        output.reshape(planes, rows, columns, wide),
        grad_volume.reshape(planes, rows, columns, channels),
        jnp.swapaxes(grad_one, 1, 2).reshape(3, 3, 3, channels, mid // count),
        jnp.swapaxes(grad_two, 1, 2).reshape(3, 3, 3, mid, wide // count),
    )


def solution(mesh):
    cells = P(("groups", "space"), None, None, None)
    kernel = P("groups", None, None, None, "space")
    return jax.shard_map(
        shards,
        mesh=mesh,
        in_specs=(cells, P(), P(), cells),
        out_specs=(cells, cells, kernel, kernel),
        check_vma=False,
    )
```

```python
import functools
import math

import jax
import jax.numpy as jnp
from jax import lax
from jax.experimental import pallas as pl
from jax.experimental.pallas import tpu as pltpu
from jax.sharding import PartitionSpec as P

F32, BF16 = jnp.float32, jnp.bfloat16
STEP, BLOCK = 256, 512
VMEM_LIMIT = 16 * 2**20
NN = (((1,), (0,)), ((), ()))
NT = (((1,), (1,)), ((), ()))

PLANES = (0, 1, 2, -1)


def depth_tap(source, target):
    tap = source - target + 1
    return tap if 0 <= tap <= 2 else None


def call(body, outs, ins, scratch=(), flops=0, name=None, smem=(), apart=(), far=(), alias=None):
    moved = sum(math.prod(s.shape) * s.dtype.itemsize for s in (*outs, *ins))
    return pl.pallas_call(
        body,
        out_shape=list(outs),
        in_specs=[
            pl.BlockSpec(
                memory_space=pltpu.SMEM if i in smem else pl.ANY if i in apart else pltpu.VMEM
            )
            for i in range(len(ins))
        ],
        out_specs=[
            pl.BlockSpec(memory_space=pl.ANY if i in far else pltpu.VMEM) for i in range(len(outs))
        ],
        input_output_aliases=alias or {},
        scratch_shapes=list(scratch),
        compiler_params=pltpu.CompilerParams(vmem_limit_bytes=VMEM_LIMIT),
        cost_estimate=pl.CostEstimate(flops=flops, bytes_accessed=moved, transcendentals=0),
        name=name,
    )(*ins)


def lanes_low(x):
    return lax.broadcasted_iota(jnp.int32, x.shape, 1) < 64


def swap(x):
    return pltpu.roll(x, 64, 1)


def pick(low, high):
    return jnp.where(lanes_low(low), low, high)


def fill_windows(windows, start, lane, chunk, columns, stride):
    size = chunk.shape[0]
    column = lax.broadcasted_iota(jnp.int32, chunk.shape, 0) % columns
    before = jnp.where(column == 0, 0.0, pltpu.roll(chunk, 1, 0))
    after = jnp.where(column == columns - 1, 0.0, pltpu.roll(chunk, size - 1, 0))
    at = pl.ds(pl.multiple_of(columns + start, 32), size)
    for tap, part in enumerate((before, chunk, after)):
        first = tap * stride + lane
        windows[at, first : first + chunk.shape[1]] = part.astype(BF16)


def clear_edges(windows, columns):
    rows, lanes = windows.shape
    windows[0:columns, :] = jnp.zeros((columns, lanes), BF16)
    windows[rows - columns : rows, :] = jnp.zeros((columns, lanes), BF16)


def row_windows(windows, start, columns, size=BLOCK):
    return [
        windows[start + tap * columns : start + tap * columns + size, :] for tap in range(3)
    ]


def window_dot(windows, weights, start, columns, dims, size=BLOCK):
    rows = jnp.concatenate(row_windows(windows, start, columns, size), axis=1)
    return lax.dot_general(rows, weights[...], dims, preferred_element_type=F32)


def row_blocks(first, last):
    blocks = [(start, BLOCK) for start in range(first, last - BLOCK, BLOCK)]
    return blocks + [(last - BLOCK, BLOCK // 2), (last - BLOCK // 2, BLOCK // 2)]


def packed(low, high):
    return pick(low, swap(high)), pick(swap(low), high)


def unpacked(first, second):
    return packed(first, second)


def by_side(odd, inner, outer):
    return jnp.where(odd, inner, outer), jnp.where(odd, outer, inner)


def pieces_of(source, target, sems, parts):
    size = target.shape[1] // parts
    return [
        pltpu.make_async_copy(
            source.at[:, pl.ds(i * size, size), :], target.at[:, pl.ds(i * size, size), :], sems.at[i]
        )
        for i in range(parts)
    ]


def pack_body(volume, own, held, sems):
    copies = pieces_of(volume, held, sems, sems.shape[0])
    size = own.shape[0] // len(copies)
    for copy in copies:
        copy.start()
    for i, copy in enumerate(copies):
        copy.wait()
        rows = slice(i * size, i * size + size)
        own[rows, :] = jnp.concatenate([held[0, rows, :], held[1, rows, :]], axis=1)


def leave_body(
    columns, me, far_cotangent, far_weight, own, inner, outer, turned,
    windows, taps, cotangent, weight, sems, sem,
):
    cells = own.shape[0]
    half = cells // 2
    odd = me[0] % 2 == 1
    fetch = pltpu.make_async_copy(far_weight, weight, sem)
    copies = pieces_of(far_cotangent, cotangent, sems, sems.shape[0])
    for copy in copies:
        copy.start()
    fetch.start()
    clear_edges(windows, columns)
    size = cells // len(copies)
    for at, copy in enumerate(copies):
        copy.wait()

        def fill(i, carry):
            start = pl.multiple_of(at * size + i * STEP, STEP)
            for plane in range(2):
                chunk = cotangent[plane, pl.ds(start, STEP), :].astype(F32)
                fill_windows(windows, start, plane * 128, chunk, columns, 256)
            return carry

        lax.fori_loop(0, size // STEP, fill, 0)
    fetch.wait()
    for row in range(3):
        for column in range(3):
            for source in range(2):
                first = row * 768 + column * 256 + source * 128
                for at, target in enumerate(PLANES):
                    depth = depth_tap(source, target)
                    taps[at * 64 : at * 64 + 64, first : first + 128] = (
                        jnp.zeros((64, 128), BF16)
                        if depth is None
                        else weight[(2 - depth) * 9 + (2 - row) * 3 + 2 - column]
                    )
    for start in range(0, half, BLOCK):
        sides = []
        for first in (start, start + half):
            term = window_dot(windows, taps, first, columns, NT)
            own[first : first + BLOCK, :] = term[:, :128]
            sides.append(term[:, 128:])
        upper, lower = packed(*sides)
        near = jnp.where(odd, lower, upper)
        head = near.astype(BF16)
        inner[start : start + BLOCK, :] = head
        inner[half + start : half + start + BLOCK, :] = (near - head.astype(F32)).astype(BF16)
        outer[start : start + BLOCK, :] = jnp.where(odd, upper, lower).astype(BF16)
    for plane in range(2):
        turn(cotangent.at[plane], turned, plane * 128)


def prepare_body(
    columns, me, own, inner, far_weight, own_windows, inner_windows, hidden, outer_taps,
    taps, weight, sem,
):
    fetch = pltpu.make_async_copy(far_weight, weight, sem)
    fetch.start()
    odd = me[0] % 2 == 1

    def fill(i, carry):
        start = pl.multiple_of(i * STEP, STEP)
        rows = pl.ds(start, STEP)
        fill_windows(own_windows, start, 0, own[rows, :].astype(F32), columns, 128)
        fill_windows(inner_windows, start, 0, inner[rows, :].astype(F32), columns, 128)
        return carry

    clear_edges(own_windows, columns)
    clear_edges(inner_windows, columns)
    lax.fori_loop(0, own.shape[0] // STEP, fill, 0)
    fetch.wait()
    zero = jnp.zeros((64, 64), BF16)
    for tap in range(9):

        def kernel_rows(source):
            depths = [depth_tap(source, target) for target in PLANES]
            parts = [zero if d is None else weight[d * 9 + tap] for d in depths]
            return jnp.concatenate(parts, axis=1)

        for at in range(2):
            rows = slice(tap * 128 + at * 64, tap * 128 + at * 64 + 64)
            taps[rows, :] = kernel_rows(at)
            upper, lower = kernel_rows(2 + at).astype(F32), kernel_rows(at - 2).astype(F32)
            first = 9 * 128 + rows.start
            taps[first : first + 64, :] = jnp.where(odd, lower, upper).astype(BF16)
            outer_taps[rows, :] = jnp.where(odd, upper, lower).astype(BF16)
    for start in range(0, own.shape[0], BLOCK):
        rows = row_windows(own_windows, start, columns) + row_windows(inner_windows, start, columns)
        hidden[start : start + BLOCK, :] = jnp.dot(
            jnp.concatenate(rows, axis=1), taps[...], preferred_element_type=F32
        )


def layouts_body(weight, weight_two, back_taps, out_taps, turned_taps):
    zero = jnp.zeros((64, 64), BF16)
    for row in range(3):
        for column in range(3):
            tap = row * 3 + column
            for plane in range(2):
                depths = [depth_tap(source, plane) for source in PLANES]
                parts = [zero if d is None else weight[(2 - d) * 9 + 8 - tap] for d in depths]
                at = row * 128 + plane * 64
                for pair in range(2):
                    first = pair * 384 + column * 128
                    turned_taps[at : at + 64, first : first + 128] = jnp.concatenate(
                        parts[2 * pair : 2 * pair + 2], axis=1
                    )
    back_taps[...] = turned_taps[...].astype(F32).T.astype(BF16)
    for tap in range(9):
        for at, source in enumerate(PLANES):
            first = tap * 256 + at * 64
            for plane in range(2):
                depth = depth_tap(source, plane)
                out_taps[first : first + 64, plane * 128 : plane * 128 + 128] = (
                    jnp.zeros((64, 128), BF16) if depth is None else weight_two[depth * 9 + tap]
                )


def hidden_body(
    columns, count, me, outer, part, outer_taps, inner_windows, act_windows, slope, side_windows,
    outer_windows,
):
    cells = outer.shape[0]

    def fill(i, carry):
        start = pl.multiple_of(i * STEP, STEP)
        chunk = outer[pl.ds(start, STEP), :].astype(F32)
        fill_windows(outer_windows, start, 0, chunk, columns, 128)
        return carry

    clear_edges(outer_windows, columns)
    clear_edges(act_windows, columns)
    lax.fori_loop(0, cells // STEP, fill, 0)
    from_inner = lax.broadcasted_iota(jnp.int32, (16, 128), 1) // 64 == me[0] % 2
    from_inner = jnp.where(from_inner, 1.0, 0.0).astype(BF16)[:1]
    for tap in range(3):
        at = slice(tap * 128, tap * 128 + 128)
        side_windows[:, at] = (
            inner_windows[:, at] * from_inner + outer_windows[:, at] * (1 - from_inner)
        )
    lanes = lax.broadcasted_iota(jnp.int32, (BLOCK, 128), 1)
    edges = [jnp.where(me[0] == end, 0.0, 1.0).astype(F32) for end in (count - 1, 0)]
    inside = jnp.where(lanes < 64, edges[0], edges[1])
    for start in range(0, cells, BLOCK):
        hidden = part[start : start + BLOCK, :]
        hidden = hidden + window_dot(outer_windows, outer_taps, start, columns, NN)
        gate = jax.nn.sigmoid(hidden)
        act = (hidden * gate).astype(BF16).astype(F32)
        fill_windows(act_windows, start, 0, act[:, :128], columns, 256)
        fill_windows(act_windows, start, 128, act[:, 128:] * inside, columns, 256)
        hidden, gate = hidden[:, :128], gate[:, :128]
        slope[start : start + BLOCK, :] = gate * (1.0 + hidden * (1.0 - gate))


def kernel_terms(columns, out_channels, slices, turned, terms):
    for row in range(3):
        for column in range(3):
            tap = row * 3 + column
            product = jnp.dot(turned[...], slices(row, column), preferred_element_type=F32)
            first, second = product[:out_channels], product[out_channels:]
            terms[:, tap * 128 : tap * 128 + 128] = first[:, :128] + swap(
                pick(second[:, 128:], second[:, :128])
            )
            group = 9 + tap // 2
            here = slice(group * 128, group * 128 + 128)
            if tap % 2 == 0:
                terms[:, here] = swap(first[:, 128:]) + second[:, :128]
            else:
                terms[:, here] = pick(terms[:, here], first[:, 128:] + swap(second[:, :128]))


def turn(source, target, first):
    for start in range(0, source.shape[0], STEP):
        chunk = source[start : start + STEP, :].astype(F32)
        target[first : first + chunk.shape[1], start : start + STEP] = chunk.T.astype(BF16)


def grad_two_body(columns, blocks, act_windows, turned, taps, terms, far, output, sems):
    cells = turned.shape[1]
    copies = output_rows(columns, blocks, act_windows, taps, far, output, sems)

    def slices(row, column):
        rows = slice(row * columns, row * columns + cells)
        return act_windows[rows, column * 256 : column * 256 + 256]

    kernel_terms(columns, 128, slices, turned, terms)
    for copy in copies:
        copy.wait()


def coded(value, split):
    head = value.astype(BF16)
    if split == 0:
        return head
    rest = (value[:split] - head[:split].astype(F32)).astype(BF16)
    return jnp.concatenate([head, rest], axis=0)


def decoded(value, split):
    value = value.astype(F32)
    if split == 0:
        return value
    size = value.shape[0] - split
    parts = [value[:split] + value[size:]]
    if split < size:
        parts.append(value[split:size])
    return jnp.concatenate(parts, axis=0)


def grad_one_body(
    columns, count, me, own_windows, side_windows, act_terms, inner, outer, slope, other,
    grad, to_outer, message, kept, turned, terms,
):
    cells = grad.shape[0]
    odd = me[0] % 2 == 1
    before = message.shape[0] - cells // 2
    for start in range(0, cells // 2, STEP):
        low, high = slice(start, start + STEP), slice(start + cells // 2, start + cells // 2 + STEP)
        near = inner[low, :].astype(F32) + inner[high, :].astype(F32)
        arrived = unpacked(*by_side(odd, near, outer[low, :].astype(F32)))
        sides = []
        for rows, extra in zip((low, high), arrived):
            value = ((act_terms[rows, :] + extra) * slope[rows, :]).astype(BF16)
            grad[rows, :] = value
            value = value.astype(F32)
            turned[:, rows] = value.T.astype(BF16)
            sides.append(value)
        lower, upper = packed(*sides)
        message[before + start : before + start + STEP, :] = jnp.where(
            odd, lower, upper
        ).astype(BF16)
        to_outer[low, :] = jnp.where(odd, upper, lower).astype(BF16)
    def slices(row, column):
        rows = slice(row * columns, row * columns + cells)
        lanes = slice(column * 128, column * 128 + 128)
        return jnp.concatenate([own_windows[rows, lanes], side_windows[rows, lanes]], axis=1)

    kernel_terms(columns, 64, slices, turned, terms)
    half = terms.shape[1] // 2
    split = 2 * terms.shape[0] // count

    def share(owner):
        parts = []
        for source in (terms, other):
            each = source.shape[0] // count
            block = source[owner * each : owner * each + each, :]
            parts += [block[:, :half], block[:, half:]]
        return jnp.concatenate(parts, axis=0)

    groups = half // 128
    for pair in range(count // 2):
        even_share, odd_share = share(2 * pair), share(2 * pair + 1)
        kept[pair] = jnp.where(odd, odd_share, even_share)
        given = coded(jnp.where(odd, even_share, odd_share), split)
        size = given.shape[0]
        for group in range(groups):
            first = (pair * groups + group) * size
            message[first : first + size, :] = given[:, group * 128 : group * 128 + 128]


def halve_body(split_in, split_out, owner_bit, at_bit, me, mine, arrived, sent, kept):
    side = (me[0] >> owner_bit) % 2
    size, lanes = mine.shape[1:]
    groups = lanes // 128

    def total(at):
        if len(arrived.shape) == 3:
            return mine[at] + decoded(arrived[at], split_in)
        parts = []
        for group in range(groups):
            rows = size + split_in
            first = pl.multiple_of((at * groups + group) * rows, 8)
            parts.append(decoded(arrived[pl.ds(first, rows), :], split_in))
        return mine[at] + jnp.concatenate(parts, axis=1)

    for at in range(sent.shape[0]):
        high, low = at >> at_bit, at & ((1 << at_bit) - 1)
        keep = ((2 * high + side) << at_bit) + low
        give = ((2 * high + 1 - side) << at_bit) + low
        sent[at] = coded(total(give), split_out)
        kept[at] = total(keep)


def others_of(place, places):
    return [place ^ away for away in [*range(places // 2, places), *range(1, places // 2)]]


def spread_body(split_in, owner_bits, me, mine, arrived, kept, *sent):
    place = 0
    for bit in owner_bits:
        place = 2 * place + (me[0] >> bit) % 2
    kept[...] = mine[place] + decoded(arrived[place], split_in)
    for there, out in zip(others_of(place, mine.shape[0]), sent):
        out[...] = (mine[there] + decoded(arrived[there], split_in)).astype(BF16)


def finish_body(scale, sizes, mine, *refs):
    arrived, (grad_one, grad_two) = refs[:-2], refs[-2:]
    total = mine[...]
    for part in arrived:
        total = total + part[...].astype(F32)
    total = total * scale
    half = total.shape[1]
    first = 0
    for size, out in zip(sizes, (grad_one, grad_two)):
        blocks = (total[first : first + size], total[first + size : first + 2 * size])
        first += 2 * size
        for tap in range(9):
            for depth, group, side in ((0, 9 + tap // 2, tap % 2), (1, tap, 0), (2, tap, 1)):
                lane = group * 128 + side * 64
                block, lane = (blocks[0], lane) if lane < half else (blocks[1], lane - half)
                out[depth * 9 + tap] = block[:, lane : lane + 64]


def output_rows(columns, blocks, act_windows, taps, far, output, sems):
    copies = []
    for at, (start, size) in enumerate(blocks):
        value = window_dot(act_windows, taps, start, columns, NN, size)
        here = slice(start - blocks[0][0], start - blocks[0][0] + size)
        output[0, here, :] = value[:, :128]
        output[1, here, :] = value[:, 128:]
        copies.append(
            pltpu.make_async_copy(
                output.at[:, here, :], far.at[:, start : start + size, :], sems.at[at]
            )
        )
        copies[-1].start()
    return copies


def output_first_body(
    columns, blocks, act_windows, taps, grad, begun, far, own_windows, output, sems
):
    copies = output_rows(columns, blocks, act_windows, taps, far, output, sems)

    def fill(i, carry):
        start = pl.multiple_of(i * STEP, STEP)
        chunk = grad[pl.ds(start, STEP), :].astype(F32)
        fill_windows(own_windows, start, 0, chunk, columns, 128)
        return carry

    clear_edges(own_windows, columns)
    lax.fori_loop(0, grad.shape[0] // STEP, fill, 0)
    for copy in copies:
        copy.wait()


def output_rest_body(columns, blocks, act_windows, taps, begun, far, output, sems):
    for copy in output_rows(columns, blocks, act_windows, taps, far, output, sems):
        copy.wait()


def grad_volume_body(
    columns, me, own_windows, message, outer, taps, far, side_windows, output, sems
):
    half = outer.shape[0]
    odd = me[0] % 2 == 1
    before = message.shape[0] - half

    def fill(i, carry):
        start = pl.multiple_of(i * STEP, STEP)
        near = message[pl.ds(before + start, STEP), :].astype(F32)
        below, above = by_side(odd, near, outer[pl.ds(start, STEP), :].astype(F32))
        for first, side in zip((start, start + half), unpacked(above, below)):
            fill_windows(side_windows, first, 0, side, columns, 128)
        return carry

    clear_edges(side_windows, columns)
    lax.fori_loop(0, half // STEP, fill, 0)
    copies = []
    for at, (start, size) in enumerate(row_blocks(0, output.shape[1])):
        rows = slice(start, start + size + 2 * columns)
        rows = jnp.concatenate([own_windows[rows, :], side_windows[rows, :]], axis=1)
        terms = jnp.dot(rows, taps[...], preferred_element_type=F32)
        value = terms[:size, :128]
        value = value + terms[columns : columns + size, 128:256]
        value = value + terms[2 * columns : 2 * columns + size, 256:]
        here = slice(start, start + size)
        output[0, here, :] = value[:, :64]
        output[1, here, :] = value[:, 64:]
        copies.append(
            pltpu.make_async_copy(output.at[:, here, :], far.at[:, here, :], sems.at[at])
        )
        copies[-1].start()
    for copy in copies:
        copy.wait()


def shards(volume, weight_one, weight_two, cotangent):
    count = lax.axis_size("space")
    planes, rows, columns, channels = volume.shape
    cells = rows * columns
    scale = 1.0 / math.sqrt(planes * count * cells)
    mid, wide = weight_two.shape[3], weight_two.shape[4]
    me = lax.axis_index("space").astype(jnp.int32).reshape(1)
    shape = jax.ShapeDtypeStruct
    flat, pack = shape((cells, 128), BF16), shape((cells // 2, 128), BF16)
    slab = (cells + 2 * columns, 768)
    windows = pltpu.VMEM(slab, BF16)
    lanes = 14 * 64
    split = 2 * mid // count
    chunk = 2 * (mid + wide) // count

    within = [(i, i ^ 1) for i in range(count)]
    across = [(i, i + 1) for i in range(1, count - 1, 2)]
    across += [(j, i) for i, j in across]

    volume = volume.reshape(planes, cells, channels)
    cotangent = cotangent.reshape(planes, cells, wide)
    weight_one = weight_one.reshape(27, channels, mid)
    weight_two = weight_two.reshape(27, mid, wide)
    one_flops = 2 * planes * cells * 27 * channels * mid
    two_flops = 2 * planes * cells * 27 * mid * wide

    dma = pltpu.SemaphoreType.DMA
    far_one, far_two, far_volume, far_cotangent = (
        pltpu.with_memory_space_constraint(x, pltpu.HBM)
        for x in (weight_one, weight_two, volume, cotangent)
    )
    own, = call(
        pack_body, (flat,), (far_volume,),
        (pltpu.VMEM((planes, cells, channels), BF16), dma((4,))),
        name="pack_volume", apart=(0,),
    )
    vol_outer = lax.ppermute(own, "space", across)
    vol_inner = lax.ppermute(own, "space", within)
    terms, inner, outer, turned = call(
        functools.partial(leave_body, columns),
        (
            shape((cells, 128), F32), flat, pack, shape((256, cells), BF16),
        ),
        (me, far_cotangent, far_two),
        (
            windows, pltpu.VMEM((256, 3 * 768), BF16), pltpu.VMEM(cotangent.shape, BF16),
            pltpu.VMEM(weight_two.shape, BF16), dma((4,)), dma,
        ),
        two_flops, "grad_act_terms", (0,), (1, 2),
    )
    own, terms = lax.optimization_barrier((own, terms))
    third = shape((slab[0], 384), BF16)
    own_windows, inner_windows, part, outer_taps = call(
        functools.partial(prepare_body, columns),
        (third, third, shape((cells, 256), F32), shape((9 * 128, 256), BF16)),
        (me, own, vol_inner, far_one),
        (pltpu.VMEM((2 * 9 * 128, 256), BF16), pltpu.VMEM(weight_one.shape, BF16), dma),
        one_flops, "prepare", (0,), (3,),
    )
    back_taps, out_taps = call(
        layouts_body, (shape((768, 3 * 128), BF16), shape((9 * 256, 256), BF16)),
        (weight_one, weight_two), (pltpu.VMEM((3 * 128, 768), BF16),), one_flops // 8, "layouts",
    )
    inner, outer, part, back_taps, out_taps = lax.optimization_barrier(
        (inner, outer, part, back_taps, out_taps)
    )
    terms_outer = lax.ppermute(outer, "space", across)
    terms_inner = lax.ppermute(inner, "space", within)
    act_windows, slope, side_windows = call(
        functools.partial(hidden_body, columns, count),
        (shape(slab, BF16), shape((cells, 128), F32), third),
        (me, vol_outer, part, outer_taps, inner_windows),
        (pltpu.VMEM((slab[0], 384), BF16),), 2 * one_flops, "hidden", (0,),
    )
    half = cells // 2
    early, middle = [(0, BLOCK)], [(BLOCK, BLOCK), (half, BLOCK // 2)]
    late = [(half + BLOCK // 2, BLOCK), (cells - BLOCK // 2, BLOCK // 2)]
    whole = shape((planes, cells, wide), F32)
    terms_two, output = call(
        functools.partial(grad_two_body, columns, early),
        (shape((wide, 2 * lanes), F32), whole),
        (act_windows, turned, out_taps),
        (pltpu.VMEM((planes, BLOCK, wide), F32), dma((1,))),
        two_flops, "grad_two_terms", (), (), (1,),
    )
    groups = lanes // 128
    grad_hidden, outer, message, kept = call(
        functools.partial(grad_one_body, columns, count),
        (
            flat, pack,
            shape((count // 2 * groups * (chunk + split) + cells // 2, 128), BF16),
            shape((count // 2, chunk, lanes), F32),
        ),
        (
            me, own_windows, side_windows, terms, terms_inner, terms_outer, slope, terms_two,
        ),
        (pltpu.VMEM((128, cells), BF16), pltpu.VMEM((mid, 2 * lanes), F32)),
        one_flops, "grad_one_terms", (0,),
    )
    message = lax.ppermute(message, "space", within)
    output, back_windows = call(
        functools.partial(output_first_body, columns, middle),
        (whole, third),
        (act_windows, out_taps, grad_hidden, output),
        (pltpu.VMEM((planes, BLOCK + BLOCK // 2, wide), F32), dma((2,))),
        two_flops, "output_first", (), (3,), (0,), {3: 0},
    )
    message, output, back_windows = lax.optimization_barrier((message, output, back_windows))
    def halve(bits, bit, split_in, split_out, kept, arrived):
        left = 2 ** (len(bits) - 1)
        sent, kept = call(
            functools.partial(halve_body, split_in, split_out, bit, bits[::-1].index(bit)),
            (shape((left, chunk + split_out, lanes), BF16), shape((left, chunk, lanes), F32)),
            (me, kept, arrived), name="halve", smem=(0,),
        )
        return [b for b in bits if b != bit], sent, kept

    bits = list(range(count.bit_length() - 2, 0, -1))
    bits, sent, kept = halve(bits, 2, split, 0, kept, message)
    sent, act_windows, outer = lax.optimization_barrier((sent, act_windows, outer))
    arrived = lax.ppermute(sent, "space", [(i, i ^ 4) for i in range(count)])
    output, = call(
        functools.partial(output_rest_body, columns, late),
        (whole,),
        (act_windows, out_taps, output),
        (pltpu.VMEM((planes, BLOCK + BLOCK // 2, wide), F32), dma((2,))),
        two_flops, "output_rest", (), (2,), (0,), {2: 0},
    )
    outer, output = lax.optimization_barrier((outer, output))
    grad_outer = lax.ppermute(outer, "space", across)
    others = 2 ** len(bits) - 1
    mine, *sent = call(
        functools.partial(spread_body, 0, bits),
        (shape((chunk, lanes), F32), *[shape((chunk, lanes), BF16)] * others),
        (me, kept, arrived), flops=16 * two_flops, name="spread", smem=(0,),
    )
    sent, output, back_windows = lax.optimization_barrier((sent, output, back_windows))
    arrived = []
    for at, part in zip(others_of(0, others + 1), sent):
        away = sum((at >> i & 1) << bit for i, bit in enumerate(bits[::-1]))
        arrived.append(lax.ppermute(part, "space", [(i, i ^ away) for i in range(count)]))
    grad_volume, = call(
        functools.partial(grad_volume_body, columns),
        (shape((planes, cells, channels), F32),),
        (me, back_windows, message, grad_outer, back_taps),
        (
            pltpu.VMEM((slab[0], 384), BF16), pltpu.VMEM((planes, cells, channels), F32),
            dma((cells // BLOCK + 1,)),
        ),
        one_flops, "grad_volume", (0,), (), (0,),
    )
    mine, grad_volume = lax.optimization_barrier((mine, grad_volume))
    grad_one, grad_two = call(
        functools.partial(finish_body, scale, (mid // count, wide // count)),
        (shape((27, mid // count, channels), F32), shape((27, wide // count, mid), F32)),
        (mine, *arrived), name="finish",
    )
    return (
        output.reshape(planes, rows, columns, wide),
        grad_volume.reshape(planes, rows, columns, channels),
        jnp.swapaxes(grad_one, 1, 2).reshape(3, 3, 3, channels, mid // count),
        jnp.swapaxes(grad_two, 1, 2).reshape(3, 3, 3, mid, wide // count),
    )


def solution(mesh):
    cells = P(("groups", "space"), None, None, None)
    kernel = P("groups", None, None, None, "space")
    return jax.shard_map(
        shards,
        mesh=mesh,
        in_specs=(cells, P(), P(), cells),
        out_specs=(cells, cells, kernel, kernel),
        check_vma=False,
    )
```

```python
import functools
import math

import jax
import jax.numpy as jnp
from jax import lax
from jax.experimental import pallas as pl
from jax.experimental.pallas import tpu as pltpu
from jax.sharding import PartitionSpec as P

F32, BF16 = jnp.float32, jnp.bfloat16
STEP, BLOCK = 256, 512
VMEM_LIMIT = 16 * 2**20
NN = (((1,), (0,)), ((), ()))
NT = (((1,), (1,)), ((), ()))

PLANES = (0, 1, 2, -1)


def depth_tap(source, target):
    tap = source - target + 1
    return tap if 0 <= tap <= 2 else None


def call(body, outs, ins, scratch=(), flops=0, name=None, smem=(), apart=(), far=(), alias=None):
    moved = sum(math.prod(s.shape) * s.dtype.itemsize for s in (*outs, *ins))
    return pl.pallas_call(
        body,
        out_shape=list(outs),
        in_specs=[
            pl.BlockSpec(
                memory_space=pltpu.SMEM if i in smem else pl.ANY if i in apart else pltpu.VMEM
            )
            for i in range(len(ins))
        ],
        out_specs=[
            pl.BlockSpec(memory_space=pl.ANY if i in far else pltpu.VMEM) for i in range(len(outs))
        ],
        input_output_aliases=alias or {},
        scratch_shapes=list(scratch),
        compiler_params=pltpu.CompilerParams(vmem_limit_bytes=VMEM_LIMIT),
        cost_estimate=pl.CostEstimate(flops=flops, bytes_accessed=moved, transcendentals=0),
        name=name,
    )(*ins)


def lanes_low(x):
    return lax.broadcasted_iota(jnp.int32, x.shape, 1) < 64


def swap(x):
    return pltpu.roll(x, 64, 1)


def pick(low, high):
    return jnp.where(lanes_low(low), low, high)


def fill_windows(windows, start, lane, chunk, columns, stride):
    size = chunk.shape[0]
    column = lax.broadcasted_iota(jnp.int32, chunk.shape, 0) % columns
    before = jnp.where(column == 0, 0.0, pltpu.roll(chunk, 1, 0))
    after = jnp.where(column == columns - 1, 0.0, pltpu.roll(chunk, size - 1, 0))
    at = pl.ds(pl.multiple_of(columns + start, 32), size)
    for tap, part in enumerate((before, chunk, after)):
        first = tap * stride + lane
        windows[at, first : first + chunk.shape[1]] = part.astype(BF16)


def clear_edges(windows, columns):
    rows, lanes = windows.shape
    windows[0:columns, :] = jnp.zeros((columns, lanes), BF16)
    windows[rows - columns : rows, :] = jnp.zeros((columns, lanes), BF16)


def row_windows(windows, start, columns, size=BLOCK):
    return [
        windows[start + tap * columns : start + tap * columns + size, :] for tap in range(3)
    ]


def window_dot(windows, weights, start, columns, dims, size=BLOCK):
    rows = jnp.concatenate(row_windows(windows, start, columns, size), axis=1)
    return lax.dot_general(rows, weights[...], dims, preferred_element_type=F32)


def row_blocks(first, last):
    blocks = [(start, BLOCK) for start in range(first, last - BLOCK, BLOCK)]
    return blocks + [(last - BLOCK, BLOCK // 2), (last - BLOCK // 2, BLOCK // 2)]


def packed(low, high):
    return pick(low, swap(high)), pick(swap(low), high)


def unpacked(first, second):
    return packed(first, second)


def by_side(odd, inner, outer):
    return jnp.where(odd, inner, outer), jnp.where(odd, outer, inner)


def pieces_of(source, target, sems, parts):
    size = target.shape[1] // parts
    return [
        pltpu.make_async_copy(
            source.at[:, pl.ds(i * size, size), :], target.at[:, pl.ds(i * size, size), :], sems.at[i]
        )
        for i in range(parts)
    ]


def pack_body(volume, own, held, sems):
    copies = pieces_of(volume, held, sems, sems.shape[0])
    size = own.shape[0] // len(copies)
    for copy in copies:
        copy.start()
    for i, copy in enumerate(copies):
        copy.wait()
        rows = slice(i * size, i * size + size)
        own[rows, :] = jnp.concatenate([held[0, rows, :], held[1, rows, :]], axis=1)


def leave_body(
    columns, me, far_cotangent, far_weight, own, inner, outer, turned,
    windows, taps, cotangent, weight, sems, sem,
):
    cells = own.shape[0]
    half = cells // 2
    odd = me[0] % 2 == 1
    fetch = pltpu.make_async_copy(far_weight, weight, sem)
    copies = pieces_of(far_cotangent, cotangent, sems, sems.shape[0])
    for copy in copies:
        copy.start()
    fetch.start()
    clear_edges(windows, columns)
    size = cells // len(copies)
    for at, copy in enumerate(copies):
        copy.wait()

        def fill(i, carry):
            start = pl.multiple_of(at * size + i * STEP, STEP)
            for plane in range(2):
                chunk = cotangent[plane, pl.ds(start, STEP), :].astype(F32)
                fill_windows(windows, start, plane * 128, chunk, columns, 256)
            return carry

        lax.fori_loop(0, size // STEP, fill, 0)
    fetch.wait()
    for row in range(3):
        for column in range(3):
            for source in range(2):
                first = row * 768 + column * 256 + source * 128
                for at, target in enumerate(PLANES):
                    depth = depth_tap(source, target)
                    taps[at * 64 : at * 64 + 64, first : first + 128] = (
                        jnp.zeros((64, 128), BF16)
                        if depth is None
                        else weight[(2 - depth) * 9 + (2 - row) * 3 + 2 - column]
                    )
    for start in range(0, half, BLOCK):
        sides = []
        for first in (start, start + half):
            term = window_dot(windows, taps, first, columns, NT)
            own[first : first + BLOCK, :] = term[:, :128]
            sides.append(term[:, 128:])
        upper, lower = packed(*sides)
        near = jnp.where(odd, lower, upper)
        head = near.astype(BF16)
        inner[start : start + BLOCK, :] = head
        inner[half + start : half + start + BLOCK, :] = (near - head.astype(F32)).astype(BF16)
        outer[start : start + BLOCK, :] = jnp.where(odd, upper, lower).astype(BF16)
    for plane in range(2):
        turn(cotangent.at[plane], turned, plane * 128)


def prepare_body(
    columns, me, own, inner, far_weight, own_windows, inner_windows, hidden, outer_taps,
    taps, weight, sem,
):
    fetch = pltpu.make_async_copy(far_weight, weight, sem)
    fetch.start()
    odd = me[0] % 2 == 1

    def fill(i, carry):
        start = pl.multiple_of(i * STEP, STEP)
        rows = pl.ds(start, STEP)
        fill_windows(own_windows, start, 0, own[rows, :].astype(F32), columns, 128)
        fill_windows(inner_windows, start, 0, inner[rows, :].astype(F32), columns, 128)
        return carry

    clear_edges(own_windows, columns)
    clear_edges(inner_windows, columns)
    lax.fori_loop(0, own.shape[0] // STEP, fill, 0)
    fetch.wait()
    zero = jnp.zeros((64, 64), BF16)
    for tap in range(9):

        def kernel_rows(source):
            depths = [depth_tap(source, target) for target in PLANES]
            parts = [zero if d is None else weight[d * 9 + tap] for d in depths]
            return jnp.concatenate(parts, axis=1)

        for at in range(2):
            rows = slice(tap * 128 + at * 64, tap * 128 + at * 64 + 64)
            taps[rows, :] = kernel_rows(at)
            upper, lower = kernel_rows(2 + at).astype(F32), kernel_rows(at - 2).astype(F32)
            first = 9 * 128 + rows.start
            taps[first : first + 64, :] = jnp.where(odd, lower, upper).astype(BF16)
            outer_taps[rows, :] = jnp.where(odd, upper, lower).astype(BF16)
    for start in range(0, own.shape[0], BLOCK):
        rows = row_windows(own_windows, start, columns) + row_windows(inner_windows, start, columns)
        hidden[start : start + BLOCK, :] = jnp.dot(
            jnp.concatenate(rows, axis=1), taps[...], preferred_element_type=F32
        )


def layouts_body(weight, weight_two, back_taps, out_taps, turned_taps):
    zero = jnp.zeros((64, 64), BF16)
    for row in range(3):
        for column in range(3):
            tap = row * 3 + column
            for plane in range(2):
                depths = [depth_tap(source, plane) for source in PLANES]
                parts = [zero if d is None else weight[(2 - d) * 9 + 8 - tap] for d in depths]
                at = row * 128 + plane * 64
                for pair in range(2):
                    first = pair * 384 + column * 128
                    turned_taps[at : at + 64, first : first + 128] = jnp.concatenate(
                        parts[2 * pair : 2 * pair + 2], axis=1
                    )
    back_taps[...] = turned_taps[...].astype(F32).T.astype(BF16)
    for tap in range(9):
        for at, source in enumerate(PLANES):
            first = tap * 256 + at * 64
            for plane in range(2):
                depth = depth_tap(source, plane)
                out_taps[first : first + 64, plane * 128 : plane * 128 + 128] = (
                    jnp.zeros((64, 128), BF16) if depth is None else weight_two[depth * 9 + tap]
                )


def hidden_body(
    columns, count, me, outer, part, outer_taps, inner_windows, act_windows, slope, side_windows,
    outer_windows,
):
    cells = outer.shape[0]

    def fill(i, carry):
        start = pl.multiple_of(i * STEP, STEP)
        chunk = outer[pl.ds(start, STEP), :].astype(F32)
        fill_windows(outer_windows, start, 0, chunk, columns, 128)
        return carry

    clear_edges(outer_windows, columns)
    clear_edges(act_windows, columns)
    lax.fori_loop(0, cells // STEP, fill, 0)
    from_inner = lax.broadcasted_iota(jnp.int32, (16, 128), 1) // 64 == me[0] % 2
    from_inner = jnp.where(from_inner, 1.0, 0.0).astype(BF16)[:1]
    for tap in range(3):
        at = slice(tap * 128, tap * 128 + 128)
        side_windows[:, at] = (
            inner_windows[:, at] * from_inner + outer_windows[:, at] * (1 - from_inner)
        )
    lanes = lax.broadcasted_iota(jnp.int32, (BLOCK, 128), 1)
    edges = [jnp.where(me[0] == end, 0.0, 1.0).astype(F32) for end in (count - 1, 0)]
    inside = jnp.where(lanes < 64, edges[0], edges[1])
    for start in range(0, cells, BLOCK):
        hidden = part[start : start + BLOCK, :]
        hidden = hidden + window_dot(outer_windows, outer_taps, start, columns, NN)
        gate = jax.nn.sigmoid(hidden)
        act = (hidden * gate).astype(BF16).astype(F32)
        fill_windows(act_windows, start, 0, act[:, :128], columns, 256)
        fill_windows(act_windows, start, 128, act[:, 128:] * inside, columns, 256)
        hidden, gate = hidden[:, :128], gate[:, :128]
        slope[start : start + BLOCK, :] = gate * (1.0 + hidden * (1.0 - gate))


def kernel_terms(columns, out_channels, slices, turned, terms):
    for row in range(3):
        for column in range(3):
            tap = row * 3 + column
            product = jnp.dot(turned[...], slices(row, column), preferred_element_type=F32)
            first, second = product[:out_channels], product[out_channels:]
            terms[:, tap * 128 : tap * 128 + 128] = first[:, :128] + swap(
                pick(second[:, 128:], second[:, :128])
            )
            group = 9 + tap // 2
            here = slice(group * 128, group * 128 + 128)
            if tap % 2 == 0:
                terms[:, here] = swap(first[:, 128:]) + second[:, :128]
            else:
                terms[:, here] = pick(terms[:, here], first[:, 128:] + swap(second[:, :128]))


def turn(source, target, first):
    for start in range(0, source.shape[0], STEP):
        chunk = source[start : start + STEP, :].astype(F32)
        target[first : first + chunk.shape[1], start : start + STEP] = chunk.T.astype(BF16)


def grad_two_body(columns, blocks, act_windows, turned, taps, terms, far, output, sems):
    cells = turned.shape[1]
    copies = output_rows(columns, blocks, act_windows, taps, far, output, sems)

    def slices(row, column):
        rows = slice(row * columns, row * columns + cells)
        return act_windows[rows, column * 256 : column * 256 + 256]

    kernel_terms(columns, 128, slices, turned, terms)
    for copy in copies:
        copy.wait()


def coded(value, split):
    head = value.astype(BF16)
    if split == 0:
        return head
    rest = (value[:split] - head[:split].astype(F32)).astype(BF16)
    return jnp.concatenate([head, rest], axis=0)


def decoded(value, split):
    value = value.astype(F32)
    if split == 0:
        return value
    size = value.shape[0] - split
    parts = [value[:split] + value[size:]]
    if split < size:
        parts.append(value[split:size])
    return jnp.concatenate(parts, axis=0)


def grad_one_body(
    columns, count, me, own_windows, side_windows, act_terms, inner, outer, slope, other,
    grad, to_outer, message, kept, turned, terms,
):
    cells = grad.shape[0]
    odd = me[0] % 2 == 1
    before = message.shape[0] - cells // 2
    for start in range(0, cells // 2, STEP):
        low, high = slice(start, start + STEP), slice(start + cells // 2, start + cells // 2 + STEP)
        near = inner[low, :].astype(F32) + inner[high, :].astype(F32)
        arrived = unpacked(*by_side(odd, near, outer[low, :].astype(F32)))
        sides = []
        for rows, extra in zip((low, high), arrived):
            value = ((act_terms[rows, :] + extra) * slope[rows, :]).astype(BF16)
            grad[rows, :] = value
            value = value.astype(F32)
            turned[:, rows] = value.T.astype(BF16)
            sides.append(value)
        lower, upper = packed(*sides)
        message[before + start : before + start + STEP, :] = jnp.where(
            odd, lower, upper
        ).astype(BF16)
        to_outer[low, :] = jnp.where(odd, upper, lower).astype(BF16)
    def slices(row, column):
        rows = slice(row * columns, row * columns + cells)
        lanes = slice(column * 128, column * 128 + 128)
        return jnp.concatenate([own_windows[rows, lanes], side_windows[rows, lanes]], axis=1)

    kernel_terms(columns, 64, slices, turned, terms)
    half = terms.shape[1] // 2
    split = 2 * terms.shape[0] // count

    def share(owner):
        parts = []
        for source in (terms, other):
            each = source.shape[0] // count
            block = source[owner * each : owner * each + each, :]
            parts += [block[:, :half], block[:, half:]]
        return jnp.concatenate(parts, axis=0)

    groups = half // 128
    for pair in range(count // 2):
        even_share, odd_share = share(2 * pair), share(2 * pair + 1)
        kept[pair] = jnp.where(odd, odd_share, even_share)
        given = coded(jnp.where(odd, even_share, odd_share), split)
        size = given.shape[0]
        for group in range(groups):
            first = (pair * groups + group) * size
            message[first : first + size, :] = given[:, group * 128 : group * 128 + 128]


def halve_body(split_in, split_out, owner_bit, at_bit, me, mine, arrived, sent, kept):
    side = (me[0] >> owner_bit) % 2
    size, lanes = mine.shape[1:]
    groups = lanes // 128

    def total(at):
        if len(arrived.shape) == 3:
            return mine[at] + decoded(arrived[at], split_in)
        parts = []
        for group in range(groups):
            rows = size + split_in
            first = pl.multiple_of((at * groups + group) * rows, 8)
            parts.append(decoded(arrived[pl.ds(first, rows), :], split_in))
        return mine[at] + jnp.concatenate(parts, axis=1)

    for at in range(sent.shape[0]):
        high, low = at >> at_bit, at & ((1 << at_bit) - 1)
        keep = ((2 * high + side) << at_bit) + low
        give = ((2 * high + 1 - side) << at_bit) + low
        sent[at] = coded(total(give), split_out)
        kept[at] = total(keep)


def others_of(place, places):
    return [place ^ away for away in [*range(places // 2, places), *range(1, places // 2)]]


def spread_body(split_in, owner_bits, me, mine, arrived, kept, *sent):
    place = 0
    for bit in owner_bits:
        place = 2 * place + (me[0] >> bit) % 2
    kept[...] = mine[place] + decoded(arrived[place], split_in)
    for there, out in zip(others_of(place, mine.shape[0]), sent):
        out[...] = (mine[there] + decoded(arrived[there], split_in)).astype(BF16)


def finish_body(scale, sizes, mine, *refs):
    arrived, (grad_one, grad_two) = refs[:-2], refs[-2:]
    total = mine[...]
    for part in arrived:
        total = total + part[...].astype(F32)
    total = total * scale
    half = total.shape[1]
    first = 0
    for size, out in zip(sizes, (grad_one, grad_two)):
        blocks = (total[first : first + size], total[first + size : first + 2 * size])
        first += 2 * size
        for tap in range(9):
            for depth, group, side in ((0, 9 + tap // 2, tap % 2), (1, tap, 0), (2, tap, 1)):
                lane = group * 128 + side * 64
                block, lane = (blocks[0], lane) if lane < half else (blocks[1], lane - half)
                out[depth * 9 + tap] = block[:, lane : lane + 64]


def output_rows(columns, blocks, act_windows, taps, far, output, sems):
    copies = []
    for at, (start, size) in enumerate(blocks):
        value = window_dot(act_windows, taps, start, columns, NN, size)
        here = slice(start - blocks[0][0], start - blocks[0][0] + size)
        output[0, here, :] = value[:, :128]
        output[1, here, :] = value[:, 128:]
        copies.append(
            pltpu.make_async_copy(
                output.at[:, here, :], far.at[:, start : start + size, :], sems.at[at]
            )
        )
        copies[-1].start()
    return copies


def output_rest_body(
    columns, blocks, act_windows, taps, grad, begun, far, own_windows, output, sems
):
    copies = output_rows(columns, blocks, act_windows, taps, far, output, sems)

    def fill(i, carry):
        start = pl.multiple_of(i * STEP, STEP)
        chunk = grad[pl.ds(start, STEP), :].astype(F32)
        fill_windows(own_windows, start, 0, chunk, columns, 128)
        return carry

    clear_edges(own_windows, columns)
    lax.fori_loop(0, grad.shape[0] // STEP, fill, 0)
    for copy in copies:
        copy.wait()


def grad_volume_body(
    columns, me, own_windows, message, outer, taps, far, side_windows, output, sems
):
    half = outer.shape[0]
    odd = me[0] % 2 == 1
    before = message.shape[0] - half

    def fill(i, carry):
        start = pl.multiple_of(i * STEP, STEP)
        near = message[pl.ds(before + start, STEP), :].astype(F32)
        below, above = by_side(odd, near, outer[pl.ds(start, STEP), :].astype(F32))
        for first, side in zip((start, start + half), unpacked(above, below)):
            fill_windows(side_windows, first, 0, side, columns, 128)
        return carry

    clear_edges(side_windows, columns)
    lax.fori_loop(0, half // STEP, fill, 0)
    copies = []
    for at, (start, size) in enumerate(row_blocks(0, output.shape[1])):
        rows = slice(start, start + size + 2 * columns)
        rows = jnp.concatenate([own_windows[rows, :], side_windows[rows, :]], axis=1)
        terms = jnp.dot(rows, taps[...], preferred_element_type=F32)
        value = terms[:size, :128]
        value = value + terms[columns : columns + size, 128:256]
        value = value + terms[2 * columns : 2 * columns + size, 256:]
        here = slice(start, start + size)
        output[0, here, :] = value[:, :64]
        output[1, here, :] = value[:, 64:]
        copies.append(
            pltpu.make_async_copy(output.at[:, here, :], far.at[:, here, :], sems.at[at])
        )
        copies[-1].start()
    for copy in copies:
        copy.wait()


def shards(volume, weight_one, weight_two, cotangent):
    count = lax.axis_size("space")
    planes, rows, columns, channels = volume.shape
    cells = rows * columns
    scale = 1.0 / math.sqrt(planes * count * cells)
    mid, wide = weight_two.shape[3], weight_two.shape[4]
    me = lax.axis_index("space").astype(jnp.int32).reshape(1)
    shape = jax.ShapeDtypeStruct
    flat, pack = shape((cells, 128), BF16), shape((cells // 2, 128), BF16)
    slab = (cells + 2 * columns, 768)
    windows = pltpu.VMEM(slab, BF16)
    lanes = 14 * 64
    split = 2 * mid // count
    chunk = 2 * (mid + wide) // count

    within = [(i, i ^ 1) for i in range(count)]
    across = [(i, i + 1) for i in range(1, count - 1, 2)]
    across += [(j, i) for i, j in across]

    volume = volume.reshape(planes, cells, channels)
    cotangent = cotangent.reshape(planes, cells, wide)
    weight_one = weight_one.reshape(27, channels, mid)
    weight_two = weight_two.reshape(27, mid, wide)
    one_flops = 2 * planes * cells * 27 * channels * mid
    two_flops = 2 * planes * cells * 27 * mid * wide

    dma = pltpu.SemaphoreType.DMA
    far_one, far_two, far_volume, far_cotangent = (
        pltpu.with_memory_space_constraint(x, pltpu.HBM)
        for x in (weight_one, weight_two, volume, cotangent)
    )
    own, = call(
        pack_body, (flat,), (far_volume,),
        (pltpu.VMEM((planes, cells, channels), BF16), dma((4,))),
        name="pack_volume", apart=(0,),
    )
    vol_outer = lax.ppermute(own, "space", across)
    vol_inner = lax.ppermute(own, "space", within)
    terms, inner, outer, turned = call(
        functools.partial(leave_body, columns),
        (
            shape((cells, 128), F32), flat, pack, shape((256, cells), BF16),
        ),
        (me, far_cotangent, far_two),
        (
            windows, pltpu.VMEM((256, 3 * 768), BF16), pltpu.VMEM(cotangent.shape, BF16),
            pltpu.VMEM(weight_two.shape, BF16), dma((4,)), dma,
        ),
        two_flops, "grad_act_terms", (0,), (1, 2),
    )
    own, terms = lax.optimization_barrier((own, terms))
    third = shape((slab[0], 384), BF16)
    own_windows, inner_windows, part, outer_taps = call(
        functools.partial(prepare_body, columns),
        (third, third, shape((cells, 256), F32), shape((9 * 128, 256), BF16)),
        (me, own, vol_inner, far_one),
        (pltpu.VMEM((2 * 9 * 128, 256), BF16), pltpu.VMEM(weight_one.shape, BF16), dma),
        one_flops, "prepare", (0,), (3,),
    )
    back_taps, out_taps = call(
        layouts_body, (shape((768, 3 * 128), BF16), shape((9 * 256, 256), BF16)),
        (weight_one, weight_two), (pltpu.VMEM((3 * 128, 768), BF16),), one_flops // 8, "layouts",
    )
    inner, outer, part, back_taps, out_taps = lax.optimization_barrier(
        (inner, outer, part, back_taps, out_taps)
    )
    terms_outer = lax.ppermute(outer, "space", across)
    terms_inner = lax.ppermute(inner, "space", within)
    act_windows, slope, side_windows = call(
        functools.partial(hidden_body, columns, count),
        (shape(slab, BF16), shape((cells, 128), F32), third),
        (me, vol_outer, part, outer_taps, inner_windows),
        (pltpu.VMEM((slab[0], 384), BF16),), 2 * one_flops, "hidden", (0,),
    )
    early, rest = [(0, BLOCK)], row_blocks(BLOCK, cells)
    whole = shape((planes, cells, wide), F32)
    terms_two, output = call(
        functools.partial(grad_two_body, columns, early),
        (shape((wide, 2 * lanes), F32), whole),
        (act_windows, turned, out_taps),
        (pltpu.VMEM((planes, BLOCK, wide), F32), dma((1,))),
        two_flops, "grad_two_terms", (), (), (1,),
    )
    groups = lanes // 128
    grad_hidden, outer, message, kept = call(
        functools.partial(grad_one_body, columns, count),
        (
            flat, pack,
            shape((count // 2 * groups * (chunk + split) + cells // 2, 128), BF16),
            shape((count // 2, chunk, lanes), F32),
        ),
        (
            me, own_windows, side_windows, terms, terms_inner, terms_outer, slope, terms_two,
        ),
        (pltpu.VMEM((128, cells), BF16), pltpu.VMEM((mid, 2 * lanes), F32)),
        one_flops, "grad_one_terms", (0,),
    )
    message = lax.ppermute(message, "space", within)
    def halve(bits, bit, split_in, split_out, kept, arrived):
        left = 2 ** (len(bits) - 1)
        sent, kept = call(
            functools.partial(halve_body, split_in, split_out, bit, bits[::-1].index(bit)),
            (shape((left, chunk + split_out, lanes), BF16), shape((left, chunk, lanes), F32)),
            (me, kept, arrived), name="halve", smem=(0,),
        )
        return [b for b in bits if b != bit], sent, kept

    bits = list(range(count.bit_length() - 2, 0, -1))
    bits, sent, kept = halve(bits, 2, split, 0, kept, message)
    sent, act_windows = lax.optimization_barrier((sent, act_windows))
    arrived = lax.ppermute(sent, "space", [(i, i ^ 4) for i in range(count)])
    grad_outer = lax.ppermute(outer, "space", across)
    output, back_windows = call(
        functools.partial(output_rest_body, columns, rest),
        (whole, third),
        (act_windows, out_taps, grad_hidden, output),
        (pltpu.VMEM((planes, cells - BLOCK, wide), F32), dma((len(rest),))),
        two_flops, "output_rest", (), (3,), (0,), {3: 0},
    )
    others = 2 ** len(bits) - 1
    mine, *sent = call(
        functools.partial(spread_body, 0, bits),
        (shape((chunk, lanes), F32), *[shape((chunk, lanes), BF16)] * others),
        (me, kept, arrived), name="spread", smem=(0,),
    )
    sent, output, back_windows = lax.optimization_barrier((sent, output, back_windows))
    arrived = []
    for at, part in zip(others_of(0, others + 1), sent):
        away = sum((at >> i & 1) << bit for i, bit in enumerate(bits[::-1]))
        arrived.append(lax.ppermute(part, "space", [(i, i ^ away) for i in range(count)]))
    grad_volume, = call(
        functools.partial(grad_volume_body, columns),
        (shape((planes, cells, channels), F32),),
        (me, back_windows, message, grad_outer, back_taps),
        (
            pltpu.VMEM((slab[0], 384), BF16), pltpu.VMEM((planes, cells, channels), F32),
            dma((cells // BLOCK + 1,)),
        ),
        one_flops, "grad_volume", (0,), (), (0,),
    )
    mine, grad_volume = lax.optimization_barrier((mine, grad_volume))
    grad_one, grad_two = call(
        functools.partial(finish_body, scale, (mid // count, wide // count)),
        (shape((27, mid // count, channels), F32), shape((27, wide // count, mid), F32)),
        (mine, *arrived), name="finish",
    )
    return (
        output.reshape(planes, rows, columns, wide),
        grad_volume.reshape(planes, rows, columns, channels),
        jnp.swapaxes(grad_one, 1, 2).reshape(3, 3, 3, channels, mid // count),
        jnp.swapaxes(grad_two, 1, 2).reshape(3, 3, 3, mid, wide // count),
    )


def solution(mesh):
    cells = P(("groups", "space"), None, None, None)
    kernel = P("groups", None, None, None, "space")
    return jax.shard_map(
        shards,
        mesh=mesh,
        in_specs=(cells, P(), P(), cells),
        out_specs=(cells, cells, kernel, kernel),
        check_vma=False,
    )
```

```python
import functools
import math

import jax
import jax.numpy as jnp
from jax import lax
from jax.experimental import pallas as pl
from jax.experimental.pallas import tpu as pltpu
from jax.sharding import PartitionSpec as P

F32, BF16 = jnp.float32, jnp.bfloat16
STEP, BLOCK = 256, 512
VMEM_LIMIT = 16 * 2**20
NN = (((1,), (0,)), ((), ()))
NT = (((1,), (1,)), ((), ()))

PLANES = (0, 1, 2, -1)


def depth_tap(source, target):
    tap = source - target + 1
    return tap if 0 <= tap <= 2 else None


def call(body, outs, ins, scratch=(), flops=0, name=None, smem=(), apart=(), far=(), alias=None):
    moved = sum(math.prod(s.shape) * s.dtype.itemsize for s in (*outs, *ins))
    return pl.pallas_call(
        body,
        out_shape=list(outs),
        in_specs=[
            pl.BlockSpec(
                memory_space=pltpu.SMEM if i in smem else pl.ANY if i in apart else pltpu.VMEM
            )
            for i in range(len(ins))
        ],
        out_specs=[
            pl.BlockSpec(memory_space=pl.ANY if i in far else pltpu.VMEM) for i in range(len(outs))
        ],
        input_output_aliases=alias or {},
        scratch_shapes=list(scratch),
        compiler_params=pltpu.CompilerParams(vmem_limit_bytes=VMEM_LIMIT),
        cost_estimate=pl.CostEstimate(flops=flops, bytes_accessed=moved, transcendentals=0),
        name=name,
    )(*ins)


def lanes_low(x):
    return lax.broadcasted_iota(jnp.int32, x.shape, 1) < 64


def swap(x):
    return pltpu.roll(x, 64, 1)


def pick(low, high):
    return jnp.where(lanes_low(low), low, high)


def fill_windows(windows, start, lane, chunk, columns, stride):
    size = chunk.shape[0]
    column = lax.broadcasted_iota(jnp.int32, chunk.shape, 0) % columns
    before = jnp.where(column == 0, 0.0, pltpu.roll(chunk, 1, 0))
    after = jnp.where(column == columns - 1, 0.0, pltpu.roll(chunk, size - 1, 0))
    at = pl.ds(pl.multiple_of(columns + start, 32), size)
    for tap, part in enumerate((before, chunk, after)):
        first = tap * stride + lane
        windows[at, first : first + chunk.shape[1]] = part.astype(BF16)


def clear_edges(windows, columns):
    rows, lanes = windows.shape
    windows[0:columns, :] = jnp.zeros((columns, lanes), BF16)
    windows[rows - columns : rows, :] = jnp.zeros((columns, lanes), BF16)


def row_windows(windows, start, columns, size=BLOCK):
    return [
        windows[start + tap * columns : start + tap * columns + size, :] for tap in range(3)
    ]


def window_dot(windows, weights, start, columns, dims, size=BLOCK):
    rows = jnp.concatenate(row_windows(windows, start, columns, size), axis=1)
    return lax.dot_general(rows, weights[...], dims, preferred_element_type=F32)


def row_blocks(first, last):
    blocks = [(start, BLOCK) for start in range(first, last - BLOCK, BLOCK)]
    return blocks + [(last - BLOCK, BLOCK // 2), (last - BLOCK // 2, BLOCK // 2)]


def packed(low, high):
    return pick(low, swap(high)), pick(swap(low), high)


def unpacked(first, second):
    return packed(first, second)


def by_side(odd, inner, outer):
    return jnp.where(odd, inner, outer), jnp.where(odd, outer, inner)


def pieces_of(source, target, sems, parts):
    size = target.shape[1] // parts
    return [
        pltpu.make_async_copy(
            source.at[:, pl.ds(i * size, size), :], target.at[:, pl.ds(i * size, size), :], sems.at[i]
        )
        for i in range(parts)
    ]


def pack_body(volume, own, held, sems):
    copies = pieces_of(volume, held, sems, sems.shape[0])
    size = own.shape[0] // len(copies)
    for copy in copies:
        copy.start()
    for i, copy in enumerate(copies):
        copy.wait()
        rows = slice(i * size, i * size + size)
        own[rows, :] = jnp.concatenate([held[0, rows, :], held[1, rows, :]], axis=1)


def leave_body(
    columns, me, far_cotangent, far_weight, own, inner, outer, turned,
    windows, taps, cotangent, weight, sems, sem,
):
    cells = own.shape[0]
    half = cells // 2
    odd = me[0] % 2 == 1
    fetch = pltpu.make_async_copy(far_weight, weight, sem)
    copies = pieces_of(far_cotangent, cotangent, sems, sems.shape[0])
    for copy in copies:
        copy.start()
    fetch.start()
    clear_edges(windows, columns)
    size = cells // len(copies)
    for at, copy in enumerate(copies):
        copy.wait()

        def fill(i, carry):
            start = pl.multiple_of(at * size + i * STEP, STEP)
            for plane in range(2):
                chunk = cotangent[plane, pl.ds(start, STEP), :].astype(F32)
                fill_windows(windows, start, plane * 128, chunk, columns, 256)
            return carry

        lax.fori_loop(0, size // STEP, fill, 0)
    fetch.wait()
    for row in range(3):
        for column in range(3):
            for source in range(2):
                first = row * 768 + column * 256 + source * 128
                for at, target in enumerate(PLANES):
                    depth = depth_tap(source, target)
                    taps[at * 64 : at * 64 + 64, first : first + 128] = (
                        jnp.zeros((64, 128), BF16)
                        if depth is None
                        else weight[(2 - depth) * 9 + (2 - row) * 3 + 2 - column]
                    )
    for start in range(0, half, BLOCK):
        sides = []
        for first in (start, start + half):
            term = window_dot(windows, taps, first, columns, NT)
            own[first : first + BLOCK, :] = term[:, :128]
            sides.append(term[:, 128:])
        upper, lower = packed(*sides)
        near = jnp.where(odd, lower, upper)
        head = near.astype(BF16)
        inner[start : start + BLOCK, :] = head
        inner[half + start : half + start + BLOCK, :] = (near - head.astype(F32)).astype(BF16)
        outer[start : start + BLOCK, :] = jnp.where(odd, upper, lower).astype(BF16)
    for plane in range(2):
        turn(cotangent.at[plane], turned, plane * 128)


def prepare_body(
    columns, me, own, inner, far_weight, own_windows, inner_windows, hidden, outer_taps,
    taps, weight, sem,
):
    fetch = pltpu.make_async_copy(far_weight, weight, sem)
    fetch.start()
    odd = me[0] % 2 == 1

    def fill(i, carry):
        start = pl.multiple_of(i * STEP, STEP)
        rows = pl.ds(start, STEP)
        fill_windows(own_windows, start, 0, own[rows, :].astype(F32), columns, 128)
        fill_windows(inner_windows, start, 0, inner[rows, :].astype(F32), columns, 128)
        return carry

    clear_edges(own_windows, columns)
    clear_edges(inner_windows, columns)
    lax.fori_loop(0, own.shape[0] // STEP, fill, 0)
    fetch.wait()
    zero = jnp.zeros((64, 64), BF16)
    for tap in range(9):

        def kernel_rows(source):
            depths = [depth_tap(source, target) for target in PLANES]
            parts = [zero if d is None else weight[d * 9 + tap] for d in depths]
            return jnp.concatenate(parts, axis=1)

        for at in range(2):
            rows = slice(tap * 128 + at * 64, tap * 128 + at * 64 + 64)
            taps[rows, :] = kernel_rows(at)
            upper, lower = kernel_rows(2 + at).astype(F32), kernel_rows(at - 2).astype(F32)
            first = 9 * 128 + rows.start
            taps[first : first + 64, :] = jnp.where(odd, lower, upper).astype(BF16)
            outer_taps[rows, :] = jnp.where(odd, upper, lower).astype(BF16)
    for start in range(0, own.shape[0], BLOCK):
        rows = row_windows(own_windows, start, columns) + row_windows(inner_windows, start, columns)
        hidden[start : start + BLOCK, :] = jnp.dot(
            jnp.concatenate(rows, axis=1), taps[...], preferred_element_type=F32
        )


def layouts_body(weight, weight_two, back_taps, out_taps, turned_taps):
    zero = jnp.zeros((64, 64), BF16)
    for row in range(3):
        for column in range(3):
            tap = row * 3 + column
            for plane in range(2):
                depths = [depth_tap(source, plane) for source in PLANES]
                parts = [zero if d is None else weight[(2 - d) * 9 + 8 - tap] for d in depths]
                at = row * 128 + plane * 64
                for pair in range(2):
                    first = pair * 384 + column * 128
                    turned_taps[at : at + 64, first : first + 128] = jnp.concatenate(
                        parts[2 * pair : 2 * pair + 2], axis=1
                    )
    back_taps[...] = turned_taps[...].astype(F32).T.astype(BF16)
    for tap in range(9):
        for at, source in enumerate(PLANES):
            first = tap * 256 + at * 64
            for plane in range(2):
                depth = depth_tap(source, plane)
                out_taps[first : first + 64, plane * 128 : plane * 128 + 128] = (
                    jnp.zeros((64, 128), BF16) if depth is None else weight_two[depth * 9 + tap]
                )


def hidden_body(
    columns, count, me, outer, part, outer_taps, inner_windows, act_windows, slope, side_windows,
    outer_windows,
):
    cells = outer.shape[0]

    def fill(i, carry):
        start = pl.multiple_of(i * STEP, STEP)
        chunk = outer[pl.ds(start, STEP), :].astype(F32)
        fill_windows(outer_windows, start, 0, chunk, columns, 128)
        return carry

    clear_edges(outer_windows, columns)
    clear_edges(act_windows, columns)
    lax.fori_loop(0, cells // STEP, fill, 0)
    from_inner = lax.broadcasted_iota(jnp.int32, (16, 128), 1) // 64 == me[0] % 2
    from_inner = jnp.where(from_inner, 1.0, 0.0).astype(BF16)[:1]
    for tap in range(3):
        at = slice(tap * 128, tap * 128 + 128)
        side_windows[:, at] = (
            inner_windows[:, at] * from_inner + outer_windows[:, at] * (1 - from_inner)
        )
    lanes = lax.broadcasted_iota(jnp.int32, (BLOCK, 128), 1)
    edges = [jnp.where(me[0] == end, 0.0, 1.0).astype(F32) for end in (count - 1, 0)]
    inside = jnp.where(lanes < 64, edges[0], edges[1])
    for start in range(0, cells, BLOCK):
        hidden = part[start : start + BLOCK, :]
        hidden = hidden + window_dot(outer_windows, outer_taps, start, columns, NN)
        gate = jax.nn.sigmoid(hidden)
        act = (hidden * gate).astype(BF16).astype(F32)
        fill_windows(act_windows, start, 0, act[:, :128], columns, 256)
        fill_windows(act_windows, start, 128, act[:, 128:] * inside, columns, 256)
        hidden, gate = hidden[:, :128], gate[:, :128]
        slope[start : start + BLOCK, :] = gate * (1.0 + hidden * (1.0 - gate))


def kernel_terms(columns, out_channels, slices, turned, terms):
    for row in range(3):
        for column in range(3):
            tap = row * 3 + column
            product = jnp.dot(turned[...], slices(row, column), preferred_element_type=F32)
            first, second = product[:out_channels], product[out_channels:]
            terms[:, tap * 128 : tap * 128 + 128] = first[:, :128] + swap(
                pick(second[:, 128:], second[:, :128])
            )
            group = 9 + tap // 2
            here = slice(group * 128, group * 128 + 128)
            if tap % 2 == 0:
                terms[:, here] = swap(first[:, 128:]) + second[:, :128]
            else:
                terms[:, here] = pick(terms[:, here], first[:, 128:] + swap(second[:, :128]))


def turn(source, target, first):
    for start in range(0, source.shape[0], STEP):
        chunk = source[start : start + STEP, :].astype(F32)
        target[first : first + chunk.shape[1], start : start + STEP] = chunk.T.astype(BF16)


def grad_two_body(columns, blocks, act_windows, turned, taps, terms, far, output, sems):
    cells = turned.shape[1]
    copies = output_rows(columns, blocks, act_windows, taps, far, output, sems)

    def slices(row, column):
        rows = slice(row * columns, row * columns + cells)
        return act_windows[rows, column * 256 : column * 256 + 256]

    kernel_terms(columns, 128, slices, turned, terms)
    for copy in copies:
        copy.wait()


def coded(value, split):
    head = value.astype(BF16)
    if split == 0:
        return head
    rest = (value[:split] - head[:split].astype(F32)).astype(BF16)
    return jnp.concatenate([head, rest], axis=0)


def decoded(value, split):
    value = value.astype(F32)
    if split == 0:
        return value
    size = value.shape[0] - split
    parts = [value[:split] + value[size:]]
    if split < size:
        parts.append(value[split:size])
    return jnp.concatenate(parts, axis=0)


def grad_one_body(
    columns, count, me, own_windows, side_windows, act_terms, inner, outer, slope, other,
    grad, to_inner, to_outer, message, kept, turned, terms,
):
    cells = grad.shape[0]
    odd = me[0] % 2 == 1
    for start in range(0, cells // 2, STEP):
        low, high = slice(start, start + STEP), slice(start + cells // 2, start + cells // 2 + STEP)
        near = inner[low, :].astype(F32) + inner[high, :].astype(F32)
        arrived = unpacked(*by_side(odd, near, outer[low, :].astype(F32)))
        sides = []
        for rows, extra in zip((low, high), arrived):
            value = ((act_terms[rows, :] + extra) * slope[rows, :]).astype(BF16)
            grad[rows, :] = value
            value = value.astype(F32)
            turned[:, rows] = value.T.astype(BF16)
            sides.append(value)
        lower, upper = packed(*sides)
        to_inner[low, :] = jnp.where(odd, lower, upper).astype(BF16)
        to_outer[low, :] = jnp.where(odd, upper, lower).astype(BF16)
    def slices(row, column):
        rows = slice(row * columns, row * columns + cells)
        lanes = slice(column * 128, column * 128 + 128)
        return jnp.concatenate([own_windows[rows, lanes], side_windows[rows, lanes]], axis=1)

    kernel_terms(columns, 64, slices, turned, terms)
    half = terms.shape[1] // 2
    split = 2 * terms.shape[0] // count

    def share(owner):
        parts = []
        for source in (terms, other):
            each = source.shape[0] // count
            block = source[owner * each : owner * each + each, :]
            parts += [block[:, :half], block[:, half:]]
        return jnp.concatenate(parts, axis=0)

    groups = half // 128
    for pair in range(count // 2):
        even_share, odd_share = share(2 * pair), share(2 * pair + 1)
        kept[pair] = jnp.where(odd, odd_share, even_share)
        given = coded(jnp.where(odd, even_share, odd_share), split)
        size = given.shape[0]
        for group in range(groups):
            first = (pair * groups + group) * size
            message[first : first + size, :] = given[:, group * 128 : group * 128 + 128]


def halve_body(split_in, split_out, owner_bit, at_bit, me, mine, arrived, sent, kept):
    side = (me[0] >> owner_bit) % 2
    size, lanes = mine.shape[1:]
    groups = lanes // 128

    def total(at):
        if len(arrived.shape) == 3:
            return mine[at] + decoded(arrived[at], split_in)
        parts = []
        for group in range(groups):
            rows = size + split_in
            first = pl.multiple_of((at * groups + group) * rows, 8)
            parts.append(decoded(arrived[pl.ds(first, rows), :], split_in))
        return mine[at] + jnp.concatenate(parts, axis=1)

    for at in range(sent.shape[0]):
        high, low = at >> at_bit, at & ((1 << at_bit) - 1)
        keep = ((2 * high + side) << at_bit) + low
        give = ((2 * high + 1 - side) << at_bit) + low
        sent[at] = coded(total(give), split_out)
        kept[at] = total(keep)


def others_of(place, places):
    return [place ^ away for away in [*range(places // 2, places), *range(1, places // 2)]]


def spread_body(split_in, owner_bits, me, mine, arrived, kept, *sent):
    place = 0
    for bit in owner_bits:
        place = 2 * place + (me[0] >> bit) % 2
    kept[...] = mine[place] + decoded(arrived[place], split_in)
    for there, out in zip(others_of(place, mine.shape[0]), sent):
        out[...] = (mine[there] + decoded(arrived[there], split_in)).astype(BF16)


def finish_body(scale, sizes, mine, *refs):
    arrived, (grad_one, grad_two) = refs[:-2], refs[-2:]
    total = mine[...]
    for part in arrived:
        total = total + part[...].astype(F32)
    total = total * scale
    half = total.shape[1]
    first = 0
    for size, out in zip(sizes, (grad_one, grad_two)):
        blocks = (total[first : first + size], total[first + size : first + 2 * size])
        first += 2 * size
        for tap in range(9):
            for depth, group, side in ((0, 9 + tap // 2, tap % 2), (1, tap, 0), (2, tap, 1)):
                lane = group * 128 + side * 64
                block, lane = (blocks[0], lane) if lane < half else (blocks[1], lane - half)
                out[depth * 9 + tap] = block[:, lane : lane + 64]


def output_rows(columns, blocks, act_windows, taps, far, output, sems):
    copies = []
    for at, (start, size) in enumerate(blocks):
        value = window_dot(act_windows, taps, start, columns, NN, size)
        here = slice(start - blocks[0][0], start - blocks[0][0] + size)
        output[0, here, :] = value[:, :128]
        output[1, here, :] = value[:, 128:]
        copies.append(
            pltpu.make_async_copy(
                output.at[:, here, :], far.at[:, start : start + size, :], sems.at[at]
            )
        )
        copies[-1].start()
    return copies


def output_first_body(
    columns, blocks, act_windows, taps, grad, begun, far, own_windows, output, sems
):
    copies = output_rows(columns, blocks, act_windows, taps, far, output, sems)

    def fill(i, carry):
        start = pl.multiple_of(i * STEP, STEP)
        chunk = grad[pl.ds(start, STEP), :].astype(F32)
        fill_windows(own_windows, start, 0, chunk, columns, 128)
        return carry

    clear_edges(own_windows, columns)
    lax.fori_loop(0, grad.shape[0] // STEP, fill, 0)
    for copy in copies:
        copy.wait()


def output_rest_body(columns, blocks, act_windows, taps, begun, far, output, sems):
    for copy in output_rows(columns, blocks, act_windows, taps, far, output, sems):
        copy.wait()


def grad_volume_body(
    columns, me, own_windows, inner, outer, taps, far, side_windows, output, sems
):
    half = outer.shape[0]
    odd = me[0] % 2 == 1

    def fill(i, carry):
        start = pl.multiple_of(i * STEP, STEP)
        rows = pl.ds(start, STEP)
        below, above = by_side(odd, inner[rows, :].astype(F32), outer[rows, :].astype(F32))
        for first, side in zip((start, start + half), unpacked(above, below)):
            fill_windows(side_windows, first, 0, side, columns, 128)
        return carry

    clear_edges(side_windows, columns)
    lax.fori_loop(0, half // STEP, fill, 0)
    copies = []
    for at, (start, size) in enumerate(row_blocks(0, output.shape[1])):
        rows = slice(start, start + size + 2 * columns)
        rows = jnp.concatenate([own_windows[rows, :], side_windows[rows, :]], axis=1)
        terms = jnp.dot(rows, taps[...], preferred_element_type=F32)
        value = terms[:size, :128]
        value = value + terms[columns : columns + size, 128:256]
        value = value + terms[2 * columns : 2 * columns + size, 256:]
        here = slice(start, start + size)
        output[0, here, :] = value[:, :64]
        output[1, here, :] = value[:, 64:]
        copies.append(
            pltpu.make_async_copy(output.at[:, here, :], far.at[:, here, :], sems.at[at])
        )
        copies[-1].start()
    for copy in copies:
        copy.wait()


def shards(volume, weight_one, weight_two, cotangent):
    count = lax.axis_size("space")
    planes, rows, columns, channels = volume.shape
    cells = rows * columns
    scale = 1.0 / math.sqrt(planes * count * cells)
    mid, wide = weight_two.shape[3], weight_two.shape[4]
    me = lax.axis_index("space").astype(jnp.int32).reshape(1)
    shape = jax.ShapeDtypeStruct
    flat, pack = shape((cells, 128), BF16), shape((cells // 2, 128), BF16)
    slab = (cells + 2 * columns, 768)
    windows = pltpu.VMEM(slab, BF16)
    lanes = 14 * 64
    split = 2 * mid // count
    chunk = 2 * (mid + wide) // count

    within = [(i, i ^ 1) for i in range(count)]
    across = [(i, i + 1) for i in range(1, count - 1, 2)]
    across += [(j, i) for i, j in across]

    volume = volume.reshape(planes, cells, channels)
    cotangent = cotangent.reshape(planes, cells, wide)
    weight_one = weight_one.reshape(27, channels, mid)
    weight_two = weight_two.reshape(27, mid, wide)
    one_flops = 2 * planes * cells * 27 * channels * mid
    two_flops = 2 * planes * cells * 27 * mid * wide

    dma = pltpu.SemaphoreType.DMA
    far_one, far_two, far_volume, far_cotangent = (
        pltpu.with_memory_space_constraint(x, pltpu.HBM)
        for x in (weight_one, weight_two, volume, cotangent)
    )
    own, = call(
        pack_body, (flat,), (far_volume,),
        (pltpu.VMEM((planes, cells, channels), BF16), dma((4,))),
        name="pack_volume", apart=(0,),
    )
    vol_outer = lax.ppermute(own, "space", across)
    vol_inner = lax.ppermute(own, "space", within)
    terms, inner, outer, turned = call(
        functools.partial(leave_body, columns),
        (
            shape((cells, 128), F32), flat, pack, shape((256, cells), BF16),
        ),
        (me, far_cotangent, far_two),
        (
            windows, pltpu.VMEM((256, 3 * 768), BF16), pltpu.VMEM(cotangent.shape, BF16),
            pltpu.VMEM(weight_two.shape, BF16), dma((4,)), dma,
        ),
        two_flops, "grad_act_terms", (0,), (1, 2),
    )
    own, terms = lax.optimization_barrier((own, terms))
    third = shape((slab[0], 384), BF16)
    own_windows, inner_windows, part, outer_taps = call(
        functools.partial(prepare_body, columns),
        (third, third, shape((cells, 256), F32), shape((9 * 128, 256), BF16)),
        (me, own, vol_inner, far_one),
        (pltpu.VMEM((2 * 9 * 128, 256), BF16), pltpu.VMEM(weight_one.shape, BF16), dma),
        one_flops, "prepare", (0,), (3,),
    )
    back_taps, out_taps = call(
        layouts_body, (shape((768, 3 * 128), BF16), shape((9 * 256, 256), BF16)),
        (weight_one, weight_two), (pltpu.VMEM((3 * 128, 768), BF16),), one_flops // 8, "layouts",
    )
    inner, outer, part, back_taps, out_taps = lax.optimization_barrier(
        (inner, outer, part, back_taps, out_taps)
    )
    terms_outer = lax.ppermute(outer, "space", across)
    terms_inner = lax.ppermute(inner, "space", within)
    act_windows, slope, side_windows = call(
        functools.partial(hidden_body, columns, count),
        (shape(slab, BF16), shape((cells, 128), F32), third),
        (me, vol_outer, part, outer_taps, inner_windows),
        (pltpu.VMEM((slab[0], 384), BF16),), 2 * one_flops, "hidden", (0,),
    )
    early, middle, late = [(0, BLOCK)], [(BLOCK, BLOCK)], row_blocks(2 * BLOCK, cells)
    whole = shape((planes, cells, wide), F32)
    terms_two, output = call(
        functools.partial(grad_two_body, columns, early),
        (shape((wide, 2 * lanes), F32), whole),
        (act_windows, turned, out_taps),
        (pltpu.VMEM((planes, BLOCK, wide), F32), dma((1,))),
        two_flops, "grad_two_terms", (), (), (1,),
    )
    groups = lanes // 128
    grad_hidden, inner, outer, message, kept = call(
        functools.partial(grad_one_body, columns, count),
        (
            flat, pack, pack,
            shape((count // 2 * groups * (chunk + split), 128), BF16),
            shape((count // 2, chunk, lanes), F32),
        ),
        (
            me, own_windows, side_windows, terms, terms_inner, terms_outer, slope, terms_two,
        ),
        (pltpu.VMEM((128, cells), BF16), pltpu.VMEM((mid, 2 * lanes), F32)),
        one_flops, "grad_one_terms", (0,),
    )
    message = lax.ppermute(message, "space", within)
    output, back_windows = call(
        functools.partial(output_first_body, columns, middle),
        (whole, third),
        (act_windows, out_taps, grad_hidden, output),
        (pltpu.VMEM((planes, BLOCK, wide), F32), dma((1,))),
        two_flops, "output_first", (), (3,), (0,), {3: 0},
    )
    message, output, back_windows = lax.optimization_barrier((message, output, back_windows))
    def halve(bits, bit, split_in, split_out, kept, arrived):
        left = 2 ** (len(bits) - 1)
        sent, kept = call(
            functools.partial(halve_body, split_in, split_out, bit, bits[::-1].index(bit)),
            (shape((left, chunk + split_out, lanes), BF16), shape((left, chunk, lanes), F32)),
            (me, kept, arrived), name="halve", smem=(0,),
        )
        return [b for b in bits if b != bit], sent, kept

    bits = list(range(count.bit_length() - 2, 0, -1))
    bits, sent, kept = halve(bits, 2, split, 0, kept, message)
    sent, act_windows, inner, outer = lax.optimization_barrier((sent, act_windows, inner, outer))
    arrived = lax.ppermute(sent, "space", [(i, i ^ 4) for i in range(count)])
    grad_outer = lax.ppermute(outer, "space", across)
    grad_inner = lax.ppermute(inner, "space", within)
    output, = call(
        functools.partial(output_rest_body, columns, late),
        (whole,),
        (act_windows, out_taps, output),
        (pltpu.VMEM((planes, cells - 2 * BLOCK, wide), F32), dma((len(late),))),
        two_flops, "output_rest", (), (2,), (0,), {2: 0},
    )
    others = 2 ** len(bits) - 1
    mine, *sent = call(
        functools.partial(spread_body, 0, bits),
        (shape((chunk, lanes), F32), *[shape((chunk, lanes), BF16)] * others),
        (me, kept, arrived), flops=16 * two_flops, name="spread", smem=(0,),
    )
    sent, output, back_windows = lax.optimization_barrier((sent, output, back_windows))
    arrived = []
    for at, part in zip(others_of(0, others + 1), sent):
        away = sum((at >> i & 1) << bit for i, bit in enumerate(bits[::-1]))
        arrived.append(lax.ppermute(part, "space", [(i, i ^ away) for i in range(count)]))
    grad_volume, = call(
        functools.partial(grad_volume_body, columns),
        (shape((planes, cells, channels), F32),),
        (me, back_windows, grad_inner, grad_outer, back_taps),
        (
            pltpu.VMEM((slab[0], 384), BF16), pltpu.VMEM((planes, cells, channels), F32),
            dma((cells // BLOCK + 1,)),
        ),
        one_flops, "grad_volume", (0,), (), (0,),
    )
    mine, grad_volume = lax.optimization_barrier((mine, grad_volume))
    grad_one, grad_two = call(
        functools.partial(finish_body, scale, (mid // count, wide // count)),
        (shape((27, mid // count, channels), F32), shape((27, wide // count, mid), F32)),
        (mine, *arrived), name="finish",
    )
    return (
        output.reshape(planes, rows, columns, wide),
        grad_volume.reshape(planes, rows, columns, channels),
        jnp.swapaxes(grad_one, 1, 2).reshape(3, 3, 3, channels, mid // count),
        jnp.swapaxes(grad_two, 1, 2).reshape(3, 3, 3, mid, wide // count),
    )


def solution(mesh):
    cells = P(("groups", "space"), None, None, None)
    kernel = P("groups", None, None, None, "space")
    return jax.shard_map(
        shards,
        mesh=mesh,
        in_specs=(cells, P(), P(), cells),
        out_specs=(cells, cells, kernel, kernel),
        check_vma=False,
    )
```

```python
import functools
import math

import jax
import jax.numpy as jnp
from jax import lax
from jax.experimental import pallas as pl
from jax.experimental.pallas import tpu as pltpu
from jax.sharding import PartitionSpec as P

F32, BF16 = jnp.float32, jnp.bfloat16
STEP, BLOCK = 256, 512
VMEM_LIMIT = 16 * 2**20
NN = (((1,), (0,)), ((), ()))
NT = (((1,), (1,)), ((), ()))

PLANES = (0, 1, 2, -1)


def depth_tap(source, target):
    tap = source - target + 1
    return tap if 0 <= tap <= 2 else None


def call(body, outs, ins, scratch=(), flops=0, name=None, smem=(), apart=(), far=(), alias=None):
    moved = sum(math.prod(s.shape) * s.dtype.itemsize for s in (*outs, *ins))
    return pl.pallas_call(
        body,
        out_shape=list(outs),
        in_specs=[
            pl.BlockSpec(
                memory_space=pltpu.SMEM if i in smem else pl.ANY if i in apart else pltpu.VMEM
            )
            for i in range(len(ins))
        ],
        out_specs=[
            pl.BlockSpec(memory_space=pl.ANY if i in far else pltpu.VMEM) for i in range(len(outs))
        ],
        input_output_aliases=alias or {},
        scratch_shapes=list(scratch),
        compiler_params=pltpu.CompilerParams(vmem_limit_bytes=VMEM_LIMIT),
        cost_estimate=pl.CostEstimate(flops=flops, bytes_accessed=moved, transcendentals=0),
        name=name,
    )(*ins)


def lanes_low(x):
    return lax.broadcasted_iota(jnp.int32, x.shape, 1) < 64


def swap(x):
    return pltpu.roll(x, 64, 1)


def pick(low, high):
    return jnp.where(lanes_low(low), low, high)


def fill_windows(windows, start, lane, chunk, columns, stride):
    size = chunk.shape[0]
    column = lax.broadcasted_iota(jnp.int32, chunk.shape, 0) % columns
    before = jnp.where(column == 0, 0.0, pltpu.roll(chunk, 1, 0))
    after = jnp.where(column == columns - 1, 0.0, pltpu.roll(chunk, size - 1, 0))
    at = pl.ds(pl.multiple_of(columns + start, 32), size)
    for tap, part in enumerate((before, chunk, after)):
        first = tap * stride + lane
        windows[at, first : first + chunk.shape[1]] = part.astype(BF16)


def clear_edges(windows, columns):
    rows, lanes = windows.shape
    windows[0:columns, :] = jnp.zeros((columns, lanes), BF16)
    windows[rows - columns : rows, :] = jnp.zeros((columns, lanes), BF16)


def row_windows(windows, start, columns, size=BLOCK):
    return [
        windows[start + tap * columns : start + tap * columns + size, :] for tap in range(3)
    ]


def window_dot(windows, weights, start, columns, dims, size=BLOCK):
    rows = jnp.concatenate(row_windows(windows, start, columns, size), axis=1)
    return lax.dot_general(rows, weights[...], dims, preferred_element_type=F32)


def row_blocks(first, last):
    blocks = [(start, BLOCK) for start in range(first, last - BLOCK, BLOCK)]
    return blocks + [(last - BLOCK, BLOCK // 2), (last - BLOCK // 2, BLOCK // 2)]


def packed(low, high):
    return pick(low, swap(high)), pick(swap(low), high)


def unpacked(first, second):
    return packed(first, second)


def by_side(odd, inner, outer):
    return jnp.where(odd, inner, outer), jnp.where(odd, outer, inner)


def pieces_of(source, target, sems, parts):
    size = target.shape[1] // parts
    return [
        pltpu.make_async_copy(
            source.at[:, pl.ds(i * size, size), :], target.at[:, pl.ds(i * size, size), :], sems.at[i]
        )
        for i in range(parts)
    ]


def pack_body(volume, own, held, sems):
    copies = pieces_of(volume, held, sems, sems.shape[0])
    size = own.shape[0] // len(copies)
    for copy in copies:
        copy.start()
    for i, copy in enumerate(copies):
        copy.wait()
        rows = slice(i * size, i * size + size)
        own[rows, :] = jnp.concatenate([held[0, rows, :], held[1, rows, :]], axis=1)


def leave_body(
    columns, me, far_cotangent, far_weight, own, inner, outer, turned,
    windows, taps, cotangent, weight, sems, sem,
):
    cells = own.shape[0]
    half = cells // 2
    odd = me[0] % 2 == 1
    fetch = pltpu.make_async_copy(far_weight, weight, sem)
    copies = pieces_of(far_cotangent, cotangent, sems, sems.shape[0])
    for copy in copies:
        copy.start()
    fetch.start()
    clear_edges(windows, columns)
    size = cells // len(copies)
    for at, copy in enumerate(copies):
        copy.wait()

        def fill(i, carry):
            start = pl.multiple_of(at * size + i * STEP, STEP)
            for plane in range(2):
                chunk = cotangent[plane, pl.ds(start, STEP), :].astype(F32)
                fill_windows(windows, start, plane * 128, chunk, columns, 256)
            return carry

        lax.fori_loop(0, size // STEP, fill, 0)
    fetch.wait()
    for row in range(3):
        for column in range(3):
            for source in range(2):
                first = row * 768 + column * 256 + source * 128
                for at, target in enumerate(PLANES):
                    depth = depth_tap(source, target)
                    taps[at * 64 : at * 64 + 64, first : first + 128] = (
                        jnp.zeros((64, 128), BF16)
                        if depth is None
                        else weight[(2 - depth) * 9 + (2 - row) * 3 + 2 - column]
                    )
    for start in range(0, half, BLOCK):
        sides = []
        for first in (start, start + half):
            term = window_dot(windows, taps, first, columns, NT)
            own[first : first + BLOCK, :] = term[:, :128]
            sides.append(term[:, 128:])
        upper, lower = packed(*sides)
        near = jnp.where(odd, lower, upper)
        head = near.astype(BF16)
        inner[start : start + BLOCK, :] = head
        inner[half + start : half + start + BLOCK, :] = (near - head.astype(F32)).astype(BF16)
        outer[start : start + BLOCK, :] = jnp.where(odd, upper, lower).astype(BF16)
    for plane in range(2):
        turn(cotangent.at[plane], turned, plane * 128)


def prepare_body(
    columns, me, own, inner, far_weight, own_windows, inner_windows, hidden, outer_taps,
    taps, weight, sem,
):
    fetch = pltpu.make_async_copy(far_weight, weight, sem)
    fetch.start()
    odd = me[0] % 2 == 1

    def fill(i, carry):
        start = pl.multiple_of(i * STEP, STEP)
        rows = pl.ds(start, STEP)
        fill_windows(own_windows, start, 0, own[rows, :].astype(F32), columns, 128)
        fill_windows(inner_windows, start, 0, inner[rows, :].astype(F32), columns, 128)
        return carry

    clear_edges(own_windows, columns)
    clear_edges(inner_windows, columns)
    lax.fori_loop(0, own.shape[0] // STEP, fill, 0)
    fetch.wait()
    zero = jnp.zeros((64, 64), BF16)
    for tap in range(9):

        def kernel_rows(source):
            depths = [depth_tap(source, target) for target in PLANES]
            parts = [zero if d is None else weight[d * 9 + tap] for d in depths]
            return jnp.concatenate(parts, axis=1)

        for at in range(2):
            rows = slice(tap * 128 + at * 64, tap * 128 + at * 64 + 64)
            taps[rows, :] = kernel_rows(at)
            upper, lower = kernel_rows(2 + at).astype(F32), kernel_rows(at - 2).astype(F32)
            first = 9 * 128 + rows.start
            taps[first : first + 64, :] = jnp.where(odd, lower, upper).astype(BF16)
            outer_taps[rows, :] = jnp.where(odd, upper, lower).astype(BF16)
    for start in range(0, own.shape[0], BLOCK):
        rows = row_windows(own_windows, start, columns) + row_windows(inner_windows, start, columns)
        hidden[start : start + BLOCK, :] = jnp.dot(
            jnp.concatenate(rows, axis=1), taps[...], preferred_element_type=F32
        )


def layouts_body(weight, weight_two, back_taps, out_taps, turned_taps):
    zero = jnp.zeros((64, 64), BF16)
    for row in range(3):
        for column in range(3):
            tap = row * 3 + column
            for plane in range(2):
                depths = [depth_tap(source, plane) for source in PLANES]
                parts = [zero if d is None else weight[(2 - d) * 9 + 8 - tap] for d in depths]
                at = row * 128 + plane * 64
                for pair in range(2):
                    first = pair * 384 + column * 128
                    turned_taps[at : at + 64, first : first + 128] = jnp.concatenate(
                        parts[2 * pair : 2 * pair + 2], axis=1
                    )
    back_taps[...] = turned_taps[...].astype(F32).T.astype(BF16)
    for tap in range(9):
        for at, source in enumerate(PLANES):
            first = tap * 256 + at * 64
            for plane in range(2):
                depth = depth_tap(source, plane)
                out_taps[first : first + 64, plane * 128 : plane * 128 + 128] = (
                    jnp.zeros((64, 128), BF16) if depth is None else weight_two[depth * 9 + tap]
                )


def hidden_body(
    columns, count, me, outer, part, outer_taps, inner_windows, act_windows, slope, side_windows,
    outer_windows,
):
    cells = outer.shape[0]

    def fill(i, carry):
        start = pl.multiple_of(i * STEP, STEP)
        chunk = outer[pl.ds(start, STEP), :].astype(F32)
        fill_windows(outer_windows, start, 0, chunk, columns, 128)
        return carry

    clear_edges(outer_windows, columns)
    clear_edges(act_windows, columns)
    lax.fori_loop(0, cells // STEP, fill, 0)
    from_inner = lax.broadcasted_iota(jnp.int32, (16, 128), 1) // 64 == me[0] % 2
    from_inner = jnp.where(from_inner, 1.0, 0.0).astype(BF16)[:1]
    for tap in range(3):
        at = slice(tap * 128, tap * 128 + 128)
        side_windows[:, at] = (
            inner_windows[:, at] * from_inner + outer_windows[:, at] * (1 - from_inner)
        )
    lanes = lax.broadcasted_iota(jnp.int32, (BLOCK, 128), 1)
    edges = [jnp.where(me[0] == end, 0.0, 1.0).astype(F32) for end in (count - 1, 0)]
    inside = jnp.where(lanes < 64, edges[0], edges[1])
    for start in range(0, cells, BLOCK):
        hidden = part[start : start + BLOCK, :]
        hidden = hidden + window_dot(outer_windows, outer_taps, start, columns, NN)
        gate = jax.nn.sigmoid(hidden)
        act = (hidden * gate).astype(BF16).astype(F32)
        fill_windows(act_windows, start, 0, act[:, :128], columns, 256)
        fill_windows(act_windows, start, 128, act[:, 128:] * inside, columns, 256)
        hidden, gate = hidden[:, :128], gate[:, :128]
        slope[start : start + BLOCK, :] = gate * (1.0 + hidden * (1.0 - gate))


def kernel_terms(columns, out_channels, slices, turned, terms):
    for row in range(3):
        for column in range(3):
            tap = row * 3 + column
            product = jnp.dot(turned[...], slices(row, column), preferred_element_type=F32)
            first, second = product[:out_channels], product[out_channels:]
            terms[:, tap * 128 : tap * 128 + 128] = first[:, :128] + swap(
                pick(second[:, 128:], second[:, :128])
            )
            group = 9 + tap // 2
            here = slice(group * 128, group * 128 + 128)
            if tap % 2 == 0:
                terms[:, here] = swap(first[:, 128:]) + second[:, :128]
            else:
                terms[:, here] = pick(terms[:, here], first[:, 128:] + swap(second[:, :128]))


def turn(source, target, first):
    for start in range(0, source.shape[0], STEP):
        chunk = source[start : start + STEP, :].astype(F32)
        target[first : first + chunk.shape[1], start : start + STEP] = chunk.T.astype(BF16)


def grad_two_body(columns, blocks, act_windows, turned, taps, terms, far, output, sems):
    cells = turned.shape[1]
    copies = output_rows(columns, blocks, act_windows, taps, far, output, sems)

    def slices(row, column):
        rows = slice(row * columns, row * columns + cells)
        return act_windows[rows, column * 256 : column * 256 + 256]

    kernel_terms(columns, 128, slices, turned, terms)
    for copy in copies:
        copy.wait()


def coded(value, split):
    head = value.astype(BF16)
    if split == 0:
        return head
    rest = (value[:split] - head[:split].astype(F32)).astype(BF16)
    return jnp.concatenate([head, rest], axis=0)


def decoded(value, split):
    value = value.astype(F32)
    if split == 0:
        return value
    size = value.shape[0] - split
    parts = [value[:split] + value[size:]]
    if split < size:
        parts.append(value[split:size])
    return jnp.concatenate(parts, axis=0)


def grad_one_body(
    columns, count, me, own_windows, side_windows, act_terms, inner, outer, slope, other,
    grad, to_inner, to_outer, message, kept, turned, terms,
):
    cells = grad.shape[0]
    odd = me[0] % 2 == 1
    for start in range(0, cells // 2, STEP):
        low, high = slice(start, start + STEP), slice(start + cells // 2, start + cells // 2 + STEP)
        near = inner[low, :].astype(F32) + inner[high, :].astype(F32)
        arrived = unpacked(*by_side(odd, near, outer[low, :].astype(F32)))
        sides = []
        for rows, extra in zip((low, high), arrived):
            value = ((act_terms[rows, :] + extra) * slope[rows, :]).astype(BF16)
            grad[rows, :] = value
            value = value.astype(F32)
            turned[:, rows] = value.T.astype(BF16)
            sides.append(value)
        lower, upper = packed(*sides)
        to_inner[low, :] = jnp.where(odd, lower, upper).astype(BF16)
        to_outer[low, :] = jnp.where(odd, upper, lower).astype(BF16)
    def slices(row, column):
        rows = slice(row * columns, row * columns + cells)
        lanes = slice(column * 128, column * 128 + 128)
        return jnp.concatenate([own_windows[rows, lanes], side_windows[rows, lanes]], axis=1)

    kernel_terms(columns, 64, slices, turned, terms)
    half = terms.shape[1] // 2
    split = 2 * terms.shape[0] // count

    def share(owner):
        parts = []
        for source in (terms, other):
            each = source.shape[0] // count
            block = source[owner * each : owner * each + each, :]
            parts += [block[:, :half], block[:, half:]]
        return jnp.concatenate(parts, axis=0)

    groups = half // 128
    for pair in range(count // 2):
        even_share, odd_share = share(2 * pair), share(2 * pair + 1)
        kept[pair] = jnp.where(odd, odd_share, even_share)
        given = coded(jnp.where(odd, even_share, odd_share), split)
        size = given.shape[0]
        for group in range(groups):
            first = (pair * groups + group) * size
            message[first : first + size, :] = given[:, group * 128 : group * 128 + 128]


def halve_body(split_in, split_out, owner_bit, at_bit, me, mine, arrived, sent, kept):
    side = (me[0] >> owner_bit) % 2
    size, lanes = mine.shape[1:]
    groups = lanes // 128

    def total(at):
        if len(arrived.shape) == 3:
            return mine[at] + decoded(arrived[at], split_in)
        parts = []
        for group in range(groups):
            rows = size + split_in
            first = pl.multiple_of((at * groups + group) * rows, 8)
            parts.append(decoded(arrived[pl.ds(first, rows), :], split_in))
        return mine[at] + jnp.concatenate(parts, axis=1)

    for at in range(sent.shape[0]):
        high, low = at >> at_bit, at & ((1 << at_bit) - 1)
        keep = ((2 * high + side) << at_bit) + low
        give = ((2 * high + 1 - side) << at_bit) + low
        sent[at] = coded(total(give), split_out)
        kept[at] = total(keep)


def others_of(place, places):
    return [place ^ away for away in [*range(places // 2, places), *range(1, places // 2)]]


def spread_body(split_in, owner_bits, me, mine, arrived, kept, *sent):
    place = 0
    for bit in owner_bits:
        place = 2 * place + (me[0] >> bit) % 2
    kept[...] = mine[place] + decoded(arrived[place], split_in)
    for there, out in zip(others_of(place, mine.shape[0]), sent):
        out[...] = (mine[there] + decoded(arrived[there], split_in)).astype(BF16)


def finish_body(scale, sizes, mine, *refs):
    arrived, (grad_one, grad_two) = refs[:-2], refs[-2:]
    total = mine[...]
    for part in arrived:
        total = total + part[...].astype(F32)
    total = total * scale
    half = total.shape[1]
    first = 0
    for size, out in zip(sizes, (grad_one, grad_two)):
        blocks = (total[first : first + size], total[first + size : first + 2 * size])
        first += 2 * size
        for tap in range(9):
            for depth, group, side in ((0, 9 + tap // 2, tap % 2), (1, tap, 0), (2, tap, 1)):
                lane = group * 128 + side * 64
                block, lane = (blocks[0], lane) if lane < half else (blocks[1], lane - half)
                out[depth * 9 + tap] = block[:, lane : lane + 64]


def output_rows(columns, blocks, act_windows, taps, far, output, sems):
    copies = []
    for at, (start, size) in enumerate(blocks):
        value = window_dot(act_windows, taps, start, columns, NN, size)
        here = slice(start - blocks[0][0], start - blocks[0][0] + size)
        output[0, here, :] = value[:, :128]
        output[1, here, :] = value[:, 128:]
        copies.append(
            pltpu.make_async_copy(
                output.at[:, here, :], far.at[:, start : start + size, :], sems.at[at]
            )
        )
        copies[-1].start()
    return copies


def output_first_body(
    columns, blocks, act_windows, taps, grad, begun, far, own_windows, output, sems
):
    copies = output_rows(columns, blocks, act_windows, taps, far, output, sems)

    def fill(i, carry):
        start = pl.multiple_of(i * STEP, STEP)
        chunk = grad[pl.ds(start, STEP), :].astype(F32)
        fill_windows(own_windows, start, 0, chunk, columns, 128)
        return carry

    clear_edges(own_windows, columns)
    lax.fori_loop(0, grad.shape[0] // STEP, fill, 0)
    for copy in copies:
        copy.wait()


def output_rest_body(columns, blocks, act_windows, taps, begun, far, output, sems):
    for copy in output_rows(columns, blocks, act_windows, taps, far, output, sems):
        copy.wait()


def grad_volume_body(
    columns, me, own_windows, inner, outer, taps, far, side_windows, output, sems
):
    half = outer.shape[0]
    odd = me[0] % 2 == 1

    def fill(i, carry):
        start = pl.multiple_of(i * STEP, STEP)
        rows = pl.ds(start, STEP)
        below, above = by_side(odd, inner[rows, :].astype(F32), outer[rows, :].astype(F32))
        for first, side in zip((start, start + half), unpacked(above, below)):
            fill_windows(side_windows, first, 0, side, columns, 128)
        return carry

    clear_edges(side_windows, columns)
    lax.fori_loop(0, half // STEP, fill, 0)
    copies = []
    for at, (start, size) in enumerate(row_blocks(0, output.shape[1])):
        rows = slice(start, start + size + 2 * columns)
        rows = jnp.concatenate([own_windows[rows, :], side_windows[rows, :]], axis=1)
        terms = jnp.dot(rows, taps[...], preferred_element_type=F32)
        value = terms[:size, :128]
        value = value + terms[columns : columns + size, 128:256]
        value = value + terms[2 * columns : 2 * columns + size, 256:]
        here = slice(start, start + size)
        output[0, here, :] = value[:, :64]
        output[1, here, :] = value[:, 64:]
        copies.append(
            pltpu.make_async_copy(output.at[:, here, :], far.at[:, here, :], sems.at[at])
        )
        copies[-1].start()
    for copy in copies:
        copy.wait()


def shards(volume, weight_one, weight_two, cotangent):
    count = lax.axis_size("space")
    planes, rows, columns, channels = volume.shape
    cells = rows * columns
    scale = 1.0 / math.sqrt(planes * count * cells)
    mid, wide = weight_two.shape[3], weight_two.shape[4]
    me = lax.axis_index("space").astype(jnp.int32).reshape(1)
    shape = jax.ShapeDtypeStruct
    flat, pack = shape((cells, 128), BF16), shape((cells // 2, 128), BF16)
    slab = (cells + 2 * columns, 768)
    windows = pltpu.VMEM(slab, BF16)
    lanes = 14 * 64
    split = 2 * mid // count
    chunk = 2 * (mid + wide) // count

    within = [(i, i ^ 1) for i in range(count)]
    across = [(i, i + 1) for i in range(1, count - 1, 2)]
    across += [(j, i) for i, j in across]

    volume = volume.reshape(planes, cells, channels)
    cotangent = cotangent.reshape(planes, cells, wide)
    weight_one = weight_one.reshape(27, channels, mid)
    weight_two = weight_two.reshape(27, mid, wide)
    one_flops = 2 * planes * cells * 27 * channels * mid
    two_flops = 2 * planes * cells * 27 * mid * wide

    dma = pltpu.SemaphoreType.DMA
    far_one, far_two, far_volume, far_cotangent = (
        pltpu.with_memory_space_constraint(x, pltpu.HBM)
        for x in (weight_one, weight_two, volume, cotangent)
    )
    own, = call(
        pack_body, (flat,), (far_volume,),
        (pltpu.VMEM((planes, cells, channels), BF16), dma((4,))),
        name="pack_volume", apart=(0,),
    )
    vol_outer = lax.ppermute(own, "space", across)
    vol_inner = lax.ppermute(own, "space", within)
    terms, inner, outer, turned = call(
        functools.partial(leave_body, columns),
        (
            shape((cells, 128), F32), flat, pack, shape((256, cells), BF16),
        ),
        (me, far_cotangent, far_two),
        (
            windows, pltpu.VMEM((256, 3 * 768), BF16), pltpu.VMEM(cotangent.shape, BF16),
            pltpu.VMEM(weight_two.shape, BF16), dma((4,)), dma,
        ),
        two_flops, "grad_act_terms", (0,), (1, 2),
    )
    own, terms = lax.optimization_barrier((own, terms))
    third = shape((slab[0], 384), BF16)
    own_windows, inner_windows, part, outer_taps = call(
        functools.partial(prepare_body, columns),
        (third, third, shape((cells, 256), F32), shape((9 * 128, 256), BF16)),
        (me, own, vol_inner, far_one),
        (pltpu.VMEM((2 * 9 * 128, 256), BF16), pltpu.VMEM(weight_one.shape, BF16), dma),
        one_flops, "prepare", (0,), (3,),
    )
    back_taps, out_taps = call(
        layouts_body, (shape((768, 3 * 128), BF16), shape((9 * 256, 256), BF16)),
        (weight_one, weight_two), (pltpu.VMEM((3 * 128, 768), BF16),), one_flops // 8, "layouts",
    )
    inner, outer, part, back_taps, out_taps = lax.optimization_barrier(
        (inner, outer, part, back_taps, out_taps)
    )
    terms_outer = lax.ppermute(outer, "space", across)
    terms_inner = lax.ppermute(inner, "space", within)
    act_windows, slope, side_windows = call(
        functools.partial(hidden_body, columns, count),
        (shape(slab, BF16), shape((cells, 128), F32), third),
        (me, vol_outer, part, outer_taps, inner_windows),
        (pltpu.VMEM((slab[0], 384), BF16),), 2 * one_flops, "hidden", (0,),
    )
    early, middle, late = [(0, BLOCK)], [(BLOCK, BLOCK)], row_blocks(2 * BLOCK, cells)
    whole = shape((planes, cells, wide), F32)
    terms_two, output = call(
        functools.partial(grad_two_body, columns, early),
        (shape((wide, 2 * lanes), F32), whole),
        (act_windows, turned, out_taps),
        (pltpu.VMEM((planes, BLOCK, wide), F32), dma((1,))),
        two_flops, "grad_two_terms", (), (), (1,),
    )
    groups = lanes // 128
    grad_hidden, inner, outer, message, kept = call(
        functools.partial(grad_one_body, columns, count),
        (
            flat, pack, pack,
            shape((count // 2 * groups * (chunk + split), 128), BF16),
            shape((count // 2, chunk, lanes), F32),
        ),
        (
            me, own_windows, side_windows, terms, terms_inner, terms_outer, slope, terms_two,
        ),
        (pltpu.VMEM((128, cells), BF16), pltpu.VMEM((mid, 2 * lanes), F32)),
        one_flops, "grad_one_terms", (0,),
    )
    message = lax.ppermute(message, "space", within)
    output, back_windows = call(
        functools.partial(output_first_body, columns, middle),
        (whole, third),
        (act_windows, out_taps, grad_hidden, output),
        (pltpu.VMEM((planes, BLOCK, wide), F32), dma((1,))),
        two_flops, "output_first", (), (3,), (0,), {3: 0},
    )
    message, output, back_windows = lax.optimization_barrier((message, output, back_windows))
    def halve(bits, bit, split_in, split_out, kept, arrived):
        left = 2 ** (len(bits) - 1)
        sent, kept = call(
            functools.partial(halve_body, split_in, split_out, bit, bits[::-1].index(bit)),
            (shape((left, chunk + split_out, lanes), BF16), shape((left, chunk, lanes), F32)),
            (me, kept, arrived), name="halve", smem=(0,),
        )
        return [b for b in bits if b != bit], sent, kept

    bits = list(range(count.bit_length() - 2, 0, -1))
    bits, sent, kept = halve(bits, 2, split, 0, kept, message)
    sent, act_windows, outer = lax.optimization_barrier((sent, act_windows, outer))
    arrived = lax.ppermute(sent, "space", [(i, i ^ 4) for i in range(count)])
    grad_outer = lax.ppermute(outer, "space", across)
    output, = call(
        functools.partial(output_rest_body, columns, late),
        (whole,),
        (act_windows, out_taps, output),
        (pltpu.VMEM((planes, cells - 2 * BLOCK, wide), F32), dma((len(late),))),
        two_flops, "output_rest", (), (2,), (0,), {2: 0},
    )
    others = 2 ** len(bits) - 1
    mine, *sent = call(
        functools.partial(spread_body, 0, bits),
        (shape((chunk, lanes), F32), *[shape((chunk, lanes), BF16)] * others),
        (me, kept, arrived), flops=16 * two_flops, name="spread", smem=(0,),
    )
    sent, output, back_windows, inner = lax.optimization_barrier(
        (sent, output, back_windows, inner)
    )
    grad_inner = lax.ppermute(inner, "space", within)
    arrived = []
    for at, part in zip(others_of(0, others + 1), sent):
        away = sum((at >> i & 1) << bit for i, bit in enumerate(bits[::-1]))
        arrived.append(lax.ppermute(part, "space", [(i, i ^ away) for i in range(count)]))
    grad_volume, = call(
        functools.partial(grad_volume_body, columns),
        (shape((planes, cells, channels), F32),),
        (me, back_windows, grad_inner, grad_outer, back_taps),
        (
            pltpu.VMEM((slab[0], 384), BF16), pltpu.VMEM((planes, cells, channels), F32),
            dma((cells // BLOCK + 1,)),
        ),
        one_flops, "grad_volume", (0,), (), (0,),
    )
    mine, grad_volume = lax.optimization_barrier((mine, grad_volume))
    grad_one, grad_two = call(
        functools.partial(finish_body, scale, (mid // count, wide // count)),
        (shape((27, mid // count, channels), F32), shape((27, wide // count, mid), F32)),
        (mine, *arrived), name="finish",
    )
    return (
        output.reshape(planes, rows, columns, wide),
        grad_volume.reshape(planes, rows, columns, channels),
        jnp.swapaxes(grad_one, 1, 2).reshape(3, 3, 3, channels, mid // count),
        jnp.swapaxes(grad_two, 1, 2).reshape(3, 3, 3, mid, wide // count),
    )


def solution(mesh):
    cells = P(("groups", "space"), None, None, None)
    kernel = P("groups", None, None, None, "space")
    return jax.shard_map(
        shards,
        mesh=mesh,
        in_specs=(cells, P(), P(), cells),
        out_specs=(cells, cells, kernel, kernel),
        check_vma=False,
    )
```

```python
import functools
import math

import jax
import jax.numpy as jnp
from jax import lax
from jax.experimental import pallas as pl
from jax.experimental.pallas import tpu as pltpu
from jax.sharding import PartitionSpec as P

F32, BF16 = jnp.float32, jnp.bfloat16
STEP, BLOCK = 256, 512
VMEM_LIMIT = 16 * 2**20
NN = (((1,), (0,)), ((), ()))
NT = (((1,), (1,)), ((), ()))

PLANES = (0, 1, 2, -1)


def depth_tap(source, target):
    tap = source - target + 1
    return tap if 0 <= tap <= 2 else None


def call(body, outs, ins, scratch=(), flops=0, name=None, smem=(), apart=(), far=(), alias=None):
    moved = sum(math.prod(s.shape) * s.dtype.itemsize for s in (*outs, *ins))
    return pl.pallas_call(
        body,
        out_shape=list(outs),
        in_specs=[
            pl.BlockSpec(
                memory_space=pltpu.SMEM if i in smem else pl.ANY if i in apart else pltpu.VMEM
            )
            for i in range(len(ins))
        ],
        out_specs=[
            pl.BlockSpec(memory_space=pl.ANY if i in far else pltpu.VMEM) for i in range(len(outs))
        ],
        input_output_aliases=alias or {},
        scratch_shapes=list(scratch),
        compiler_params=pltpu.CompilerParams(vmem_limit_bytes=VMEM_LIMIT),
        cost_estimate=pl.CostEstimate(flops=flops, bytes_accessed=moved, transcendentals=0),
        name=name,
    )(*ins)


def lanes_low(x):
    return lax.broadcasted_iota(jnp.int32, x.shape, 1) < 64


def swap(x):
    return pltpu.roll(x, 64, 1)


def pick(low, high):
    return jnp.where(lanes_low(low), low, high)


def fill_windows(windows, start, lane, chunk, columns, stride):
    size = chunk.shape[0]
    column = lax.broadcasted_iota(jnp.int32, chunk.shape, 0) % columns
    before = jnp.where(column == 0, 0.0, pltpu.roll(chunk, 1, 0))
    after = jnp.where(column == columns - 1, 0.0, pltpu.roll(chunk, size - 1, 0))
    at = pl.ds(pl.multiple_of(columns + start, 32), size)
    for tap, part in enumerate((before, chunk, after)):
        first = tap * stride + lane
        windows[at, first : first + chunk.shape[1]] = part.astype(BF16)


def clear_edges(windows, columns):
    rows, lanes = windows.shape
    windows[0:columns, :] = jnp.zeros((columns, lanes), BF16)
    windows[rows - columns : rows, :] = jnp.zeros((columns, lanes), BF16)


def row_windows(windows, start, columns, size=BLOCK):
    return [
        windows[start + tap * columns : start + tap * columns + size, :] for tap in range(3)
    ]


def window_dot(windows, weights, start, columns, dims, size=BLOCK):
    rows = jnp.concatenate(row_windows(windows, start, columns, size), axis=1)
    return lax.dot_general(rows, weights[...], dims, preferred_element_type=F32)


def row_blocks(first, last):
    blocks = [(start, BLOCK) for start in range(first, last - BLOCK, BLOCK)]
    return blocks + [(last - BLOCK, BLOCK // 2), (last - BLOCK // 2, BLOCK // 2)]


def packed(low, high):
    return pick(low, swap(high)), pick(swap(low), high)


def unpacked(first, second):
    return packed(first, second)


def by_side(odd, inner, outer):
    return jnp.where(odd, inner, outer), jnp.where(odd, outer, inner)


def pieces_of(source, target, sems, parts):
    size = target.shape[1] // parts
    return [
        pltpu.make_async_copy(
            source.at[:, pl.ds(i * size, size), :], target.at[:, pl.ds(i * size, size), :], sems.at[i]
        )
        for i in range(parts)
    ]


def pack_body(volume, own, held, sems):
    copies = pieces_of(volume, held, sems, sems.shape[0])
    size = own.shape[0] // len(copies)
    for copy in copies:
        copy.start()
    for i, copy in enumerate(copies):
        copy.wait()
        rows = slice(i * size, i * size + size)
        own[rows, :] = jnp.concatenate([held[0, rows, :], held[1, rows, :]], axis=1)


def leave_body(
    columns, me, far_cotangent, far_weight, own, inner, outer, turned,
    windows, taps, cotangent, weight, sems, sem,
):
    cells = own.shape[0]
    half = cells // 2
    odd = me[0] % 2 == 1
    fetch = pltpu.make_async_copy(far_weight, weight, sem)
    copies = pieces_of(far_cotangent, cotangent, sems, sems.shape[0])
    for copy in copies:
        copy.start()
    fetch.start()
    clear_edges(windows, columns)
    size = cells // len(copies)
    for at, copy in enumerate(copies):
        copy.wait()

        def fill(i, carry):
            start = pl.multiple_of(at * size + i * STEP, STEP)
            for plane in range(2):
                chunk = cotangent[plane, pl.ds(start, STEP), :].astype(F32)
                fill_windows(windows, start, plane * 128, chunk, columns, 256)
            return carry

        lax.fori_loop(0, size // STEP, fill, 0)
    fetch.wait()
    for row in range(3):
        for column in range(3):
            for source in range(2):
                first = row * 768 + column * 256 + source * 128
                for at, target in enumerate(PLANES):
                    depth = depth_tap(source, target)
                    taps[at * 64 : at * 64 + 64, first : first + 128] = (
                        jnp.zeros((64, 128), BF16)
                        if depth is None
                        else weight[(2 - depth) * 9 + (2 - row) * 3 + 2 - column]
                    )
    for start in range(0, half, BLOCK):
        sides = []
        for first in (start, start + half):
            term = window_dot(windows, taps, first, columns, NT)
            own[first : first + BLOCK, :] = term[:, :128]
            sides.append(term[:, 128:])
        upper, lower = packed(*sides)
        near = jnp.where(odd, lower, upper)
        head = near.astype(BF16)
        inner[start : start + BLOCK, :] = head
        inner[half + start : half + start + BLOCK, :] = (near - head.astype(F32)).astype(BF16)
        outer[start : start + BLOCK, :] = jnp.where(odd, upper, lower).astype(BF16)
    for plane in range(2):
        turn(cotangent.at[plane], turned, plane * 128)


def prepare_body(
    columns, me, own, inner, far_weight, own_windows, inner_windows, hidden, outer_taps,
    taps, weight, sem,
):
    fetch = pltpu.make_async_copy(far_weight, weight, sem)
    fetch.start()
    odd = me[0] % 2 == 1

    def fill(i, carry):
        start = pl.multiple_of(i * STEP, STEP)
        rows = pl.ds(start, STEP)
        fill_windows(own_windows, start, 0, own[rows, :].astype(F32), columns, 128)
        fill_windows(inner_windows, start, 0, inner[rows, :].astype(F32), columns, 128)
        return carry

    clear_edges(own_windows, columns)
    clear_edges(inner_windows, columns)
    lax.fori_loop(0, own.shape[0] // STEP, fill, 0)
    fetch.wait()
    zero = jnp.zeros((64, 64), BF16)
    for tap in range(9):

        def kernel_rows(source):
            depths = [depth_tap(source, target) for target in PLANES]
            parts = [zero if d is None else weight[d * 9 + tap] for d in depths]
            return jnp.concatenate(parts, axis=1)

        for at in range(2):
            rows = slice(tap * 128 + at * 64, tap * 128 + at * 64 + 64)
            taps[rows, :] = kernel_rows(at)
            upper, lower = kernel_rows(2 + at).astype(F32), kernel_rows(at - 2).astype(F32)
            first = 9 * 128 + rows.start
            taps[first : first + 64, :] = jnp.where(odd, lower, upper).astype(BF16)
            outer_taps[rows, :] = jnp.where(odd, upper, lower).astype(BF16)
    for start in range(0, own.shape[0], BLOCK):
        rows = row_windows(own_windows, start, columns) + row_windows(inner_windows, start, columns)
        hidden[start : start + BLOCK, :] = jnp.dot(
            jnp.concatenate(rows, axis=1), taps[...], preferred_element_type=F32
        )


def back_taps_body(weight, back_taps, turned_taps):
    zero = jnp.zeros((64, 64), BF16)
    for row in range(3):
        for column in range(3):
            tap = row * 3 + column
            for plane in range(2):
                depths = [depth_tap(source, plane) for source in PLANES]
                parts = [zero if d is None else weight[(2 - d) * 9 + 8 - tap] for d in depths]
                at = row * 128 + plane * 64
                for pair in range(2):
                    first = pair * 384 + column * 128
                    turned_taps[at : at + 64, first : first + 128] = jnp.concatenate(
                        parts[2 * pair : 2 * pair + 2], axis=1
                    )
    back_taps[...] = turned_taps[...].astype(F32).T.astype(BF16)


def hidden_body(
    columns, count, me, outer, part, outer_taps, inner_windows, act_windows, slope, side_windows,
    outer_windows,
):
    cells = outer.shape[0]

    def fill(i, carry):
        start = pl.multiple_of(i * STEP, STEP)
        chunk = outer[pl.ds(start, STEP), :].astype(F32)
        fill_windows(outer_windows, start, 0, chunk, columns, 128)
        return carry

    clear_edges(outer_windows, columns)
    clear_edges(act_windows, columns)
    lax.fori_loop(0, cells // STEP, fill, 0)
    from_inner = lax.broadcasted_iota(jnp.int32, (16, 128), 1) // 64 == me[0] % 2
    from_inner = jnp.where(from_inner, 1.0, 0.0).astype(BF16)[:1]
    for tap in range(3):
        at = slice(tap * 128, tap * 128 + 128)
        side_windows[:, at] = (
            inner_windows[:, at] * from_inner + outer_windows[:, at] * (1 - from_inner)
        )
    lanes = lax.broadcasted_iota(jnp.int32, (BLOCK, 128), 1)
    edges = [jnp.where(me[0] == end, 0.0, 1.0).astype(F32) for end in (count - 1, 0)]
    inside = jnp.where(lanes < 64, edges[0], edges[1])
    for start in range(0, cells, BLOCK):
        hidden = part[start : start + BLOCK, :]
        hidden = hidden + window_dot(outer_windows, outer_taps, start, columns, NN)
        gate = jax.nn.sigmoid(hidden)
        act = (hidden * gate).astype(BF16).astype(F32)
        fill_windows(act_windows, start, 0, act[:, :128], columns, 256)
        fill_windows(act_windows, start, 128, act[:, 128:] * inside, columns, 256)
        hidden, gate = hidden[:, :128], gate[:, :128]
        slope[start : start + BLOCK, :] = gate * (1.0 + hidden * (1.0 - gate))


def kernel_terms(columns, out_channels, slices, turned, terms):
    for row in range(3):
        for column in range(3):
            tap = row * 3 + column
            product = jnp.dot(turned[...], slices(row, column), preferred_element_type=F32)
            first, second = product[:out_channels], product[out_channels:]
            terms[:, tap * 128 : tap * 128 + 128] = first[:, :128] + swap(
                pick(second[:, 128:], second[:, :128])
            )
            group = 9 + tap // 2
            here = slice(group * 128, group * 128 + 128)
            if tap % 2 == 0:
                terms[:, here] = swap(first[:, 128:]) + second[:, :128]
            else:
                terms[:, here] = pick(terms[:, here], first[:, 128:] + swap(second[:, :128]))


def turn(source, target, first):
    for start in range(0, source.shape[0], STEP):
        chunk = source[start : start + STEP, :].astype(F32)
        target[first : first + chunk.shape[1], start : start + STEP] = chunk.T.astype(BF16)


def grad_two_body(columns, act_windows, turned, terms):
    cells = turned.shape[1]

    def slices(row, column):
        rows = slice(row * columns, row * columns + cells)
        return act_windows[rows, column * 256 : column * 256 + 256]

    kernel_terms(columns, 128, slices, turned, terms)


def coded(value, split):
    head = value.astype(BF16)
    if split == 0:
        return head
    rest = (value[:split] - head[:split].astype(F32)).astype(BF16)
    return jnp.concatenate([head, rest], axis=0)


def decoded(value, split):
    value = value.astype(F32)
    if split == 0:
        return value
    size = value.shape[0] - split
    parts = [value[:split] + value[size:]]
    if split < size:
        parts.append(value[split:size])
    return jnp.concatenate(parts, axis=0)


def grad_one_body(
    columns, count, me, own_windows, side_windows, act_terms, inner, outer, slope, other,
    grad, to_outer, message, kept, turned, terms,
):
    cells = grad.shape[0]
    odd = me[0] % 2 == 1
    before = message.shape[0] - cells // 2
    for start in range(0, cells // 2, STEP):
        low, high = slice(start, start + STEP), slice(start + cells // 2, start + cells // 2 + STEP)
        near = inner[low, :].astype(F32) + inner[high, :].astype(F32)
        arrived = unpacked(*by_side(odd, near, outer[low, :].astype(F32)))
        sides = []
        for rows, extra in zip((low, high), arrived):
            value = ((act_terms[rows, :] + extra) * slope[rows, :]).astype(BF16)
            grad[rows, :] = value
            value = value.astype(F32)
            turned[:, rows] = value.T.astype(BF16)
            sides.append(value)
        lower, upper = packed(*sides)
        message[before + start : before + start + STEP, :] = jnp.where(
            odd, lower, upper
        ).astype(BF16)
        to_outer[low, :] = jnp.where(odd, upper, lower).astype(BF16)
    def slices(row, column):
        rows = slice(row * columns, row * columns + cells)
        lanes = slice(column * 128, column * 128 + 128)
        return jnp.concatenate([own_windows[rows, lanes], side_windows[rows, lanes]], axis=1)

    kernel_terms(columns, 64, slices, turned, terms)
    half = terms.shape[1] // 2
    split = 2 * terms.shape[0] // count

    def share(owner):
        parts = []
        for source in (terms, other):
            each = source.shape[0] // count
            block = source[owner * each : owner * each + each, :]
            parts += [block[:, :half], block[:, half:]]
        return jnp.concatenate(parts, axis=0)

    groups = half // 128
    for pair in range(count // 2):
        even_share, odd_share = share(2 * pair), share(2 * pair + 1)
        kept[pair] = jnp.where(odd, odd_share, even_share)
        given = coded(jnp.where(odd, even_share, odd_share), split)
        size = given.shape[0]
        for group in range(groups):
            first = (pair * groups + group) * size
            message[first : first + size, :] = given[:, group * 128 : group * 128 + 128]


def halve_body(split_in, split_out, owner_bit, at_bit, me, mine, arrived, sent, kept):
    side = (me[0] >> owner_bit) % 2
    size, lanes = mine.shape[1:]
    groups = lanes // 128

    def total(at):
        if len(arrived.shape) == 3:
            return mine[at] + decoded(arrived[at], split_in)
        parts = []
        for group in range(groups):
            rows = size + split_in
            first = pl.multiple_of((at * groups + group) * rows, 8)
            parts.append(decoded(arrived[pl.ds(first, rows), :], split_in))
        return mine[at] + jnp.concatenate(parts, axis=1)

    for at in range(sent.shape[0]):
        high, low = at >> at_bit, at & ((1 << at_bit) - 1)
        keep = ((2 * high + side) << at_bit) + low
        give = ((2 * high + 1 - side) << at_bit) + low
        sent[at] = coded(total(give), split_out)
        kept[at] = total(keep)


def others_of(place, places):
    return [place ^ away for away in [*range(places // 2, places), *range(1, places // 2)]]


def spread_body(split_in, owner_bits, me, mine, arrived, kept, *sent):
    place = 0
    for bit in owner_bits:
        place = 2 * place + (me[0] >> bit) % 2
    kept[...] = mine[place] + decoded(arrived[place], split_in)
    for there, out in zip(others_of(place, mine.shape[0]), sent):
        out[...] = (mine[there] + decoded(arrived[there], split_in)).astype(BF16)


def finish_body(scale, sizes, mine, *refs):
    arrived, (grad_one, grad_two) = refs[:-2], refs[-2:]
    total = mine[...]
    for part in arrived:
        total = total + part[...].astype(F32)
    total = total * scale
    half = total.shape[1]
    first = 0
    for size, out in zip(sizes, (grad_one, grad_two)):
        blocks = (total[first : first + size], total[first + size : first + 2 * size])
        first += 2 * size
        for tap in range(9):
            for depth, group, side in ((0, 9 + tap // 2, tap % 2), (1, tap, 0), (2, tap, 1)):
                lane = group * 128 + side * 64
                block, lane = (blocks[0], lane) if lane < half else (blocks[1], lane - half)
                out[depth * 9 + tap] = block[:, lane : lane + 64]


def output_rows(columns, blocks, act_windows, taps, far, output, sems):
    copies = []
    for at, (start, size) in enumerate(blocks):
        value = window_dot(act_windows, taps, start, columns, NN, size)
        here = slice(start - blocks[0][0], start - blocks[0][0] + size)
        output[0, here, :] = value[:, :128]
        output[1, here, :] = value[:, 128:]
        copies.append(
            pltpu.make_async_copy(
                output.at[:, here, :], far.at[:, start : start + size, :], sems.at[at]
            )
        )
        copies[-1].start()
    return copies


def output_first_body(
    columns, blocks, act_windows, weight, grad, far, taps, own_windows, output, sems
):
    for row in range(3):
        for column in range(3):
            for at, source in enumerate(PLANES):
                first = row * 768 + column * 256 + at * 64
                for plane in range(2):
                    depth = depth_tap(source, plane)
                    taps[first : first + 64, plane * 128 : plane * 128 + 128] = (
                        jnp.zeros((64, 128), BF16)
                        if depth is None
                        else weight[depth * 9 + row * 3 + column]
                    )
    copies = output_rows(columns, blocks, act_windows, taps, far, output, sems)

    def fill(i, carry):
        start = pl.multiple_of(i * STEP, STEP)
        chunk = grad[pl.ds(start, STEP), :].astype(F32)
        fill_windows(own_windows, start, 0, chunk, columns, 128)
        return carry

    clear_edges(own_windows, columns)
    lax.fori_loop(0, grad.shape[0] // STEP, fill, 0)
    for copy in copies:
        copy.wait()


def output_rest_body(columns, blocks, act_windows, taps, begun, far, output, sems):
    for copy in output_rows(columns, blocks, act_windows, taps, far, output, sems):
        copy.wait()


def grad_windows_body(columns, me, message, outer, windows):
    half = outer.shape[0]
    odd = me[0] % 2 == 1
    before = message.shape[0] - half

    def fill(i, carry):
        start = pl.multiple_of(i * STEP, STEP)
        near = message[pl.ds(before + start, STEP), :].astype(F32)
        below, above = by_side(odd, near, outer[pl.ds(start, STEP), :].astype(F32))
        for first, side in zip((start, start + half), unpacked(above, below)):
            fill_windows(windows, first, 0, side, columns, 128)
        return carry

    clear_edges(windows, columns)
    lax.fori_loop(0, half // STEP, fill, 0)


def grad_volume_body(columns, own_windows, side_windows, taps, far, output, sems):
    copies = []
    for at, (start, size) in enumerate(row_blocks(0, output.shape[1])):
        rows = slice(start, start + size + 2 * columns)
        rows = jnp.concatenate([own_windows[rows, :], side_windows[rows, :]], axis=1)
        terms = jnp.dot(rows, taps[...], preferred_element_type=F32)
        value = terms[:size, :128]
        value = value + terms[columns : columns + size, 128:256]
        value = value + terms[2 * columns : 2 * columns + size, 256:]
        here = slice(start, start + size)
        output[0, here, :] = value[:, :64]
        output[1, here, :] = value[:, 64:]
        copies.append(
            pltpu.make_async_copy(output.at[:, here, :], far.at[:, here, :], sems.at[at])
        )
        copies[-1].start()
    for copy in copies:
        copy.wait()


def shards(volume, weight_one, weight_two, cotangent):
    count = lax.axis_size("space")
    planes, rows, columns, channels = volume.shape
    cells = rows * columns
    scale = 1.0 / math.sqrt(planes * count * cells)
    mid, wide = weight_two.shape[3], weight_two.shape[4]
    me = lax.axis_index("space").astype(jnp.int32).reshape(1)
    shape = jax.ShapeDtypeStruct
    flat, pack = shape((cells, 128), BF16), shape((cells // 2, 128), BF16)
    slab = (cells + 2 * columns, 768)
    windows = pltpu.VMEM(slab, BF16)
    lanes = 14 * 64
    split = 2 * mid // count
    chunk = 2 * (mid + wide) // count

    within = [(i, i ^ 1) for i in range(count)]
    across = [(i, i + 1) for i in range(1, count - 1, 2)]
    across += [(j, i) for i, j in across]

    volume = volume.reshape(planes, cells, channels)
    cotangent = cotangent.reshape(planes, cells, wide)
    weight_one = weight_one.reshape(27, channels, mid)
    weight_two = weight_two.reshape(27, mid, wide)
    one_flops = 2 * planes * cells * 27 * channels * mid
    two_flops = 2 * planes * cells * 27 * mid * wide

    dma = pltpu.SemaphoreType.DMA
    far_one, far_two, far_volume, far_cotangent = (
        pltpu.with_memory_space_constraint(x, pltpu.HBM)
        for x in (weight_one, weight_two, volume, cotangent)
    )
    own, = call(
        pack_body, (flat,), (far_volume,),
        (pltpu.VMEM((planes, cells, channels), BF16), dma((8,))),
        name="pack_volume", apart=(0,),
    )
    vol_outer = lax.ppermute(own, "space", across)
    vol_inner = lax.ppermute(own, "space", within)
    terms, inner, outer, turned = call(
        functools.partial(leave_body, columns),
        (
            shape((cells, 128), F32), flat, pack, shape((256, cells), BF16),
        ),
        (me, far_cotangent, far_two),
        (
            windows, pltpu.VMEM((256, 3 * 768), BF16), pltpu.VMEM(cotangent.shape, BF16),
            pltpu.VMEM(weight_two.shape, BF16), dma((4,)), dma,
        ),
        two_flops, "grad_act_terms", (0,), (1, 2),
    )
    own, terms = lax.optimization_barrier((own, terms))
    third = shape((slab[0], 384), BF16)
    own_windows, inner_windows, part, outer_taps = call(
        functools.partial(prepare_body, columns),
        (third, third, shape((cells, 256), F32), shape((9 * 128, 256), BF16)),
        (me, own, vol_inner, far_one),
        (pltpu.VMEM((2 * 9 * 128, 256), BF16), pltpu.VMEM(weight_one.shape, BF16), dma),
        one_flops, "prepare", (0,), (3,),
    )
    back_taps, = call(
        back_taps_body, (shape((768, 3 * 128), BF16),), (weight_one,),
        (pltpu.VMEM((3 * 128, 768), BF16),), one_flops // 8, "back_taps",
    )
    inner, outer, part, back_taps = lax.optimization_barrier((inner, outer, part, back_taps))
    terms_outer = lax.ppermute(outer, "space", across)
    terms_inner = lax.ppermute(inner, "space", within)
    act_windows, slope, side_windows = call(
        functools.partial(hidden_body, columns, count),
        (shape(slab, BF16), shape((cells, 128), F32), third),
        (me, vol_outer, part, outer_taps, inner_windows),
        (pltpu.VMEM((slab[0], 384), BF16),), 2 * one_flops, "hidden", (0,),
    )
    terms_two, = call(
        functools.partial(grad_two_body, columns),
        (shape((wide, 2 * lanes), F32),),
        (act_windows, turned), (), two_flops, "grad_two_terms",
    )
    groups = lanes // 128
    grad_hidden, outer, message, kept = call(
        functools.partial(grad_one_body, columns, count),
        (
            flat, pack,
            shape((count // 2 * groups * (chunk + split) + cells // 2, 128), BF16),
            shape((count // 2, chunk, lanes), F32),
        ),
        (
            me, own_windows, side_windows, terms, terms_inner, terms_outer, slope, terms_two,
        ),
        (pltpu.VMEM((128, cells), BF16), pltpu.VMEM((mid, 2 * lanes), F32)),
        one_flops, "grad_one_terms", (0,),
    )
    message = lax.ppermute(message, "space", within)
    rest = row_blocks(BLOCK, cells)
    output, out_taps, back_windows = call(
        functools.partial(output_first_body, columns, [(0, BLOCK)]),
        (shape((planes, cells, wide), F32), shape((9 * 256, 256), BF16), third),
        (act_windows, weight_two, grad_hidden),
        (pltpu.VMEM((planes, BLOCK, wide), F32), dma((1,))),
        two_flops, "output_first", (), (), (0,),
    )
    message, output, out_taps, back_windows = lax.optimization_barrier(
        (message, output, out_taps, back_windows)
    )
    def halve(bits, bit, split_in, split_out, kept, arrived):
        left = 2 ** (len(bits) - 1)
        sent, kept = call(
            functools.partial(halve_body, split_in, split_out, bit, bits[::-1].index(bit)),
            (shape((left, chunk + split_out, lanes), BF16), shape((left, chunk, lanes), F32)),
            (me, kept, arrived), name="halve", smem=(0,),
        )
        return [b for b in bits if b != bit], sent, kept

    bits = list(range(count.bit_length() - 2, 0, -1))
    bits, sent, kept = halve(bits, 2, split, 0, kept, message)
    sent, act_windows, outer = lax.optimization_barrier((sent, act_windows, outer))
    arrived = lax.ppermute(sent, "space", [(i, i ^ 4) for i in range(count)])
    grad_outer = lax.ppermute(outer, "space", across)
    output, = call(
        functools.partial(output_rest_body, columns, rest),
        (shape((planes, cells, wide), F32),),
        (act_windows, out_taps, output),
        (pltpu.VMEM((planes, cells - BLOCK, wide), F32), dma((len(rest),))),
        two_flops, "output_rest", (), (2,), (0,), {2: 0},
    )
    others = 2 ** len(bits) - 1
    mine, *sent = call(
        functools.partial(spread_body, 0, bits),
        (shape((chunk, lanes), F32), *[shape((chunk, lanes), BF16)] * others),
        (me, kept, arrived), flops=16 * two_flops, name="spread", smem=(0,),
    )
    sent, output, back_windows = lax.optimization_barrier((sent, output, back_windows))
    arrived = []
    for at, part in zip(others_of(0, others + 1), sent):
        away = sum((at >> i & 1) << bit for i, bit in enumerate(bits[::-1]))
        arrived.append(lax.ppermute(part, "space", [(i, i ^ away) for i in range(count)]))
    grad_windows, = call(
        functools.partial(grad_windows_body, columns), (third,), (me, message, grad_outer),
        (), one_flops // 4, "grad_windows", (0,),
    )
    grad_volume, = call(
        functools.partial(grad_volume_body, columns),
        (shape((planes, cells, channels), F32),),
        (back_windows, grad_windows, back_taps),
        (pltpu.VMEM((planes, cells, channels), F32), dma((cells // BLOCK + 1,))),
        one_flops, "grad_volume", (), (), (0,),
    )
    mine, grad_volume = lax.optimization_barrier((mine, grad_volume))
    grad_one, grad_two = call(
        functools.partial(finish_body, scale, (mid // count, wide // count)),
        (shape((27, mid // count, channels), F32), shape((27, wide // count, mid), F32)),
        (mine, *arrived), name="finish",
    )
    return (
        output.reshape(planes, rows, columns, wide),
        grad_volume.reshape(planes, rows, columns, channels),
        jnp.swapaxes(grad_one, 1, 2).reshape(3, 3, 3, channels, mid // count),
        jnp.swapaxes(grad_two, 1, 2).reshape(3, 3, 3, mid, wide // count),
    )


def solution(mesh):
    cells = P(("groups", "space"), None, None, None)
    kernel = P("groups", None, None, None, "space")
    return jax.shard_map(
        shards,
        mesh=mesh,
        in_specs=(cells, P(), P(), cells),
        out_specs=(cells, cells, kernel, kernel),
        check_vma=False,
    )
```
